32 devices in a mesh: dp: 8 (over y, x, core), tensor: 4 (over z).
Axes of the slice: x: 2, y: 2, z: 4, core: 2. Of those that a mesh axis runs over, the one named last changes fastest.
Arguments:
- tokens: bfloat16 [8, 1024, 2048], P('dp', 'tensor'), may hold values from -6 to 6
- seq_lengths: int32 [8, 4], P('dp'), may hold values from 0 to 1024, as said below
- attention_gain: bfloat16 [2048], P('dp'), may hold values from 0.5 to 1.5
- query_matrix: bfloat16 [2048, 2048], P('dp', 'tensor'), may hold values from -0.125 to 0.125
- key_matrix: bfloat16 [2048, 512], P('dp', 'tensor'), may hold values from -0.125 to 0.125
- value_matrix: bfloat16 [2048, 512], P('dp', 'tensor'), may hold values from -0.125 to 0.125
- output_weight: bfloat16 [2048, 2048], P('tensor', 'dp'), may hold values from -0.5 to 0.5
- feedforward_gain: bfloat16 [2048], P('dp'), may hold values from 0.5 to 1.5
- gate_weight: bfloat16 [2048, 8192], P('dp', 'tensor'), may hold values from -0.125 to 0.125
- up_weight: bfloat16 [2048, 8192], P('dp', 'tensor'), may hold values from -0.125 to 0.125
- down_weight: bfloat16 [8192, 2048], P('tensor', 'dp'), may hold values from -0.0625 to 0.0625
- cotangent: bfloat16 [8, 1024, 2048], P('dp', 'tensor'), may hold values from -6 to 6
Outputs:
- block_output: bfloat16 [8, 1024, 2048], P('dp', 'tensor')
- input_gradient: float32 [8, 1024, 2048], P('dp', 'tensor')
- attention_gain_gradient: float32 [2048], P('dp')
- query_weight_gradient: float32 [2048, 2048], P('dp', 'tensor')
- key_weight_gradient: float32 [2048, 512], P('dp', 'tensor')
- value_weight_gradient: float32 [2048, 512], P('dp', 'tensor')
- output_weight_gradient: float32 [2048, 2048], P('tensor', 'dp')
- feedforward_gain_gradient: float32 [2048], P('dp')
- gate_weight_gradient: float32 [2048, 8192], P('dp', 'tensor')
- up_weight_gradient: float32 [2048, 8192], P('dp', 'tensor')
- down_weight_gradient: float32 [8192, 2048], P('tensor', 'dp')
The draws below stay inside these ranges and needn't reach their ends.
Inputs may be any that keep to these rules, and one draw needn't show every extreme that they name: `seq_lengths`: each row lists the lengths of 4 documents packed from the start of one slot of 1024 positions; a length may be 0 and a row sums to at most 1024. Row g belongs to data group g (one slot per group); in every group one slot's first document is longer than 896, and some slot's first document has exactly 1024 tokens.
All inputs are finite; a program needn't handle non-finite values.
Results may differ from the reference program's by a relative error of at most 0.023.
Values may be sent and summed in bfloat16 or wider, within the bound.
No kernel may reach another device: no remote copies, remote signals or barrier semaphores. Data moves between devices by JAX's collectives and lax.ppermute only.
A program may use at most 256 MiB of HBM per device.

```python
import math
import jax
import jax.numpy as jnp
from jax import lax

MODEL_DIM = 2048
QUERY_HEADS = 32
KEY_VALUE_HEADS = 8
HEAD_SIZE = 64
FF = 8192
SEQ_LEN = 1024
PIECES = 4
SLOTS = 1
SLOT_ALL = 8


def draw_seq_lengths(key, part):
    key = jax.random.fold_in(key, 7)
    group_count = SLOT_ALL // SLOTS
    key_list = jax.random.split(key, 6)
    main_slot = jax.random.randint(key_list[0], (group_count,), 0, SLOTS)
    leading = SEQ_LEN - jax.random.randint(key_list[1], (group_count,), 0, SEQ_LEN // 8)
    full_group = jax.random.randint(key_list[2], (), 0, group_count)
    leading = jnp.where(jnp.arange(group_count) == full_group, SEQ_LEN, leading)
    slot_index = jnp.arange(SLOT_ALL)
    is_main = slot_index % SLOTS == jnp.repeat(main_slot, SLOTS)
    leading_all = jnp.repeat(leading, SLOTS)
    other_fill = jax.random.randint(key_list[3], (SLOT_ALL,), SEQ_LEN // 4, SEQ_LEN + 1)
    rest_fill = jax.random.randint(key_list[4], (SLOT_ALL,), 0, SEQ_LEN - leading_all + 1)
    filled = jnp.where(is_main, rest_fill, other_fill).astype(jnp.int32)
    cut_points = jnp.sort(jax.random.randint(key_list[5], (SLOT_ALL, PIECES - 1), 0, filled[:, None] + 1), axis=1)
    edges = jnp.concatenate([jnp.zeros((SLOT_ALL, 1), jnp.int32), cut_points.astype(jnp.int32), filled[:, None]], axis=1)
    pieces = edges[:, 1:] - edges[:, :-1]
    main_rows = jnp.concatenate([leading_all[:, None].astype(jnp.int32), pieces[:, :PIECES - 2], jnp.sum(pieces[:, PIECES - 2:], axis=1, keepdims=True)], axis=1)
    return jnp.where(is_main[:, None], main_rows, pieces).astype(jnp.int32)


def strengthened(result, rng, source, target, blocks, factor):
    owner, partner = [(jnp.arange(result.shape[position]) // (result.shape[position] // blocks)).reshape([-1 if axis == position else 1 for axis in range(result.ndim)]) for position in (source, target)]
    chosen = jax.random.permutation(rng, blocks)[partner]
    strong = (owner == chosen) | (owner == (partner + blocks // 2) % blocks)
    return jnp.where(strong, factor * result, result)


def block_levels(own_key, dims, cuts, low, top_value):
    gain = 1.0
    for position, shards_of in cuts:
        steps = jax.random.uniform(jax.random.fold_in(jax.random.fold_in(own_key, 6), position), (shards_of,), jnp.float32, low / len(cuts), top_value / len(cuts))
        gain = gain * jnp.repeat(jnp.exp(steps), dims[position] // shards_of).reshape((-1,) + (1,) * (len(dims) - 1 - position))
    return gain


def normal_values(rng, dims, scale, limit, cuts=(), kind=jnp.bfloat16):
    array = jax.random.normal(rng, dims, jnp.float32) * scale
    if len(cuts) > 0:
        array = block_levels(rng, dims, cuts, -0.22, 0.18) * array
    return jnp.clip(array, min=-limit, max=limit).astype(kind)


def bell_draw_with(rng, dims, scale, limit, cuts, heavy, kind=jnp.bfloat16):
    entries = scale * jax.random.normal(rng, dims, jnp.float32)
    if cuts:
        entries = entries * block_levels(rng, dims, cuts, -0.22, 0.18)
    return jnp.clip(strengthened(entries, jax.random.fold_in(rng, 3), *heavy), -limit, limit).astype(kind)


def setup_inputs(seed: int = 0) -> dict:
    keys = jax.random.split(jax.random.key(seed), 13)
    return {
        "tokens": normal_values(keys[0], (SLOT_ALL, SEQ_LEN, MODEL_DIM), 1.0, 6.0, ((0, 8), (1, 4))),
        "seq_lengths": draw_seq_lengths(jax.random.fold_in(keys[12], 71), 0),
        "attention_gain": jnp.clip(1.0 + 0.1 * jax.random.normal(keys[2], (MODEL_DIM,), jnp.float32), 0.5, 1.5).astype(jnp.bfloat16),
        "query_matrix": normal_values(keys[3], (MODEL_DIM, QUERY_HEADS * HEAD_SIZE), MODEL_DIM ** -0.5, 0.125, ((0, 8), (1, 4))),
        "key_matrix": normal_values(keys[4], (MODEL_DIM, KEY_VALUE_HEADS * HEAD_SIZE), MODEL_DIM ** -0.5, 0.125, ((0, 8), (1, 4))),
        "value_matrix": normal_values(keys[5], (MODEL_DIM, KEY_VALUE_HEADS * HEAD_SIZE), MODEL_DIM ** -0.5, 0.125, ((0, 8), (1, 4))),
        "output_weight": normal_values(keys[6], (QUERY_HEADS * HEAD_SIZE, MODEL_DIM), (QUERY_HEADS * HEAD_SIZE // 16) ** -0.5, 0.5, ((0, 4), (1, 8))),
        "feedforward_gain": jnp.clip(1.0 + 0.1 * jax.random.normal(keys[7], (MODEL_DIM,), jnp.float32), 0.5, 1.5).astype(jnp.bfloat16),
        "gate_weight": normal_values(keys[8], (MODEL_DIM, FF), MODEL_DIM ** -0.5, 0.125, ((0, 8), (1, 4))),
        "up_weight": normal_values(keys[9], (MODEL_DIM, FF), MODEL_DIM ** -0.5, 0.125, ((0, 8), (1, 4))),
        "down_weight": normal_values(keys[10], (FF, MODEL_DIM), FF ** -0.5, 0.0625, ((0, 4), (1, 8))),
        "cotangent": bell_draw_with(keys[11], (SLOT_ALL, SEQ_LEN, MODEL_DIM), 1.0, 6.0, ((0, 8), (1, 4)), (0, 2, 8, 2.0)),
    }


@jax.custom_vjp
def reduced_precision(v):
    return lax.optimization_barrier(v.astype(jnp.bfloat16)).astype(jnp.float32)

@jax.custom_vjp
def reduced_backward(v):
    return v

def low_keep(v):
    return (reduced_precision(v), None)

def low_pass(kept, grad):
    return (grad,)

def back_keep(v):
    return (v, None)

def back_low(kept, grad):
    return (reduced_precision(grad),)
reduced_precision.defvjp(low_keep, low_pass)
reduced_backward.defvjp(back_keep, back_low)
EPSILON = 1e-05
ROPE_BASE = 500000.0
NEGATIVE = -1e+30

def exact_precision(left, right):
    return jnp.dot(left, right, precision=lax.Precision.HIGHEST)

def layout(lengths, complete_rows):
    doc_ends = jnp.cumsum(lengths, axis=-1).astype(jnp.int32)
    row_index = jnp.arange(complete_rows, dtype=jnp.int32)
    piece_count = lengths.shape[-1]
    doc_ids = lax.optimization_barrier(jnp.sum((row_index[None, :, None] >= doc_ends[:, None, :]).astype(jnp.int32), axis=2)).astype(jnp.int32)
    starts = (doc_ends - lengths).astype(jnp.int32)
    chosen = doc_ids[:, :, None] == jnp.arange(piece_count, dtype=jnp.int32)[None, None, :]
    doc_begin = lax.optimization_barrier(jnp.sum(jnp.where(chosen, starts[:, None, :], 0), axis=2)) + jnp.where(doc_ids == piece_count, doc_ends[:, -1:], 0)
    return (doc_ids, (row_index[None, :] - doc_begin).astype(jnp.int32))

def rope_tables(positions, head_dim):
    half_dim = head_dim // 2
    frequency = ROPE_BASE ** (-(jnp.arange(half_dim, dtype=jnp.float32) * (2.0 / head_dim)))
    angles = positions.astype(jnp.float32)[..., None] * frequency
    return (jnp.cos(angles), jnp.sin(angles))

def rotate(vectors, cosine, sine):
    half_dim = vectors.shape[-1] // 2
    first_half = vectors[..., :half_dim]
    second_half = vectors[..., half_dim:]
    return jnp.concatenate([first_half * cosine - second_half * sine, second_half * cosine + first_half * sine], axis=-1)

def rms_scale(values, scale_row):
    return values * lax.rsqrt(lax.optimization_barrier(jnp.mean(values * values, axis=-1, keepdims=True)) + EPSILON) * scale_row

def attend(query_rows, key_rows, value_rows, doc_ids):
    complete_rows = query_rows.shape[0]
    position_ids = jnp.arange(complete_rows, dtype=jnp.int32)
    same_doc = doc_ids[:, None] == doc_ids[None, :]
    causal = position_ids[None, :] <= position_ids[:, None]
    own_row = position_ids[None, :] == position_ids[:, None]
    allowed = same_doc & causal & ((doc_ids[:, None] < PIECES) | own_row)

    def one_head(head_items):
        query_head, key_head, value_head = head_items
        scores = reduced_backward(jnp.einsum('qgd,kd->gqk', query_head, key_head, precision=lax.Precision.HIGHEST) * HEAD_SIZE ** (-0.5))
        scores = jnp.where(allowed[None], scores, NEGATIVE)
        row_peak = lax.optimization_barrier(jnp.max(scores, axis=-1, keepdims=True))
        exp_scores = jnp.exp(scores - row_peak)
        soft_probs = exp_scores / lax.optimization_barrier(jnp.sum(exp_scores, axis=-1, keepdims=True))
        return jnp.einsum('gqk,kd->qgd', reduced_precision(soft_probs), value_head, precision=lax.Precision.HIGHEST)
    head_outputs = lax.map(one_head, (jnp.moveaxis(query_rows, 1, 0), jnp.moveaxis(key_rows, 1, 0), jnp.moveaxis(value_rows, 1, 0)))
    return jnp.moveaxis(head_outputs, 0, 1).reshape(complete_rows, QUERY_HEADS * HEAD_SIZE)

def bunch_layer(inputs, lengths, weights):
    attention_gain, query_matrix, key_matrix, value_matrix, output_weight, feedforward_gain, gate_weight, up_weight, down_weight = weights
    bundle_count, complete_rows, model_width = inputs.shape
    group_width = QUERY_HEADS // KEY_VALUE_HEADS
    doc_ids, positions = layout(lengths, complete_rows)
    cosine, sine = rope_tables(positions, HEAD_SIZE)
    normed_one = reduced_precision(rms_scale(inputs, attention_gain))
    flattened_first = normed_one.reshape(bundle_count * complete_rows, model_width)
    query_linear = reduced_backward(exact_precision(flattened_first, query_matrix)).reshape(bundle_count, complete_rows, KEY_VALUE_HEADS, group_width, HEAD_SIZE)
    query_rot = reduced_precision(rotate(query_linear, cosine[:, :, None, None], sine[:, :, None, None]))
    key_linear = reduced_backward(exact_precision(flattened_first, key_matrix)).reshape(bundle_count, complete_rows, KEY_VALUE_HEADS, HEAD_SIZE)
    key_rot = reduced_precision(rotate(key_linear, cosine[:, :, None], sine[:, :, None]))
    value_every_head = reduced_precision(reduced_backward(exact_precision(flattened_first, value_matrix))).reshape(bundle_count, complete_rows, KEY_VALUE_HEADS, HEAD_SIZE)
    attended = jax.vmap(attend)(query_rot, key_rot, value_every_head, doc_ids)
    attended = reduced_precision(reduced_backward(attended)).reshape(bundle_count * complete_rows, QUERY_HEADS * HEAD_SIZE)
    branch_one = reduced_backward(exact_precision(attended, output_weight)).reshape(bundle_count, complete_rows, model_width)
    hidden_res = inputs + branch_one
    normed_two = reduced_precision(rms_scale(hidden_res, feedforward_gain))
    flat_two = normed_two.reshape(bundle_count * complete_rows, model_width)
    gate_lin = reduced_backward(exact_precision(flat_two, gate_weight))
    up_lin = reduced_backward(exact_precision(flat_two, up_weight))
    product = reduced_precision(jax.nn.silu(gate_lin) * up_lin)
    branch_two = reduced_backward(exact_precision(product, down_weight)).reshape(bundle_count, complete_rows, model_width)
    return hidden_res + branch_two

def reference(tokens, seq_lengths, attention_gain, query_matrix, key_matrix, value_matrix, output_weight, feedforward_gain, gate_weight, up_weight, down_weight, cotangent):
    bundle_count = math.gcd(SLOT_ALL, max(1, 4096 // SEQ_LEN))
    step_count = SLOT_ALL // bundle_count
    weights = (attention_gain.astype(jnp.float32), query_matrix.astype(jnp.float32), key_matrix.astype(jnp.float32), value_matrix.astype(jnp.float32), output_weight.astype(jnp.float32), feedforward_gain.astype(jnp.float32), gate_weight.astype(jnp.float32), up_weight.astype(jnp.float32), down_weight.astype(jnp.float32))
    inputs = tokens.astype(jnp.float32).reshape(step_count, bundle_count, SEQ_LEN, MODEL_DIM)
    lengths = seq_lengths.reshape(step_count, bundle_count, PIECES)

    def forward(layer_inputs, layer_weights):

        def layer_step(step_items):
            return bunch_layer(step_items[0], step_items[1], layer_weights)
        return lax.map(jax.checkpoint(layer_step), (layer_inputs, lengths))
    outputs, pullback = jax.vjp(forward, inputs, weights)
    grad_inputs, grad_weights = pullback(cotangent.astype(jnp.float32).reshape(outputs.shape))
    return (outputs.reshape(SLOT_ALL, SEQ_LEN, MODEL_DIM).astype(jnp.bfloat16), grad_inputs.reshape(SLOT_ALL, SEQ_LEN, MODEL_DIM), grad_weights[0], grad_weights[1], grad_weights[2], grad_weights[3], grad_weights[4], grad_weights[5], grad_weights[6], grad_weights[7], grad_weights[8])
```

```python
import jax
import jax.numpy as jnp
from jax import lax
from jax.sharding import PartitionSpec as P

QUERY_HEADS = 32
KEY_VALUE_HEADS = 8
HEAD_SIZE = 64
PIECES = 4


EPSILON = 1e-05
ROPE_BASE = 500000.0
NEGATIVE = -1e30


def layout(lengths, complete_rows):
    doc_ends = jnp.cumsum(lengths, axis=-1)
    row_index = jnp.arange(complete_rows, dtype=jnp.int32)
    piece_count = lengths.shape[-1]
    doc_ids = jnp.sum((row_index[None, :, None] >= doc_ends[:, None, :]).astype(jnp.int32), axis=2)
    starts = doc_ends - lengths
    chosen = doc_ids[:, :, None] == jnp.arange(piece_count, dtype=jnp.int32)[None, None, :]
    doc_begin = jnp.sum(jnp.where(chosen, starts[:, None, :], 0), axis=2) + jnp.where(
        doc_ids == piece_count, doc_ends[:, -1:], 0
    )
    return (doc_ids, row_index[None, :] - doc_begin)


def rope_tables(positions, head_dim):
    half_dim = head_dim // 2
    frequency = ROPE_BASE ** (-(jnp.arange(half_dim, dtype=jnp.float32) * (2.0 / head_dim)))
    angles = positions.astype(jnp.float32)[..., None] * frequency
    return (jnp.cos(angles), jnp.sin(angles))


def rotate(vectors, cosine, sine):
    half_dim = vectors.shape[-1] // 2
    first_half = vectors[..., :half_dim]
    second_half = vectors[..., half_dim:]
    return jnp.concatenate(
        [first_half * cosine - second_half * sine, second_half * cosine + first_half * sine],
        axis=-1,
    )


def unrotate(vectors, cosine, sine):
    half_dim = vectors.shape[-1] // 2
    first_half = vectors[..., :half_dim]
    second_half = vectors[..., half_dim:]
    return jnp.concatenate(
        [first_half * cosine + second_half * sine, second_half * cosine - first_half * sine],
        axis=-1,
    )


def norm_rows(values):
    inverse = lax.rsqrt(jnp.mean(values * values, axis=-1, keepdims=True) + EPSILON)
    return (values * inverse, inverse)


def norm_back(grad_normed, scaled, inverse, scale_row):
    grad_scaled = grad_normed * scale_row
    projection = jnp.mean(grad_scaled * scaled, axis=-1, keepdims=True)
    return (
        inverse * (grad_scaled - scaled * projection),
        jnp.sum(grad_normed * scaled, axis=(0, 1)),
    )


def contract(left, right, left_dim, right_dim):
    return lax.dot_general(
        left, right, (((left_dim,), (right_dim,)), ((), ())), preferred_element_type=jnp.float32
    )


def masked_scores(query_block, key_rows, doc_ids, first_row, last_row):
    scores = jnp.einsum(
        "qhgd,khd->hgqk", query_block, key_rows[:last_row], preferred_element_type=jnp.float32
    ) * HEAD_SIZE ** (-0.5)
    query_pos = jnp.arange(first_row, last_row, dtype=jnp.int32)
    key_pos = jnp.arange(last_row, dtype=jnp.int32)
    query_doc = doc_ids[first_row:last_row]
    key_doc = doc_ids[:last_row]
    allowed = (query_doc[:, None] == key_doc[None, :]) & (key_pos[None, :] <= query_pos[:, None])
    allowed = allowed & ((query_doc[:, None] < PIECES) | (key_pos[None, :] == query_pos[:, None]))
    return jnp.where(allowed[None, None], scores, NEGATIVE)


def attend_slot(query_rows, key_rows, value_rows, doc_ids, block_rows):
    complete_rows = query_rows.shape[0]
    outputs = []
    totals = []
    for first_row in range(0, complete_rows, block_rows):
        last_row = first_row + block_rows
        scores = masked_scores(
            query_rows[first_row:last_row], key_rows, doc_ids, first_row, last_row
        )
        row_peak = jnp.max(scores, axis=-1, keepdims=True)
        exp_scores = jnp.exp(scores - row_peak)
        row_total = jnp.sum(exp_scores, axis=-1, keepdims=True)
        soft_probs = (exp_scores / row_total).astype(jnp.bfloat16)
        block_out = jnp.einsum(
            "hgqk,khd->qhgd", soft_probs, value_rows[:last_row], preferred_element_type=jnp.float32
        )
        outputs.append(block_out.astype(jnp.bfloat16))
        totals.append((row_peak + jnp.log(row_total))[..., 0])
    return (jnp.concatenate(outputs, axis=0), jnp.concatenate(totals, axis=-1))


def attend_back(query_rows, key_rows, value_rows, doc_ids, totals, grad_rows, block_rows):
    complete_rows = query_rows.shape[0]
    score_scale = HEAD_SIZE ** (-0.5)
    grad_query_list = []
    grad_key = jnp.zeros(key_rows.shape, jnp.float32)
    grad_value = jnp.zeros(value_rows.shape, jnp.float32)
    for first_row in range(0, complete_rows, block_rows):
        last_row = first_row + block_rows
        query_block = query_rows[first_row:last_row]
        grad_block = grad_rows[first_row:last_row]
        scores = masked_scores(query_block, key_rows, doc_ids, first_row, last_row)
        soft_probs = jnp.exp(scores - totals[:, :, first_row:last_row, None])
        grad_probs = jnp.einsum(
            "qhgd,khd->hgqk", grad_block, value_rows[:last_row], preferred_element_type=jnp.float32
        )
        row_inner = jnp.sum(soft_probs * grad_probs, axis=-1, keepdims=True)
        grad_scores = (soft_probs * (grad_probs - row_inner)).astype(jnp.bfloat16)
        grad_query_list.append(
            jnp.einsum(
                "hgqk,khd->qhgd",
                grad_scores,
                key_rows[:last_row],
                preferred_element_type=jnp.float32,
            )
            * score_scale
        )
        key_part = (
            jnp.einsum(
                "hgqk,qhgd->khd", grad_scores, query_block, preferred_element_type=jnp.float32
            )
            * score_scale
        )
        value_part = jnp.einsum(
            "hgqk,qhgd->khd",
            soft_probs.astype(jnp.bfloat16),
            grad_block,
            preferred_element_type=jnp.float32,
        )
        padding = ((0, complete_rows - last_row), (0, 0), (0, 0))
        grad_key = grad_key + jnp.pad(key_part, padding)
        grad_value = grad_value + jnp.pad(value_part, padding)
    return (jnp.concatenate(grad_query_list, axis=0), grad_key, grad_value)


def swap_columns(values, place, count):
    width = values.shape[-1] // count
    blocks = [values[:, j * width : (j + 1) * width] for j in range(count)]
    step = 1
    while step < count:
        bit = (place & step) != 0
        blocks = [jnp.where(bit, blocks[j ^ step], blocks[j]) for j in range(count)]
        step *= 2
    return jnp.concatenate(blocks, axis=-1)


def partner(value, step):
    count = lax.axis_size("dp")
    return lax.ppermute(value, "dp", [(i, i ^ step) for i in range(count)])


def dp_steps(turn):
    count = lax.axis_size("dp")
    steps = []
    step = 2
    while step < count:
        steps.append(step)
        step *= 2
    turn = turn % max(1, len(steps))
    return steps[turn:] + steps[:turn]


def gather_dp(piece, turn):
    held = {0: piece}
    for step in dp_steps(turn) + [1]:
        held.update({j ^ step: partner(value, step) for j, value in held.items()})
    return [held[j] for j in range(len(held))]


def reduce_dp(parts, turn):
    held = dict(enumerate(parts))
    for step in [1] + dp_steps(turn)[::-1]:
        kept = {}
        for j in held:
            if not j & step:
                moved = partner(held[j ^ step].astype(jnp.bfloat16), step)
                kept[j] = held[j].astype(jnp.float32) + moved.astype(jnp.float32)
        held = kept
    return held[0]


def gather_ring(block, shift):
    count = lax.axis_size("tensor")
    held = [block]
    for _ in range(count - 1):
        held.append(
            lax.ppermute(held[-1], "tensor", [(i, (i + shift) % count) for i in range(count)])
        )
    return held


def reduce_ring(parts, shift):
    count = lax.axis_size("tensor")
    total = parts[1 % count].astype(jnp.float32)
    for j in range(1, count):
        moved = lax.ppermute(
            total.astype(jnp.bfloat16), "tensor", [(i, (i + shift) % count) for i in range(count)]
        )
        total = moved.astype(jnp.float32) + parts[(j + 1) % count].astype(jnp.float32)
    return total


def exchange(parts, shift):
    count = lax.axis_size("tensor")
    return [parts[0]] + [
        lax.ppermute(parts[j], "tensor", [(i, (i + shift * j) % count) for i in range(count)])
        for j in range(1, count)
    ]


def halves(values, count, axis):
    return jnp.split(values, count, axis=axis)


def back_norm(grad_normed, scaled, inverse, scale_row):
    grad_scaled = grad_normed * scale_row
    projection = jnp.mean(grad_scaled * scaled, axis=-1, keepdims=True)
    return inverse * (grad_scaled - scaled * projection)


def per_device(
    tokens,
    seq_lengths,
    attention_gain,
    query_matrix,
    key_matrix,
    value_matrix,
    output_weight,
    feedforward_gain,
    gate_weight,
    up_weight,
    down_weight,
    cotangent,
):
    dp_count = lax.axis_size("dp")
    ring = lax.axis_size("tensor")
    dp_place = lax.axis_index("dp")
    ring_place = lax.axis_index("tensor")
    _, local_rows, model_width = tokens.shape
    complete_rows = local_rows * ring
    block_rows = min(512, complete_rows)
    query_width = query_matrix.shape[1]
    key_width = key_matrix.shape[1]
    kv_heads = key_width // HEAD_SIZE
    group_width = QUERY_HEADS // KEY_VALUE_HEADS
    doc_ids, positions = layout(seq_lengths, complete_rows)
    doc_ids = doc_ids[0]
    cosine, sine = rope_tables(positions[0], HEAD_SIZE)
    f32 = jnp.float32
    b16 = jnp.bfloat16

    local_tokens = swap_columns(tokens[0], dp_place, dp_count)
    local_cotangent = swap_columns(cotangent[0], dp_place, dp_count)

    token_chunks = gather_ring(local_tokens, 1)
    gains = jnp.concatenate(
        gather_dp(jnp.stack([attention_gain, feedforward_gain]), 0), axis=1
    ).astype(f32)
    gain_one, gain_two = gains[0], gains[1]
    joint_matrix = jnp.concatenate([query_matrix, key_matrix, value_matrix], axis=1)
    joint_full = jnp.concatenate(gather_dp(joint_matrix, 0), axis=0)
    output_ring = jnp.concatenate(gather_ring(output_weight, -1), axis=0)
    output_full = jnp.concatenate(gather_dp(output_ring, 1), axis=1)
    gate_full = jnp.concatenate(gather_dp(gate_weight, 0), axis=0)
    up_full = jnp.concatenate(gather_dp(up_weight, 1), axis=0)
    down_a, down_b = halves(down_weight, 2, 0)
    down_full = jnp.concatenate(
        [
            jnp.concatenate(gather_dp(down_a, 0), axis=1),
            jnp.concatenate(gather_dp(down_b, 1), axis=1),
        ],
        axis=0,
    )
    cotangent_chunks = gather_ring(local_cotangent, 1)

    def to_absolute(values):
        flipped = values.reshape((ring, local_rows) + values.shape[1:])[::-1]
        return jnp.roll(flipped, ring_place + 1, axis=0).reshape(values.shape)

    def to_relative(values):
        view = values.reshape((ring, local_rows) + values.shape[1:])
        return jnp.roll(view, -(ring_place + 1), axis=0)[::-1].reshape(values.shape)

    normed_chunks = []
    for chunk in token_chunks:
        scaled, _ = norm_rows(chunk.astype(f32))
        normed_chunks.append((scaled * gain_one).astype(b16))
    normed_one = jnp.concatenate(normed_chunks, axis=0)
    joint = to_absolute(jnp.dot(normed_one, joint_full, preferred_element_type=f32))
    query_rot = rotate(
        joint[:, :query_width].reshape(complete_rows, kv_heads, group_width, HEAD_SIZE),
        cosine[:, None, None],
        sine[:, None, None],
    ).astype(b16)
    key_rot = rotate(
        joint[:, query_width : query_width + key_width].reshape(complete_rows, kv_heads, HEAD_SIZE),
        cosine[:, None],
        sine[:, None],
    ).astype(b16)
    value_rows = (
        joint[:, query_width + key_width :].astype(b16).reshape(complete_rows, kv_heads, HEAD_SIZE)
    )
    attended, totals = attend_slot(query_rot, key_rot, value_rows, doc_ids, block_rows)
    attended = to_relative(attended.reshape(complete_rows, query_width))
    attended_local = jnp.concatenate(exchange(halves(attended, ring, 0), -1), axis=1)
    inputs = local_tokens.astype(f32)
    scaled_one, inverse_one = norm_rows(inputs)
    hidden_res = inputs + jnp.dot(attended_local, output_full, preferred_element_type=f32)

    scaled_two, inverse_two = norm_rows(hidden_res)
    normed_two = jnp.concatenate(gather_ring((scaled_two * gain_two).astype(b16), 1), axis=0)
    gate_lin = jnp.dot(normed_two, gate_full, preferred_element_type=f32)
    up_lin = jnp.dot(normed_two, up_full, preferred_element_type=f32)
    sigmoid_gate = jax.nn.sigmoid(gate_lin)
    product = (gate_lin * sigmoid_gate * up_lin).astype(b16)
    gate_kept = gate_lin.astype(b16)
    up_kept = up_lin.astype(b16)
    branch_two = jnp.dot(product, down_full, preferred_element_type=f32).astype(b16)
    mixed_two = reduce_ring(halves(branch_two, ring, 0), 1)
    block_output = (hidden_res + mixed_two).astype(b16)

    whole_cotangent = jnp.concatenate(cotangent_chunks, axis=0)
    grad_product = contract(whole_cotangent, down_full, 1, 1)
    gate_lin = gate_kept.astype(f32)
    up_lin = up_kept.astype(f32)
    sigmoid_gate = jax.nn.sigmoid(gate_lin)
    grad_gate = (
        grad_product * up_lin * sigmoid_gate * (1.0 + gate_lin * (1.0 - sigmoid_gate))
    ).astype(b16)
    grad_up = (grad_product * gate_lin * sigmoid_gate).astype(b16)
    grad_normed_two = (
        contract(grad_gate, gate_full, 1, 1) + contract(grad_up, up_full, 1, 1)
    ).astype(b16)
    local_two = reduce_ring(halves(grad_normed_two, ring, 0), 1)
    gate_grad = contract(normed_two, grad_gate, 0, 0).astype(b16)
    up_grad = contract(normed_two, grad_up, 0, 0).astype(b16)
    down_grad = contract(product, whole_cotangent, 0, 0).astype(b16)
    gate_out = reduce_dp(halves(gate_grad, dp_count, 0), 0)
    up_out = reduce_dp(halves(up_grad, dp_count, 0), 1)
    grad_a, grad_b = halves(down_grad, 2, 0)
    down_out = jnp.concatenate(
        [
            reduce_dp(halves(grad_a, dp_count, 1), 0),
            reduce_dp(halves(grad_b, dp_count, 1), 1),
        ],
        axis=0,
    )
    gain_two_part = jnp.sum(local_two * scaled_two, axis=0)
    grad_hidden = local_cotangent.astype(f32) + back_norm(
        local_two, scaled_two, inverse_two, gain_two
    )

    grad_branch = grad_hidden.astype(b16)
    grad_attended_local = contract(grad_branch, output_full, 1, 1).astype(b16)
    grad_attended = jnp.concatenate(exchange(halves(grad_attended_local, ring, 1), 1), axis=0)
    output_grad = contract(attended_local, grad_branch, 0, 0).astype(b16)
    output_part = reduce_dp(halves(output_grad, dp_count, 1), 1)
    output_out = reduce_ring(halves(output_part, ring, 0), -1)
    grad_attended = to_absolute(grad_attended).reshape(
        complete_rows, kv_heads, group_width, HEAD_SIZE
    )
    grad_query_rot, grad_key_rot, grad_value = attend_back(
        query_rot, key_rot, value_rows, doc_ids, totals, grad_attended, block_rows
    )
    grad_query = unrotate(grad_query_rot, cosine[:, None, None], sine[:, None, None])
    grad_key = unrotate(grad_key_rot, cosine[:, None], sine[:, None])
    grad_joint = to_relative(
        jnp.concatenate(
            [
                grad_query.reshape(complete_rows, query_width).astype(b16),
                grad_key.reshape(complete_rows, key_width).astype(b16),
                grad_value.reshape(complete_rows, key_width).astype(b16),
            ],
            axis=1,
        )
    )
    grad_normed_one = contract(grad_joint, joint_full, 1, 1).astype(b16)
    local_one = reduce_ring(halves(grad_normed_one, ring, 0), 1)
    joint_grad = contract(normed_one, grad_joint, 0, 0).astype(b16)
    joint_out = reduce_dp(halves(joint_grad, dp_count, 0), 0)
    gain_one_part = jnp.sum(local_one * scaled_one, axis=0)
    input_gradient = grad_hidden + back_norm(local_one, scaled_one, inverse_one, gain_one)

    gain_parts = jnp.stack([gain_one_part, gain_two_part])
    width = model_width // dp_count
    held = {j: gain_parts[:, j * width : (j + 1) * width] for j in range(dp_count)}
    for step in [1] + dp_steps(0)[::-1]:
        held = {j: held[j] + partner(held[j ^ step], step) for j in held if not j & step}
    gain_out = held[0]
    for shift in range(1, ring):
        gain_out = gain_out + lax.ppermute(
            held[0], "tensor", [(i, (i + shift) % ring) for i in range(ring)]
        )
    return (
        swap_columns(block_output, dp_place, dp_count)[None],
        swap_columns(input_gradient, dp_place, dp_count)[None],
        gain_out[0],
        joint_out[:, :query_width],
        joint_out[:, query_width : query_width + key_width],
        joint_out[:, query_width + key_width :],
        output_out,
        gain_out[1],
        gate_out,
        up_out,
        down_out,
    )


def solution(mesh):
    return jax.shard_map(
        per_device,
        mesh=mesh,
        in_specs=(
            P("dp", "tensor", None),
            P("dp", None),
            P("dp"),
            P("dp", "tensor"),
            P("dp", "tensor"),
            P("dp", "tensor"),
            P("tensor", "dp"),
            P("dp"),
            P("dp", "tensor"),
            P("dp", "tensor"),
            P("tensor", "dp"),
            P("dp", "tensor", None),
        ),
        out_specs=(
            P("dp", "tensor", None),
            P("dp", "tensor", None),
            P("dp"),
            P("dp", "tensor"),
            P("dp", "tensor"),
            P("dp", "tensor"),
            P("tensor", "dp"),
            P("dp"),
            P("dp", "tensor"),
            P("dp", "tensor"),
            P("tensor", "dp"),
        ),
        check_vma=False,
    )
```

```python
import functools

import jax
import jax.numpy as jnp
from jax import lax
from jax.experimental import pallas as pl
from jax.experimental.pallas import tpu as pltpu
from jax.sharding import PartitionSpec as P

QUERY_HEADS = 32
KEY_VALUE_HEADS = 8
HEAD_SIZE = 64
PIECES = 4


EPSILON = 1e-05
ROPE_BASE = 500000.0
NEGATIVE = -1e30
KERNEL_VMEM = 60 * 1024 * 1024
SMALL_COST = pl.CostEstimate(flops=1, bytes_accessed=1, transcendentals=0)


def layout(lengths, complete_rows):
    doc_ends = jnp.cumsum(lengths, axis=-1)
    row_index = jnp.arange(complete_rows, dtype=jnp.int32)
    piece_count = lengths.shape[-1]
    doc_ids = jnp.sum((row_index[None, :, None] >= doc_ends[:, None, :]).astype(jnp.int32), axis=2)
    starts = doc_ends - lengths
    chosen = doc_ids[:, :, None] == jnp.arange(piece_count, dtype=jnp.int32)[None, None, :]
    doc_begin = jnp.sum(jnp.where(chosen, starts[:, None, :], 0), axis=2) + jnp.where(
        doc_ids == piece_count, doc_ends[:, -1:], 0
    )
    return (doc_ids, row_index[None, :] - doc_begin)


def rope_tables(positions, head_dim):
    half_dim = head_dim // 2
    frequency = ROPE_BASE ** (-(jnp.arange(half_dim, dtype=jnp.float32) * (2.0 / head_dim)))
    angles = positions.astype(jnp.float32)[..., None] * frequency
    return (jnp.cos(angles), jnp.sin(angles))


def norm_rows(values):
    inverse = lax.rsqrt(jnp.mean(values * values, axis=-1, keepdims=True) + EPSILON)
    return (values * inverse, inverse)


def dot_nt(left, right):
    return lax.dot_general(
        left, right, (((1,), (1,)), ((), ())), preferred_element_type=jnp.float32
    )


def dot_nn(left, right):
    return jnp.dot(left, right, preferred_element_type=jnp.float32)


def dot_tn(left, right):
    return lax.dot_general(
        left, right, (((0,), (0,)), ((), ())), preferred_element_type=jnp.float32
    )


def swap_halves(values):
    lane = lax.broadcasted_iota(jnp.int32, values.shape, 1)
    half = HEAD_SIZE // 2
    return jnp.where(
        lane % HEAD_SIZE < half, pltpu.roll(values, 128 - half, 1), pltpu.roll(values, half, 1)
    )


def turned(values, cosine, sine, rotated, start):
    if start >= rotated:
        return values
    result = values * cosine + swap_halves(values) * sine
    if start + 128 <= rotated:
        return result
    lane = lax.broadcasted_iota(jnp.int32, values.shape, 1)
    return jnp.where(lane < rotated - start, result, values)


def project_kernel(
    query_width, rotated, x_ref, gain_ref, weight_ref, cos_ref, sin_ref, normed_ref, joint_ref
):
    step = pl.program_id(0)

    @pl.when(step == 0)
    def _():
        values = x_ref[...].astype(jnp.float32)
        inverse = lax.rsqrt(jnp.mean(values * values, axis=-1, keepdims=True) + EPSILON)
        normed_ref[...] = (values * inverse * gain_ref[...]).astype(jnp.bfloat16)

    width = weight_ref.shape[1]
    product = dot_nn(normed_ref[...], weight_ref[...])
    for index in range(pl.cdiv(query_width + 2 * (rotated - query_width), width)):

        @pl.when(step == index)
        def _():
            for start in range(0, width, 128):
                column = index * width + start
                part = turned(
                    product[:, start : start + 128], cos_ref[...], sin_ref[...], rotated, column
                )
                if column < query_width:
                    part = part * HEAD_SIZE ** (-0.5)
                joint_ref[:, start : start + 128] = part.astype(jnp.bfloat16)


def project(x, gain, weight, cosine, sine, index, query_width, rotated):
    rows, depth = x.shape
    total = 2 * rotated - query_width
    width = tile_of(total, 256)
    return pl.pallas_call(
        functools.partial(project_kernel, query_width, rotated),
        grid=(total // width,),
        in_specs=[
            pl.BlockSpec((rows, depth), lambda i: (0, 0)),
            pl.BlockSpec((1, depth), lambda i: (0, 0)),
            pl.BlockSpec((depth, width), lambda i: (0, i)),
            pl.BlockSpec((rows, 128), lambda i: (index, 0)),
            pl.BlockSpec((rows, 128), lambda i: (index, 0)),
        ],
        out_specs=[
            pl.BlockSpec((rows, depth), lambda i: (0, 0)),
            pl.BlockSpec((rows, width), lambda i: (0, i)),
        ],
        out_shape=[
            jax.ShapeDtypeStruct((rows, depth), jnp.bfloat16),
            jax.ShapeDtypeStruct((rows, total), jnp.bfloat16),
        ],
        compiler_params=pltpu.CompilerParams(vmem_limit_bytes=KERNEL_VMEM),
        cost_estimate=SMALL_COST,
        name="project",
    )(x, gain, weight, cosine, sine)


def ring_offset(place, chunk, count, rows):
    return pl.multiple_of(lax.rem(place - chunk + count, count) * rows, rows)


def forward_kernel(
    count, place_ref, q_ref, kv_ref, docq_ref, dock_ref, o_ref, lse_ref, bias, scores
):
    chunk = pl.program_id(0)
    place = place_ref[0]
    rows = q_ref.shape[0]
    kv_width = kv_ref.shape[1] // 2
    heads = kv_width // HEAD_SIZE
    group = q_ref.shape[1] // kv_width
    row_index = lax.broadcasted_iota(jnp.int32, (rows, rows), 0)
    column_index = lax.broadcasted_iota(jnp.int32, (rows, rows), 1)

    def score(j, peaks):
        offset = ring_offset(place, j, count, rows)
        same = dock_ref[pl.ds(offset, rows), :] == docq_ref[...]
        same = same & ((row_index <= column_index) | (j < chunk))
        bias[...] = jnp.where(same, 0.0, NEGATIVE)
        result = []
        for head in range(heads * group):
            h = head // group
            keys = kv_ref[pl.ds(offset, rows), h * HEAD_SIZE : (h + 1) * HEAD_SIZE]
            query = q_ref[:, head * HEAD_SIZE : (head + 1) * HEAD_SIZE]
            block = dot_nt(keys, query) + bias[...]
            scores[head, j] = block
            result.append(jnp.maximum(peaks[head], jnp.max(block, axis=0, keepdims=True)))
        return tuple(result)

    peaks = lax.fori_loop(
        0,
        chunk + 1,
        score,
        tuple(jnp.full((1, rows), NEGATIVE, jnp.float32) for _ in range(heads * group)),
    )
    for h in range(heads):
        first_value = kv_width + h * HEAD_SIZE

        def mix(j, carry):
            offset = ring_offset(place, j, count, rows)
            values = kv_ref[pl.ds(offset, rows), first_value : first_value + HEAD_SIZE]
            values = jnp.concatenate([values, jnp.ones_like(values)], axis=1)
            result = []
            for g in range(group):
                probs = jnp.exp(scores[h * group + g, j] - peaks[h * group + g])
                total = carry[g][1] + jnp.sum(probs, axis=0, keepdims=True)
                result.append(
                    (carry[g][0] + dot_tn(probs.astype(jnp.bfloat16), values), total)
                )
            return tuple(result)

        sums = lax.fori_loop(
            0,
            chunk + 1,
            mix,
            tuple(
                (
                    jnp.zeros((rows, 2 * HEAD_SIZE), jnp.float32),
                    jnp.zeros((1, rows), jnp.float32),
                )
                for _ in range(group)
            ),
        )
        for g in range(group):
            head = h * group + g
            mixed, total = sums[g]
            o_ref[:, head * HEAD_SIZE : (head + 1) * HEAD_SIZE] = (
                mixed[:, :HEAD_SIZE] / mixed[:, HEAD_SIZE:]
            ).astype(jnp.bfloat16)
            lse_ref[head : head + 1, :] = peaks[head] + jnp.log(total)


def attention_forward(joint, docs, place, count, query_width, kv_width):
    total_rows = joint.shape[0]
    rows = total_rows // count
    heads = query_width // HEAD_SIZE
    padded = max(8, heads)
    group = query_width // kv_width

    def chunk_row(c, place_ref):
        return lax.rem(place_ref[0] - c + count, count)

    spec = pltpu.PrefetchScalarGridSpec(
        num_scalar_prefetch=1,
        grid=(count,),
        in_specs=[
            pl.BlockSpec((rows, query_width), lambda c, p: (chunk_row(c, p), 0)),
            pl.BlockSpec(
                (total_rows, 2 * kv_width), lambda c, p: (0, query_width // (2 * kv_width))
            ),
            pl.BlockSpec((1, rows), lambda c, p: (0, chunk_row(c, p))),
            pl.BlockSpec((total_rows, 1), lambda c, p: (0, 0)),
        ],
        out_specs=[
            pl.BlockSpec((rows, query_width), lambda c, p: (chunk_row(c, p), 0)),
            pl.BlockSpec((padded, rows), lambda c, p: (0, chunk_row(c, p))),
        ],
        scratch_shapes=[
            pltpu.VMEM((rows, rows), jnp.float32),
            pltpu.VMEM((heads, count, rows, rows), jnp.float32),
        ],
    )
    return pl.pallas_call(
        functools.partial(forward_kernel, count),
        grid_spec=spec,
        out_shape=[
            jax.ShapeDtypeStruct((total_rows, query_width), jnp.bfloat16),
            jax.ShapeDtypeStruct((padded, total_rows), jnp.float32),
        ],
        compiler_params=pltpu.CompilerParams(vmem_limit_bytes=KERNEL_VMEM),
        cost_estimate=SMALL_COST,
        name="attend",
    )(place, joint, joint, docs[None, :], docs[:, None])


def backward_kernel(
    count,
    place_ref,
    q_ref,
    kv_ref,
    o_ref,
    do_ref,
    lse_ref,
    docq_ref,
    dock_ref,
    cos_ref,
    sin_ref,
    out_ref,
    bias,
    sum_q,
    sum_kv,
):
    chunk = pl.program_id(0)
    place = place_ref[0]
    rows, query_width = q_ref.shape
    kv_width = kv_ref.shape[1] // 2
    heads = kv_width // HEAD_SIZE
    group = query_width // kv_width
    row_index = lax.broadcasted_iota(jnp.int32, (rows, rows), 0)
    column_index = lax.broadcasted_iota(jnp.int32, (rows, rows), 1)

    @pl.when(chunk == 0)
    def _():
        sum_kv[...] = jnp.zeros_like(sum_kv)

    sum_q[...] = jnp.zeros_like(sum_q)
    padded = lse_ref.shape[0]
    owner = lax.broadcasted_iota(jnp.int32, (padded, query_width), 0)
    head_of = lax.broadcasted_iota(jnp.int32, (padded, query_width), 1) // HEAD_SIZE
    selector = jnp.where(owner == head_of, 1.0, 0.0).astype(jnp.bfloat16)
    both = o_ref[...].astype(jnp.float32) * do_ref[...].astype(jnp.float32)
    high = both.astype(jnp.bfloat16)
    low = (both - high.astype(jnp.float32)).astype(jnp.bfloat16)
    inner = dot_nt(selector, high) + dot_nt(selector, low)

    def block(j, carry):
        offset = ring_offset(place, j, count, rows)
        same = dock_ref[pl.ds(offset, rows), :] == docq_ref[...]
        same = same & ((row_index <= column_index) | (j < chunk))
        bias[...] = jnp.where(same, 0.0, NEGATIVE)
        for h in range(heads):
            keys = kv_ref[pl.ds(offset, rows), h * HEAD_SIZE : (h + 1) * HEAD_SIZE]
            first_value = kv_width + h * HEAD_SIZE
            values = kv_ref[pl.ds(offset, rows), first_value : first_value + HEAD_SIZE]
            key_sum = jnp.zeros((rows, HEAD_SIZE), jnp.float32)
            value_sum = jnp.zeros((rows, HEAD_SIZE), jnp.float32)
            for g in range(group):
                head = h * group + g
                lanes = slice(head * HEAD_SIZE, (head + 1) * HEAD_SIZE)
                query = q_ref[:, lanes]
                grad = do_ref[:, lanes]
                probs = jnp.exp(dot_nt(keys, query) + bias[...] - lse_ref[head : head + 1, :])
                grad_probs = dot_nt(values, grad)
                grad_scores = (probs * (grad_probs - inner[head : head + 1, :])).astype(
                    jnp.bfloat16
                )
                value_sum += dot_nn(probs.astype(jnp.bfloat16), grad)
                key_sum += dot_nn(grad_scores, query)
                sum_q[:, lanes] += dot_tn(grad_scores, keys)
            sum_kv[pl.ds(offset, rows), h * HEAD_SIZE : (h + 1) * HEAD_SIZE] += key_sum
            sum_kv[pl.ds(offset, rows), first_value : first_value + HEAD_SIZE] += value_sum
        return carry

    lax.fori_loop(0, chunk + 1, block, 0)
    offset = ring_offset(place, chunk, count, rows)
    own = pl.ds(offset, rows)
    for start in range(0, query_width, 128):
        part = turned(
            sum_q[:, start : start + 128], cos_ref[own, :], -sin_ref[own, :], query_width, start
        )
        out_ref[own, start : start + 128] = (part * HEAD_SIZE ** (-0.5)).astype(jnp.bfloat16)

    @pl.when(chunk == count - 1)
    def _():
        for start in range(0, 2 * kv_width, 128):
            part = turned(
                sum_kv[:, start : start + 128], cos_ref[...], -sin_ref[...], kv_width, start
            )
            out_ref[:, query_width + start : query_width + start + 128] = part.astype(jnp.bfloat16)


def attention_backward(
    joint, attended, grad_attended, lse, docs, cosine, sine, place, count, query_width, kv_width
):
    total_rows, total_width = joint.shape
    rows = total_rows // count
    heads = query_width // HEAD_SIZE
    padded = lse.shape[0]

    def chunk_row(c, place_ref):
        return lax.rem(place_ref[0] - c + count, count)

    own = pl.BlockSpec((rows, query_width), lambda c, p: (chunk_row(c, p), 0))
    table = pl.BlockSpec((total_rows, 128), lambda c, p: (0, 0))
    spec = pltpu.PrefetchScalarGridSpec(
        num_scalar_prefetch=1,
        grid=(count,),
        in_specs=[
            own,
            pl.BlockSpec(
                (total_rows, 2 * kv_width), lambda c, p: (0, query_width // (2 * kv_width))
            ),
            own,
            own,
            pl.BlockSpec((padded, rows), lambda c, p: (0, chunk_row(c, p))),
            pl.BlockSpec((1, rows), lambda c, p: (0, chunk_row(c, p))),
            pl.BlockSpec((total_rows, 1), lambda c, p: (0, 0)),
            table,
            table,
        ],
        out_specs=pl.BlockSpec((total_rows, total_width), lambda c, p: (0, 0)),
        scratch_shapes=[
            pltpu.VMEM((rows, rows), jnp.float32),
            pltpu.VMEM((rows, query_width), jnp.float32),
            pltpu.VMEM((total_rows, 2 * kv_width), jnp.float32),
        ],
    )
    return pl.pallas_call(
        functools.partial(backward_kernel, count),
        grid_spec=spec,
        out_shape=jax.ShapeDtypeStruct((total_rows, total_width), jnp.bfloat16),
        compiler_params=pltpu.CompilerParams(vmem_limit_bytes=KERNEL_VMEM),
        cost_estimate=SMALL_COST,
        name="attend_back",
    )(
        place,
        joint,
        joint,
        attended,
        grad_attended,
        lse,
        docs[None, :],
        docs[:, None],
        cosine,
        sine,
    )


def tile_of(size, limit=512):
    tile = limit
    while size % tile:
        tile //= 2
    return tile


def transposed_kernel(x_ref, weight_ref, out_ref):
    out_ref[...] = dot_nt(x_ref[...], weight_ref[...]).astype(out_ref.dtype)


def transposed_product(x, weight, dtype):
    rows, depth = x.shape
    width = weight.shape[0]
    tile = tile_of(width)
    return pl.pallas_call(
        transposed_kernel,
        grid=(width // tile,),
        in_specs=[
            pl.BlockSpec((rows, depth), lambda t: (0, 0)),
            pl.BlockSpec((tile, depth), lambda t: (t, 0)),
        ],
        out_specs=pl.BlockSpec((rows, tile), lambda t: (0, t)),
        out_shape=jax.ShapeDtypeStruct((rows, width), dtype),
        compiler_params=pltpu.CompilerParams(vmem_limit_bytes=KERNEL_VMEM),
        cost_estimate=SMALL_COST,
        name="transposed",
    )(x, weight)


def join_kernel(axis, *refs):
    place = 0
    for ref in refs[:-1]:
        size = ref.shape[axis]
        if axis == 0:
            refs[-1][place : place + size, :] = ref[...]
        else:
            refs[-1][:, place : place + size] = ref[...]
        place += size


def join(parts, axis):
    shape = list(parts[0].shape)
    shape[axis] = sum(part.shape[axis] for part in parts)
    return pl.pallas_call(
        functools.partial(join_kernel, axis),
        out_shape=jax.ShapeDtypeStruct(tuple(shape), parts[0].dtype),
        compiler_params=pltpu.CompilerParams(vmem_limit_bytes=KERNEL_VMEM),
        cost_estimate=SMALL_COST,
        name="join",
    )(*parts)


def attended_kernel(o_ref, weight_ref, tokens_ref, gain_ref, hidden_ref, normed_ref):
    step = pl.program_id(0)
    tile = weight_ref.shape[0]
    columns = pl.ds(pl.multiple_of(step * tile, tile), tile)
    hidden_ref[:, columns] = tokens_ref[...].astype(jnp.float32) + dot_nt(
        o_ref[...], weight_ref[...]
    )

    @pl.when(step == pl.num_programs(0) - 1)
    def _():
        values = hidden_ref[...]
        inverse = lax.rsqrt(jnp.mean(values * values, axis=-1, keepdims=True) + EPSILON)
        normed_ref[...] = (values * inverse * gain_ref[...]).astype(jnp.bfloat16)


def after_attention(attended, weight, tokens, gain):
    rows, depth = attended.shape
    width = weight.shape[0]
    tile = tile_of(width)
    whole = pl.BlockSpec((rows, width), lambda t: (0, 0))
    return pl.pallas_call(
        attended_kernel,
        grid=(width // tile,),
        in_specs=[
            pl.BlockSpec((rows, depth), lambda t: (0, 0)),
            pl.BlockSpec((tile, depth), lambda t: (t, 0)),
            pl.BlockSpec((rows, tile), lambda t: (0, t)),
            pl.BlockSpec((1, width), lambda t: (0, 0)),
        ],
        out_specs=[whole, whole],
        out_shape=[
            jax.ShapeDtypeStruct((rows, width), jnp.float32),
            jax.ShapeDtypeStruct((rows, width), jnp.bfloat16),
        ],
        compiler_params=pltpu.CompilerParams(vmem_limit_bytes=KERNEL_VMEM),
        cost_estimate=SMALL_COST,
        name="after_attention",
    )(attended, weight, tokens, gain)


def join_rows(parts, out_ref):
    rows = parts[0].shape[0]
    for index, part in enumerate(parts):
        out_ref[index * rows : (index + 1) * rows, :] = part[...]


def up_kernel(parts, *refs):
    gate_ref, up_ref = refs[parts : parts + 2]
    a_ref, u_ref, g_ref, x_out = refs[-4:]

    @pl.when(pl.program_id(0) == 0)
    def _():
        join_rows(refs[:parts], x_out)

    gate = dot_nn(x_out[...], gate_ref[...])
    up = dot_nn(x_out[...], up_ref[...])
    a_ref[...] = gate.astype(jnp.bfloat16)
    u_ref[...] = up.astype(jnp.bfloat16)
    g_ref[...] = (gate * jax.nn.sigmoid(gate) * up).astype(jnp.bfloat16)


def up_chunk(xs, weight, kept, index, count):
    rows = len(xs) * xs[0].shape[0]
    depth, width = weight.shape
    hidden = width // 2
    tile = tile_of(hidden)
    tiles = hidden // tile
    specs = [pl.BlockSpec(xs[0].shape, lambda t: (0, 0))] * len(xs)
    specs.append(pl.BlockSpec((depth, tile), lambda t: (0, t)))
    specs.append(pl.BlockSpec((depth, tile), lambda t: (0, tiles + t)))
    operands = [*xs, weight, weight]
    shapes = [jax.ShapeDtypeStruct((rows * count, hidden), jnp.bfloat16)] * 3 + [
        jax.ShapeDtypeStruct((rows * count, depth), jnp.bfloat16)
    ]
    aliases = {}
    if kept is not None:
        specs.extend([pl.BlockSpec(memory_space=pl.ANY)] * 4)
        aliases = {len(operands) + i: i for i in range(4)}
        operands.extend(kept)
    return pl.pallas_call(
        functools.partial(up_kernel, len(xs)),
        grid=(tiles,),
        in_specs=specs,
        out_specs=[pl.BlockSpec((rows, tile), lambda t: (index, t))] * 3
        + [pl.BlockSpec((rows, depth), lambda t: (index, 0))],
        out_shape=shapes,
        input_output_aliases=aliases,
        compiler_params=pltpu.CompilerParams(vmem_limit_bytes=KERNEL_VMEM),
        cost_estimate=SMALL_COST,
        name="up_chunk",
    )(*operands)


def down_kernel(parts, tiles, *refs):
    down_ref, a_ref, u_ref, gate_ref, up_ref = refs[parts : parts + 5]
    da_ref, du_ref, e_out, dx_ref, da_kept, du_kept = refs[-6:]
    step = pl.program_id(0)

    @pl.when(step == 0)
    def _():
        join_rows(refs[:parts], e_out)

    @pl.when(step < tiles)
    def _():
        grad = dot_nn(e_out[...], down_ref[...])
        gate = a_ref[...].astype(jnp.float32)
        up = u_ref[...].astype(jnp.float32)
        sigmoid = jax.nn.sigmoid(gate)
        da = (grad * up * sigmoid * (1.0 + gate * (1.0 - sigmoid))).astype(jnp.bfloat16)
        du = (grad * gate * sigmoid).astype(jnp.bfloat16)
        da_ref[...] = da
        du_ref[...] = du
        tile = da.shape[1]
        for index in range(tiles):

            @pl.when(step == index)
            def _():
                da_kept[:, index * tile : (index + 1) * tile] = da
                du_kept[:, index * tile : (index + 1) * tile] = du

    @pl.when(step >= tiles)
    def _():
        dx_ref[...] = (
            dot_nt(da_kept[...], gate_ref[...]) + dot_nt(du_kept[...], up_ref[...])
        ).astype(jnp.bfloat16)


def down_chunk(es, down_weight, a, u, weight, kept, index, count):
    rows = len(es) * es[0].shape[0]
    depth, width = weight.shape
    hidden = width // 2
    tile = tile_of(hidden)
    tiles = hidden // tile
    row_tile = tile_of(depth)

    def column(t):
        return jnp.minimum(t, tiles - 1)

    def row(t):
        return jnp.maximum(t - tiles, 0)

    specs = [pl.BlockSpec(es[0].shape, lambda t: (0, 0))] * len(es) + [
        pl.BlockSpec((depth, tile), lambda t: (0, column(t))),
        pl.BlockSpec((rows, tile), lambda t: (index, column(t))),
        pl.BlockSpec((rows, tile), lambda t: (index, column(t))),
        pl.BlockSpec((row_tile, hidden), lambda t: (row(t), 0)),
        pl.BlockSpec((row_tile, hidden), lambda t: (row(t), 1)),
    ]
    operands = [*es, down_weight, a, u, weight, weight]
    shapes = [
        jax.ShapeDtypeStruct((rows * count, hidden), jnp.bfloat16),
        jax.ShapeDtypeStruct((rows * count, hidden), jnp.bfloat16),
        jax.ShapeDtypeStruct((rows * count, depth), jnp.bfloat16),
        jax.ShapeDtypeStruct((rows, depth), jnp.bfloat16),
    ]
    aliases = {}
    if kept is not None:
        specs.extend([pl.BlockSpec(memory_space=pl.ANY)] * 3)
        aliases = {len(operands) + i: i for i in range(3)}
        operands.extend(kept)
    return pl.pallas_call(
        functools.partial(down_kernel, len(es), tiles),
        grid=(tiles + depth // row_tile,),
        in_specs=specs,
        out_specs=[
            pl.BlockSpec((rows, tile), lambda t: (index, column(t))),
            pl.BlockSpec((rows, tile), lambda t: (index, column(t))),
            pl.BlockSpec((rows, depth), lambda t: (index, 0)),
            pl.BlockSpec((rows, row_tile), lambda t: (0, row(t))),
        ],
        out_shape=shapes,
        input_output_aliases=aliases,
        scratch_shapes=[
            pltpu.VMEM((rows, hidden), jnp.bfloat16),
            pltpu.VMEM((rows, hidden), jnp.bfloat16),
        ],
        compiler_params=pltpu.CompilerParams(vmem_limit_bytes=KERNEL_VMEM),
        cost_estimate=SMALL_COST,
        name="down_chunk",
    )(*operands)


def weight_kernel(count, core_ref, x_ref, *refs):
    out_ref = refs[-1]
    column = 0
    for y_ref in refs[:count]:
        width = y_ref.shape[1]
        piece = 1024 if width % 1024 == 0 else width
        for first in range(0, width, piece):
            total = dot_tn(x_ref[...], y_ref[:, first : first + piece])
            place = slice(column + first, column + first + piece)
            if len(refs) > count + 1:
                total += refs[count][:, place].astype(jnp.float32)
            out_ref[:, place] = total.astype(jnp.bfloat16)
        column += width


def weight_product(x, ys, core, count, received):
    rows, depth = x.shape
    tile = depth // count
    total = sum(y.shape[1] for y in ys)
    side = 1 if received is None else 0
    block = pl.BlockSpec((tile, total), lambda t, c: (t, 0))
    specs = [pl.BlockSpec((rows, tile), lambda t, c: (0, 2 * t + lax.rem(c[0] + side, 2)))]
    specs += [pl.BlockSpec((rows, y.shape[1]), lambda t, c: (0, 0)) for y in ys]
    operands = [x, *ys]
    if received is not None:
        specs.append(block)
        operands.append(received)
    return pl.pallas_call(
        functools.partial(weight_kernel, len(ys)),
        grid_spec=pltpu.PrefetchScalarGridSpec(
            num_scalar_prefetch=1, grid=(count // 2,), in_specs=specs, out_specs=block
        ),
        out_shape=jax.ShapeDtypeStruct((depth // 2, total), jnp.bfloat16),
        compiler_params=pltpu.CompilerParams(vmem_limit_bytes=KERNEL_VMEM),
        cost_estimate=SMALL_COST,
        name="weight_product",
    )(core, *operands)


def residual_kernel(
    e_ref, hidden_ref, first_ref, second_ref, gain_ref, weight_ref, dh_ref, dz_ref, do_ref
):
    @pl.when(pl.program_id(0) == 0)
    def _():
        values = hidden_ref[...]
        inverse = lax.rsqrt(jnp.mean(values * values, axis=-1, keepdims=True) + EPSILON)
        scaled = values * inverse
        grad = first_ref[...].astype(jnp.float32) + second_ref[...].astype(jnp.float32)
        grad = grad * gain_ref[...]
        projection = jnp.mean(grad * scaled, axis=-1, keepdims=True)
        total = e_ref[...].astype(jnp.float32) + inverse * (grad - scaled * projection)
        dh_ref[...] = total
        dz_ref[...] = total.astype(jnp.bfloat16)

    do_ref[...] = dot_nn(dz_ref[...], weight_ref[...]).astype(jnp.bfloat16)


def residual_gradient(e, hidden_res, first, second, gain, weight):
    rows, depth = e.shape
    width = weight.shape[1]
    tile = tile_of(width)
    whole = pl.BlockSpec((rows, depth), lambda t: (0, 0))
    return pl.pallas_call(
        residual_kernel,
        grid=(width // tile,),
        in_specs=[
            whole,
            whole,
            whole,
            whole,
            pl.BlockSpec((1, depth), lambda t: (0, 0)),
            pl.BlockSpec((depth, tile), lambda t: (0, t)),
        ],
        out_specs=[whole, whole, pl.BlockSpec((rows, tile), lambda t: (0, t))],
        out_shape=[
            jax.ShapeDtypeStruct((rows, depth), jnp.float32),
            jax.ShapeDtypeStruct((rows, depth), jnp.bfloat16),
            jax.ShapeDtypeStruct((rows, width), jnp.bfloat16),
        ],
        compiler_params=pltpu.CompilerParams(vmem_limit_bytes=KERNEL_VMEM),
        cost_estimate=SMALL_COST,
        name="residual_gradient",
    )(e, hidden_res, first, second, gain, weight)


def tie(value, *others):
    return lax.optimization_barrier((value, others))[0]


def together(*values):
    return lax.optimization_barrier(values)


class Mover:
    def __init__(self):
        self.dp_count = lax.axis_size("dp")
        self.ring = lax.axis_size("tensor")
        self.groups = [list(range(core, self.dp_count, 2)) for core in range(2)]

    def swap(self, value, step):
        return lax.ppermute(value, "dp", [(i, i ^ step) for i in range(self.dp_count)])

    def gather(self, shard):
        return lax.all_gather(shard, "dp", axis=0, tiled=True)

    def scatter(self, total):
        return lax.psum_scatter(
            total, "dp", scatter_dimension=0, tiled=True, axis_index_groups=self.groups
        )

    def hop(self, value, shift=1):
        return lax.ppermute(
            value, "tensor", [(i, (i + shift) % self.ring) for i in range(self.ring)]
        )

    def spread(self, value):
        ring = self.ring
        return [value] + [
            lax.ppermute(value, "tensor", [(i, (i - j) % ring) for i in range(ring)])
            for j in range(1, ring)
        ]

    def exchange(self, parts, shift):
        ring = self.ring
        return [parts[0]] + [
            lax.ppermute(parts[j], "tensor", [(i, (i + shift * j) % ring) for i in range(ring)])
            for j in range(1, ring)
        ]


def add(first, second):
    return (first.astype(jnp.float32) + second.astype(jnp.float32)).astype(jnp.bfloat16)


def back_norm(grad_normed, scaled, inverse, scale_row):
    grad_scaled = grad_normed * scale_row
    projection = jnp.mean(grad_scaled * scaled, axis=-1, keepdims=True)
    return inverse * (grad_scaled - scaled * projection)


def per_device(
    tokens,
    seq_lengths,
    attention_gain,
    query_matrix,
    key_matrix,
    value_matrix,
    output_weight,
    feedforward_gain,
    gate_weight,
    up_weight,
    down_weight,
    cotangent,
):
    mover = Mover()
    dp_count = mover.dp_count
    ring = mover.ring
    core = (lax.axis_index("dp") % 2).astype(jnp.int32).reshape(1)
    ring_place = lax.axis_index("tensor")
    _, local_rows, model_width = tokens.shape
    complete_rows = local_rows * ring
    query_width = query_matrix.shape[1]
    key_width = key_matrix.shape[1]
    joint_width = query_width + 2 * key_width
    hidden = gate_weight.shape[1]
    f32 = jnp.float32
    b16 = jnp.bfloat16

    doc_ids, positions = layout(seq_lengths, complete_rows)
    row_index = jnp.arange(complete_rows, dtype=jnp.int32)
    doc_ids = jnp.where(doc_ids[0] < PIECES, doc_ids[0], PIECES + row_index)

    def to_relative(values):
        view = values.reshape((ring, local_rows) + values.shape[1:])
        return jnp.roll(view, -(ring_place + 1), axis=0)[::-1].reshape(values.shape)

    doc_ids = to_relative(doc_ids)
    cosine, sine = rope_tables(to_relative(positions[0]), HEAD_SIZE)
    cosine_table = jnp.tile(cosine, (1, 128 // cosine.shape[1]))
    sine_table = jnp.tile(jnp.concatenate([-sine, sine], axis=1), (1, 128 // HEAD_SIZE))
    place = ring_place.astype(jnp.int32).reshape(1)

    local_tokens = tokens[0]
    local_cotangent = cotangent[0]
    joint_matrix = jnp.concatenate([query_matrix, key_matrix, value_matrix], axis=1)
    own_gains = jnp.stack([attention_gain, feedforward_gain], axis=1)
    joint_full = mover.gather(
        jnp.concatenate([joint_matrix, jnp.pad(own_gains, ((0, 0), (0, 126)))], axis=1)
    )
    token = mover.hop(local_tokens)
    output_parts = mover.spread(output_weight.T)
    up_shard = jnp.concatenate([gate_weight, up_weight], axis=1)
    down_shard = down_weight.T
    token, output_ring, cosine_table, sine_table, doc_ids, up_shard, down_shard = together(
        token, join(output_parts, 1), cosine_table, sine_table, doc_ids, up_shard, down_shard
    )
    output_full = mover.gather(output_ring)
    up_full = mover.gather(tie(up_shard, output_ring))
    down_full = mover.gather(tie(down_shard, output_ring))
    gains = joint_full[:, joint_width : joint_width + 2].T.astype(f32)
    gain_one, gain_two = gains[:1], gains[1:]

    def projection(x, index):
        return project(
            x,
            gain_one,
            joint_full,
            cosine_table,
            sine_table,
            index,
            query_width,
            query_width + key_width,
        )

    projected = [projection(local_tokens, 0)]
    for j in range(1, ring):
        if j + 1 < ring:
            moved = mover.hop(token)
        else:
            moved = mover.hop(local_cotangent)
        projected.append(projection(tie(token, projected[-1]), j))
        if j + 1 < ring:
            token, projected[-1] = together(moved, projected[-1])
    cotangent_chunks = [local_cotangent, moved]
    joint = join([p[1] for p in projected], 0)
    attended, totals = attention_forward(joint, doc_ids, place, ring, query_width, key_width)
    cotangent_chunks[1], attended = together(cotangent_chunks[1], attended)
    attended_parts = together(*mover.exchange(jnp.split(attended, ring, axis=0), -1))
    attended_local = join(attended_parts, 1)
    hidden_res, normed_two = after_attention(
        attended_local, output_full, local_tokens, gain_two
    )

    def upward(chunks, kept, index):
        return up_chunk(chunks, up_full, kept, index, ring // 2)

    def downward(chunks, kept, index):
        result = down_chunk(
            chunks, down_full, gate_all, up_all, up_full, kept, index, ring // 2
        )
        return result[:3], jnp.split(result[3], 2, axis=0)

    normed_chunks = [normed_two]
    kept = None
    for j in range(1, ring):
        moved = mover.hop(normed_chunks[-1])
        if j % 2 and j > 1:
            kept = upward(normed_chunks[j - 3 : j - 1], kept, (j - 3) // 2)
            moved, kept = together(moved, kept)
        normed_chunks.append(moved)
    moved = mover.hop(cotangent_chunks[-1])
    kept = upward(normed_chunks[ring - 2 :], kept, ring // 2 - 1)
    moved, kept = together(moved, kept)
    cotangent_chunks.append(moved)
    gate_all, up_all, product, normed_all = kept
    kept = None
    grads = []
    for j in range(3, ring):
        moved = mover.hop(cotangent_chunks[-1])
        if j % 2:
            kept, parts = downward(cotangent_chunks[j - 3 : j - 1], kept, (j - 3) // 2)
            moved, kept, parts = together(moved, kept, parts)
            grads.extend(parts)
        cotangent_chunks.append(moved)
    total = grads[1]
    moved = mover.hop(total)
    kept, parts = downward(tie(cotangent_chunks[ring - 2 :], total), kept, ring // 2 - 1)
    moved, kept, parts = together(moved, kept, parts)
    grads.extend(parts)
    grad_gate, grad_up, cotangent_all = kept

    def weights(x, ys, received=None):
        return weight_product(x, ys, core, dp_count, received)

    for j in range(2, ring):
        total = add(moved, grads[j])
        moved = mover.hop(total)
        if j == 2:
            down_part = weights(tie(cotangent_all, total), [product])
            up_part = weights(tie(normed_all, down_part), [grad_gate, grad_up])
            moved, down_part, up_part = together(moved, down_part, up_part)
            down_part = mover.swap(down_part, 1)
            up_part = mover.swap(up_part, 1)
        if j == 3:
            branch = transposed_product(tie(product, total), down_full, b16)
            down_part = weights(tie(cotangent_all, branch), [product], down_part)
            moved, branch, down_part = together(moved, branch, down_part)
    down_out = mover.scatter(down_part)
    grad_hidden, grad_branch, grad_attended_local = residual_gradient(
        local_cotangent, hidden_res, moved, grads[0], gain_two, output_full
    )

    grad_attended = mover.exchange(jnp.split(grad_attended_local, ring, axis=1), 1)
    up_part = weights(tie(normed_all, grad_branch), [grad_gate, grad_up], up_part)
    output_part = weights(tie(grad_branch, up_part), [attended_local])
    grad_attended, up_part, output_part = together(grad_attended, up_part, output_part)
    up_out = mover.scatter(tie(up_part, down_part))
    output_part = mover.swap(output_part, 1)
    branch_parts = jnp.split(branch, ring, axis=0)
    moved = mover.hop(tie(branch_parts[1], grad_attended))
    grad_joint = attention_backward(
        joint,
        attended,
        join(grad_attended, 0),
        totals,
        doc_ids,
        cosine_table,
        sine_table,
        place,
        ring,
        query_width,
        key_width,
    )
    branch_moved, grad_joint = together(moved, grad_joint)
    grads = jnp.split(transposed_product(grad_joint, joint_full, b16), ring, axis=0)
    normed_one = join([p[0] for p in projected], 0)
    moved = grads[0]
    for j in range(1, ring):
        total = grads[1] if j == 1 else add(moved, grads[j])
        moved = mover.hop(total)
        if j == 1:
            joint_part = weights(tie(normed_one, total), [grad_joint])
            output_part = weights(
                tie(grad_branch, joint_part), [attended_local], output_part
            )
            moved, joint_part, output_part = together(moved, joint_part, output_part)
            joint_part = mover.swap(joint_part, 1)
            output_out = mover.scatter(tie(output_part, up_part))
        if j == 2:
            joint_part = weights(tie(normed_one, total), [grad_joint], joint_part)
            moved, joint_part, up_out = together(moved, joint_part, up_out)
            joint_out = mover.scatter(tie(joint_part, output_part))
    scaled_one, inverse_one = norm_rows(local_tokens.astype(f32))
    local_one = moved.astype(f32) + grads[0].astype(f32)
    input_gradient = grad_hidden + back_norm(local_one, scaled_one, inverse_one, gain_one)
    branch_moved = tie(branch_moved, moved)
    for j in range(2, ring):
        branch_moved = mover.hop(add(branch_moved, branch_parts[j]))
    block_output = (
        hidden_res + (branch_moved.astype(f32) + branch_parts[0].astype(f32))
    ).astype(b16)
    output_parts = jnp.split(output_out, ring, axis=1)
    moved = output_parts[0]
    for j in range(1, ring):
        moved = mover.hop(output_parts[1] if j == 1 else add(moved, output_parts[j]), -1)
    output_out = (moved.astype(f32) + output_parts[0].astype(f32)).T
    joint_out = joint_out.astype(f32)

    gate_out = up_out[:, :hidden].astype(f32)
    up_out = up_out[:, hidden:].astype(f32)
    sums = jnp.stack(
        [
            jnp.sum(joint_out * joint_matrix.astype(f32), axis=1) / attention_gain.astype(f32),
            jnp.sum(gate_out * gate_weight.astype(f32) + up_out * up_weight.astype(f32), axis=1)
            / feedforward_gain.astype(f32),
        ]
    )
    gain_out = sums
    for shift in range(1, ring):
        gain_out = gain_out + lax.ppermute(
            sums, "tensor", [(i, (i + shift) % ring) for i in range(ring)]
        )
    return (
        block_output[None],
        input_gradient[None],
        gain_out[0],
        joint_out[:, :query_width],
        joint_out[:, query_width : query_width + key_width],
        joint_out[:, query_width + key_width :],
        output_out,
        gain_out[1],
        gate_out,
        up_out,
        down_out.astype(f32).T,
    )


def solution(mesh):
    return jax.shard_map(
        per_device,
        mesh=mesh,
        in_specs=(
            P("dp", "tensor", None),
            P("dp", None),
            P("dp"),
            P("dp", "tensor"),
            P("dp", "tensor"),
            P("dp", "tensor"),
            P("tensor", "dp"),
            P("dp"),
            P("dp", "tensor"),
            P("dp", "tensor"),
            P("tensor", "dp"),
            P("dp", "tensor", None),
        ),
        out_specs=(
            P("dp", "tensor", None),
            P("dp", "tensor", None),
            P("dp"),
            P("dp", "tensor"),
            P("dp", "tensor"),
            P("dp", "tensor"),
            P("tensor", "dp"),
            P("dp"),
            P("dp", "tensor"),
            P("dp", "tensor"),
            P("tensor", "dp"),
        ),
        check_vma=False,
    )
```

```python
import functools
import math

import jax
import jax.numpy as jnp
from jax import lax
from jax.experimental import pallas as pl
from jax.experimental.pallas import tpu as pltpu
from jax.sharding import PartitionSpec as P

QUERY_HEADS = 32
KEY_VALUE_HEADS = 8
HEAD_SIZE = 64
PIECES = 4


EPSILON = 1e-05
ROPE_BASE = 500000.0
NEGATIVE = -1e30
GROUP_QUERY = QUERY_HEADS // KEY_VALUE_HEADS * HEAD_SIZE
GROUP_WIDTH = GROUP_QUERY + 2 * HEAD_SIZE
KERNEL_VMEM = 60 * 1024 * 1024
SMALL_COST = pl.CostEstimate(flops=1, bytes_accessed=1, transcendentals=0)


def layout(lengths, complete_rows):
    doc_ends = jnp.cumsum(lengths, axis=-1)
    row_index = jnp.arange(complete_rows, dtype=jnp.int32)
    piece_count = lengths.shape[-1]
    doc_ids = jnp.sum((row_index[None, :, None] >= doc_ends[:, None, :]).astype(jnp.int32), axis=2)
    starts = doc_ends - lengths
    chosen = doc_ids[:, :, None] == jnp.arange(piece_count, dtype=jnp.int32)[None, None, :]
    doc_begin = jnp.sum(jnp.where(chosen, starts[:, None, :], 0), axis=2) + jnp.where(
        doc_ids == piece_count, doc_ends[:, -1:], 0
    )
    return (doc_ids, row_index[None, :] - doc_begin)


def rope_tables(positions, head_dim):
    half_dim = head_dim // 2
    frequency = ROPE_BASE ** (-(jnp.arange(half_dim, dtype=jnp.float32) * (2.0 / head_dim)))
    angles = positions.astype(jnp.float32)[..., None] * frequency
    return (jnp.cos(angles), jnp.sin(angles))


def norm_rows(values):
    inverse = lax.rsqrt(jnp.mean(values * values, axis=-1, keepdims=True) + EPSILON)
    return (values * inverse, inverse)


def dot_nt(left, right):
    return lax.dot_general(
        left, right, (((1,), (1,)), ((), ())), preferred_element_type=jnp.float32
    )


def dot_nn(left, right):
    return jnp.dot(left, right, preferred_element_type=jnp.float32)


def dot_tn(left, right):
    return lax.dot_general(
        left, right, (((0,), (0,)), ((), ())), preferred_element_type=jnp.float32
    )


def tile_of(size, limit=512):
    tile = limit
    while size % tile:
        tile //= 2
    return tile


def parameters():
    return pltpu.CompilerParams(vmem_limit_bytes=KERNEL_VMEM)


def swap_halves(values):
    lane = lax.broadcasted_iota(jnp.int32, values.shape, 1)
    half = HEAD_SIZE // 2
    return jnp.where(
        lane % HEAD_SIZE < half, pltpu.roll(values, 128 - half, 1), pltpu.roll(values, half, 1)
    )


def turned(values, cosine, sine, start):
    result = values * cosine + swap_halves(values) * sine
    rotated = GROUP_WIDTH - HEAD_SIZE
    if start + 128 <= rotated:
        return result
    lane = lax.broadcasted_iota(jnp.int32, values.shape, 1)
    return jnp.where(lane < rotated - start, result, values)


def project_kernel(x_ref, gain_ref, weight_ref, cos_ref, sin_ref, *refs):
    normed_ref, joint_ref = refs[-2:]

    @pl.when(pl.program_id(0) == 0)
    def _():
        values = x_ref[...].astype(jnp.float32)
        inverse = lax.rsqrt(jnp.mean(values * values, axis=-1, keepdims=True) + EPSILON)
        normed_ref[...] = (values * inverse * gain_ref[...]).astype(jnp.bfloat16)

    product = dot_nn(normed_ref[...], weight_ref[...])
    for start in range(0, GROUP_WIDTH, 128):
        part = turned(product[:, start : start + 128], cos_ref[...], sin_ref[...], start)
        if start < GROUP_QUERY:
            part = part * HEAD_SIZE ** (-0.5)
        joint_ref[:, start : start + 128] = part.astype(jnp.bfloat16)


def project(x, gain, weight, cosine, sine, kept, index, count, groups):
    rows, depth = x.shape
    specs = [
        pl.BlockSpec((rows, depth), lambda g: (0, 0)),
        pl.BlockSpec((1, depth), lambda g: (0, 0)),
        pl.BlockSpec((depth, GROUP_WIDTH), lambda g: (0, g)),
        pl.BlockSpec((rows, 128), lambda g: (index, 0)),
        pl.BlockSpec((rows, 128), lambda g: (index, 0)),
    ]
    operands = [x, gain, weight, cosine, sine]
    aliases = {}
    if kept is not None:
        specs.extend([pl.BlockSpec(memory_space=pl.ANY)] * 2)
        aliases = {len(operands) + i: i for i in range(2)}
        operands.extend(kept)
    return pl.pallas_call(
        project_kernel,
        grid=(groups,),
        in_specs=specs,
        out_specs=[
            pl.BlockSpec((rows, depth), lambda g: (index, 0)),
            pl.BlockSpec((rows, GROUP_WIDTH), lambda g: (index, g)),
        ],
        out_shape=[
            jax.ShapeDtypeStruct((rows * count, depth), jnp.bfloat16),
            jax.ShapeDtypeStruct((rows * count, GROUP_WIDTH * groups), jnp.bfloat16),
        ],
        input_output_aliases=aliases,
        compiler_params=parameters(),
        cost_estimate=SMALL_COST,
        name="project",
    )(*operands)


def ring_offset(place, chunk, count, rows):
    return pl.multiple_of(lax.rem(place - chunk + count, count) * rows, rows)


def forward_kernel(
    count, place_ref, own_ref, all_ref, docq_ref, dock_ref, o_ref, lse_ref, bias, scores
):
    chunk = pl.program_id(1)
    place = place_ref[0]
    rows = own_ref.shape[0]
    heads = GROUP_QUERY // HEAD_SIZE
    row_index = lax.broadcasted_iota(jnp.int32, (rows, rows), 0)
    column_index = lax.broadcasted_iota(jnp.int32, (rows, rows), 1)

    def score(j, peaks):
        offset = ring_offset(place, j, count, rows)
        same = dock_ref[pl.ds(offset, rows), :] == docq_ref[...]
        same = same & ((row_index <= column_index) | (j < chunk))
        bias[...] = jnp.where(same, 0.0, NEGATIVE)
        keys = all_ref[pl.ds(offset, rows), GROUP_QUERY : GROUP_QUERY + HEAD_SIZE]
        result = []
        for head in range(heads):
            query = own_ref[:, head * HEAD_SIZE : (head + 1) * HEAD_SIZE]
            block = dot_nt(keys, query) + bias[...]
            scores[head, j] = block
            result.append(jnp.maximum(peaks[head], jnp.max(block, axis=0, keepdims=True)))
        return tuple(result)

    peaks = lax.fori_loop(
        0,
        chunk + 1,
        score,
        tuple(jnp.full((1, rows), NEGATIVE, jnp.float32) for _ in range(heads)),
    )

    def mix(j, carry):
        offset = ring_offset(place, j, count, rows)
        values = all_ref[pl.ds(offset, rows), GROUP_QUERY + HEAD_SIZE :]
        values = jnp.concatenate([values, jnp.ones_like(values)], axis=1)
        result = []
        for head in range(heads):
            probs = jnp.exp(scores[head, j] - peaks[head])
            total = carry[head][1] + jnp.sum(probs, axis=0, keepdims=True)
            result.append((carry[head][0] + dot_tn(probs.astype(jnp.bfloat16), values), total))
        return tuple(result)

    sums = lax.fori_loop(
        0,
        chunk + 1,
        mix,
        tuple(
            (
                jnp.zeros((rows, 2 * HEAD_SIZE), jnp.float32),
                jnp.zeros((1, rows), jnp.float32),
            )
            for _ in range(heads)
        ),
    )
    for head in range(heads):
        mixed, total = sums[head]
        o_ref[:, head * HEAD_SIZE : (head + 1) * HEAD_SIZE] = (
            mixed[:, :HEAD_SIZE] / mixed[:, HEAD_SIZE:]
        ).astype(jnp.bfloat16)
        lse_ref[head : head + 1, :] = peaks[head] + jnp.log(total)


def attention_forward(joint, docs, place, count, groups):
    total_rows = joint.shape[0]
    rows = total_rows // count

    def block(c, place_ref):
        return lax.rem(place_ref[0] - c + count, count)

    spec = pltpu.PrefetchScalarGridSpec(
        num_scalar_prefetch=1,
        grid=(groups, count),
        in_specs=[
            pl.BlockSpec((rows, GROUP_WIDTH), lambda g, c, p: (block(c, p), g)),
            pl.BlockSpec((total_rows, GROUP_WIDTH), lambda g, c, p: (0, g)),
            pl.BlockSpec((1, rows), lambda g, c, p: (0, block(c, p))),
            pl.BlockSpec((total_rows, 1), lambda g, c, p: (0, 0)),
        ],
        out_specs=[
            pl.BlockSpec((rows, GROUP_QUERY), lambda g, c, p: (block(c, p), g)),
            pl.BlockSpec((8, rows), lambda g, c, p: (g, block(c, p))),
        ],
        scratch_shapes=[
            pltpu.VMEM((rows, rows), jnp.float32),
            pltpu.VMEM((GROUP_QUERY // HEAD_SIZE, count, rows, rows), jnp.float32),
        ],
    )
    return pl.pallas_call(
        functools.partial(forward_kernel, count),
        grid_spec=spec,
        out_shape=[
            jax.ShapeDtypeStruct((total_rows, GROUP_QUERY * groups), jnp.bfloat16),
            jax.ShapeDtypeStruct((8 * groups, total_rows), jnp.float32),
        ],
        compiler_params=parameters(),
        cost_estimate=SMALL_COST,
        name="attend",
    )(place, joint, joint, docs[None, :], docs[:, None])


def backward_kernel(count, place_ref, *refs):
    own_ref, all_ref, o_ref = refs[:3]
    lse_ref, docq_ref, dock_ref, cos_ref, sin_ref = refs[3 + count : 8 + count]
    out_ref, bias, grad_out, sum_q, sum_kv = refs[8 + count :]
    chunk = pl.program_id(0)
    place = place_ref[0]
    rows = own_ref.shape[0]
    heads = GROUP_QUERY // HEAD_SIZE
    row_index = lax.broadcasted_iota(jnp.int32, (rows, rows), 0)
    column_index = lax.broadcasted_iota(jnp.int32, (rows, rows), 1)

    for index in range(count):

        @pl.when(lax.rem(place - chunk + count, count) == index)
        def _():
            grad_out[...] = refs[3 + index][...]

    @pl.when(chunk == 0)
    def _():
        sum_kv[...] = jnp.zeros_like(sum_kv)

    sum_q[...] = jnp.zeros_like(sum_q)
    owner = lax.broadcasted_iota(jnp.int32, (8, GROUP_QUERY), 0)
    head_of = lax.broadcasted_iota(jnp.int32, (8, GROUP_QUERY), 1) // HEAD_SIZE
    selector = jnp.where(owner == head_of, 1.0, 0.0).astype(jnp.bfloat16)
    both = o_ref[...].astype(jnp.float32) * grad_out[...].astype(jnp.float32)
    high = both.astype(jnp.bfloat16)
    low = (both - high.astype(jnp.float32)).astype(jnp.bfloat16)
    inner = dot_nt(selector, high) + dot_nt(selector, low)

    def block(j, carry):
        offset = ring_offset(place, j, count, rows)
        same = dock_ref[pl.ds(offset, rows), :] == docq_ref[...]
        same = same & ((row_index <= column_index) | (j < chunk))
        bias[...] = jnp.where(same, 0.0, NEGATIVE)
        keys = all_ref[pl.ds(offset, rows), GROUP_QUERY : GROUP_QUERY + HEAD_SIZE]
        values = all_ref[pl.ds(offset, rows), GROUP_QUERY + HEAD_SIZE :]
        key_sum = jnp.zeros((rows, HEAD_SIZE), jnp.float32)
        value_sum = jnp.zeros((rows, HEAD_SIZE), jnp.float32)
        for head in range(heads):
            lanes = slice(head * HEAD_SIZE, (head + 1) * HEAD_SIZE)
            query = own_ref[:, lanes]
            grad = grad_out[:, lanes]
            probs = jnp.exp(dot_nt(keys, query) + bias[...] - lse_ref[head : head + 1, :])
            grad_probs = dot_nt(values, grad)
            grad_scores = (probs * (grad_probs - inner[head : head + 1, :])).astype(jnp.bfloat16)
            value_sum += dot_nn(probs.astype(jnp.bfloat16), grad)
            key_sum += dot_nn(grad_scores, query)
            sum_q[:, lanes] += dot_tn(grad_scores, keys)
        sum_kv[pl.ds(offset, rows), :HEAD_SIZE] += key_sum
        sum_kv[pl.ds(offset, rows), HEAD_SIZE:] += value_sum
        return carry

    lax.fori_loop(0, chunk + 1, block, 0)
    own = pl.ds(ring_offset(place, chunk, count, rows), rows)
    for start in range(0, GROUP_QUERY, 128):
        part = turned(sum_q[:, start : start + 128], cos_ref[own, :], -sin_ref[own, :], start)
        out_ref[own, start : start + 128] = (part * HEAD_SIZE ** (-0.5)).astype(jnp.bfloat16)

    @pl.when(chunk == count - 1)
    def _():
        part = turned(sum_kv[...], cos_ref[...], -sin_ref[...], GROUP_QUERY)
        out_ref[:, GROUP_QUERY:] = part.astype(jnp.bfloat16)


def attention_backward(joint, attended, grads, lse, docs, cosine, sine, place, group):
    count = len(grads)
    total_rows = joint.shape[0]
    rows = total_rows // count

    def block(c, place_ref):
        return lax.rem(place_ref[0] - c + count, count)

    table = pl.BlockSpec((total_rows, 128), lambda c, p: (0, 0))
    spec = pltpu.PrefetchScalarGridSpec(
        num_scalar_prefetch=1,
        grid=(count,),
        in_specs=[
            pl.BlockSpec((rows, GROUP_WIDTH), lambda c, p: (block(c, p), group)),
            pl.BlockSpec((total_rows, GROUP_WIDTH), lambda c, p: (0, group)),
            pl.BlockSpec((rows, GROUP_QUERY), lambda c, p: (block(c, p), group)),
            *[pl.BlockSpec((rows, GROUP_QUERY), lambda c, p: (0, group))] * count,
            pl.BlockSpec((8, rows), lambda c, p: (group, block(c, p))),
            pl.BlockSpec((1, rows), lambda c, p: (0, block(c, p))),
            pl.BlockSpec((total_rows, 1), lambda c, p: (0, 0)),
            table,
            table,
        ],
        out_specs=pl.BlockSpec((total_rows, GROUP_WIDTH), lambda c, p: (0, 0)),
        scratch_shapes=[
            pltpu.VMEM((rows, rows), jnp.float32),
            pltpu.VMEM((rows, GROUP_QUERY), jnp.bfloat16),
            pltpu.VMEM((rows, GROUP_QUERY), jnp.float32),
            pltpu.VMEM((total_rows, 2 * HEAD_SIZE), jnp.float32),
        ],
    )
    return pl.pallas_call(
        functools.partial(backward_kernel, count),
        grid_spec=spec,
        out_shape=jax.ShapeDtypeStruct((total_rows, GROUP_WIDTH), jnp.bfloat16),
        compiler_params=parameters(),
        cost_estimate=SMALL_COST,
        name="attend_back",
    )(
        place,
        joint,
        joint,
        attended,
        *grads,
        lse,
        docs[None, :],
        docs[:, None],
        cosine,
        sine,
    )


def join_kernel(*refs):
    place = 0
    for ref in refs[:-1]:
        size = ref.shape[1]
        refs[-1][:, place : place + size] = ref[...]
        place += size


def join(parts, blocks):
    rows = parts[0].shape[0] // (max(blocks) + 1)
    width = sum(part.shape[1] for part in parts)
    return pl.pallas_call(
        join_kernel,
        grid=(1,),
        in_specs=[
            pl.BlockSpec((rows, part.shape[1]), lambda i, block=block: (block, 0))
            for part, block in zip(parts, blocks)
        ],
        out_specs=pl.BlockSpec((rows, width), lambda i: (0, 0)),
        out_shape=jax.ShapeDtypeStruct((rows, width), parts[0].dtype),
        compiler_params=parameters(),
        cost_estimate=SMALL_COST,
        name="join",
    )(*parts)


def transposed_kernel(count, parts, *refs):
    total = dot_nt(refs[0][...], refs[count][...])
    for index in range(1, count):
        total += dot_nt(refs[index][...], refs[count + index][...])
    rows = total.shape[0] // parts
    for index in range(parts):
        refs[2 * count + index][...] = total[index * rows : (index + 1) * rows].astype(
            jnp.bfloat16
        )


def transposed_product(xs, weight, block, parts):
    rows, depth = xs[0].shape
    width = weight.shape[0]
    tile = tile_of(width)
    specs = [pl.BlockSpec((rows, depth), lambda t: (0, 0))] * len(xs)
    for index in range(len(xs)):
        specs.append(pl.BlockSpec((tile, depth), lambda t, index=index: (t, block + index)))
    part = (rows // parts, width)
    return pl.pallas_call(
        functools.partial(transposed_kernel, len(xs), parts),
        grid=(width // tile,),
        in_specs=specs,
        out_specs=[pl.BlockSpec((part[0], tile), lambda t: (0, t))] * parts,
        out_shape=[jax.ShapeDtypeStruct(part, jnp.bfloat16)] * parts,
        compiler_params=parameters(),
        cost_estimate=SMALL_COST,
        name="transposed",
    )(*xs, *[weight] * len(xs))


def heads_kernel(count, *refs):
    parts = refs[:count]
    weight_ref = refs[count]
    tokens = refs[count + 1 : -1]
    out_ref = refs[-1]
    step = pl.program_id(0)
    width = parts[0].shape[1]
    for j in range(count):
        term = dot_nt(parts[j][...], weight_ref[:, j * width : (j + 1) * width])
        if j == 0:
            out_ref[...] = term
        else:
            out_ref[...] += term
    for index in range(len(tokens)):

        @pl.when(step == index)
        def _():
            out_ref[...] += tokens[index][...].astype(jnp.float32)


def heads_product(parts, weight, tokens):
    blocks = len(tokens)
    rows, width = tokens[0].shape
    depth = parts[0].shape[1]
    specs = [
        pl.BlockSpec((rows, depth), lambda i, j=j: (lax.rem(i + j, blocks), 0))
        for j in range(len(parts))
    ]
    whole = pl.BlockSpec((rows, width), lambda i: (0, 0), pipeline_mode=pl.Buffered(1))
    return pl.pallas_call(
        functools.partial(heads_kernel, len(parts)),
        grid=(blocks,),
        in_specs=[
            *specs,
            pl.BlockSpec(
                (width, depth * len(parts)), lambda i: (0, 0), pipeline_mode=pl.Buffered(1)
            ),
            *[whole] * blocks,
        ],
        out_specs=pl.BlockSpec((rows, width), lambda i: (i, 0)),
        out_shape=jax.ShapeDtypeStruct((rows * blocks, width), jnp.float32),
        compiler_params=parameters(),
        cost_estimate=SMALL_COST,
        name="heads_product",
    )(*parts, weight, *tokens)


def attended_kernel(partial_ref, last_ref, weight_ref, gain_ref, hidden_ref, normed_ref):
    values = partial_ref[...] + dot_nt(last_ref[...], weight_ref[...])

    @pl.when(pl.program_id(0) == 0)
    def _():
        hidden_ref[...] = values

    inverse = lax.rsqrt(jnp.mean(values * values, axis=-1, keepdims=True) + EPSILON)
    normed_ref[...] = (values * inverse * gain_ref[...]).astype(jnp.bfloat16)


def after_attention(partial, last, weight, gain, count):
    total_rows, width = partial.shape
    rows = total_rows // count
    depth = last.shape[1]
    return pl.pallas_call(
        attended_kernel,
        grid=(count,),
        in_specs=[
            pl.BlockSpec((rows, width), lambda i: (i, 0)),
            pl.BlockSpec((rows, depth), lambda i: (lax.rem(i + count - 1, count), 0)),
            pl.BlockSpec((width, depth), lambda i: (0, count - 1)),
            pl.BlockSpec((1, width), lambda i: (0, 0)),
        ],
        out_specs=[
            pl.BlockSpec((rows, width), lambda i: (0, 0)),
            pl.BlockSpec((rows, width), lambda i: (lax.rem(i + count - 1, count), 0)),
        ],
        out_shape=[
            jax.ShapeDtypeStruct((rows, width), jnp.float32),
            jax.ShapeDtypeStruct((total_rows, width), jnp.bfloat16),
        ],
        compiler_params=parameters(),
        cost_estimate=SMALL_COST,
        name="after_attention",
    )(partial, last, weight, gain)


def up_kernel(x_ref, gate_ref, up_ref, *refs):
    a_ref, u_ref, g_ref = refs[-3:]
    gate = dot_nn(x_ref[...], gate_ref[...])
    up = dot_nn(x_ref[...], up_ref[...])
    a_ref[...] = gate.astype(jnp.bfloat16)
    u_ref[...] = up.astype(jnp.bfloat16)
    g_ref[...] = (gate * jax.nn.sigmoid(gate) * up).astype(jnp.bfloat16)


def up_chunk(x, weight, kept, index, count):
    total_rows, depth = x.shape
    rows = total_rows // count
    hidden = weight.shape[1] // 3
    tile = tile_of(hidden)
    tiles = hidden // tile
    specs = [
        pl.BlockSpec((rows, depth), lambda t: (index, 0)),
        pl.BlockSpec((depth, tile), lambda t: (0, t)),
        pl.BlockSpec((depth, tile), lambda t: (0, tiles + t)),
    ]
    operands = [x, weight, weight]
    aliases = {}
    if kept is not None:
        specs.extend([pl.BlockSpec(memory_space=pl.ANY)] * 3)
        aliases = {len(operands) + i: i for i in range(3)}
        operands.extend(kept)
    return pl.pallas_call(
        up_kernel,
        grid=(tiles,),
        in_specs=specs,
        out_specs=[pl.BlockSpec((rows, tile), lambda t: (index, t))] * 3,
        out_shape=[jax.ShapeDtypeStruct((total_rows, hidden), jnp.bfloat16)] * 3,
        input_output_aliases=aliases,
        compiler_params=parameters(),
        cost_estimate=SMALL_COST,
        name="up_chunk",
    )(*operands)


def down_kernel(parts, tiles, *refs):
    down_ref, a_ref, u_ref, gate_ref, up_ref = refs[parts : parts + 5]
    da_ref, du_ref = refs[-5 - parts : -3 - parts]
    dx_refs = refs[-3 - parts : -3]
    da_kept, du_kept, e_out = refs[-3:]
    step = pl.program_id(0)

    @pl.when(step == 0)
    def _():
        rows = refs[0].shape[0]
        for index in range(parts):
            e_out[index * rows : (index + 1) * rows, :] = refs[index][...]

    @pl.when(step < tiles)
    def _():
        grad = dot_nn(e_out[...], down_ref[...])
        gate = a_ref[...].astype(jnp.float32)
        up = u_ref[...].astype(jnp.float32)
        sigmoid = jax.nn.sigmoid(gate)
        da = (grad * up * sigmoid * (1.0 + gate * (1.0 - sigmoid))).astype(jnp.bfloat16)
        du = (grad * gate * sigmoid).astype(jnp.bfloat16)
        da_ref[...] = da
        du_ref[...] = du
        tile = da.shape[1]
        for index in range(tiles):

            @pl.when(step == index)
            def _():
                da_kept[:, index * tile : (index + 1) * tile] = da
                du_kept[:, index * tile : (index + 1) * tile] = du

    @pl.when(step >= tiles)
    def _():
        total = dot_nt(da_kept[...], gate_ref[...]) + dot_nt(du_kept[...], up_ref[...])
        rows = total.shape[0] // parts
        for index in range(parts):
            dx_refs[index][...] = total[index * rows : (index + 1) * rows].astype(jnp.bfloat16)


def down_chunk(es, a, u, weight, kept, index, count):
    depth, width = weight.shape
    rows = len(es) * es[0].shape[0]
    hidden = width // 3
    tile = tile_of(hidden)
    tiles = hidden // tile
    row_tile = tile_of(depth)

    def column(t):
        return jnp.minimum(t, tiles - 1)

    def row(t):
        return jnp.maximum(t - tiles, 0)

    specs = [pl.BlockSpec(es[0].shape, lambda t: (0, 0))] * len(es) + [
        pl.BlockSpec((depth, tile), lambda t: (0, 2 * tiles + column(t))),
        pl.BlockSpec((rows, tile), lambda t: (index, column(t))),
        pl.BlockSpec((rows, tile), lambda t: (index, column(t))),
        pl.BlockSpec((row_tile, hidden), lambda t: (row(t), 0)),
        pl.BlockSpec((row_tile, hidden), lambda t: (row(t), 1)),
    ]
    operands = [*es, weight, a, u, weight, weight]
    part = es[0].shape
    shapes = [
        jax.ShapeDtypeStruct((rows * count, hidden), jnp.bfloat16),
        jax.ShapeDtypeStruct((rows * count, hidden), jnp.bfloat16),
        *[jax.ShapeDtypeStruct(part, jnp.bfloat16)] * len(es),
    ]
    aliases = {}
    if kept is not None:
        specs.extend([pl.BlockSpec(memory_space=pl.ANY)] * 2)
        aliases = {len(operands) + i: i for i in range(2)}
        operands.extend(kept)
    result = pl.pallas_call(
        functools.partial(down_kernel, len(es), tiles),
        grid=(tiles + depth // row_tile,),
        in_specs=specs,
        out_specs=[
            pl.BlockSpec((rows, tile), lambda t: (index, column(t))),
            pl.BlockSpec((rows, tile), lambda t: (index, column(t))),
            *[pl.BlockSpec((part[0], row_tile), lambda t: (0, row(t)))] * len(es),
        ],
        out_shape=shapes,
        input_output_aliases=aliases,
        scratch_shapes=[
            pltpu.VMEM((rows, hidden), jnp.bfloat16),
            pltpu.VMEM((rows, hidden), jnp.bfloat16),
            pltpu.VMEM((rows, depth), jnp.bfloat16),
        ],
        compiler_params=parameters(),
        cost_estimate=SMALL_COST,
        name="down_chunk",
    )(*operands)
    return result[:2], list(result[2:])


def weight_kernel(parts, count, blocks, split, place_ref, *refs):
    if parts == 1:
        x = refs[0][...]
    else:
        x = jnp.concatenate([ref[...] for ref in refs[:parts]], axis=0)
    ys = refs[parts : parts + count]
    step = pl.program_id(0)
    column = 0
    for y_ref in ys:
        width = y_ref.shape[1]
        piece = math.gcd(width, split) if width > split else width
        piece = math.gcd(piece, 1024) if piece > 1024 else piece
        for first in range(0, width, piece):
            total = dot_tn(x, y_ref[:, first : first + piece])
            start = column + first
            if len(refs) == parts + count + 1:
                refs[-1][:, start : start + piece] = total.astype(jnp.bfloat16)
                continue
            total += refs[parts + count][:, start : start + piece].astype(jnp.float32)
            total = total.astype(jnp.bfloat16)
            keep = step < blocks // 2 if start < split else lax.rem(step, 2) == 0
            keep_ref, send_ref = refs[-4:-2] if start < split else refs[-2:]
            columns = slice(start % split, start % split + piece)

            @pl.when(keep)
            def _():
                keep_ref[:, columns] = total

            @pl.when(jnp.logical_not(keep))
            def _():
                send_ref[:, columns] = total

        column += width


def weight_product(xs, ys, place, count, received):
    depth = xs[0].shape[1]
    rows = xs[0].shape[0]
    blocks = count // 2
    tile = depth // count
    total = sum(y.shape[1] for y in ys)
    split = -(-total // 256) * 128
    side = 1 if received is None else 0
    whole = pl.BlockSpec((tile, total), lambda t, p: (t, 0))
    if received is None:
        out_specs = whole
        out_shape = jax.ShapeDtypeStruct((depth // 2, total), jnp.bfloat16)
    else:
        half = blocks // 2
        out_specs = [
            pl.BlockSpec((tile, split), lambda t, p: (jnp.minimum(t, half - 1), 0)),
            pl.BlockSpec((tile, split), lambda t, p: (jnp.maximum(t - half, 0), 0)),
            pl.BlockSpec((tile, total - split), lambda t, p: (t // 2, 0)),
            pl.BlockSpec((tile, total - split), lambda t, p: (t // 2, 0)),
        ]
        out_shape = [
            jax.ShapeDtypeStruct((depth // 4, width), jnp.bfloat16)
            for width in (split, split, total - split, total - split)
        ]
    specs = [
        pl.BlockSpec((rows, tile), lambda t, p: (0, lax.bitwise_xor(p[0], 2 * t + side)))
    ] * len(xs)
    specs += [pl.BlockSpec(y.shape, lambda t, p: (0, 0)) for y in ys]
    operands = [*xs, *ys]
    if received is not None:
        specs.append(whole)
        operands.append(received)
    return pl.pallas_call(
        functools.partial(weight_kernel, len(xs), len(ys), blocks, split),
        grid_spec=pltpu.PrefetchScalarGridSpec(
            num_scalar_prefetch=1, grid=(blocks,), in_specs=specs, out_specs=out_specs
        ),
        out_shape=out_shape,
        compiler_params=parameters(),
        cost_estimate=SMALL_COST,
        name="weight_product",
    )(place, *operands)


def fold_kernel(count, *refs):
    for index in range(count):
        first, second = refs[2 * index : 2 * index + 2]
        keep, send = refs[2 * count + 2 * index : 2 * count + 2 * index + 2]
        rows = keep.shape[0]
        total = first[...].astype(jnp.float32) + second[...].astype(jnp.float32)
        total = total.astype(jnp.bfloat16)
        keep[...] = total[:rows]
        send[...] = total[rows:]


def fold(values):
    shapes = []
    for value in values[::2]:
        shape = (value.shape[0] // 2, value.shape[1])
        shapes.extend([jax.ShapeDtypeStruct(shape, jnp.bfloat16)] * 2)
    return pl.pallas_call(
        functools.partial(fold_kernel, len(values) // 2),
        out_shape=shapes,
        compiler_params=parameters(),
        cost_estimate=SMALL_COST,
        name="fold",
    )(*values)


def residual_kernel(parts, e_ref, hidden_ref, first_ref, second_ref, gain_ref, weight_ref, *refs):
    dh_ref, dz_ref = refs[:2]
    step = pl.program_id(0)

    @pl.when(step == 0)
    def _():
        values = hidden_ref[...]
        inverse = lax.rsqrt(jnp.mean(values * values, axis=-1, keepdims=True) + EPSILON)
        scaled = values * inverse
        grad = first_ref[...].astype(jnp.float32) + second_ref[...].astype(jnp.float32)
        grad = grad * gain_ref[...]
        projection = jnp.mean(grad * scaled, axis=-1, keepdims=True)
        total = e_ref[...].astype(jnp.float32) + inverse * (grad - scaled * projection)
        dh_ref[...] = total
        dz_ref[...] = total.astype(jnp.bfloat16)

    result = dot_nn(dz_ref[...], weight_ref[...]).astype(jnp.bfloat16)
    for index in range(parts):

        @pl.when(step == index)
        def _():
            refs[2 + index][...] = result


def residual_gradient(e, hidden_res, first, second, gain, weight, parts):
    rows, depth = e.shape
    tile = weight.shape[1] // parts
    whole = pl.BlockSpec((rows, depth), lambda t: (0, 0))
    result = pl.pallas_call(
        functools.partial(residual_kernel, parts),
        grid=(parts,),
        in_specs=[
            whole,
            whole,
            whole,
            whole,
            pl.BlockSpec((1, depth), lambda t: (0, 0)),
            pl.BlockSpec((depth, tile), lambda t: (0, t)),
        ],
        out_specs=[whole, whole] + [pl.BlockSpec((rows, tile), lambda t: (0, 0))] * parts,
        out_shape=[
            jax.ShapeDtypeStruct((rows, depth), jnp.float32),
            jax.ShapeDtypeStruct((rows, depth), jnp.bfloat16),
            *[jax.ShapeDtypeStruct((rows, tile), jnp.bfloat16)] * parts,
        ],
        compiler_params=parameters(),
        cost_estimate=SMALL_COST,
        name="residual_gradient",
    )(e, hidden_res, first, second, gain, weight)
    return result[0], result[1], list(result[2:])


def tie(value, *others):
    return lax.optimization_barrier((value, others))[0]


def together(*values):
    return lax.optimization_barrier(values)


def add(first, second):
    return (first.astype(jnp.float32) + second.astype(jnp.float32)).astype(jnp.bfloat16)


class Mover:
    def __init__(self):
        self.dp_count = lax.axis_size("dp")
        self.ring = lax.axis_size("tensor")
        self.steps = []
        step = 2
        while step < self.dp_count:
            self.steps.append(step)
            step *= 2

    def swap(self, value, step):
        return lax.ppermute(value, "dp", [(i, i ^ step) for i in range(self.dp_count)])

    def gather(self, shard):
        return lax.all_gather(shard, "dp", axis=0, tiled=True)

    def begin(self, pieces, level):
        orders = (self.steps[::-1], self.steps[:1] + self.steps[:0:-1])
        result = []
        for side in range(2):
            keep, send = pieces[2 * side : 2 * side + 2]
            result.extend([keep, self.swap(send, orders[side][level])])
        return result

    def advance(self, values, level=1):
        while level < len(self.steps):
            values = self.begin(fold(values), level)
            level += 1
        return values

    def hop(self, value, shift=1):
        return lax.ppermute(
            value, "tensor", [(i, (i + shift) % self.ring) for i in range(self.ring)]
        )

    def spread(self, value):
        ring = self.ring
        return [value] + [
            lax.ppermute(value, "tensor", [(i, (i - j) % ring) for i in range(ring)])
            for j in range(1, ring)
        ]

    def collect(self, parts):
        ring = self.ring
        total = parts[0]
        for j in range(1, ring):
            moved = lax.ppermute(
                parts[j].astype(jnp.bfloat16), "tensor", [(i, (i + j) % ring) for i in range(ring)]
            )
            total = total + moved.astype(jnp.float32)
        return total

    def exchange(self, parts):
        ring = self.ring
        return [parts[0]] + [
            lax.ppermute(parts[j], "tensor", [(i, (i + j) % ring) for i in range(ring)])
            for j in range(1, ring)
        ]


def total_of(values):
    return jnp.concatenate(
        [
            first.astype(jnp.float32) + second.astype(jnp.float32)
            for first, second in zip(values[::2], values[1::2])
        ],
        axis=1,
    )


def back_norm(grad_normed, scaled, inverse, scale_row):
    grad_scaled = grad_normed * scale_row
    projection = jnp.mean(grad_scaled * scaled, axis=-1, keepdims=True)
    return inverse * (grad_scaled - scaled * projection)


def per_device(
    tokens,
    seq_lengths,
    attention_gain,
    query_matrix,
    key_matrix,
    value_matrix,
    output_weight,
    feedforward_gain,
    gate_weight,
    up_weight,
    down_weight,
    cotangent,
):
    mover = Mover()
    dp_count = mover.dp_count
    ring = mover.ring
    dp_place = lax.axis_index("dp").astype(jnp.int32).reshape(1)
    ring_place = lax.axis_index("tensor")
    place = ring_place.astype(jnp.int32).reshape(1)
    _, local_rows, model_width = tokens.shape
    complete_rows = local_rows * ring
    hidden = gate_weight.shape[1]
    groups = key_matrix.shape[1] // HEAD_SIZE
    joint_width = groups * GROUP_WIDTH
    f32 = jnp.float32
    b16 = jnp.bfloat16

    doc_ids, positions = layout(seq_lengths, complete_rows)
    row_index = jnp.arange(complete_rows, dtype=jnp.int32)
    doc_ids = jnp.where(doc_ids[0] < PIECES, doc_ids[0], PIECES + row_index)

    def to_relative(values):
        view = values.reshape((ring, local_rows) + values.shape[1:])
        return jnp.roll(view, -(ring_place + 1), axis=0)[::-1].reshape(values.shape)

    doc_ids = to_relative(doc_ids)
    cosine, sine = rope_tables(to_relative(positions[0]), HEAD_SIZE)
    cosine_table = jnp.tile(cosine, (1, 128 // cosine.shape[1]))
    sine_table = jnp.tile(jnp.concatenate([-sine, sine], axis=1), (1, 128 // HEAD_SIZE))

    def grouped(query, key, value):
        pieces = []
        for g in range(groups):
            pieces.append(query[:, g * GROUP_QUERY : (g + 1) * GROUP_QUERY])
            pieces.append(key[:, g * HEAD_SIZE : (g + 1) * HEAD_SIZE])
            pieces.append(value[:, g * HEAD_SIZE : (g + 1) * HEAD_SIZE])
        return jnp.concatenate(pieces, axis=1)

    joint_matrix = grouped(query_matrix, key_matrix, value_matrix)
    own_gains = jnp.stack([attention_gain, feedforward_gain], axis=1)
    joint_full = mover.gather(
        jnp.concatenate([joint_matrix, jnp.pad(own_gains, ((0, 0), (0, 126)))], axis=1)
    )
    output_parts = mover.spread(output_weight.T)
    ff_shard = jnp.concatenate([gate_weight, up_weight, down_weight.T], axis=1)
    output_parts, cosine_table, sine_table, doc_ids, ff_shard, local_tokens = together(
        output_parts, cosine_table, sine_table, doc_ids, ff_shard, tokens[0]
    )
    token_chunks = [local_tokens, mover.hop(local_tokens)]
    output_ring = join(output_parts, [0] * ring)
    output_full = mover.gather(output_ring)
    ff_full = mover.gather(tie(ff_shard, output_ring))
    gains = joint_full[:, joint_width : joint_width + 2].T.astype(f32)
    gain_one, gain_two = gains[:1], gains[1:]

    def projection(kept, index):
        return project(
            token_chunks[index],
            gain_one,
            joint_full,
            cosine_table,
            sine_table,
            kept,
            index,
            ring,
            groups,
        )

    kept = projection(None, 0)
    for j in range(1, ring):
        token_chunks[j], kept = together(token_chunks[j], kept)
        if j + 1 < ring:
            token_chunks.append(mover.hop(token_chunks[j]))
        else:
            local_cotangent = tie(cotangent[0], token_chunks[j])
            moved = mover.hop(local_cotangent)
        kept = projection(kept, j)
    normed_one, joint = kept
    attended, totals = attention_forward(joint, doc_ids, place, ring, groups)
    moved, attended = together(moved, attended)
    cotangent_chunks = [local_cotangent, moved]
    attended_parts = [attended]
    while len(attended_parts) < ring:
        part = mover.hop(attended_parts[-1], -1)
        if len(attended_parts) == ring - 1:
            partial = heads_product(
                tie(attended_parts, attended_parts[-1]), output_full, token_chunks
            )
            part, partial = together(part, partial)
        attended_parts.append(part)
    moved, last = together(moved, attended_parts[-1])

    pairs = ring // 2
    moved = mover.hop(moved)
    hidden_res, normed_two = after_attention(partial, last, output_full, gain_two, ring)
    upward = up_chunk(normed_two, ff_full, None, 0, pairs)
    downward = None
    grads = []

    def chunks_of(pair):
        return [cotangent_chunks[(2 * pair + i) % ring] for i in (1, 2)]

    def lower(pair, kept):
        return down_chunk(chunks_of(pair), upward[0], upward[1], ff_full, kept, pair, pairs)

    for j in range(2, ring):
        if j > 2:
            moved = mover.hop(moved)
            if j % 2:
                downward, parts = lower((j - 3) // 2, downward)
                grads.extend(parts)
            else:
                upward = up_chunk(normed_two, ff_full, upward, j // 2 - 1, pairs)
        moved, upward, downward, grads = together(moved, upward, downward, grads)
        cotangent_chunks.append(moved)

    def weights(xs, ys, received=None):
        return weight_product(xs, ys, dp_place, dp_count, received)

    ordered = cotangent_chunks[1:] + cotangent_chunks[:1]
    total = grads[0]
    moved = mover.hop(total)
    upward = up_chunk(tie(normed_two, total), ff_full, upward, pairs - 1, pairs)
    product = upward[2]
    down_part = weights(ordered, [product])
    moved, upward, down_part = together(moved, upward, down_part)
    down_part = mover.swap(down_part, 1)
    for j in range(2, ring):
        total = add(moved, grads[j - 1])
        moved = mover.hop(total)
        if j == 2:
            downward, parts = lower(pairs - 1, tie(downward, total))
            grads.extend(parts)
            moved, downward, grads = together(moved, downward, grads)
            grad_gate, grad_up = downward
        if j == 3:
            gate_part = weights([tie(normed_two, total)], [grad_gate])
            up_part = weights([tie(normed_two, gate_part)], [grad_up])
            down_part = weights(tie(ordered, up_part), [product], down_part)
            moved, gate_part, up_part, down_part = together(moved, gate_part, up_part, down_part)
    grad_hidden, grad_branch, grad_parts = residual_gradient(
        local_cotangent, hidden_res, moved, grads[-1], gain_two, output_full, ring
    )

    grad_parts = mover.exchange(grad_parts)
    gate_part, up_part = mover.swap(gate_part, 1), mover.swap(up_part, 1)
    down_part = mover.begin(down_part, 0)
    branch = transposed_product([tie(product, grad_branch)], ff_full, 2, ring)
    gate_part = weights([tie(normed_two, branch)], [grad_gate], gate_part)
    grad_parts, branch, gate_part, up_part, down_part = together(
        grad_parts, branch, gate_part, up_part, down_part
    )
    grad_joint = []
    sent = 0
    moved = branch[0]
    for group in range(groups):
        moved = mover.hop(moved)
        grad_joint.append(
            attention_backward(
                joint,
                attended,
                tie(grad_parts, grad_joint),
                totals,
                doc_ids,
                cosine_table,
                sine_table,
                place,
                group,
            )
        )
        if group == 0:
            up_part = weights([tie(normed_two, grad_joint)], [grad_up], up_part)
            gate_part = mover.begin(gate_part, 0)
        else:
            up_part = mover.begin(up_part, 0)
        if group + 1 == groups:
            grads = transposed_product(grad_joint, joint_full, 0, ring)
        moved, grad_joint, grads, gate_part, up_part = together(
            moved, grad_joint, grads, gate_part, up_part
        )
        sent += 1
        if group + 1 < groups:
            moved = add(moved, branch[sent])
    if groups == 1:
        up_part = mover.begin(up_part, 0)
    branch_moved = moved
    attended_local = join(attended_parts, list(range(ring)))
    moved = grads[0]
    for j in range(1, ring):
        total = grads[1] if j == 1 else add(moved, grads[j])
        moved = mover.hop(total)
        if j == 1:
            gate_part, down_part = mover.advance(gate_part), mover.advance(down_part)
            output_part = weights([tie(grad_branch, total)], [attended_local])
            joint_part = weights([tie(normed_one, output_part)], grad_joint)
            output_part = mover.swap(output_part, 1)
            output_part = weights([tie(grad_branch, joint_part)], [attended_local], output_part)
            moved, joint_part, output_part, gate_part, down_part = together(
                moved, joint_part, output_part, gate_part, down_part
            )
        if j == 2:
            output_part = mover.begin(output_part, 0)
            joint_part = mover.swap(joint_part, 1)
            joint_part = weights([tie(normed_one, total)], grad_joint, joint_part)
            moved, joint_part, output_part = together(moved, joint_part, output_part)
        if j == 3:
            output_part = mover.advance(output_part)
            up_part = mover.advance(up_part)
            joint_part = mover.begin(joint_part, 0)
            moved, joint_part, output_part, up_part = together(
                moved, joint_part, output_part, up_part
            )
    joint_part = mover.advance(joint_part)
    for j in range(sent, ring - 1):
        branch_moved = mover.hop(add(branch_moved, branch[j]))
    output_out = mover.collect(jnp.split(total_of(output_part), ring, axis=1)).T
    scaled_one, inverse_one = norm_rows(local_tokens.astype(f32))
    local_one = moved.astype(f32) + grads[0].astype(f32)
    input_gradient = grad_hidden + back_norm(local_one, scaled_one, inverse_one, gain_one)
    block_output = (
        hidden_res + (branch_moved.astype(f32) + branch[-1].astype(f32))
    ).astype(b16)
    gate_out, up_out, joint_out = total_of(gate_part), total_of(up_part), total_of(joint_part)
    down_out = total_of(down_part).T

    sums = jnp.stack(
        [
            jnp.sum(joint_out * joint_matrix.astype(f32), axis=1) / attention_gain.astype(f32),
            jnp.sum(gate_out * gate_weight.astype(f32) + up_out * up_weight.astype(f32), axis=1)
            / feedforward_gain.astype(f32),
        ]
    )
    gain_out = sums
    for shift in range(1, ring):
        gain_out = gain_out + lax.ppermute(
            sums, "tensor", [(i, (i + shift) % ring) for i in range(ring)]
        )

    def ungrouped(first, width):
        return jnp.concatenate(
            [
                joint_out[:, g * GROUP_WIDTH + first : g * GROUP_WIDTH + first + width]
                for g in range(groups)
            ],
            axis=1,
        )

    return (
        block_output[None],
        input_gradient[None],
        gain_out[0],
        ungrouped(0, GROUP_QUERY),
        ungrouped(GROUP_QUERY, HEAD_SIZE),
        ungrouped(GROUP_QUERY + HEAD_SIZE, HEAD_SIZE),
        output_out,
        gain_out[1],
        gate_out,
        up_out,
        down_out,
    )


def solution(mesh):
    return jax.shard_map(
        per_device,
        mesh=mesh,
        in_specs=(
            P("dp", "tensor", None),
            P("dp", None),
            P("dp"),
            P("dp", "tensor"),
            P("dp", "tensor"),
            P("dp", "tensor"),
            P("tensor", "dp"),
            P("dp"),
            P("dp", "tensor"),
            P("dp", "tensor"),
            P("tensor", "dp"),
            P("dp", "tensor", None),
        ),
        out_specs=(
            P("dp", "tensor", None),
            P("dp", "tensor", None),
            P("dp"),
            P("dp", "tensor"),
            P("dp", "tensor"),
            P("dp", "tensor"),
            P("tensor", "dp"),
            P("dp"),
            P("dp", "tensor"),
            P("dp", "tensor"),
            P("tensor", "dp"),
        ),
        check_vma=False,
    )
```

```python
import functools
import math

import jax
import jax.numpy as jnp
from jax import lax
from jax.experimental import pallas as pl
from jax.experimental.pallas import tpu as pltpu
from jax.sharding import PartitionSpec as P

QUERY_HEADS = 32
KEY_VALUE_HEADS = 8
HEAD_SIZE = 64
PIECES = 4


EPSILON = 1e-05
ROPE_BASE = 500000.0
NEGATIVE = -1e30
GROUP_QUERY = QUERY_HEADS // KEY_VALUE_HEADS * HEAD_SIZE
GROUP_WIDTH = GROUP_QUERY + 2 * HEAD_SIZE
KERNEL_VMEM = 60 * 1024 * 1024
SMALL_COST = pl.CostEstimate(flops=1, bytes_accessed=1, transcendentals=0)


def layout(lengths, complete_rows):
    doc_ends = jnp.cumsum(lengths, axis=-1)
    row_index = jnp.arange(complete_rows, dtype=jnp.int32)
    piece_count = lengths.shape[-1]
    doc_ids = jnp.sum((row_index[None, :, None] >= doc_ends[:, None, :]).astype(jnp.int32), axis=2)
    starts = doc_ends - lengths
    chosen = doc_ids[:, :, None] == jnp.arange(piece_count, dtype=jnp.int32)[None, None, :]
    doc_begin = jnp.sum(jnp.where(chosen, starts[:, None, :], 0), axis=2) + jnp.where(
        doc_ids == piece_count, doc_ends[:, -1:], 0
    )
    return (doc_ids, row_index[None, :] - doc_begin)


def rope_tables(positions, head_dim):
    half_dim = head_dim // 2
    frequency = ROPE_BASE ** (-(jnp.arange(half_dim, dtype=jnp.float32) * (2.0 / head_dim)))
    angles = positions.astype(jnp.float32)[..., None] * frequency
    return (jnp.cos(angles), jnp.sin(angles))


def norm_rows(values):
    inverse = lax.rsqrt(jnp.mean(values * values, axis=-1, keepdims=True) + EPSILON)
    return (values * inverse, inverse)


def dot_nt(left, right):
    return lax.dot_general(
        left, right, (((1,), (1,)), ((), ())), preferred_element_type=jnp.float32
    )


def dot_nn(left, right):
    return jnp.dot(left, right, preferred_element_type=jnp.float32)


def dot_tn(left, right):
    return lax.dot_general(
        left, right, (((0,), (0,)), ((), ())), preferred_element_type=jnp.float32
    )


def tile_of(size, limit=512):
    tile = limit
    while size % tile:
        tile //= 2
    return tile


def parameters():
    return pltpu.CompilerParams(vmem_limit_bytes=KERNEL_VMEM)


def swap_halves(values):
    lane = lax.broadcasted_iota(jnp.int32, values.shape, 1)
    half = HEAD_SIZE // 2
    return jnp.where(
        lane % HEAD_SIZE < half, pltpu.roll(values, 128 - half, 1), pltpu.roll(values, half, 1)
    )


def turned(values, cosine, sine, start):
    result = values * cosine + swap_halves(values) * sine
    rotated = GROUP_WIDTH - HEAD_SIZE
    if start + 128 <= rotated:
        return result
    lane = lax.broadcasted_iota(jnp.int32, values.shape, 1)
    return jnp.where(lane < rotated - start, result, values)


def project_kernel(x_ref, gain_ref, weight_ref, cos_ref, sin_ref, *refs):
    normed_ref, joint_ref = refs[-2:]

    @pl.when(pl.program_id(0) == 0)
    def _():
        values = x_ref[...].astype(jnp.float32)
        inverse = lax.rsqrt(jnp.mean(values * values, axis=-1, keepdims=True) + EPSILON)
        normed_ref[...] = (values * inverse * gain_ref[...]).astype(jnp.bfloat16)

    product = dot_nn(normed_ref[...], weight_ref[...])
    for start in range(0, GROUP_WIDTH, 128):
        part = turned(product[:, start : start + 128], cos_ref[...], sin_ref[...], start)
        if start < GROUP_QUERY:
            part = part * HEAD_SIZE ** (-0.5)
        joint_ref[:, start : start + 128] = part.astype(jnp.bfloat16)


def project(x, gain, weight, cosine, sine, kept, index, count, groups):
    rows, depth = x.shape
    specs = [
        pl.BlockSpec((rows, depth), lambda g: (0, 0)),
        pl.BlockSpec((1, depth), lambda g: (0, 0)),
        pl.BlockSpec((depth, GROUP_WIDTH), lambda g: (0, g)),
        pl.BlockSpec((rows, 128), lambda g: (index, 0)),
        pl.BlockSpec((rows, 128), lambda g: (index, 0)),
    ]
    operands = [x, gain, weight, cosine, sine]
    aliases = {}
    if kept is not None:
        specs.extend([pl.BlockSpec(memory_space=pl.ANY)] * 2)
        aliases = {len(operands) + i: i for i in range(2)}
        operands.extend(kept)
    return pl.pallas_call(
        project_kernel,
        grid=(groups,),
        in_specs=specs,
        out_specs=[
            pl.BlockSpec((rows, depth), lambda g: (index, 0)),
            pl.BlockSpec((rows, GROUP_WIDTH), lambda g: (index, g)),
        ],
        out_shape=[
            jax.ShapeDtypeStruct((rows * count, depth), jnp.bfloat16),
            jax.ShapeDtypeStruct((rows * count, GROUP_WIDTH * groups), jnp.bfloat16),
        ],
        input_output_aliases=aliases,
        compiler_params=parameters(),
        cost_estimate=SMALL_COST,
        name="project",
    )(*operands)


def ring_offset(place, chunk, count, rows):
    return pl.multiple_of(lax.rem(place - chunk + count, count) * rows, rows)


def stack_heads(target, source):
    rows, width = source.shape
    for head in range(width // HEAD_SIZE):
        target[head * rows : (head + 1) * rows, :] = source[
            :, head * HEAD_SIZE : (head + 1) * HEAD_SIZE
        ]


def fill_bias(bias, key_docs, query_docs, earlier):
    rows = key_docs.shape[0]
    row_index = lax.broadcasted_iota(jnp.int32, (rows, rows), 0)
    column_index = lax.broadcasted_iota(jnp.int32, (rows, rows), 1)
    same = (key_docs == query_docs) & ((row_index <= column_index) | earlier)
    values = jnp.where(same, 0.0, NEGATIVE)
    for first in range(0, bias.shape[1], rows):
        bias[:, first : first + rows] = values


def forward_kernel(
    count,
    place_ref,
    own_ref,
    all_ref,
    docq_ref,
    dock_ref,
    o_ref,
    lse_ref,
    bias,
    queries,
    values_all,
    mixed,
):
    chunk = pl.program_id(1)
    place = place_ref[0]
    rows = own_ref.shape[0]
    heads = GROUP_QUERY // HEAD_SIZE
    stack_heads(queries, own_ref.at[:, :GROUP_QUERY])

    @pl.when(chunk == 0)
    def _():
        values = all_ref[:, GROUP_QUERY:].astype(jnp.float32)
        values_all[...] = values.T[HEAD_SIZE:].astype(jnp.bfloat16)

    mixed[...] = jnp.zeros_like(mixed)

    def block(j, carry):
        peaks, total = carry
        offset = ring_offset(place, j, count, rows)
        piece = pl.ds(offset, rows)
        fill_bias(bias, dock_ref[piece, :], docq_ref[...], j < chunk)
        keys = all_ref[piece, GROUP_QUERY : GROUP_QUERY + HEAD_SIZE]
        scores = dot_nt(keys, queries[...]) + bias[...]
        higher = jnp.maximum(peaks, jnp.max(scores, axis=0, keepdims=True))
        probs = jnp.exp(scores - higher)
        scale = jnp.exp(peaks - higher)
        mixed[...] = mixed[...] * scale + dot_nn(
            values_all[:, piece], probs.astype(jnp.bfloat16)
        )
        return higher, total * scale + jnp.sum(probs, axis=0, keepdims=True)

    peaks, total = lax.fori_loop(
        0,
        chunk + 1,
        block,
        (
            jnp.full((1, heads * rows), NEGATIVE, jnp.float32),
            jnp.zeros((1, heads * rows), jnp.float32),
        ),
    )
    lse_ref[:1, :] = peaks + jnp.log(total)
    result = mixed[...] / total
    for head in range(0, heads, 2):
        pair = jnp.concatenate(
            [result[:, (head + i) * rows : (head + i + 1) * rows] for i in range(2)], axis=0
        )
        o_ref[:, head * HEAD_SIZE : (head + 2) * HEAD_SIZE] = pair.T.astype(jnp.bfloat16)


def attention_forward(joint, docs, place, count, groups):
    total_rows = joint.shape[0]
    rows = total_rows // count
    stacked = rows * GROUP_QUERY // HEAD_SIZE

    def block(c, place_ref):
        return lax.rem(place_ref[0] - c + count, count)

    spec = pltpu.PrefetchScalarGridSpec(
        num_scalar_prefetch=1,
        grid=(groups, count),
        in_specs=[
            pl.BlockSpec((rows, GROUP_WIDTH), lambda g, c, p: (block(c, p), g)),
            pl.BlockSpec((total_rows, GROUP_WIDTH), lambda g, c, p: (0, g)),
            pl.BlockSpec((1, rows), lambda g, c, p: (0, block(c, p))),
            pl.BlockSpec((total_rows, 1), lambda g, c, p: (0, 0)),
        ],
        out_specs=[
            pl.BlockSpec((rows, GROUP_QUERY), lambda g, c, p: (block(c, p), g)),
            pl.BlockSpec((8, stacked), lambda g, c, p: (g, block(c, p))),
        ],
        scratch_shapes=[
            pltpu.VMEM((rows, stacked), jnp.float32),
            pltpu.VMEM((stacked, HEAD_SIZE), jnp.bfloat16),
            pltpu.VMEM((HEAD_SIZE, total_rows), jnp.bfloat16),
            pltpu.VMEM((HEAD_SIZE, stacked), jnp.float32),
        ],
    )
    return pl.pallas_call(
        functools.partial(forward_kernel, count),
        grid_spec=spec,
        out_shape=[
            jax.ShapeDtypeStruct((total_rows, GROUP_QUERY * groups), jnp.bfloat16),
            jax.ShapeDtypeStruct((8 * groups, stacked * count), jnp.float32),
        ],
        compiler_params=parameters(),
        cost_estimate=SMALL_COST,
        name="attend",
    )(place, joint, joint, docs[None, :], docs[:, None])


def backward_kernel(count, place_ref, *refs):
    own_ref, all_ref, o_ref = refs[:3]
    lse_ref, docq_ref, dock_ref, cos_ref, sin_ref = refs[3 + count : 8 + count]
    out_ref, bias, queries, grads, keys_all, values_all, sum_q, sum_k, sum_v = refs[8 + count :]
    chunk = pl.program_id(0)
    place = place_ref[0]
    rows = own_ref.shape[0]
    heads = GROUP_QUERY // HEAD_SIZE
    stack_heads(queries, own_ref.at[:, :GROUP_QUERY])
    for index in range(count):

        @pl.when(lax.rem(place - chunk + count, count) == index)
        def _():
            stack_heads(grads, refs[3 + index])

    @pl.when(chunk == 0)
    def _():
        keys_all[...] = all_ref[:, GROUP_QUERY : GROUP_QUERY + HEAD_SIZE]
        values_all[...] = all_ref[:, GROUP_QUERY + HEAD_SIZE :]
        sum_k[...] = jnp.zeros_like(sum_k)
        sum_v[...] = jnp.zeros_like(sum_v)

    sum_q[...] = jnp.zeros_like(sum_q)
    ones = jnp.ones((8, HEAD_SIZE), jnp.bfloat16)
    inner = []
    for head in range(heads):
        attended = o_ref[:, head * HEAD_SIZE : (head + 1) * HEAD_SIZE].astype(jnp.float32)
        both = attended * grads[head * rows : (head + 1) * rows, :].astype(jnp.float32)
        high = both.astype(jnp.bfloat16)
        low = (both - high.astype(jnp.float32)).astype(jnp.bfloat16)
        inner.append((dot_nt(ones, high) + dot_nt(ones, low))[:1])
    inner = jnp.concatenate(inner, axis=1)

    def block(j, carry):
        offset = ring_offset(place, j, count, rows)
        piece = pl.ds(offset, rows)
        fill_bias(bias, dock_ref[piece, :], docq_ref[...], j < chunk)
        probs = jnp.exp(dot_nt(keys_all[piece, :], queries[...]) + bias[...] - lse_ref[:1, :])
        grad_probs = dot_nt(values_all[piece, :], grads[...])
        grad_scores = (probs * (grad_probs - inner)).astype(jnp.bfloat16)
        sum_v[piece, :] += dot_nn(probs.astype(jnp.bfloat16), grads[...])
        sum_k[piece, :] += dot_nn(grad_scores, queries[...])
        sum_q[...] += dot_tn(grad_scores, keys_all[piece, :])
        return carry

    lax.fori_loop(0, chunk + 1, block, 0)
    own = pl.ds(ring_offset(place, chunk, count, rows), rows)
    for first in range(0, heads, 2):
        start = first * HEAD_SIZE
        part = jnp.concatenate(
            [sum_q[(first + i) * rows : (first + i + 1) * rows, :] for i in range(2)], axis=1
        )
        part = turned(part, cos_ref[own, :], -sin_ref[own, :], start)
        out_ref[own, start : start + 128] = (part * HEAD_SIZE ** (-0.5)).astype(jnp.bfloat16)

    @pl.when(chunk == count - 1)
    def _():
        part = jnp.concatenate([sum_k[...], sum_v[...]], axis=1)
        part = turned(part, cos_ref[...], -sin_ref[...], GROUP_QUERY)
        out_ref[:, GROUP_QUERY:] = part.astype(jnp.bfloat16)


def attention_backward(joint, attended, grads, lse, docs, cosine, sine, place, group):
    count = len(grads)
    total_rows = joint.shape[0]
    rows = total_rows // count
    stacked = rows * GROUP_QUERY // HEAD_SIZE

    def block(c, place_ref):
        return lax.rem(place_ref[0] - c + count, count)

    table = pl.BlockSpec((total_rows, 128), lambda c, p: (0, 0))
    spec = pltpu.PrefetchScalarGridSpec(
        num_scalar_prefetch=1,
        grid=(count,),
        in_specs=[
            pl.BlockSpec((rows, GROUP_WIDTH), lambda c, p: (block(c, p), group)),
            pl.BlockSpec((total_rows, GROUP_WIDTH), lambda c, p: (0, group)),
            pl.BlockSpec((rows, GROUP_QUERY), lambda c, p: (block(c, p), group)),
            *[pl.BlockSpec((rows, GROUP_QUERY), lambda c, p: (0, group))] * count,
            pl.BlockSpec((8, stacked), lambda c, p: (group, block(c, p))),
            pl.BlockSpec((1, rows), lambda c, p: (0, block(c, p))),
            pl.BlockSpec((total_rows, 1), lambda c, p: (0, 0)),
            table,
            table,
        ],
        out_specs=pl.BlockSpec((total_rows, GROUP_WIDTH), lambda c, p: (0, 0)),
        scratch_shapes=[
            pltpu.VMEM((rows, stacked), jnp.float32),
            *[pltpu.VMEM((stacked, HEAD_SIZE), jnp.bfloat16)] * 2,
            *[pltpu.VMEM((total_rows, HEAD_SIZE), jnp.bfloat16)] * 2,
            pltpu.VMEM((stacked, HEAD_SIZE), jnp.float32),
            *[pltpu.VMEM((total_rows, HEAD_SIZE), jnp.float32)] * 2,
        ],
    )
    return pl.pallas_call(
        functools.partial(backward_kernel, count),
        grid_spec=spec,
        out_shape=jax.ShapeDtypeStruct((total_rows, GROUP_WIDTH), jnp.bfloat16),
        compiler_params=parameters(),
        cost_estimate=SMALL_COST,
        name="attend_back",
    )(
        place,
        joint,
        joint,
        attended,
        *grads,
        lse,
        docs[None, :],
        docs[:, None],
        cosine,
        sine,
    )


def join_kernel(*refs):
    place = 0
    for ref in refs[:-1]:
        size = ref.shape[1]
        refs[-1][:, place : place + size] = ref[...]
        place += size


def join(parts, blocks):
    rows = parts[0].shape[0] // (max(blocks) + 1)
    width = sum(part.shape[1] for part in parts)
    return pl.pallas_call(
        join_kernel,
        grid=(1,),
        in_specs=[
            pl.BlockSpec((rows, part.shape[1]), lambda i, block=block: (block, 0))
            for part, block in zip(parts, blocks)
        ],
        out_specs=pl.BlockSpec((rows, width), lambda i: (0, 0)),
        out_shape=jax.ShapeDtypeStruct((rows, width), parts[0].dtype),
        compiler_params=parameters(),
        cost_estimate=SMALL_COST,
        name="join",
    )(*parts)


def transposed_kernel(count, parts, *refs):
    total = dot_nt(refs[0][...], refs[count][...])
    for index in range(1, count):
        total += dot_nt(refs[index][...], refs[count + index][...])
    rows = total.shape[0] // parts
    for index in range(parts):
        refs[2 * count + index][...] = total[index * rows : (index + 1) * rows].astype(
            jnp.bfloat16
        )


def transposed_product(xs, weight, column, parts, block=0, blocks=1):
    rows, depth = xs[0].shape
    rows //= blocks
    width = weight.shape[0]
    tile = tile_of(width)
    specs = [pl.BlockSpec((rows, depth), lambda t: (block, 0))] * len(xs)
    for index in range(len(xs)):
        specs.append(pl.BlockSpec((tile, depth), lambda t, index=index: (t, column + index)))
    part = (rows // parts, width)
    return pl.pallas_call(
        functools.partial(transposed_kernel, len(xs), parts),
        grid=(width // tile,),
        in_specs=specs,
        out_specs=[pl.BlockSpec((part[0], tile), lambda t: (0, t))] * parts,
        out_shape=[jax.ShapeDtypeStruct(part, jnp.bfloat16)] * parts,
        compiler_params=parameters(),
        cost_estimate=SMALL_COST,
        name="transposed",
    )(*xs, *[weight] * len(xs))


def heads_kernel(count, *refs):
    parts = refs[:count]
    weight_ref = refs[count]
    tokens = refs[count + 1 : -1]
    out_ref = refs[-1]
    step = pl.program_id(0)
    width = parts[0].shape[1]
    for j in range(count):
        term = dot_nt(parts[j][...], weight_ref[:, j * width : (j + 1) * width])
        if j == 0:
            out_ref[...] = term
        else:
            out_ref[...] += term
    for index in range(len(tokens)):

        @pl.when(step == index)
        def _():
            out_ref[...] += tokens[index][...].astype(jnp.float32)


def heads_product(parts, weight, tokens):
    blocks = len(tokens)
    rows, width = tokens[0].shape
    depth = parts[0].shape[1]
    specs = [
        pl.BlockSpec((rows, depth), lambda i, j=j: (lax.rem(i + j, blocks), 0))
        for j in range(len(parts))
    ]
    whole = pl.BlockSpec((rows, width), lambda i: (0, 0), pipeline_mode=pl.Buffered(1))
    return pl.pallas_call(
        functools.partial(heads_kernel, len(parts)),
        grid=(blocks,),
        in_specs=[
            *specs,
            pl.BlockSpec(
                (width, depth * len(parts)), lambda i: (0, 0), pipeline_mode=pl.Buffered(1)
            ),
            *[whole] * blocks,
        ],
        out_specs=pl.BlockSpec((rows, width), lambda i: (i, 0)),
        out_shape=jax.ShapeDtypeStruct((rows * blocks, width), jnp.float32),
        compiler_params=parameters(),
        cost_estimate=SMALL_COST,
        name="heads_product",
    )(*parts, weight, *tokens)


def attended_kernel(partial_ref, last_ref, weight_ref, gain_ref, hidden_ref, normed_ref):
    values = partial_ref[...] + dot_nt(last_ref[...], weight_ref[...])

    @pl.when(pl.program_id(0) == 0)
    def _():
        hidden_ref[...] = values

    inverse = lax.rsqrt(jnp.mean(values * values, axis=-1, keepdims=True) + EPSILON)
    normed_ref[...] = (values * inverse * gain_ref[...]).astype(jnp.bfloat16)


def after_attention(partial, last, weight, gain, count):
    total_rows, width = partial.shape
    rows = total_rows // count
    depth = last.shape[1]
    return pl.pallas_call(
        attended_kernel,
        grid=(count,),
        in_specs=[
            pl.BlockSpec((rows, width), lambda i: (i, 0)),
            pl.BlockSpec((rows, depth), lambda i: (lax.rem(i + count - 1, count), 0)),
            pl.BlockSpec((width, depth), lambda i: (0, count - 1)),
            pl.BlockSpec((1, width), lambda i: (0, 0)),
        ],
        out_specs=[
            pl.BlockSpec((rows, width), lambda i: (0, 0)),
            pl.BlockSpec((rows, width), lambda i: (lax.rem(i + count - 1, count), 0)),
        ],
        out_shape=[
            jax.ShapeDtypeStruct((rows, width), jnp.float32),
            jax.ShapeDtypeStruct((total_rows, width), jnp.bfloat16),
        ],
        compiler_params=parameters(),
        cost_estimate=SMALL_COST,
        name="after_attention",
    )(partial, last, weight, gain)


def up_kernel(x_ref, gate_ref, up_ref, *refs):
    a_ref, u_ref, g_ref = refs[-3:]
    gate = dot_nn(x_ref[...], gate_ref[...])
    up = dot_nn(x_ref[...], up_ref[...])
    a_ref[...] = gate.astype(jnp.bfloat16)
    u_ref[...] = up.astype(jnp.bfloat16)
    g_ref[...] = (gate * jax.nn.sigmoid(gate) * up).astype(jnp.bfloat16)


def up_chunk(x, weight, kept, index, count):
    total_rows, depth = x.shape
    rows = total_rows // count
    hidden = weight.shape[1] // 3
    tile = tile_of(hidden)
    tiles = hidden // tile
    specs = [
        pl.BlockSpec((rows, depth), lambda t: (index, 0)),
        pl.BlockSpec((depth, tile), lambda t: (0, t)),
        pl.BlockSpec((depth, tile), lambda t: (0, tiles + t)),
    ]
    operands = [x, weight, weight]
    aliases = {}
    if kept is not None:
        specs.extend([pl.BlockSpec(memory_space=pl.ANY)] * 3)
        aliases = {len(operands) + i: i for i in range(3)}
        operands.extend(kept)
    return pl.pallas_call(
        up_kernel,
        grid=(tiles,),
        in_specs=specs,
        out_specs=[pl.BlockSpec((rows, tile), lambda t: (index, t))] * 3,
        out_shape=[jax.ShapeDtypeStruct((total_rows, hidden), jnp.bfloat16)] * 3,
        input_output_aliases=aliases,
        compiler_params=parameters(),
        cost_estimate=SMALL_COST,
        name="up_chunk",
    )(*operands)


def down_kernel(parts, tiles, *refs):
    down_ref, a_ref, u_ref, gate_ref, up_ref = refs[parts : parts + 5]
    da_ref, du_ref = refs[-5 - parts : -3 - parts]
    dx_refs = refs[-3 - parts : -3]
    da_kept, du_kept, e_out = refs[-3:]
    step = pl.program_id(0)

    @pl.when(step == 0)
    def _():
        rows = refs[0].shape[0]
        for index in range(parts):
            e_out[index * rows : (index + 1) * rows, :] = refs[index][...]

    @pl.when(step < tiles)
    def _():
        grad = dot_nn(e_out[...], down_ref[...])
        gate = a_ref[...].astype(jnp.float32)
        up = u_ref[...].astype(jnp.float32)
        sigmoid = jax.nn.sigmoid(gate)
        da = (grad * up * sigmoid * (1.0 + gate * (1.0 - sigmoid))).astype(jnp.bfloat16)
        du = (grad * gate * sigmoid).astype(jnp.bfloat16)
        da_ref[...] = da
        du_ref[...] = du
        tile = da.shape[1]
        for index in range(tiles):

            @pl.when(step == index)
            def _():
                da_kept[:, index * tile : (index + 1) * tile] = da
                du_kept[:, index * tile : (index + 1) * tile] = du

    @pl.when(step >= tiles)
    def _():
        total = dot_nt(da_kept[...], gate_ref[...]) + dot_nt(du_kept[...], up_ref[...])
        rows = total.shape[0] // parts
        for index in range(parts):
            dx_refs[index][...] = total[index * rows : (index + 1) * rows].astype(jnp.bfloat16)


def down_chunk(es, a, u, weight, kept, index, count):
    depth, width = weight.shape
    rows = len(es) * es[0].shape[0]
    hidden = width // 3
    tile = tile_of(hidden)
    tiles = hidden // tile
    row_tile = tile_of(depth)

    def column(t):
        return jnp.minimum(t, tiles - 1)

    def row(t):
        return jnp.maximum(t - tiles, 0)

    specs = [pl.BlockSpec(es[0].shape, lambda t: (0, 0))] * len(es) + [
        pl.BlockSpec((depth, tile), lambda t: (0, 2 * tiles + column(t))),
        pl.BlockSpec((rows, tile), lambda t: (index, column(t))),
        pl.BlockSpec((rows, tile), lambda t: (index, column(t))),
        pl.BlockSpec((row_tile, hidden), lambda t: (row(t), 0)),
        pl.BlockSpec((row_tile, hidden), lambda t: (row(t), 1)),
    ]
    operands = [*es, weight, a, u, weight, weight]
    part = es[0].shape
    shapes = [
        jax.ShapeDtypeStruct((rows * count, hidden), jnp.bfloat16),
        jax.ShapeDtypeStruct((rows * count, hidden), jnp.bfloat16),
        *[jax.ShapeDtypeStruct(part, jnp.bfloat16)] * len(es),
    ]
    aliases = {}
    if kept is not None:
        specs.extend([pl.BlockSpec(memory_space=pl.ANY)] * 2)
        aliases = {len(operands) + i: i for i in range(2)}
        operands.extend(kept)
    result = pl.pallas_call(
        functools.partial(down_kernel, len(es), tiles),
        grid=(tiles + depth // row_tile,),
        in_specs=specs,
        out_specs=[
            pl.BlockSpec((rows, tile), lambda t: (index, column(t))),
            pl.BlockSpec((rows, tile), lambda t: (index, column(t))),
            *[pl.BlockSpec((part[0], row_tile), lambda t: (0, row(t)))] * len(es),
        ],
        out_shape=shapes,
        input_output_aliases=aliases,
        scratch_shapes=[
            pltpu.VMEM((rows, hidden), jnp.bfloat16),
            pltpu.VMEM((rows, hidden), jnp.bfloat16),
            pltpu.VMEM((rows, depth), jnp.bfloat16),
        ],
        compiler_params=parameters(),
        cost_estimate=SMALL_COST,
        name="down_chunk",
    )(*operands)
    return result[:2], list(result[2:])


def weight_kernel(counts, blocks, split, place_ref, *refs):
    step = pl.program_id(0)
    total_refs = sum(parts + widths for parts, widths in counts)
    received = refs[total_refs] if len(refs) > total_refs + 1 else None
    place = 0
    column = 0
    for parts, widths in counts:
        x = refs[place][...]
        if parts > 1:
            x = jnp.concatenate([ref[...] for ref in refs[place : place + parts]], axis=0)
        for y_ref in refs[place + parts : place + parts + widths]:
            width = y_ref.shape[1]
            cuts = set(range(0, width, 1024)) | {width}
            if column < split < column + width:
                cuts.add(split - column)
            cuts = sorted(cuts)
            for first, last in zip(cuts[:-1], cuts[1:]):
                total = dot_tn(x, y_ref[:, first:last])
                start, end = column + first, column + last
                if received is None:
                    refs[-1][:, start:end] = total.astype(jnp.bfloat16)
                    continue
                total += received[:, start:end].astype(jnp.float32)
                total = total.astype(jnp.bfloat16)
                low = start < split
                keep = step < blocks // 2 if low else lax.rem(step, 2) == 0
                keep_ref, send_ref = refs[-4:-2] if low else refs[-2:]
                columns = slice(start, end) if low else slice(start - split, end - split)

                @pl.when(keep)
                def _():
                    keep_ref[:, columns] = total

                @pl.when(jnp.logical_not(keep))
                def _():
                    send_ref[:, columns] = total

            column += width
        place += parts + widths


def weight_product(pairs, place, count, received):
    depth = pairs[0][0][0].shape[1]
    blocks = count // 2
    tile = depth // count
    total = sum(y.shape[1] for _, ys in pairs for y in ys)
    split = -(-total // 256) * 128
    side = 1 if received is None else 0
    whole = pl.BlockSpec((tile, total), lambda t, p: (t, 0))
    if received is None:
        out_specs = whole
        out_shape = jax.ShapeDtypeStruct((depth // 2, total), jnp.bfloat16)
    else:
        half = blocks // 2
        out_specs = [
            pl.BlockSpec((tile, split), lambda t, p: (jnp.minimum(t, half - 1), 0)),
            pl.BlockSpec((tile, split), lambda t, p: (jnp.maximum(t - half, 0), 0)),
            pl.BlockSpec((tile, total - split), lambda t, p: (t // 2, 0)),
            pl.BlockSpec((tile, total - split), lambda t, p: (t // 2, 0)),
        ]
        out_shape = [
            jax.ShapeDtypeStruct((depth // 4, width), jnp.bfloat16)
            for width in (split, split, total - split, total - split)
        ]
    specs = []
    operands = []
    for xs, ys in pairs:
        for x in xs:
            specs.append(
                pl.BlockSpec(
                    (x.shape[0], tile), lambda t, p: (0, lax.bitwise_xor(p[0], 2 * t + side))
                )
            )
        specs += [
            pl.BlockSpec(y.shape, lambda t, p: (0, 0), pipeline_mode=pl.Buffered(1)) for y in ys
        ]
        operands.extend([*xs, *ys])
    if received is not None:
        specs.append(whole)
        operands.append(received)
    return pl.pallas_call(
        functools.partial(
            weight_kernel, [(len(xs), len(ys)) for xs, ys in pairs], blocks, split
        ),
        grid_spec=pltpu.PrefetchScalarGridSpec(
            num_scalar_prefetch=1, grid=(blocks,), in_specs=specs, out_specs=out_specs
        ),
        out_shape=out_shape,
        compiler_params=parameters(),
        cost_estimate=SMALL_COST,
        name="weight_product",
    )(place, *operands)


def fold_kernel(counts, *refs):
    outs = refs[sum(counts) :]
    place = 0
    row = 0
    for index, count in enumerate(counts):
        total = refs[place][...].astype(jnp.float32)
        for ref in refs[place + 1 : place + count]:
            total += ref[...].astype(jnp.float32)
        out = outs[index % 2]
        rows = total.shape[0]
        out[row : row + rows, :] = total.astype(jnp.bfloat16)
        row += rows * (index % 2)
        place += count


def fold(sums, rows):
    counts = [len(terms) for pair in sums for terms in pair]
    values = [value for pair in sums for terms in pair for value in terms]
    widths = [terms[0].shape[1] for terms in sums[0]]
    steps = 2 if all(width % 256 == 0 for width in widths) else 1
    return pl.pallas_call(
        functools.partial(fold_kernel, counts),
        grid=(steps,),
        in_specs=[
            pl.BlockSpec((rows, value.shape[1] // steps), lambda t: (1, t)) for value in values
        ],
        out_specs=[
            pl.BlockSpec((rows * len(sums), width // steps), lambda t: (0, t))
            for width in widths
        ],
        out_shape=[
            jax.ShapeDtypeStruct((rows * len(sums), width), jnp.bfloat16) for width in widths
        ],
        compiler_params=parameters(),
        cost_estimate=SMALL_COST,
        name="fold",
    )(*values)


def residual_kernel(parts, e_ref, hidden_ref, first_ref, second_ref, gain_ref, weight_ref, *refs):
    dh_ref, dz_ref = refs[:2]
    step = pl.program_id(0)

    @pl.when(step == 0)
    def _():
        values = hidden_ref[...]
        inverse = lax.rsqrt(jnp.mean(values * values, axis=-1, keepdims=True) + EPSILON)
        scaled = values * inverse
        grad = first_ref[...].astype(jnp.float32) + second_ref[...].astype(jnp.float32)
        grad = grad * gain_ref[...]
        projection = jnp.mean(grad * scaled, axis=-1, keepdims=True)
        total = e_ref[...].astype(jnp.float32) + inverse * (grad - scaled * projection)
        dh_ref[...] = total
        dz_ref[...] = total.astype(jnp.bfloat16)

    result = dot_nn(dz_ref[...], weight_ref[...]).astype(jnp.bfloat16)
    for index in range(parts):

        @pl.when(step == index)
        def _():
            refs[2 + index][...] = result


def residual_gradient(e, hidden_res, first, second, gain, weight, parts):
    rows, depth = e.shape
    tile = weight.shape[1] // parts
    whole = pl.BlockSpec((rows, depth), lambda t: (0, 0))
    result = pl.pallas_call(
        functools.partial(residual_kernel, parts),
        grid=(parts,),
        in_specs=[
            whole,
            whole,
            whole,
            whole,
            pl.BlockSpec((1, depth), lambda t: (0, 0)),
            pl.BlockSpec((depth, tile), lambda t: (0, t)),
        ],
        out_specs=[whole, whole] + [pl.BlockSpec((rows, tile), lambda t: (0, 0))] * parts,
        out_shape=[
            jax.ShapeDtypeStruct((rows, depth), jnp.float32),
            jax.ShapeDtypeStruct((rows, depth), jnp.bfloat16),
            *[jax.ShapeDtypeStruct((rows, tile), jnp.bfloat16)] * parts,
        ],
        compiler_params=parameters(),
        cost_estimate=SMALL_COST,
        name="residual_gradient",
    )(e, hidden_res, first, second, gain, weight)
    return result[0], result[1], list(result[2:])


def tie(value, *others):
    return lax.optimization_barrier((value, others))[0]


def together(*values):
    return lax.optimization_barrier(values)


def add(first, second):
    return (first.astype(jnp.float32) + second.astype(jnp.float32)).astype(jnp.bfloat16)


class Mover:
    def __init__(self):
        self.dp_count = lax.axis_size("dp")
        self.ring = lax.axis_size("tensor")
        self.steps = []
        step = 2
        while step < self.dp_count:
            self.steps.append(step)
            step *= 2

    def swap(self, value, step):
        return lax.ppermute(value, "dp", [(i, i ^ step) for i in range(self.dp_count)])

    def gather(self, shard):
        return lax.all_gather(shard, "dp", axis=0, tiled=True)


    def send(self, pieces, level):
        orders = (self.steps[::-1], self.steps[:1] + self.steps[:0:-1])
        return [self.swap(piece, order[level]) for piece, order in zip(pieces, orders)]

    def begin(self, pieces):
        moved = self.send([pieces[1], pieces[3]], 0)
        return [[pieces[0], moved[0]], [pieces[2], moved[1]]]

    def fold(self, sums, level=1):
        return fold(sums, sums[0][0][0].shape[0] >> level)

    def advance(self, sums, folded):
        level = 1
        while True:
            moved = self.send(folded, level)
            level += 1
            if level == len(self.steps):
                return sums, moved
            rows = moved[0].shape[0] // len(sums)
            sums = [
                [
                    terms + [part[index * rows : (index + 1) * rows]]
                    for terms, part in zip(pair, moved)
                ]
                for index, pair in enumerate(sums)
            ]
            folded = self.fold(sums, level)

    def hop(self, value, shift=1):
        return lax.ppermute(
            value, "tensor", [(i, (i + shift) % self.ring) for i in range(self.ring)]
        )

    def spread(self, value):
        ring = self.ring
        return [value] + [
            lax.ppermute(value, "tensor", [(i, (i - j) % ring) for i in range(ring)])
            for j in range(1, ring)
        ]

    def collect(self, parts):
        ring = self.ring
        total = parts[0]
        for j in range(1, ring):
            moved = lax.ppermute(
                parts[j].astype(jnp.bfloat16), "tensor", [(i, (i + j) % ring) for i in range(ring)]
            )
            total = total + moved.astype(jnp.float32)
        return total

    def exchange(self, parts):
        ring = self.ring
        return [parts[0]] + [
            lax.ppermute(parts[j], "tensor", [(i, (i + j) % ring) for i in range(ring)])
            for j in range(1, ring)
        ]


def totals_of(sums, moved):
    rows = moved[0].shape[0] // len(sums)
    result = []
    for index, pair in enumerate(sums):
        halves = []
        for terms, last in zip(pair, moved):
            total = last[index * rows : (index + 1) * rows].astype(jnp.float32)
            for term in terms:
                total = total + term[:rows].astype(jnp.float32)
            halves.append(total)
        result.append(jnp.concatenate(halves, axis=1))
    return result


def back_norm(grad_normed, scaled, inverse, scale_row):
    grad_scaled = grad_normed * scale_row
    projection = jnp.mean(grad_scaled * scaled, axis=-1, keepdims=True)
    return inverse * (grad_scaled - scaled * projection)


def per_device(
    tokens,
    seq_lengths,
    attention_gain,
    query_matrix,
    key_matrix,
    value_matrix,
    output_weight,
    feedforward_gain,
    gate_weight,
    up_weight,
    down_weight,
    cotangent,
):
    mover = Mover()
    dp_count = mover.dp_count
    ring = mover.ring
    dp_place = lax.axis_index("dp").astype(jnp.int32).reshape(1)
    ring_place = lax.axis_index("tensor")
    place = ring_place.astype(jnp.int32).reshape(1)
    _, local_rows, model_width = tokens.shape
    complete_rows = local_rows * ring
    hidden = gate_weight.shape[1]
    groups = key_matrix.shape[1] // HEAD_SIZE
    joint_width = groups * GROUP_WIDTH
    f32 = jnp.float32
    b16 = jnp.bfloat16

    doc_ids, positions = layout(seq_lengths, complete_rows)
    row_index = jnp.arange(complete_rows, dtype=jnp.int32)
    doc_ids = jnp.where(doc_ids[0] < PIECES, doc_ids[0], PIECES + row_index)

    def to_relative(values):
        view = values.reshape((ring, local_rows) + values.shape[1:])
        return jnp.roll(view, -(ring_place + 1), axis=0)[::-1].reshape(values.shape)

    doc_ids = to_relative(doc_ids)
    cosine, sine = rope_tables(to_relative(positions[0]), HEAD_SIZE)
    cosine_table = jnp.tile(cosine, (1, 128 // cosine.shape[1]))
    sine_table = jnp.tile(jnp.concatenate([-sine, sine], axis=1), (1, 128 // HEAD_SIZE))

    def grouped(query, key, value):
        pieces = []
        for g in range(groups):
            pieces.append(query[:, g * GROUP_QUERY : (g + 1) * GROUP_QUERY])
            pieces.append(key[:, g * HEAD_SIZE : (g + 1) * HEAD_SIZE])
            pieces.append(value[:, g * HEAD_SIZE : (g + 1) * HEAD_SIZE])
        return jnp.concatenate(pieces, axis=1)

    joint_matrix = grouped(query_matrix, key_matrix, value_matrix)
    own_gains = jnp.stack([attention_gain, feedforward_gain], axis=1)
    joint_full = mover.gather(
        jnp.concatenate([joint_matrix, jnp.pad(own_gains, ((0, 0), (0, 126)))], axis=1)
    )
    output_parts = mover.spread(output_weight.T)
    ff_shard = jnp.concatenate([gate_weight, up_weight, down_weight.T], axis=1)
    output_parts, cosine_table, sine_table, doc_ids, ff_shard, local_tokens = together(
        output_parts, cosine_table, sine_table, doc_ids, ff_shard, tokens[0]
    )
    token_chunks = [local_tokens, mover.hop(local_tokens)]
    output_ring = join(output_parts, [0] * ring)
    output_full = mover.gather(output_ring)
    ff_full = mover.gather(tie(ff_shard, output_ring))
    gains = joint_full[:, joint_width : joint_width + 2].T.astype(f32)
    gain_one, gain_two = gains[:1], gains[1:]

    def projection(kept, index):
        return project(
            token_chunks[index],
            gain_one,
            joint_full,
            cosine_table,
            sine_table,
            kept,
            index,
            ring,
            groups,
        )

    kept = projection(None, 0)
    for j in range(1, ring):
        token_chunks[j], kept = together(token_chunks[j], kept)
        if j + 1 < ring:
            token_chunks.append(mover.hop(token_chunks[j]))
        else:
            local_cotangent = tie(cotangent[0], token_chunks[j])
            moved = mover.hop(local_cotangent)
        kept = projection(kept, j)
    normed_one, joint = kept
    attended, totals = attention_forward(joint, doc_ids, place, ring, groups)
    moved, attended = together(moved, attended)
    cotangent_chunks = [local_cotangent, moved]
    attended_parts = [attended]
    while len(attended_parts) < ring:
        part = mover.hop(attended_parts[-1], -1)
        if len(attended_parts) == ring - 1:
            partial = heads_product(
                tie(attended_parts, attended_parts[-1]), output_full, token_chunks
            )
            part, partial = together(part, partial)
        attended_parts.append(part)
    moved, last = together(moved, attended_parts[-1])

    pairs = ring // 2
    moved = mover.hop(moved)
    hidden_res, normed_two = after_attention(partial, last, output_full, gain_two, ring)
    upward = up_chunk(normed_two, ff_full, None, 0, pairs)
    downward = None
    grads = []

    def chunks_of(pair):
        return [cotangent_chunks[(2 * pair + i) % ring] for i in (1, 2)]

    def lower(pair, kept):
        return down_chunk(chunks_of(pair), upward[0], upward[1], ff_full, kept, pair, pairs)

    for j in range(2, ring):
        if j > 2:
            moved = mover.hop(moved)
            if j % 2:
                downward, parts = lower((j - 3) // 2, downward)
                grads.extend(parts)
            else:
                upward = up_chunk(normed_two, ff_full, upward, j // 2 - 1, pairs)
        moved, upward, downward, grads = together(moved, upward, downward, grads)
        cotangent_chunks.append(moved)

    def weights(xs, ys, received=None):
        return weight_product([(xs, ys)], dp_place, dp_count, received)

    ordered = cotangent_chunks[1:] + cotangent_chunks[:1]
    total = grads[0]
    moved = mover.hop(total)
    upward = up_chunk(tie(normed_two, total), ff_full, upward, pairs - 1, pairs)
    product = upward[2]
    down_part = weights(ordered, [product])
    moved, upward, down_part = together(moved, upward, down_part)
    down_part = mover.swap(down_part, 1)
    for j in range(2, ring):
        total = add(moved, grads[j - 1])
        moved = mover.hop(total)
        if j == 2:
            downward, parts = lower(pairs - 1, tie(downward, total))
            grads.extend(parts)
            attended_local = join(tie(attended_parts, parts), list(range(ring)))
            moved, downward, grads, attended_local = together(
                moved, downward, grads, attended_local
            )
            grad_gate, grad_up = downward
        if j == 3:
            gate_part = weights([tie(normed_two, total)], [grad_gate])
            branch = transposed_product(
                [tie(product, gate_part)], ff_full, 2, ring // 2, 0, 2
            )
            down_part = weights(tie(ordered, branch), [product], down_part)
            moved, gate_part, branch, down_part = together(moved, gate_part, branch, down_part)
    gate_part = mover.swap(gate_part, 1)
    down_part = mover.begin(down_part)
    grad_hidden, grad_branch, grad_parts = residual_gradient(
        local_cotangent, hidden_res, moved, grads[-1], gain_two, output_full, ring
    )
    grad_hidden, grad_branch, grad_parts, gate_part = together(
        grad_hidden, grad_branch, grad_parts, gate_part
    )

    grad_parts = mover.exchange(grad_parts)
    output_part = weights([grad_branch], [attended_local])
    gate_part = weights([tie(normed_two, output_part)], [grad_gate], gate_part)
    grad_parts, output_part, gate_part, down_part = together(
        grad_parts, output_part, gate_part, down_part
    )
    grad_joint = []
    sent = 0
    folded = []
    moved = branch[0]
    for group in range(groups):
        moved = mover.hop(moved)
        sent += 1
        if group == 0:
            output_part = mover.swap(output_part, 1)
            gate_part = mover.begin(gate_part)
        else:
            output_part = mover.begin(output_part)
        grad_joint.append(
            attention_backward(
                joint,
                attended,
                tie(grad_parts, grad_joint),
                totals,
                doc_ids,
                cosine_table,
                sine_table,
                place,
                group,
            )
        )
        if group == 0:
            output_part = weights(
                [tie(grad_branch, grad_joint)], [attended_local], output_part
            )
        if group + 1 == groups:
            grads = transposed_product(grad_joint, joint_full, 0, ring)
            folded = mover.fold(tie([gate_part, down_part], grads))
        moved, grad_joint, grads, gate_part, output_part, folded = together(
            moved, grad_joint, grads, gate_part, output_part, folded
        )
        if group + 1 < groups:
            moved = add(moved, branch[sent])
    if groups == 1:
        output_part = mover.begin(output_part)
    branch_moved = moved
    moved = grads[0]

    def last_weights(total, received):
        return weight_product(
            [([tie(normed_two, total)], [grad_up]), ([normed_one], grad_joint)],
            dp_place,
            dp_count,
            received,
        )

    for j in range(1, ring):
        total = grads[1] if j == 1 else add(moved, grads[j])
        moved = mover.hop(total)
        if j == 1:
            first_parts = mover.advance([gate_part, down_part], folded)
            folded = mover.fold(tie([output_part], total))
            last_part = last_weights(folded, None)
            branch = branch + transposed_product(
                [tie(product, last_part)], ff_full, 2, ring // 2, 1, 2
            )
            moved, last_part, branch, folded, first_parts = together(
                moved, last_part, branch, folded, first_parts
            )
        if j == 2:
            output_part = mover.advance([output_part], folded)
            last_part = last_weights(total, mover.swap(last_part, 1))
            gate_out, down_out = totals_of(*first_parts)
            down_out = down_out.T
            next_branch = add(branch_moved, branch[sent])
            moved, last_part, output_part, gate_out, down_out, next_branch = together(
                moved, last_part, output_part, gate_out, down_out, next_branch
            )
        if j == 3:
            last_part = mover.begin(last_part)
            branch_moved = mover.hop(tie(next_branch, total))
            sent += 1
            output_out = jnp.split(totals_of(*output_part)[0], ring, axis=1)
            moved, last_part, output_out = together(moved, last_part, output_out)
    folded, output_out = together(mover.fold([last_part]), output_out)
    last_part = mover.advance([last_part], folded)
    output_out = mover.collect(output_out[:-1] + [tie(output_out[-1], last_part)]).T
    scaled_one, inverse_one = norm_rows(local_tokens.astype(f32))
    local_one = moved.astype(f32) + grads[0].astype(f32)
    input_gradient = grad_hidden + back_norm(local_one, scaled_one, inverse_one, gain_one)
    branch_moved = tie(branch_moved, last_part)
    for j in range(sent, ring - 1):
        branch_moved = mover.hop(add(branch_moved, branch[j]))
    block_output = (
        hidden_res + (branch_moved.astype(f32) + branch[-1].astype(f32))
    ).astype(b16)
    last_out = totals_of(*last_part)[0]
    up_out, joint_out = last_out[:, :hidden], last_out[:, hidden:]

    sums = jnp.stack(
        [
            jnp.sum(joint_out * joint_matrix.astype(f32), axis=1) / attention_gain.astype(f32),
            jnp.sum(gate_out * gate_weight.astype(f32) + up_out * up_weight.astype(f32), axis=1)
            / feedforward_gain.astype(f32),
        ]
    )
    gain_out = sums
    for shift in range(1, ring):
        gain_out = gain_out + lax.ppermute(
            sums, "tensor", [(i, (i + shift) % ring) for i in range(ring)]
        )

    def ungrouped(first, width):
        return jnp.concatenate(
            [
                joint_out[:, g * GROUP_WIDTH + first : g * GROUP_WIDTH + first + width]
                for g in range(groups)
            ],
            axis=1,
        )

    return (
        block_output[None],
        input_gradient[None],
        gain_out[0],
        ungrouped(0, GROUP_QUERY),
        ungrouped(GROUP_QUERY, HEAD_SIZE),
        ungrouped(GROUP_QUERY + HEAD_SIZE, HEAD_SIZE),
        output_out,
        gain_out[1],
        gate_out,
        up_out,
        down_out,
    )


def solution(mesh):
    return jax.shard_map(
        per_device,
        mesh=mesh,
        in_specs=(
            P("dp", "tensor", None),
            P("dp", None),
            P("dp"),
            P("dp", "tensor"),
            P("dp", "tensor"),
            P("dp", "tensor"),
            P("tensor", "dp"),
            P("dp"),
            P("dp", "tensor"),
            P("dp", "tensor"),
            P("tensor", "dp"),
            P("dp", "tensor", None),
        ),
        out_specs=(
            P("dp", "tensor", None),
            P("dp", "tensor", None),
            P("dp"),
            P("dp", "tensor"),
            P("dp", "tensor"),
            P("dp", "tensor"),
            P("tensor", "dp"),
            P("dp"),
            P("dp", "tensor"),
            P("dp", "tensor"),
            P("tensor", "dp"),
        ),
        check_vma=False,
    )
```

```python
import functools
import math

import jax
import jax.numpy as jnp
from jax import lax
from jax.experimental import pallas as pl
from jax.experimental.pallas import tpu as pltpu
from jax.sharding import PartitionSpec as P

QUERY_HEADS = 32
KEY_VALUE_HEADS = 8
HEAD_SIZE = 64
PIECES = 4


EPSILON = 1e-05
ROPE_BASE = 500000.0
NEGATIVE = -1e30
GROUP_QUERY = QUERY_HEADS // KEY_VALUE_HEADS * HEAD_SIZE
GROUP_WIDTH = GROUP_QUERY + 2 * HEAD_SIZE
KERNEL_VMEM = 60 * 1024 * 1024
SMALL_COST = pl.CostEstimate(flops=1, bytes_accessed=1, transcendentals=0)


def layout(lengths, complete_rows):
    doc_ends = jnp.cumsum(lengths, axis=-1)
    row_index = jnp.arange(complete_rows, dtype=jnp.int32)
    piece_count = lengths.shape[-1]
    doc_ids = jnp.sum((row_index[None, :, None] >= doc_ends[:, None, :]).astype(jnp.int32), axis=2)
    starts = doc_ends - lengths
    chosen = doc_ids[:, :, None] == jnp.arange(piece_count, dtype=jnp.int32)[None, None, :]
    doc_begin = jnp.sum(jnp.where(chosen, starts[:, None, :], 0), axis=2) + jnp.where(
        doc_ids == piece_count, doc_ends[:, -1:], 0
    )
    return (doc_ids, row_index[None, :] - doc_begin)


def rope_tables(positions, head_dim):
    half_dim = head_dim // 2
    frequency = ROPE_BASE ** (-(jnp.arange(half_dim, dtype=jnp.float32) * (2.0 / head_dim)))
    angles = positions.astype(jnp.float32)[..., None] * frequency
    return (jnp.cos(angles), jnp.sin(angles))


def norm_rows(values):
    inverse = lax.rsqrt(jnp.mean(values * values, axis=-1, keepdims=True) + EPSILON)
    return (values * inverse, inverse)


def dot_nt(left, right):
    return lax.dot_general(
        left, right, (((1,), (1,)), ((), ())), preferred_element_type=jnp.float32
    )


def dot_nn(left, right):
    return jnp.dot(left, right, preferred_element_type=jnp.float32)


def dot_tn(left, right):
    return lax.dot_general(
        left, right, (((0,), (0,)), ((), ())), preferred_element_type=jnp.float32
    )


def tile_of(size, limit=512):
    tile = limit
    while size % tile:
        tile //= 2
    return tile


def parameters():
    return pltpu.CompilerParams(vmem_limit_bytes=KERNEL_VMEM)


def swap_halves(values):
    lane = lax.broadcasted_iota(jnp.int32, values.shape, 1)
    half = HEAD_SIZE // 2
    return jnp.where(
        lane % HEAD_SIZE < half, pltpu.roll(values, 128 - half, 1), pltpu.roll(values, half, 1)
    )


def turned(values, cosine, sine, start):
    result = values * cosine + swap_halves(values) * sine
    rotated = GROUP_WIDTH - HEAD_SIZE
    if start + 128 <= rotated:
        return result
    lane = lax.broadcasted_iota(jnp.int32, values.shape, 1)
    return jnp.where(lane < rotated - start, result, values)


def project_kernel(x_ref, gain_ref, weight_ref, cos_ref, sin_ref, *refs):
    normed_ref, joint_ref = refs[-2:]

    @pl.when(pl.program_id(0) == 0)
    def _():
        values = x_ref[...].astype(jnp.float32)
        inverse = lax.rsqrt(jnp.mean(values * values, axis=-1, keepdims=True) + EPSILON)
        normed_ref[...] = (values * inverse * gain_ref[:1, :]).astype(jnp.bfloat16)

    product = dot_nn(normed_ref[...], weight_ref[...])
    for start in range(0, GROUP_WIDTH, 128):
        part = turned(product[:, start : start + 128], cos_ref[...], sin_ref[...], start)
        if start < GROUP_QUERY:
            part = part * HEAD_SIZE ** (-0.5)
        joint_ref[:, start : start + 128] = part.astype(jnp.bfloat16)


def project(x, gain, weight, cosine, sine, kept, index, count, groups):
    rows, depth = x.shape
    specs = [
        pl.BlockSpec((rows, depth), lambda g: (0, 0)),
        pl.BlockSpec((2, depth), lambda g: (0, 0)),
        pl.BlockSpec((depth, GROUP_WIDTH), lambda g: (0, g)),
        pl.BlockSpec((rows, 128), lambda g: (index, 0)),
        pl.BlockSpec((rows, 128), lambda g: (index, 0)),
    ]
    operands = [x, gain, weight, cosine, sine]
    aliases = {}
    if kept is not None:
        specs.extend([pl.BlockSpec(memory_space=pl.ANY)] * 2)
        aliases = {len(operands) + i: i for i in range(2)}
        operands.extend(kept)
    return pl.pallas_call(
        project_kernel,
        grid=(groups,),
        in_specs=specs,
        out_specs=[
            pl.BlockSpec((rows, depth), lambda g: (index, 0)),
            pl.BlockSpec((rows, GROUP_WIDTH), lambda g: (index, g)),
        ],
        out_shape=[
            jax.ShapeDtypeStruct((rows * count, depth), jnp.bfloat16),
            jax.ShapeDtypeStruct((rows * count, GROUP_WIDTH * groups), jnp.bfloat16),
        ],
        input_output_aliases=aliases,
        compiler_params=parameters(),
        cost_estimate=SMALL_COST,
        name="project",
    )(*operands)


def ring_offset(place, chunk, count, rows):
    return pl.multiple_of(lax.rem(place - chunk + count, count) * rows, rows)


def stack_heads(target, source):
    rows, width = source.shape
    for head in range(width // HEAD_SIZE):
        target[head * rows : (head + 1) * rows, :] = source[
            :, head * HEAD_SIZE : (head + 1) * HEAD_SIZE
        ]


def fill_bias(bias, key_docs, query_docs, earlier):
    rows = key_docs.shape[0]
    row_index = lax.broadcasted_iota(jnp.int32, (rows, rows), 0)
    column_index = lax.broadcasted_iota(jnp.int32, (rows, rows), 1)
    same = (key_docs == query_docs) & ((row_index <= column_index) | earlier)
    values = jnp.where(same, 0.0, NEGATIVE)
    for first in range(0, bias.shape[1], rows):
        bias[:, first : first + rows] = values


def forward_kernel(
    count,
    place_ref,
    own_ref,
    all_ref,
    docq_ref,
    dock_ref,
    o_ref,
    lse_ref,
    bias,
    queries,
    values_all,
    mixed,
):
    chunk = pl.program_id(1)
    place = place_ref[0]
    rows = own_ref.shape[0]
    heads = GROUP_QUERY // HEAD_SIZE
    stack_heads(queries, own_ref.at[:, :GROUP_QUERY])

    @pl.when(chunk == 0)
    def _():
        values = all_ref[:, GROUP_QUERY:].astype(jnp.float32)
        values_all[...] = values.T[HEAD_SIZE:].astype(jnp.bfloat16)

    mixed[...] = jnp.zeros_like(mixed)

    def block(j, carry):
        peaks, total = carry
        offset = ring_offset(place, j, count, rows)
        piece = pl.ds(offset, rows)
        fill_bias(bias, dock_ref[piece, :], docq_ref[...], j < chunk)
        keys = all_ref[piece, GROUP_QUERY : GROUP_QUERY + HEAD_SIZE]
        scores = dot_nt(keys, queries[...]) + bias[...]
        higher = jnp.maximum(peaks, jnp.max(scores, axis=0, keepdims=True))
        probs = jnp.exp(scores - higher)
        scale = jnp.exp(peaks - higher)
        mixed[...] = mixed[...] * scale + dot_nn(
            values_all[:, piece], probs.astype(jnp.bfloat16)
        )
        return higher, total * scale + jnp.sum(probs, axis=0, keepdims=True)

    peaks, total = lax.fori_loop(
        0,
        chunk + 1,
        block,
        (
            jnp.full((1, heads * rows), NEGATIVE, jnp.float32),
            jnp.zeros((1, heads * rows), jnp.float32),
        ),
    )
    lse_ref[:1, :] = peaks + jnp.log(total)
    result = mixed[...] / total
    for head in range(0, heads, 2):
        pair = jnp.concatenate(
            [result[:, (head + i) * rows : (head + i + 1) * rows] for i in range(2)], axis=0
        )
        o_ref[:, head * HEAD_SIZE : (head + 2) * HEAD_SIZE] = pair.T.astype(jnp.bfloat16)


def attention_forward(joint, docs, place, count, groups):
    total_rows = joint.shape[0]
    rows = total_rows // count
    stacked = rows * GROUP_QUERY // HEAD_SIZE

    def block(c, place_ref):
        return lax.rem(place_ref[0] - c + count, count)

    spec = pltpu.PrefetchScalarGridSpec(
        num_scalar_prefetch=1,
        grid=(groups, count),
        in_specs=[
            pl.BlockSpec((rows, GROUP_WIDTH), lambda g, c, p: (block(c, p), g)),
            pl.BlockSpec((total_rows, GROUP_WIDTH), lambda g, c, p: (0, g)),
            pl.BlockSpec((1, rows), lambda g, c, p: (0, block(c, p))),
            pl.BlockSpec((total_rows, 1), lambda g, c, p: (0, 0)),
        ],
        out_specs=[
            pl.BlockSpec((rows, GROUP_QUERY), lambda g, c, p: (block(c, p), g)),
            pl.BlockSpec((8, stacked), lambda g, c, p: (g, block(c, p))),
        ],
        scratch_shapes=[
            pltpu.VMEM((rows, stacked), jnp.float32),
            pltpu.VMEM((stacked, HEAD_SIZE), jnp.bfloat16),
            pltpu.VMEM((HEAD_SIZE, total_rows), jnp.bfloat16),
            pltpu.VMEM((HEAD_SIZE, stacked), jnp.float32),
        ],
    )
    return pl.pallas_call(
        functools.partial(forward_kernel, count),
        grid_spec=spec,
        out_shape=[
            jax.ShapeDtypeStruct((total_rows, GROUP_QUERY * groups), jnp.bfloat16),
            jax.ShapeDtypeStruct((8 * groups, stacked * count), jnp.float32),
        ],
        compiler_params=parameters(),
        cost_estimate=SMALL_COST,
        name="attend",
    )(place, joint, joint, docs[None, :], docs[:, None])


def backward_kernel(count, place_ref, *refs):
    own_ref, all_ref, o_ref = refs[:3]
    lse_ref, docq_ref, dock_ref, cos_ref, sin_ref = refs[3 + count : 8 + count]
    out_ref, bias, queries, grads, keys_all, values_all, sum_q, sum_k, sum_v = refs[8 + count :]
    chunk = pl.program_id(0)
    place = place_ref[0]
    rows = own_ref.shape[0]
    heads = GROUP_QUERY // HEAD_SIZE
    stack_heads(queries, own_ref.at[:, :GROUP_QUERY])
    for index in range(count):

        @pl.when(lax.rem(place - chunk + count, count) == index)
        def _():
            stack_heads(grads, refs[3 + index])

    @pl.when(chunk == 0)
    def _():
        keys_all[...] = all_ref[:, GROUP_QUERY : GROUP_QUERY + HEAD_SIZE]
        values_all[...] = all_ref[:, GROUP_QUERY + HEAD_SIZE :]
        sum_k[...] = jnp.zeros_like(sum_k)
        sum_v[...] = jnp.zeros_like(sum_v)

    sum_q[...] = jnp.zeros_like(sum_q)
    ones = jnp.ones((8, HEAD_SIZE), jnp.bfloat16)
    inner = []
    for head in range(heads):
        attended = o_ref[:, head * HEAD_SIZE : (head + 1) * HEAD_SIZE].astype(jnp.float32)
        both = attended * grads[head * rows : (head + 1) * rows, :].astype(jnp.float32)
        high = both.astype(jnp.bfloat16)
        low = (both - high.astype(jnp.float32)).astype(jnp.bfloat16)
        inner.append((dot_nt(ones, high) + dot_nt(ones, low))[:1])
    inner = jnp.concatenate(inner, axis=1)

    def block(j, carry):
        offset = ring_offset(place, j, count, rows)
        piece = pl.ds(offset, rows)
        fill_bias(bias, dock_ref[piece, :], docq_ref[...], j < chunk)
        probs = jnp.exp(dot_nt(keys_all[piece, :], queries[...]) + bias[...] - lse_ref[:1, :])
        grad_probs = dot_nt(values_all[piece, :], grads[...])
        grad_scores = (probs * (grad_probs - inner)).astype(jnp.bfloat16)
        sum_v[piece, :] += dot_nn(probs.astype(jnp.bfloat16), grads[...])
        sum_k[piece, :] += dot_nn(grad_scores, queries[...])
        sum_q[...] += dot_tn(grad_scores, keys_all[piece, :])
        return carry

    lax.fori_loop(0, chunk + 1, block, 0)
    own = pl.ds(ring_offset(place, chunk, count, rows), rows)
    for first in range(0, heads, 2):
        start = first * HEAD_SIZE
        part = jnp.concatenate(
            [sum_q[(first + i) * rows : (first + i + 1) * rows, :] for i in range(2)], axis=1
        )
        part = turned(part, cos_ref[own, :], -sin_ref[own, :], start)
        out_ref[own, start : start + 128] = (part * HEAD_SIZE ** (-0.5)).astype(jnp.bfloat16)

    @pl.when(chunk == count - 1)
    def _():
        part = jnp.concatenate([sum_k[...], sum_v[...]], axis=1)
        part = turned(part, cos_ref[...], -sin_ref[...], GROUP_QUERY)
        out_ref[:, GROUP_QUERY:] = part.astype(jnp.bfloat16)


def attention_backward(joint, attended, grads, lse, docs, cosine, sine, place, group):
    count = len(grads)
    total_rows = joint.shape[0]
    rows = total_rows // count
    stacked = rows * GROUP_QUERY // HEAD_SIZE

    def block(c, place_ref):
        return lax.rem(place_ref[0] - c + count, count)

    table = pl.BlockSpec((total_rows, 128), lambda c, p: (0, 0))
    spec = pltpu.PrefetchScalarGridSpec(
        num_scalar_prefetch=1,
        grid=(count,),
        in_specs=[
            pl.BlockSpec((rows, GROUP_WIDTH), lambda c, p: (block(c, p), group)),
            pl.BlockSpec((total_rows, GROUP_WIDTH), lambda c, p: (0, group)),
            pl.BlockSpec((rows, GROUP_QUERY), lambda c, p: (block(c, p), group)),
            *[pl.BlockSpec((rows, GROUP_QUERY), lambda c, p: (0, group))] * count,
            pl.BlockSpec((8, stacked), lambda c, p: (group, block(c, p))),
            pl.BlockSpec((1, rows), lambda c, p: (0, block(c, p))),
            pl.BlockSpec((total_rows, 1), lambda c, p: (0, 0)),
            table,
            table,
        ],
        out_specs=pl.BlockSpec((total_rows, GROUP_WIDTH), lambda c, p: (0, 0)),
        scratch_shapes=[
            pltpu.VMEM((rows, stacked), jnp.float32),
            *[pltpu.VMEM((stacked, HEAD_SIZE), jnp.bfloat16)] * 2,
            *[pltpu.VMEM((total_rows, HEAD_SIZE), jnp.bfloat16)] * 2,
            pltpu.VMEM((stacked, HEAD_SIZE), jnp.float32),
            *[pltpu.VMEM((total_rows, HEAD_SIZE), jnp.float32)] * 2,
        ],
    )
    return pl.pallas_call(
        functools.partial(backward_kernel, count),
        grid_spec=spec,
        out_shape=jax.ShapeDtypeStruct((total_rows, GROUP_WIDTH), jnp.bfloat16),
        compiler_params=parameters(),
        cost_estimate=SMALL_COST,
        name="attend_back",
    )(
        place,
        joint,
        joint,
        attended,
        *grads,
        lse,
        docs[None, :],
        docs[:, None],
        cosine,
        sine,
    )


def pack_kernel(groups, query_ref, key_ref, value_ref, gain_ref, joint_ref, out_ref):
    for g in range(groups):
        start = g * GROUP_WIDTH
        columns = slice(g * HEAD_SIZE, (g + 1) * HEAD_SIZE)
        joint_ref[:, start : start + GROUP_QUERY] = query_ref[
            :, g * GROUP_QUERY : (g + 1) * GROUP_QUERY
        ]
        joint_ref[:, start + GROUP_QUERY : start + GROUP_WIDTH] = jnp.concatenate(
            [key_ref[:, columns], value_ref[:, columns]], axis=1
        )
    width = groups * GROUP_WIDTH
    out_ref[:, :width] = joint_ref[...]
    out_ref[:, width:] = gain_ref[...].astype(jnp.float32).T.astype(jnp.bfloat16)


def pack(query, key, value, gains, groups):
    rows = query.shape[0]
    width = groups * GROUP_WIDTH
    return pl.pallas_call(
        functools.partial(pack_kernel, groups),
        out_shape=[
            jax.ShapeDtypeStruct((rows, width), jnp.bfloat16),
            jax.ShapeDtypeStruct((rows, width + 128), jnp.bfloat16),
        ],
        compiler_params=parameters(),
        cost_estimate=SMALL_COST,
        name="pack",
    )(query, key, value, gains)


def join_kernel(*refs):
    place = 0
    for ref in refs[:-1]:
        size = ref.shape[1]
        refs[-1][:, place : place + size] = ref[...]
        place += size


def join(parts, blocks):
    rows = parts[0].shape[0] // (max(blocks) + 1)
    width = sum(part.shape[1] for part in parts)
    return pl.pallas_call(
        join_kernel,
        grid=(1,),
        in_specs=[
            pl.BlockSpec((rows, part.shape[1]), lambda i, block=block: (block, 0))
            for part, block in zip(parts, blocks)
        ],
        out_specs=pl.BlockSpec((rows, width), lambda i: (0, 0)),
        out_shape=jax.ShapeDtypeStruct((rows, width), parts[0].dtype),
        compiler_params=parameters(),
        cost_estimate=SMALL_COST,
        name="join",
    )(*parts)


def transposed_kernel(count, parts, *refs):
    total = dot_nt(refs[0][...], refs[count][...])
    for index in range(1, count):
        total += dot_nt(refs[index][...], refs[count + index][...])
    rows = total.shape[0] // parts
    for index in range(parts):
        refs[2 * count + index][...] = total[index * rows : (index + 1) * rows].astype(
            jnp.bfloat16
        )


def transposed_product(xs, weight, column, parts, block=0, blocks=1):
    rows, depth = xs[0].shape
    rows //= blocks
    width = weight.shape[0]
    tile = tile_of(width)
    specs = [pl.BlockSpec((rows, depth), lambda t: (block, 0))] * len(xs)
    for index in range(len(xs)):
        specs.append(pl.BlockSpec((tile, depth), lambda t, index=index: (t, column + index)))
    part = (rows // parts, width)
    return pl.pallas_call(
        functools.partial(transposed_kernel, len(xs), parts),
        grid=(width // tile,),
        in_specs=specs,
        out_specs=[pl.BlockSpec((part[0], tile), lambda t: (0, t))] * parts,
        out_shape=[jax.ShapeDtypeStruct(part, jnp.bfloat16)] * parts,
        compiler_params=parameters(),
        cost_estimate=SMALL_COST,
        name="transposed",
    )(*xs, *[weight] * len(xs))


def heads_kernel(count, *refs):
    parts = refs[:count]
    weight_ref = refs[count]
    tokens = refs[count + 1 : -2]
    out_ref, local_ref = refs[-2:]
    step = pl.program_id(0)
    width = parts[0].shape[1]

    @pl.when(step == 0)
    def _():
        for j in range(count):
            local_ref[:, j * width : (j + 1) * width] = parts[j][...]

    for j in range(count):
        term = dot_nt(parts[j][...], weight_ref[:, j * width : (j + 1) * width])
        if j == 0:
            out_ref[...] = term
        else:
            out_ref[...] += term
    for index in range(len(tokens)):

        @pl.when(step == index)
        def _():
            out_ref[...] += tokens[index][...].astype(jnp.float32)


def heads_product(parts, weight, tokens):
    blocks = len(tokens)
    rows, width = tokens[0].shape
    depth = parts[0].shape[1]
    specs = [
        pl.BlockSpec((rows, depth), lambda i, j=j: (lax.rem(i + j, blocks), 0))
        for j in range(len(parts))
    ]
    whole = pl.BlockSpec((rows, width), lambda i: (0, 0), pipeline_mode=pl.Buffered(1))
    return pl.pallas_call(
        functools.partial(heads_kernel, len(parts)),
        grid=(blocks,),
        in_specs=[
            *specs,
            pl.BlockSpec(
                (width, depth * len(parts)), lambda i: (0, 0), pipeline_mode=pl.Buffered(1)
            ),
            *[whole] * blocks,
        ],
        out_specs=[
            pl.BlockSpec((rows, width), lambda i: (i, 0)),
            pl.BlockSpec((rows, depth * len(parts)), lambda i: (0, 0)),
        ],
        out_shape=[
            jax.ShapeDtypeStruct((rows * blocks, width), jnp.float32),
            jax.ShapeDtypeStruct((rows, depth * len(parts)), jnp.bfloat16),
        ],
        compiler_params=parameters(),
        cost_estimate=SMALL_COST,
        name="heads_product",
    )(*parts, weight, *tokens)


def attended_kernel(
    partial_ref, last_ref, weight_ref, gain_ref, hidden_ref, normed_ref, local_ref
):
    values = partial_ref[...] + dot_nt(last_ref[...], weight_ref[...])

    @pl.when(pl.program_id(0) == 0)
    def _():
        hidden_ref[...] = values
        local_ref[...] = last_ref[...]

    inverse = lax.rsqrt(jnp.mean(values * values, axis=-1, keepdims=True) + EPSILON)
    normed_ref[...] = (values * inverse * gain_ref[1:, :]).astype(jnp.bfloat16)


def after_attention(partial, last, weight, gain, count):
    total_rows, width = partial.shape
    rows = total_rows // count
    depth = last.shape[1]
    return pl.pallas_call(
        attended_kernel,
        grid=(count,),
        in_specs=[
            pl.BlockSpec((rows, width), lambda i: (i, 0)),
            pl.BlockSpec((rows, depth), lambda i: (lax.rem(i + count - 1, count), 0)),
            pl.BlockSpec((width, depth), lambda i: (0, count - 1)),
            pl.BlockSpec((2, width), lambda i: (0, 0)),
        ],
        out_specs=[
            pl.BlockSpec((rows, width), lambda i: (0, 0)),
            pl.BlockSpec((rows, width), lambda i: (lax.rem(i + count - 1, count), 0)),
            pl.BlockSpec((rows, depth), lambda i: (0, 0)),
        ],
        out_shape=[
            jax.ShapeDtypeStruct((rows, width), jnp.float32),
            jax.ShapeDtypeStruct((total_rows, width), jnp.bfloat16),
            jax.ShapeDtypeStruct((rows, depth), jnp.bfloat16),
        ],
        compiler_params=parameters(),
        cost_estimate=SMALL_COST,
        name="after_attention",
    )(partial, last, weight, gain)


def up_kernel(x_ref, gate_ref, up_ref, *refs):
    a_ref, u_ref, g_ref = refs[-3:]
    gate = dot_nn(x_ref[...], gate_ref[...])
    up = dot_nn(x_ref[...], up_ref[...])
    a_ref[...] = gate.astype(jnp.bfloat16)
    u_ref[...] = up.astype(jnp.bfloat16)
    g_ref[...] = (gate * jax.nn.sigmoid(gate) * up).astype(jnp.bfloat16)


def up_chunk(x, weight, kept, index, count):
    total_rows, depth = x.shape
    rows = total_rows // count
    hidden = (weight.shape[1] - depth) // 2
    tile = tile_of(hidden)
    tiles = hidden // tile
    start = depth // tile
    specs = [
        pl.BlockSpec((rows, depth), lambda t: (index, 0)),
        pl.BlockSpec((depth, tile), lambda t: (0, start + t)),
        pl.BlockSpec((depth, tile), lambda t: (0, start + tiles + t)),
    ]
    operands = [x, weight, weight]
    aliases = {}
    if kept is not None:
        specs.extend([pl.BlockSpec(memory_space=pl.ANY)] * 3)
        aliases = {len(operands) + i: i for i in range(3)}
        operands.extend(kept)
    return pl.pallas_call(
        up_kernel,
        grid=(tiles,),
        in_specs=specs,
        out_specs=[pl.BlockSpec((rows, tile), lambda t: (index, t))] * 3,
        out_shape=[jax.ShapeDtypeStruct((total_rows, hidden), jnp.bfloat16)] * 3,
        input_output_aliases=aliases,
        compiler_params=parameters(),
        cost_estimate=SMALL_COST,
        name="up_chunk",
    )(*operands)


def down_kernel(parts, tiles, *refs):
    down_ref, a_ref, u_ref, gate_ref, up_ref = refs[parts : parts + 5]
    da_ref, du_ref = refs[-5 - parts : -3 - parts]
    dx_refs = refs[-3 - parts : -3]
    da_kept, du_kept, e_out = refs[-3:]
    step = pl.program_id(0)

    @pl.when(step == 0)
    def _():
        rows = refs[0].shape[0]
        for index in range(parts):
            e_out[index * rows : (index + 1) * rows, :] = refs[index][...]

    @pl.when(step < tiles)
    def _():
        grad = dot_nn(e_out[...], down_ref[...])
        gate = a_ref[...].astype(jnp.float32)
        up = u_ref[...].astype(jnp.float32)
        sigmoid = jax.nn.sigmoid(gate)
        da = (grad * up * sigmoid * (1.0 + gate * (1.0 - sigmoid))).astype(jnp.bfloat16)
        du = (grad * gate * sigmoid).astype(jnp.bfloat16)
        da_ref[...] = da
        du_ref[...] = du
        tile = da.shape[1]
        for index in range(tiles):

            @pl.when(step == index)
            def _():
                da_kept[:, index * tile : (index + 1) * tile] = da
                du_kept[:, index * tile : (index + 1) * tile] = du

    @pl.when(step >= tiles)
    def _():
        total = dot_nt(da_kept[...], gate_ref[...]) + dot_nt(du_kept[...], up_ref[...])
        rows = total.shape[0] // parts
        for index in range(parts):
            dx_refs[index][...] = total[index * rows : (index + 1) * rows].astype(jnp.bfloat16)


def down_chunk(es, a, u, down_weight, weight, kept, index, count):
    depth, hidden = down_weight.shape
    rows = len(es) * es[0].shape[0]
    start = depth // hidden
    tile = tile_of(hidden)
    tiles = hidden // tile
    row_tile = tile_of(depth)

    def column(t):
        return jnp.minimum(t, tiles - 1)

    def row(t):
        return jnp.maximum(t - tiles, 0)

    specs = [pl.BlockSpec(es[0].shape, lambda t: (0, 0))] * len(es) + [
        pl.BlockSpec((depth, tile), lambda t: (0, column(t))),
        pl.BlockSpec((rows, tile), lambda t: (index, column(t))),
        pl.BlockSpec((rows, tile), lambda t: (index, column(t))),
        pl.BlockSpec((row_tile, hidden), lambda t: (row(t), start)),
        pl.BlockSpec((row_tile, hidden), lambda t: (row(t), start + 1)),
    ]
    operands = [*es, down_weight, a, u, weight, weight]
    part = es[0].shape
    shapes = [
        jax.ShapeDtypeStruct((rows * count, hidden), jnp.bfloat16),
        jax.ShapeDtypeStruct((rows * count, hidden), jnp.bfloat16),
        *[jax.ShapeDtypeStruct(part, jnp.bfloat16)] * len(es),
    ]
    aliases = {}
    if kept is not None:
        specs.extend([pl.BlockSpec(memory_space=pl.ANY)] * 2)
        aliases = {len(operands) + i: i for i in range(2)}
        operands.extend(kept)
    result = pl.pallas_call(
        functools.partial(down_kernel, len(es), tiles),
        grid=(tiles + depth // row_tile,),
        in_specs=specs,
        out_specs=[
            pl.BlockSpec((rows, tile), lambda t: (index, column(t))),
            pl.BlockSpec((rows, tile), lambda t: (index, column(t))),
            *[pl.BlockSpec((part[0], row_tile), lambda t: (0, row(t)))] * len(es),
        ],
        out_shape=shapes,
        input_output_aliases=aliases,
        scratch_shapes=[
            pltpu.VMEM((rows, hidden), jnp.bfloat16),
            pltpu.VMEM((rows, hidden), jnp.bfloat16),
            pltpu.VMEM((rows, depth), jnp.bfloat16),
        ],
        compiler_params=parameters(),
        cost_estimate=SMALL_COST,
        name="down_chunk",
    )(*operands)
    return result[:2], list(result[2:])


def weight_kernel(counts, blocks, split, place_ref, *refs):
    step = pl.program_id(0)
    total_refs = sum(parts + widths for parts, widths in counts)
    received = refs[total_refs] if len(refs) > total_refs + 1 else None
    place = 0
    column = 0
    for parts, widths in counts:
        x = refs[place][...]
        if parts > 1:
            x = jnp.concatenate([ref[...] for ref in refs[place : place + parts]], axis=0)
        for y_ref in refs[place + parts : place + parts + widths]:
            width = y_ref.shape[1]
            cuts = set(range(0, width, 1024)) | {width}
            if column < split < column + width:
                cuts.add(split - column)
            cuts = sorted(cuts)
            for first, last in zip(cuts[:-1], cuts[1:]):
                total = dot_tn(x, y_ref[:, first:last])
                start, end = column + first, column + last
                if received is None:
                    refs[-1][:, start:end] = total.astype(jnp.bfloat16)
                    continue
                total += received[:, start:end].astype(jnp.float32)
                total = total.astype(jnp.bfloat16)
                low = start < split
                keep = step < blocks // 2 if low else lax.rem(step, 2) == 0
                keep_ref, send_ref = refs[-4:-2] if low else refs[-2:]
                columns = slice(start, end) if low else slice(start - split, end - split)

                @pl.when(keep)
                def _():
                    keep_ref[:, columns] = total

                @pl.when(jnp.logical_not(keep))
                def _():
                    send_ref[:, columns] = total

            column += width
        place += parts + widths


def weight_product(pairs, place, count, received):
    depth = pairs[0][0][0].shape[1]
    blocks = count // 2
    tile = depth // count
    total = sum(y.shape[1] for _, ys in pairs for y in ys)
    split = -(-total // 256) * 128
    side = 1 if received is None else 0
    whole = pl.BlockSpec((tile, total), lambda t, p: (t, 0))
    if received is None:
        out_specs = whole
        out_shape = jax.ShapeDtypeStruct((depth // 2, total), jnp.bfloat16)
    else:
        half = blocks // 2
        out_specs = [
            pl.BlockSpec((tile, split), lambda t, p: (jnp.minimum(t, half - 1), 0)),
            pl.BlockSpec((tile, split), lambda t, p: (jnp.maximum(t - half, 0), 0)),
            pl.BlockSpec((tile, total - split), lambda t, p: (t // 2, 0)),
            pl.BlockSpec((tile, total - split), lambda t, p: (t // 2, 0)),
        ]
        out_shape = [
            jax.ShapeDtypeStruct((depth // 4, width), jnp.bfloat16)
            for width in (split, split, total - split, total - split)
        ]
    specs = []
    operands = []
    for xs, ys in pairs:
        for x in xs:
            specs.append(
                pl.BlockSpec(
                    (x.shape[0], tile), lambda t, p: (0, lax.bitwise_xor(p[0], 2 * t + side))
                )
            )
        specs += [
            pl.BlockSpec(y.shape, lambda t, p: (0, 0), pipeline_mode=pl.Buffered(1)) for y in ys
        ]
        operands.extend([*xs, *ys])
    if received is not None:
        specs.append(whole)
        operands.append(received)
    return pl.pallas_call(
        functools.partial(
            weight_kernel, [(len(xs), len(ys)) for xs, ys in pairs], blocks, split
        ),
        grid_spec=pltpu.PrefetchScalarGridSpec(
            num_scalar_prefetch=1, grid=(blocks,), in_specs=specs, out_specs=out_specs
        ),
        out_shape=out_shape,
        compiler_params=parameters(),
        cost_estimate=SMALL_COST,
        name="weight_product",
    )(place, *operands)


def fold_kernel(counts, *refs):
    outs = refs[sum(counts) :]
    place = 0
    row = 0
    for index, count in enumerate(counts):
        total = refs[place][...].astype(jnp.float32)
        for ref in refs[place + 1 : place + count]:
            total += ref[...].astype(jnp.float32)
        out = outs[index % 2]
        rows = total.shape[0]
        out[row : row + rows, :] = total.astype(jnp.bfloat16)
        row += rows * (index % 2)
        place += count


def fold(sums, rows):
    counts = [len(terms) for pair in sums for terms in pair]
    values = [value for pair in sums for terms in pair for value in terms]
    widths = [terms[0].shape[1] for terms in sums[0]]
    steps = 2 if all(width % 256 == 0 for width in widths) else 1
    return pl.pallas_call(
        functools.partial(fold_kernel, counts),
        grid=(steps,),
        in_specs=[
            pl.BlockSpec((rows, value.shape[1] // steps), lambda t: (1, t)) for value in values
        ],
        out_specs=[
            pl.BlockSpec((rows * len(sums), width // steps), lambda t: (0, t))
            for width in widths
        ],
        out_shape=[
            jax.ShapeDtypeStruct((rows * len(sums), width), jnp.bfloat16) for width in widths
        ],
        compiler_params=parameters(),
        cost_estimate=SMALL_COST,
        name="fold",
    )(*values)


def residual_kernel(parts, e_ref, hidden_ref, first_ref, second_ref, gain_ref, weight_ref, *refs):
    dh_ref, dz_ref = refs[:2]
    step = pl.program_id(0)

    @pl.when(step == 0)
    def _():
        values = hidden_ref[...]
        inverse = lax.rsqrt(jnp.mean(values * values, axis=-1, keepdims=True) + EPSILON)
        scaled = values * inverse
        grad = first_ref[...].astype(jnp.float32) + second_ref[...].astype(jnp.float32)
        grad = grad * gain_ref[1:, :]
        projection = jnp.mean(grad * scaled, axis=-1, keepdims=True)
        total = e_ref[...].astype(jnp.float32) + inverse * (grad - scaled * projection)
        dh_ref[...] = total
        dz_ref[...] = total.astype(jnp.bfloat16)

    result = dot_nn(dz_ref[...], weight_ref[...]).astype(jnp.bfloat16)
    for index in range(parts):

        @pl.when(step == index)
        def _():
            refs[2 + index][...] = result


def residual_gradient(e, hidden_res, first, second, gain, weight, parts):
    rows, depth = e.shape
    tile = depth // parts
    whole = pl.BlockSpec((rows, depth), lambda t: (0, 0))
    result = pl.pallas_call(
        functools.partial(residual_kernel, parts),
        grid=(parts,),
        in_specs=[
            whole,
            whole,
            whole,
            whole,
            pl.BlockSpec((2, depth), lambda t: (0, 0)),
            pl.BlockSpec((depth, tile), lambda t: (0, t)),
        ],
        out_specs=[whole, whole] + [pl.BlockSpec((rows, tile), lambda t: (0, 0))] * parts,
        out_shape=[
            jax.ShapeDtypeStruct((rows, depth), jnp.float32),
            jax.ShapeDtypeStruct((rows, depth), jnp.bfloat16),
            *[jax.ShapeDtypeStruct((rows, tile), jnp.bfloat16)] * parts,
        ],
        compiler_params=parameters(),
        cost_estimate=SMALL_COST,
        name="residual_gradient",
    )(e, hidden_res, first, second, gain, weight)
    return result[0], result[1], list(result[2:])


def tie(value, *others):
    return lax.optimization_barrier((value, others))[0]


def together(*values):
    return lax.optimization_barrier(values)


def add(first, second):
    return (first.astype(jnp.float32) + second.astype(jnp.float32)).astype(jnp.bfloat16)


class Mover:
    def __init__(self):
        self.dp_count = lax.axis_size("dp")
        self.ring = lax.axis_size("tensor")
        self.steps = []
        step = 2
        while step < self.dp_count:
            self.steps.append(step)
            step *= 2

    def swap(self, value, step):
        return lax.ppermute(value, "dp", [(i, i ^ step) for i in range(self.dp_count)])

    def gather(self, shard):
        return lax.all_gather(shard, "dp", axis=0, tiled=True)


    def send(self, pieces, level):
        orders = (self.steps[::-1], self.steps[:1] + self.steps[:0:-1])
        return [self.swap(piece, order[level]) for piece, order in zip(pieces, orders)]

    def begin(self, pieces):
        moved = self.send([pieces[1], pieces[3]], 0)
        return [[pieces[0], moved[0]], [pieces[2], moved[1]]]

    def fold(self, sums, level=1):
        return fold(sums, sums[0][0][0].shape[0] >> level)

    def advance(self, sums, folded):
        level = 1
        while True:
            moved = self.send(folded, level)
            level += 1
            if level == len(self.steps):
                return sums, moved
            rows = moved[0].shape[0] // len(sums)
            sums = [
                [
                    terms + [part[index * rows : (index + 1) * rows]]
                    for terms, part in zip(pair, moved)
                ]
                for index, pair in enumerate(sums)
            ]
            folded = self.fold(sums, level)

    def hop(self, value, shift=1):
        return lax.ppermute(
            value, "tensor", [(i, (i + shift) % self.ring) for i in range(self.ring)]
        )

    def spread(self, value):
        ring = self.ring
        return [value] + [
            lax.ppermute(value, "tensor", [(i, (i - j) % ring) for i in range(ring)])
            for j in range(1, ring)
        ]

    def collect(self, parts):
        ring = self.ring
        total = parts[0]
        for j in range(1, ring):
            moved = lax.ppermute(
                parts[j].astype(jnp.bfloat16), "tensor", [(i, (i + j) % ring) for i in range(ring)]
            )
            total = total + moved.astype(jnp.float32)
        return total

    def exchange(self, parts):
        ring = self.ring
        return [parts[0]] + [
            lax.ppermute(parts[j], "tensor", [(i, (i + j) % ring) for i in range(ring)])
            for j in range(1, ring)
        ]


def totals_of(sums, moved):
    rows = moved[0].shape[0] // len(sums)
    result = []
    for index, pair in enumerate(sums):
        halves = []
        for terms, last in zip(pair, moved):
            total = last[index * rows : (index + 1) * rows].astype(jnp.float32)
            for term in terms:
                total = total + term[:rows].astype(jnp.float32)
            halves.append(total)
        result.append(jnp.concatenate(halves, axis=1))
    return result


def back_norm(grad_normed, scaled, inverse, scale_row):
    grad_scaled = grad_normed * scale_row
    projection = jnp.mean(grad_scaled * scaled, axis=-1, keepdims=True)
    return inverse * (grad_scaled - scaled * projection)


def per_device(
    tokens,
    seq_lengths,
    attention_gain,
    query_matrix,
    key_matrix,
    value_matrix,
    output_weight,
    feedforward_gain,
    gate_weight,
    up_weight,
    down_weight,
    cotangent,
):
    mover = Mover()
    dp_count = mover.dp_count
    ring = mover.ring
    dp_place = lax.axis_index("dp").astype(jnp.int32).reshape(1)
    ring_place = lax.axis_index("tensor")
    place = ring_place.astype(jnp.int32).reshape(1)
    _, local_rows, model_width = tokens.shape
    complete_rows = local_rows * ring
    hidden = gate_weight.shape[1]
    groups = key_matrix.shape[1] // HEAD_SIZE
    joint_width = groups * GROUP_WIDTH
    f32 = jnp.float32
    b16 = jnp.bfloat16

    doc_ids, positions = layout(seq_lengths, complete_rows)
    row_index = jnp.arange(complete_rows, dtype=jnp.int32)
    doc_ids = jnp.where(doc_ids[0] < PIECES, doc_ids[0], PIECES + row_index)

    def to_relative(values):
        view = values.reshape((ring, local_rows) + values.shape[1:])
        return jnp.roll(view, -(ring_place + 1), axis=0)[::-1].reshape(values.shape)

    doc_ids = to_relative(doc_ids)
    cosine, sine = rope_tables(to_relative(positions[0]), HEAD_SIZE)
    cosine_table = jnp.tile(cosine, (1, 128 // cosine.shape[1]))
    sine_table = jnp.tile(jnp.concatenate([-sine, sine], axis=1), (1, 128 // HEAD_SIZE))

    own_gains = jnp.pad(jnp.stack([attention_gain, feedforward_gain]), ((0, 126), (0, 0)))
    joint_matrix, packed = pack(query_matrix, key_matrix, value_matrix, own_gains, groups)
    joint_full = mover.gather(packed)
    output_parts = mover.spread(output_weight.T)
    up_shard = jnp.concatenate([gate_weight, up_weight], axis=1)
    output_parts, cosine_table, sine_table, doc_ids, up_shard, down_shard = together(
        output_parts, cosine_table, sine_table, doc_ids, up_shard, down_weight.T
    )
    local_tokens = tokens[0]
    token_chunks = [local_tokens, mover.hop(local_tokens)]
    up_shard = join(output_parts + [up_shard], [0] * (ring + 1))
    up_full = mover.gather(up_shard)
    down_full = mover.gather(tie(down_shard, up_shard))
    gains = joint_full[:, joint_width : joint_width + 2].T.astype(f32)

    def projection(kept, index):
        return project(
            token_chunks[index],
            gains,
            joint_full,
            cosine_table,
            sine_table,
            kept,
            index,
            ring,
            groups,
        )

    kept = projection(None, 0)
    for j in range(1, ring):
        token_chunks[j], kept, gains = together(token_chunks[j], kept, gains)
        if j + 1 < ring:
            token_chunks.append(mover.hop(token_chunks[j]))
        else:
            local_cotangent = tie(cotangent[0], token_chunks[j])
            moved = mover.hop(local_cotangent)
        kept = projection(kept, j)
    normed_one, joint = kept
    attended, totals = attention_forward(joint, doc_ids, place, ring, groups)
    moved, attended = together(moved, attended)
    cotangent_chunks = [local_cotangent, moved]
    attended_parts = [attended]
    while len(attended_parts) < ring:
        part = mover.hop(attended_parts[-1], -1)
        if len(attended_parts) == ring - 1:
            partial, attended_local = heads_product(
                tie(attended_parts, attended_parts[-1]), up_full, token_chunks
            )
            part, partial, attended_local = together(part, partial, attended_local)
        attended_parts.append(part)
    moved, last = together(moved, attended_parts[-1])

    pairs = ring // 2
    moved = mover.hop(moved)
    hidden_res, normed_two, attended_last = after_attention(partial, last, up_full, gains, ring)
    upward = up_chunk(normed_two, up_full, None, 0, pairs)
    downward = None
    grads = []

    def chunks_of(pair):
        return [cotangent_chunks[(2 * pair + i) % ring] for i in (1, 2)]

    def lower(pair, kept):
        return down_chunk(
            chunks_of(pair), upward[0], upward[1], down_full, up_full, kept, pair, pairs
        )

    for j in range(2, ring):
        if j > 2:
            moved = mover.hop(moved)
            if j % 2:
                downward, parts = lower((j - 3) // 2, downward)
                grads.extend(parts)
            else:
                upward = up_chunk(normed_two, up_full, upward, j // 2 - 1, pairs)
        moved, upward, downward, grads = together(moved, upward, downward, grads)
        cotangent_chunks.append(moved)

    def weights(xs, ys, received=None):
        return weight_product([(xs, ys)], dp_place, dp_count, received)

    ordered = cotangent_chunks[1:] + cotangent_chunks[:1]
    total = grads[0]
    moved = mover.hop(total)
    upward = up_chunk(tie(normed_two, total), up_full, upward, pairs - 1, pairs)
    product = upward[2]
    down_part = weights(ordered, [product])
    moved, upward, down_part = together(moved, upward, down_part)
    down_part = mover.swap(down_part, 1)
    for j in range(2, ring):
        total = add(moved, grads[j - 1])
        moved = mover.hop(total)
        if j == 2:
            downward, parts = lower(pairs - 1, tie(downward, total))
            grads.extend(parts)
            moved, downward, grads = together(moved, downward, grads)
            grad_gate, grad_up = downward
        if j == 3:
            gate_part = weights([tie(normed_two, total)], [grad_gate])
            branch = transposed_product(
                [tie(product, gate_part)], down_full, 0, ring // 2, 0, 2
            )
            down_part = weights(tie(ordered, branch), [product], down_part)
            moved, gate_part, branch, down_part = together(moved, gate_part, branch, down_part)
    gate_part = mover.swap(gate_part, 1)
    down_part = mover.begin(down_part)
    grad_hidden, grad_branch, grad_parts = residual_gradient(
        local_cotangent, hidden_res, moved, grads[-1], gains, up_full, ring
    )
    grad_hidden, grad_branch, grad_parts, gate_part = together(
        grad_hidden, grad_branch, grad_parts, gate_part
    )

    grad_parts = mover.exchange(grad_parts)
    output_part = weights([grad_branch], [attended_local, attended_last])
    gate_part = weights([tie(normed_two, output_part)], [grad_gate], gate_part)
    grad_parts, output_part, gate_part, down_part = together(
        grad_parts, output_part, gate_part, down_part
    )
    grad_joint = []
    sent = 0
    folded = []
    moved = branch[0]
    for group in range(groups):
        moved = mover.hop(moved)
        sent += 1
        if group == 0:
            output_part = mover.swap(output_part, 1)
            gate_part = mover.begin(gate_part)
        else:
            output_part = mover.begin(output_part)
        grad_joint.append(
            attention_backward(
                joint,
                attended,
                tie(grad_parts, grad_joint),
                totals,
                doc_ids,
                cosine_table,
                sine_table,
                place,
                group,
            )
        )
        if group == 0:
            output_part = weights(
                [tie(grad_branch, grad_joint)], [attended_local, attended_last], output_part
            )
        if group + 1 == groups:
            grads = transposed_product(grad_joint, joint_full, 0, ring)
            folded = mover.fold(tie([gate_part, down_part], grads))
        moved, grad_joint, grads, gate_part, output_part, folded = together(
            moved, grad_joint, grads, gate_part, output_part, folded
        )
        if group + 1 < groups:
            moved = add(moved, branch[sent])
    if groups == 1:
        output_part = mover.begin(output_part)
    branch_moved = moved
    moved = grads[0]

    def last_weights(total, received):
        return weight_product(
            [([tie(normed_two, total)], [grad_up]), ([normed_one], grad_joint)],
            dp_place,
            dp_count,
            received,
        )

    for j in range(1, ring):
        total = grads[1] if j == 1 else add(moved, grads[j])
        moved = mover.hop(total)
        if j == 1:
            first_parts = mover.advance([gate_part, down_part], folded)
            folded = mover.fold(tie([output_part], total))
            last_part = last_weights(folded, None)
            branch = branch + transposed_product(
                [tie(product, last_part)], down_full, 0, ring // 2, 1, 2
            )
            moved, last_part, branch, folded, first_parts = together(
                moved, last_part, branch, folded, first_parts
            )
        if j == 2:
            output_part = mover.advance([output_part], folded)
            last_part = last_weights(total, mover.swap(last_part, 1))
            gate_out, down_out = totals_of(*first_parts)
            down_out = down_out.T
            next_branch = add(tie(branch_moved, last_part), branch[sent])
            moved, last_part, output_part, gate_out, down_out, next_branch = together(
                moved, last_part, output_part, gate_out, down_out, next_branch
            )
        if j == 3:
            last_part = mover.begin(last_part)
            branch_moved = mover.hop(tie(next_branch, total))
            sent += 1
            output_out = jnp.split(totals_of(*output_part)[0], ring, axis=1)
            moved, last_part, output_out = together(moved, last_part, output_out)
    folded, output_out = together(mover.fold([last_part]), output_out)
    last_part = mover.advance([last_part], folded)
    output_out = mover.collect(output_out[:-1] + [tie(output_out[-1], last_part)]).T
    scaled_one, inverse_one = norm_rows(local_tokens.astype(f32))
    local_one = moved.astype(f32) + grads[0].astype(f32)
    input_gradient = grad_hidden + back_norm(local_one, scaled_one, inverse_one, gains[:1])
    branch_moved = tie(branch_moved, last_part)
    for j in range(sent, ring - 1):
        branch_moved = mover.hop(add(branch_moved, branch[j]))
    block_output = (
        hidden_res + (branch_moved.astype(f32) + branch[-1].astype(f32))
    ).astype(b16)
    last_out = totals_of(*last_part)[0]
    up_out, joint_out = last_out[:, :hidden], last_out[:, hidden:]

    sums = jnp.stack(
        [
            jnp.sum(joint_out * joint_matrix.astype(f32), axis=1) / attention_gain.astype(f32),
            jnp.sum(gate_out * gate_weight.astype(f32) + up_out * up_weight.astype(f32), axis=1)
            / feedforward_gain.astype(f32),
        ]
    )
    gain_out = sums
    for shift in range(1, ring):
        gain_out = gain_out + lax.ppermute(
            sums, "tensor", [(i, (i + shift) % ring) for i in range(ring)]
        )

    def ungrouped(first, width):
        return jnp.concatenate(
            [
                joint_out[:, g * GROUP_WIDTH + first : g * GROUP_WIDTH + first + width]
                for g in range(groups)
            ],
            axis=1,
        )

    return (
        block_output[None],
        input_gradient[None],
        gain_out[0],
        ungrouped(0, GROUP_QUERY),
        ungrouped(GROUP_QUERY, HEAD_SIZE),
        ungrouped(GROUP_QUERY + HEAD_SIZE, HEAD_SIZE),
        output_out,
        gain_out[1],
        gate_out,
        up_out,
        down_out,
    )


def solution(mesh):
    return jax.shard_map(
        per_device,
        mesh=mesh,
        in_specs=(
            P("dp", "tensor", None),
            P("dp", None),
            P("dp"),
            P("dp", "tensor"),
            P("dp", "tensor"),
            P("dp", "tensor"),
            P("tensor", "dp"),
            P("dp"),
            P("dp", "tensor"),
            P("dp", "tensor"),
            P("tensor", "dp"),
            P("dp", "tensor", None),
        ),
        out_specs=(
            P("dp", "tensor", None),
            P("dp", "tensor", None),
            P("dp"),
            P("dp", "tensor"),
            P("dp", "tensor"),
            P("dp", "tensor"),
            P("tensor", "dp"),
            P("dp"),
            P("dp", "tensor"),
            P("dp", "tensor"),
            P("tensor", "dp"),
        ),
        check_vma=False,
    )
```

```python
import functools
import math

import jax
import jax.numpy as jnp
from jax import lax
from jax.experimental import pallas as pl
from jax.experimental.pallas import tpu as pltpu
from jax.sharding import PartitionSpec as P

QUERY_HEADS = 32
KEY_VALUE_HEADS = 8
HEAD_SIZE = 64
PIECES = 4


EPSILON = 1e-05
ROPE_BASE = 500000.0
NEGATIVE = -1e30
GROUP_QUERY = QUERY_HEADS // KEY_VALUE_HEADS * HEAD_SIZE
GROUP_WIDTH = GROUP_QUERY + 2 * HEAD_SIZE
KERNEL_VMEM = 60 * 1024 * 1024
SMALL_COST = pl.CostEstimate(flops=1, bytes_accessed=1, transcendentals=0)


def layout(lengths, complete_rows):
    doc_ends = jnp.cumsum(lengths, axis=-1)
    row_index = jnp.arange(complete_rows, dtype=jnp.int32)
    piece_count = lengths.shape[-1]
    doc_ids = jnp.sum((row_index[None, :, None] >= doc_ends[:, None, :]).astype(jnp.int32), axis=2)
    starts = doc_ends - lengths
    chosen = doc_ids[:, :, None] == jnp.arange(piece_count, dtype=jnp.int32)[None, None, :]
    doc_begin = jnp.sum(jnp.where(chosen, starts[:, None, :], 0), axis=2) + jnp.where(
        doc_ids == piece_count, doc_ends[:, -1:], 0
    )
    return (doc_ids, row_index[None, :] - doc_begin)


def rope_tables(positions, head_dim):
    half_dim = head_dim // 2
    frequency = ROPE_BASE ** (-(jnp.arange(half_dim, dtype=jnp.float32) * (2.0 / head_dim)))
    angles = positions.astype(jnp.float32)[..., None] * frequency
    return (jnp.cos(angles), jnp.sin(angles))


def norm_rows(values):
    inverse = lax.rsqrt(jnp.mean(values * values, axis=-1, keepdims=True) + EPSILON)
    return (values * inverse, inverse)


def dot_nt(left, right):
    return lax.dot_general(
        left, right, (((1,), (1,)), ((), ())), preferred_element_type=jnp.float32
    )


def dot_nn(left, right):
    return jnp.dot(left, right, preferred_element_type=jnp.float32)


def dot_tn(left, right):
    return lax.dot_general(
        left, right, (((0,), (0,)), ((), ())), preferred_element_type=jnp.float32
    )


def tile_of(size, limit=512):
    tile = limit
    while size % tile:
        tile //= 2
    return tile


def parameters():
    return pltpu.CompilerParams(vmem_limit_bytes=KERNEL_VMEM)


def swap_halves(values):
    lane = lax.broadcasted_iota(jnp.int32, values.shape, 1)
    half = HEAD_SIZE // 2
    return jnp.where(
        lane % HEAD_SIZE < half, pltpu.roll(values, 128 - half, 1), pltpu.roll(values, half, 1)
    )


def turned(values, cosine, sine, start):
    result = values * cosine + swap_halves(values) * sine
    rotated = GROUP_WIDTH - HEAD_SIZE
    if start + 128 <= rotated:
        return result
    lane = lax.broadcasted_iota(jnp.int32, values.shape, 1)
    return jnp.where(lane < rotated - start, result, values)


def project_kernel(x_ref, gain_ref, weight_ref, cos_ref, sin_ref, *refs):
    normed_ref, joint_ref = refs[-2:]

    @pl.when(pl.program_id(0) == 0)
    def _():
        values = x_ref[...].astype(jnp.float32)
        inverse = lax.rsqrt(jnp.mean(values * values, axis=-1, keepdims=True) + EPSILON)
        normed_ref[...] = (values * inverse * gain_ref[:1, :]).astype(jnp.bfloat16)

    product = dot_nn(normed_ref[...], weight_ref[...])
    for start in range(0, GROUP_WIDTH, 128):
        part = turned(product[:, start : start + 128], cos_ref[...], sin_ref[...], start)
        if start < GROUP_QUERY:
            part = part * HEAD_SIZE ** (-0.5)
        joint_ref[:, start : start + 128] = part.astype(jnp.bfloat16)


def project(x, gain, weight, cosine, sine, kept, index, count, groups):
    rows, depth = x.shape
    specs = [
        pl.BlockSpec((rows, depth), lambda g: (0, 0)),
        pl.BlockSpec((2, depth), lambda g: (0, 0)),
        pl.BlockSpec((depth, GROUP_WIDTH), lambda g: (0, g)),
        pl.BlockSpec((rows, 128), lambda g: (index, 0)),
        pl.BlockSpec((rows, 128), lambda g: (index, 0)),
    ]
    operands = [x, gain, weight, cosine, sine]
    aliases = {}
    if kept is not None:
        specs.extend([pl.BlockSpec(memory_space=pl.ANY)] * 2)
        aliases = {len(operands) + i: i for i in range(2)}
        operands.extend(kept)
    return pl.pallas_call(
        project_kernel,
        grid=(groups,),
        in_specs=specs,
        out_specs=[
            pl.BlockSpec((rows, depth), lambda g: (index, 0)),
            pl.BlockSpec((rows, GROUP_WIDTH), lambda g: (index, g)),
        ],
        out_shape=[
            jax.ShapeDtypeStruct((rows * count, depth), jnp.bfloat16),
            jax.ShapeDtypeStruct((rows * count, GROUP_WIDTH * groups), jnp.bfloat16),
        ],
        input_output_aliases=aliases,
        compiler_params=parameters(),
        cost_estimate=SMALL_COST,
        name="project",
    )(*operands)


def ring_offset(place, chunk, count, rows):
    return pl.multiple_of(lax.rem(place - chunk + count, count) * rows, rows)


def stack_heads(target, source):
    rows, width = source.shape
    for head in range(width // HEAD_SIZE):
        target[head * rows : (head + 1) * rows, :] = source[
            :, head * HEAD_SIZE : (head + 1) * HEAD_SIZE
        ]


def fill_bias(bias, key_docs, query_docs, earlier):
    rows = key_docs.shape[0]
    row_index = lax.broadcasted_iota(jnp.int32, (rows, rows), 0)
    column_index = lax.broadcasted_iota(jnp.int32, (rows, rows), 1)
    same = (key_docs == query_docs) & ((row_index <= column_index) | earlier)
    values = jnp.where(same, 0.0, NEGATIVE)
    for first in range(0, bias.shape[1], rows):
        bias[:, first : first + rows] = values


def forward_kernel(
    count,
    place_ref,
    own_ref,
    all_ref,
    docq_ref,
    dock_ref,
    o_ref,
    lse_ref,
    bias,
    queries,
    values_all,
    mixed,
):
    chunk = pl.program_id(1)
    place = place_ref[0]
    rows = own_ref.shape[0]
    heads = GROUP_QUERY // HEAD_SIZE
    stack_heads(queries, own_ref.at[:, :GROUP_QUERY])

    @pl.when(chunk == 0)
    def _():
        values = all_ref[:, GROUP_QUERY:].astype(jnp.float32)
        values_all[...] = values.T[HEAD_SIZE:].astype(jnp.bfloat16)

    mixed[...] = jnp.zeros_like(mixed)

    def block(j, carry):
        peaks, total = carry
        offset = ring_offset(place, j, count, rows)
        piece = pl.ds(offset, rows)
        fill_bias(bias, dock_ref[piece, :], docq_ref[...], j < chunk)
        keys = all_ref[piece, GROUP_QUERY : GROUP_QUERY + HEAD_SIZE]
        scores = dot_nt(keys, queries[...]) + bias[...]
        higher = jnp.maximum(peaks, jnp.max(scores, axis=0, keepdims=True))
        probs = jnp.exp(scores - higher)
        scale = jnp.exp(peaks - higher)
        mixed[...] = mixed[...] * scale + dot_nn(
            values_all[:, piece], probs.astype(jnp.bfloat16)
        )
        return higher, total * scale + jnp.sum(probs, axis=0, keepdims=True)

    peaks, total = lax.fori_loop(
        0,
        chunk + 1,
        block,
        (
            jnp.full((1, heads * rows), NEGATIVE, jnp.float32),
            jnp.zeros((1, heads * rows), jnp.float32),
        ),
    )
    lse_ref[:1, :] = peaks + jnp.log(total)
    result = mixed[...] / total
    for head in range(0, heads, 2):
        pair = jnp.concatenate(
            [result[:, (head + i) * rows : (head + i + 1) * rows] for i in range(2)], axis=0
        )
        o_ref[:, head * HEAD_SIZE : (head + 2) * HEAD_SIZE] = pair.T.astype(jnp.bfloat16)


def attention_forward(joint, docs, place, count, groups):
    total_rows = joint.shape[0]
    rows = total_rows // count
    stacked = rows * GROUP_QUERY // HEAD_SIZE

    def block(c, place_ref):
        return lax.rem(place_ref[0] - c + count, count)

    spec = pltpu.PrefetchScalarGridSpec(
        num_scalar_prefetch=1,
        grid=(groups, count),
        in_specs=[
            pl.BlockSpec((rows, GROUP_WIDTH), lambda g, c, p: (block(c, p), g)),
            pl.BlockSpec((total_rows, GROUP_WIDTH), lambda g, c, p: (0, g)),
            pl.BlockSpec((1, rows), lambda g, c, p: (0, block(c, p))),
            pl.BlockSpec((total_rows, 1), lambda g, c, p: (0, 0)),
        ],
        out_specs=[
            pl.BlockSpec((rows, GROUP_QUERY), lambda g, c, p: (block(c, p), g)),
            pl.BlockSpec((8, stacked), lambda g, c, p: (g, block(c, p))),
        ],
        scratch_shapes=[
            pltpu.VMEM((rows, stacked), jnp.float32),
            pltpu.VMEM((stacked, HEAD_SIZE), jnp.bfloat16),
            pltpu.VMEM((HEAD_SIZE, total_rows), jnp.bfloat16),
            pltpu.VMEM((HEAD_SIZE, stacked), jnp.float32),
        ],
    )
    return pl.pallas_call(
        functools.partial(forward_kernel, count),
        grid_spec=spec,
        out_shape=[
            jax.ShapeDtypeStruct((total_rows, GROUP_QUERY * groups), jnp.bfloat16),
            jax.ShapeDtypeStruct((8 * groups, stacked * count), jnp.float32),
        ],
        compiler_params=parameters(),
        cost_estimate=SMALL_COST,
        name="attend",
    )(place, joint, joint, docs[None, :], docs[:, None])


def backward_kernel(count, place_ref, *refs):
    own_ref, all_ref, o_ref = refs[:3]
    lse_ref, docq_ref, dock_ref, cos_ref, sin_ref = refs[3 + count : 8 + count]
    out_ref, bias, queries, grads, keys_all, values_all, sum_q, sum_k, sum_v = refs[8 + count :]
    chunk = pl.program_id(0)
    place = place_ref[0]
    rows = own_ref.shape[0]
    heads = GROUP_QUERY // HEAD_SIZE
    stack_heads(queries, own_ref.at[:, :GROUP_QUERY])
    for index in range(count):

        @pl.when(lax.rem(place - chunk + count, count) == index)
        def _():
            stack_heads(grads, refs[3 + index])

    @pl.when(chunk == 0)
    def _():
        keys_all[...] = all_ref[:, GROUP_QUERY : GROUP_QUERY + HEAD_SIZE]
        values_all[...] = all_ref[:, GROUP_QUERY + HEAD_SIZE :]
        sum_k[...] = jnp.zeros_like(sum_k)
        sum_v[...] = jnp.zeros_like(sum_v)

    sum_q[...] = jnp.zeros_like(sum_q)
    ones = jnp.ones((8, HEAD_SIZE), jnp.bfloat16)
    inner = []
    for head in range(heads):
        attended = o_ref[:, head * HEAD_SIZE : (head + 1) * HEAD_SIZE].astype(jnp.float32)
        both = attended * grads[head * rows : (head + 1) * rows, :].astype(jnp.float32)
        high = both.astype(jnp.bfloat16)
        low = (both - high.astype(jnp.float32)).astype(jnp.bfloat16)
        inner.append((dot_nt(ones, high) + dot_nt(ones, low))[:1])
    inner = jnp.concatenate(inner, axis=1)

    def block(j, carry):
        offset = ring_offset(place, j, count, rows)
        piece = pl.ds(offset, rows)
        fill_bias(bias, dock_ref[piece, :], docq_ref[...], j < chunk)
        probs = jnp.exp(dot_nt(keys_all[piece, :], queries[...]) + bias[...] - lse_ref[:1, :])
        grad_probs = dot_nt(values_all[piece, :], grads[...])
        grad_scores = (probs * (grad_probs - inner)).astype(jnp.bfloat16)
        sum_v[piece, :] += dot_nn(probs.astype(jnp.bfloat16), grads[...])
        sum_k[piece, :] += dot_nn(grad_scores, queries[...])
        sum_q[...] += dot_tn(grad_scores, keys_all[piece, :])
        return carry

    lax.fori_loop(0, chunk + 1, block, 0)
    own = pl.ds(ring_offset(place, chunk, count, rows), rows)
    for first in range(0, heads, 2):
        start = first * HEAD_SIZE
        part = jnp.concatenate(
            [sum_q[(first + i) * rows : (first + i + 1) * rows, :] for i in range(2)], axis=1
        )
        part = turned(part, cos_ref[own, :], -sin_ref[own, :], start)
        out_ref[own, start : start + 128] = (part * HEAD_SIZE ** (-0.5)).astype(jnp.bfloat16)

    @pl.when(chunk == count - 1)
    def _():
        part = jnp.concatenate([sum_k[...], sum_v[...]], axis=1)
        part = turned(part, cos_ref[...], -sin_ref[...], GROUP_QUERY)
        out_ref[:, GROUP_QUERY:] = part.astype(jnp.bfloat16)


def attention_backward(joint, attended, grads, lse, docs, cosine, sine, place, group):
    count = len(grads)
    total_rows = joint.shape[0]
    rows = total_rows // count
    stacked = rows * GROUP_QUERY // HEAD_SIZE

    def block(c, place_ref):
        return lax.rem(place_ref[0] - c + count, count)

    table = pl.BlockSpec((total_rows, 128), lambda c, p: (0, 0))
    spec = pltpu.PrefetchScalarGridSpec(
        num_scalar_prefetch=1,
        grid=(count,),
        in_specs=[
            pl.BlockSpec((rows, GROUP_WIDTH), lambda c, p: (block(c, p), group)),
            pl.BlockSpec((total_rows, GROUP_WIDTH), lambda c, p: (0, group)),
            pl.BlockSpec((rows, GROUP_QUERY), lambda c, p: (block(c, p), group)),
            *[pl.BlockSpec((rows, GROUP_QUERY), lambda c, p: (0, group))] * count,
            pl.BlockSpec((8, stacked), lambda c, p: (group, block(c, p))),
            pl.BlockSpec((1, rows), lambda c, p: (0, block(c, p))),
            pl.BlockSpec((total_rows, 1), lambda c, p: (0, 0)),
            table,
            table,
        ],
        out_specs=pl.BlockSpec((total_rows, GROUP_WIDTH), lambda c, p: (0, 0)),
        scratch_shapes=[
            pltpu.VMEM((rows, stacked), jnp.float32),
            *[pltpu.VMEM((stacked, HEAD_SIZE), jnp.bfloat16)] * 2,
            *[pltpu.VMEM((total_rows, HEAD_SIZE), jnp.bfloat16)] * 2,
            pltpu.VMEM((stacked, HEAD_SIZE), jnp.float32),
            *[pltpu.VMEM((total_rows, HEAD_SIZE), jnp.float32)] * 2,
        ],
    )
    return pl.pallas_call(
        functools.partial(backward_kernel, count),
        grid_spec=spec,
        out_shape=jax.ShapeDtypeStruct((total_rows, GROUP_WIDTH), jnp.bfloat16),
        compiler_params=parameters(),
        cost_estimate=SMALL_COST,
        name="attend_back",
    )(
        place,
        joint,
        joint,
        attended,
        *grads,
        lse,
        docs[None, :],
        docs[:, None],
        cosine,
        sine,
    )


def pack_kernel(groups, query_ref, key_ref, value_ref, gain_ref, joint_ref, out_ref):
    for g in range(groups):
        start = g * GROUP_WIDTH
        columns = slice(g * HEAD_SIZE, (g + 1) * HEAD_SIZE)
        joint_ref[:, start : start + GROUP_QUERY] = query_ref[
            :, g * GROUP_QUERY : (g + 1) * GROUP_QUERY
        ]
        joint_ref[:, start + GROUP_QUERY : start + GROUP_WIDTH] = jnp.concatenate(
            [key_ref[:, columns], value_ref[:, columns]], axis=1
        )
    width = groups * GROUP_WIDTH
    out_ref[:, :width] = joint_ref[...]
    out_ref[:, width:] = gain_ref[...].astype(jnp.float32).T.astype(jnp.bfloat16)


def pack(query, key, value, gains, groups):
    rows = query.shape[0]
    width = groups * GROUP_WIDTH
    return pl.pallas_call(
        functools.partial(pack_kernel, groups),
        out_shape=[
            jax.ShapeDtypeStruct((rows, width), jnp.bfloat16),
            jax.ShapeDtypeStruct((rows, width + 128), jnp.bfloat16),
        ],
        compiler_params=parameters(),
        cost_estimate=SMALL_COST,
        name="pack",
    )(query, key, value, gains)


def join_kernel(*refs):
    place = 0
    for ref in refs[:-2]:
        size = ref.shape[1]
        refs[-1][:, place : place + size] = ref[...]
        place += size


def join(parts, rest):
    rows = rest.shape[0]
    width = sum(part.shape[1] for part in parts)
    return pl.pallas_call(
        join_kernel,
        grid=(1,),
        in_specs=[pl.BlockSpec(part.shape, lambda i: (0, 0)) for part in parts]
        + [pl.BlockSpec(memory_space=pl.ANY)],
        out_specs=pl.BlockSpec((rows, width), lambda i: (0, 0)),
        out_shape=jax.ShapeDtypeStruct(rest.shape, rest.dtype),
        input_output_aliases={len(parts): 0},
        compiler_params=parameters(),
        cost_estimate=SMALL_COST,
        name="join",
    )(*parts, rest)


def transposed_kernel(count, parts, *refs):
    total = dot_nt(refs[0][...], refs[count][...])
    for index in range(1, count):
        total += dot_nt(refs[index][...], refs[count + index][...])
    rows = total.shape[0] // parts
    for index in range(parts):
        refs[2 * count + index][...] = total[index * rows : (index + 1) * rows].astype(
            jnp.bfloat16
        )


def transposed_product(xs, weight, column, parts, block=0, blocks=1):
    rows, depth = xs[0].shape
    rows //= blocks
    width = weight.shape[0]
    tile = tile_of(width)
    specs = [pl.BlockSpec((rows, depth), lambda t: (block, 0))] * len(xs)
    for index in range(len(xs)):
        specs.append(pl.BlockSpec((tile, depth), lambda t, index=index: (t, column + index)))
    part = (rows // parts, width)
    return pl.pallas_call(
        functools.partial(transposed_kernel, len(xs), parts),
        grid=(width // tile,),
        in_specs=specs,
        out_specs=[pl.BlockSpec((part[0], tile), lambda t: (0, t))] * parts,
        out_shape=[jax.ShapeDtypeStruct(part, jnp.bfloat16)] * parts,
        compiler_params=parameters(),
        cost_estimate=SMALL_COST,
        name="transposed",
    )(*xs, *[weight] * len(xs))


def heads_kernel(count, *refs):
    parts = refs[:count]
    weight_ref = refs[count]
    tokens = refs[count + 1 : -2]
    out_ref, local_ref = refs[-2:]
    step = pl.program_id(0)
    width = parts[0].shape[1]

    @pl.when(step == 0)
    def _():
        for j in range(count):
            local_ref[:, j * width : (j + 1) * width] = parts[j][...]

    for j in range(count):
        term = dot_nt(parts[j][...], weight_ref[:, j * width : (j + 1) * width])
        if j == 0:
            out_ref[...] = term
        else:
            out_ref[...] += term
    for index in range(len(tokens)):

        @pl.when(step == index)
        def _():
            out_ref[...] += tokens[index][...].astype(jnp.float32)


def heads_product(parts, weight, tokens):
    blocks = len(tokens)
    rows, width = tokens[0].shape
    depth = parts[0].shape[1]
    specs = [
        pl.BlockSpec((rows, depth), lambda i, j=j: (lax.rem(i + j, blocks), 0))
        for j in range(len(parts))
    ]
    whole = pl.BlockSpec((rows, width), lambda i: (0, 0), pipeline_mode=pl.Buffered(1))
    return pl.pallas_call(
        functools.partial(heads_kernel, len(parts)),
        grid=(blocks,),
        in_specs=[
            *specs,
            pl.BlockSpec(
                (width, depth * len(parts)), lambda i: (0, 0), pipeline_mode=pl.Buffered(1)
            ),
            *[whole] * blocks,
        ],
        out_specs=[
            pl.BlockSpec((rows, width), lambda i: (i, 0)),
            pl.BlockSpec((rows, depth * len(parts)), lambda i: (0, 0)),
        ],
        out_shape=[
            jax.ShapeDtypeStruct((rows * blocks, width), jnp.float32),
            jax.ShapeDtypeStruct((rows, depth * len(parts)), jnp.bfloat16),
        ],
        compiler_params=parameters(),
        cost_estimate=SMALL_COST,
        name="heads_product",
    )(*parts, weight, *tokens)


def attended_kernel(
    partial_ref, last_ref, weight_ref, gain_ref, hidden_ref, normed_ref, local_ref
):
    values = partial_ref[...] + dot_nt(last_ref[...], weight_ref[...])

    @pl.when(pl.program_id(0) == 0)
    def _():
        hidden_ref[...] = values
        local_ref[...] = last_ref[...]

    inverse = lax.rsqrt(jnp.mean(values * values, axis=-1, keepdims=True) + EPSILON)
    normed_ref[...] = (values * inverse * gain_ref[1:, :]).astype(jnp.bfloat16)


def after_attention(partial, last, weight, gain, count):
    total_rows, width = partial.shape
    rows = total_rows // count
    depth = last.shape[1]
    return pl.pallas_call(
        attended_kernel,
        grid=(count,),
        in_specs=[
            pl.BlockSpec((rows, width), lambda i: (i, 0)),
            pl.BlockSpec((rows, depth), lambda i: (lax.rem(i + count - 1, count), 0)),
            pl.BlockSpec((width, depth), lambda i: (0, count - 1)),
            pl.BlockSpec((2, width), lambda i: (0, 0)),
        ],
        out_specs=[
            pl.BlockSpec((rows, width), lambda i: (0, 0)),
            pl.BlockSpec((rows, width), lambda i: (lax.rem(i + count - 1, count), 0)),
            pl.BlockSpec((rows, depth), lambda i: (0, 0)),
        ],
        out_shape=[
            jax.ShapeDtypeStruct((rows, width), jnp.float32),
            jax.ShapeDtypeStruct((total_rows, width), jnp.bfloat16),
            jax.ShapeDtypeStruct((rows, depth), jnp.bfloat16),
        ],
        compiler_params=parameters(),
        cost_estimate=SMALL_COST,
        name="after_attention",
    )(partial, last, weight, gain)


def up_kernel(x_ref, gate_ref, up_ref, *refs):
    a_ref, u_ref, g_ref = refs[-3:]
    gate = dot_nn(x_ref[...], gate_ref[...])
    up = dot_nn(x_ref[...], up_ref[...])
    a_ref[...] = gate.astype(jnp.bfloat16)
    u_ref[...] = up.astype(jnp.bfloat16)
    g_ref[...] = (gate * jax.nn.sigmoid(gate) * up).astype(jnp.bfloat16)


def up_chunk(x, weight, kept, index, count):
    total_rows, depth = x.shape
    rows = total_rows // count
    hidden = (weight.shape[1] - depth) // 2
    tile = tile_of(hidden)
    tiles = hidden // tile
    start = depth // tile
    specs = [
        pl.BlockSpec((rows, depth), lambda t: (index, 0)),
        pl.BlockSpec((depth, tile), lambda t: (0, start + t)),
        pl.BlockSpec((depth, tile), lambda t: (0, start + tiles + t)),
    ]
    operands = [x, weight, weight]
    aliases = {}
    if kept is not None:
        specs.extend([pl.BlockSpec(memory_space=pl.ANY)] * 3)
        aliases = {len(operands) + i: i for i in range(3)}
        operands.extend(kept)
    return pl.pallas_call(
        up_kernel,
        grid=(tiles,),
        in_specs=specs,
        out_specs=[pl.BlockSpec((rows, tile), lambda t: (index, t))] * 3,
        out_shape=[jax.ShapeDtypeStruct((total_rows, hidden), jnp.bfloat16)] * 3,
        input_output_aliases=aliases,
        compiler_params=parameters(),
        cost_estimate=SMALL_COST,
        name="up_chunk",
    )(*operands)


def down_kernel(parts, tiles, *refs):
    down_ref, a_ref, u_ref, gate_ref, up_ref = refs[parts : parts + 5]
    da_ref, du_ref = refs[-5 - parts : -3 - parts]
    dx_refs = refs[-3 - parts : -3]
    da_kept, du_kept, e_out = refs[-3:]
    step = pl.program_id(0)

    @pl.when(step == 0)
    def _():
        rows = refs[0].shape[0]
        for index in range(parts):
            e_out[index * rows : (index + 1) * rows, :] = refs[index][...]

    @pl.when(step < tiles)
    def _():
        grad = dot_nn(e_out[...], down_ref[...])
        gate = a_ref[...].astype(jnp.float32)
        up = u_ref[...].astype(jnp.float32)
        sigmoid = jax.nn.sigmoid(gate)
        da = (grad * up * sigmoid * (1.0 + gate * (1.0 - sigmoid))).astype(jnp.bfloat16)
        du = (grad * gate * sigmoid).astype(jnp.bfloat16)
        da_ref[...] = da
        du_ref[...] = du
        tile = da.shape[1]
        for index in range(tiles):

            @pl.when(step == index)
            def _():
                da_kept[:, index * tile : (index + 1) * tile] = da
                du_kept[:, index * tile : (index + 1) * tile] = du

    @pl.when(step >= tiles)
    def _():
        total = dot_nt(da_kept[...], gate_ref[...]) + dot_nt(du_kept[...], up_ref[...])
        rows = total.shape[0] // parts
        for index in range(parts):
            dx_refs[index][...] = total[index * rows : (index + 1) * rows].astype(jnp.bfloat16)


def down_chunk(es, a, u, down_weight, weight, kept, index, count):
    depth, hidden = down_weight.shape
    rows = len(es) * es[0].shape[0]
    start = depth // hidden
    tile = tile_of(hidden)
    tiles = hidden // tile
    row_tile = tile_of(depth)

    def column(t):
        return jnp.minimum(t, tiles - 1)

    def row(t):
        return jnp.maximum(t - tiles, 0)

    specs = [pl.BlockSpec(es[0].shape, lambda t: (0, 0))] * len(es) + [
        pl.BlockSpec((depth, tile), lambda t: (0, column(t))),
        pl.BlockSpec((rows, tile), lambda t: (index, column(t))),
        pl.BlockSpec((rows, tile), lambda t: (index, column(t))),
        pl.BlockSpec((row_tile, hidden), lambda t: (row(t), start)),
        pl.BlockSpec((row_tile, hidden), lambda t: (row(t), start + 1)),
    ]
    operands = [*es, down_weight, a, u, weight, weight]
    part = es[0].shape
    shapes = [
        jax.ShapeDtypeStruct((rows * count, hidden), jnp.bfloat16),
        jax.ShapeDtypeStruct((rows * count, hidden), jnp.bfloat16),
        *[jax.ShapeDtypeStruct(part, jnp.bfloat16)] * len(es),
    ]
    aliases = {}
    if kept is not None:
        specs.extend([pl.BlockSpec(memory_space=pl.ANY)] * 2)
        aliases = {len(operands) + i: i for i in range(2)}
        operands.extend(kept)
    result = pl.pallas_call(
        functools.partial(down_kernel, len(es), tiles),
        grid=(tiles + depth // row_tile,),
        in_specs=specs,
        out_specs=[
            pl.BlockSpec((rows, tile), lambda t: (index, column(t))),
            pl.BlockSpec((rows, tile), lambda t: (index, column(t))),
            *[pl.BlockSpec((part[0], row_tile), lambda t: (0, row(t)))] * len(es),
        ],
        out_shape=shapes,
        input_output_aliases=aliases,
        scratch_shapes=[
            pltpu.VMEM((rows, hidden), jnp.bfloat16),
            pltpu.VMEM((rows, hidden), jnp.bfloat16),
            pltpu.VMEM((rows, depth), jnp.bfloat16),
        ],
        compiler_params=parameters(),
        cost_estimate=SMALL_COST,
        name="down_chunk",
    )(*operands)
    return result[:2], list(result[2:])


def weight_kernel(counts, blocks, split, place_ref, *refs):
    step = pl.program_id(0)
    total_refs = sum(parts + widths for parts, widths in counts)
    received = refs[total_refs] if len(refs) > total_refs + 1 else None
    place = 0
    column = 0
    for parts, widths in counts:
        x = refs[place][...]
        if parts > 1:
            x = jnp.concatenate([ref[...] for ref in refs[place : place + parts]], axis=0)
        for y_ref in refs[place + parts : place + parts + widths]:
            width = y_ref.shape[1]
            cuts = set(range(0, width, 1024)) | {width}
            if column < split < column + width:
                cuts.add(split - column)
            cuts = sorted(cuts)
            for first, last in zip(cuts[:-1], cuts[1:]):
                total = dot_tn(x, y_ref[:, first:last])
                start, end = column + first, column + last
                if received is None:
                    refs[-1][:, start:end] = total.astype(jnp.bfloat16)
                    continue
                total += received[:, start:end].astype(jnp.float32)
                total = total.astype(jnp.bfloat16)
                low = start < split
                keep = step < blocks // 2 if low else lax.rem(step, 2) == 0
                keep_ref, send_ref = refs[-4:-2] if low else refs[-2:]
                columns = slice(start, end) if low else slice(start - split, end - split)

                @pl.when(keep)
                def _():
                    keep_ref[:, columns] = total

                @pl.when(jnp.logical_not(keep))
                def _():
                    send_ref[:, columns] = total

            column += width
        place += parts + widths


def weight_product(pairs, place, count, received):
    depth = pairs[0][0][0].shape[1]
    blocks = count // 2
    tile = depth // count
    total = sum(y.shape[1] for _, ys in pairs for y in ys)
    split = -(-total // 256) * 128
    side = 1 if received is None else 0
    whole = pl.BlockSpec((tile, total), lambda t, p: (t, 0))
    if received is None:
        out_specs = whole
        out_shape = jax.ShapeDtypeStruct((depth // 2, total), jnp.bfloat16)
    else:
        half = blocks // 2
        out_specs = [
            pl.BlockSpec((tile, split), lambda t, p: (jnp.minimum(t, half - 1), 0)),
            pl.BlockSpec((tile, split), lambda t, p: (jnp.maximum(t - half, 0), 0)),
            pl.BlockSpec((tile, total - split), lambda t, p: (t // 2, 0)),
            pl.BlockSpec((tile, total - split), lambda t, p: (t // 2, 0)),
        ]
        out_shape = [
            jax.ShapeDtypeStruct((depth // 4, width), jnp.bfloat16)
            for width in (split, split, total - split, total - split)
        ]
    specs = []
    operands = []
    for xs, ys in pairs:
        for x in xs:
            specs.append(
                pl.BlockSpec(
                    (x.shape[0], tile), lambda t, p: (0, lax.bitwise_xor(p[0], 2 * t + side))
                )
            )
        specs += [
            pl.BlockSpec(y.shape, lambda t, p: (0, 0), pipeline_mode=pl.Buffered(1)) for y in ys
        ]
        operands.extend([*xs, *ys])
    if received is not None:
        specs.append(whole)
        operands.append(received)
    return pl.pallas_call(
        functools.partial(
            weight_kernel, [(len(xs), len(ys)) for xs, ys in pairs], blocks, split
        ),
        grid_spec=pltpu.PrefetchScalarGridSpec(
            num_scalar_prefetch=1, grid=(blocks,), in_specs=specs, out_specs=out_specs
        ),
        out_shape=out_shape,
        compiler_params=parameters(),
        cost_estimate=SMALL_COST,
        name="weight_product",
    )(place, *operands)


def fold_kernel(counts, *refs):
    outs = refs[sum(counts) :]
    place = 0
    row = 0
    for index, count in enumerate(counts):
        total = refs[place][...].astype(jnp.float32)
        for ref in refs[place + 1 : place + count]:
            total += ref[...].astype(jnp.float32)
        out = outs[index % 2]
        rows = total.shape[0]
        out[row : row + rows, :] = total.astype(jnp.bfloat16)
        row += rows * (index % 2)
        place += count


def fold(sums, rows):
    counts = [len(terms) for pair in sums for terms in pair]
    values = [value for pair in sums for terms in pair for value in terms]
    widths = [terms[0].shape[1] for terms in sums[0]]
    steps = 2 if all(width % 256 == 0 for width in widths) else 1
    return pl.pallas_call(
        functools.partial(fold_kernel, counts),
        grid=(steps,),
        in_specs=[
            pl.BlockSpec((rows, value.shape[1] // steps), lambda t: (1, t)) for value in values
        ],
        out_specs=[
            pl.BlockSpec((rows * len(sums), width // steps), lambda t: (0, t))
            for width in widths
        ],
        out_shape=[
            jax.ShapeDtypeStruct((rows * len(sums), width), jnp.bfloat16) for width in widths
        ],
        compiler_params=parameters(),
        cost_estimate=SMALL_COST,
        name="fold",
    )(*values)


def residual_kernel(parts, e_ref, hidden_ref, first_ref, second_ref, gain_ref, weight_ref, *refs):
    dh_ref, dz_ref = refs[:2]
    dh, dz = refs[-2:]
    step = pl.program_id(0)
    tile = weight_ref.shape[1]

    @pl.when(step == 0)
    def _():
        values = hidden_ref[...]
        inverse = lax.rsqrt(jnp.mean(values * values, axis=-1, keepdims=True) + EPSILON)
        scaled = values * inverse
        grad = first_ref[...].astype(jnp.float32) + second_ref[...].astype(jnp.float32)
        grad = grad * gain_ref[1:, :]
        projection = jnp.mean(grad * scaled, axis=-1, keepdims=True)
        total = e_ref[...].astype(jnp.float32) + inverse * (grad - scaled * projection)
        dh[...] = total
        dz[...] = total.astype(jnp.bfloat16)

    result = dot_nn(dz[...], weight_ref[...]).astype(jnp.bfloat16)
    for index in range(parts):

        @pl.when(step == index)
        def _():
            columns = slice(index * tile, (index + 1) * tile)
            dh_ref[...] = dh[:, columns]
            dz_ref[...] = dz[:, columns]
            refs[2 + index][...] = result


def residual_gradient(e, hidden_res, first, second, gain, weight, parts):
    rows, depth = e.shape
    tile = depth // parts
    whole = pl.BlockSpec((rows, depth), lambda t: (0, 0))
    column = pl.BlockSpec((rows, tile), lambda t: (0, t))
    result = pl.pallas_call(
        functools.partial(residual_kernel, parts),
        grid=(parts,),
        in_specs=[
            whole,
            whole,
            whole,
            whole,
            pl.BlockSpec((2, depth), lambda t: (0, 0)),
            pl.BlockSpec((depth, tile), lambda t: (0, t)),
        ],
        out_specs=[column, column] + [pl.BlockSpec((rows, tile), lambda t: (0, 0))] * parts,
        out_shape=[
            jax.ShapeDtypeStruct((rows, depth), jnp.float32),
            jax.ShapeDtypeStruct((rows, depth), jnp.bfloat16),
            *[jax.ShapeDtypeStruct((rows, tile), jnp.bfloat16)] * parts,
        ],
        scratch_shapes=[
            pltpu.VMEM((rows, depth), jnp.float32),
            pltpu.VMEM((rows, depth), jnp.bfloat16),
        ],
        compiler_params=parameters(),
        cost_estimate=SMALL_COST,
        name="residual_gradient",
    )(e, hidden_res, first, second, gain, weight)
    return result[0], result[1], list(result[2:])


def tie(value, *others):
    return lax.optimization_barrier((value, others))[0]


def together(*values):
    return lax.optimization_barrier(values)


def add(first, second):
    return (first.astype(jnp.float32) + second.astype(jnp.float32)).astype(jnp.bfloat16)


class Mover:
    def __init__(self):
        self.dp_count = lax.axis_size("dp")
        self.ring = lax.axis_size("tensor")
        self.steps = []
        step = 2
        while step < self.dp_count:
            self.steps.append(step)
            step *= 2

    def swap(self, value, step):
        return lax.ppermute(value, "dp", [(i, i ^ step) for i in range(self.dp_count)])

    def gather(self, shard):
        return lax.all_gather(shard, "dp", axis=0, tiled=True)


    def send(self, pieces, level):
        orders = (self.steps[::-1], self.steps[:1] + self.steps[:0:-1])
        return [self.swap(piece, order[level]) for piece, order in zip(pieces, orders)]

    def begin(self, pieces):
        moved = self.send([pieces[1], pieces[3]], 0)
        return [[pieces[0], moved[0]], [pieces[2], moved[1]]]

    def fold(self, sums, level=1):
        return fold(sums, sums[0][0][0].shape[0] >> level)

    def advance(self, sums, folded):
        level = 1
        while True:
            moved = self.send(folded, level)
            level += 1
            if level == len(self.steps):
                return sums, moved
            rows = moved[0].shape[0] // len(sums)
            sums = [
                [
                    terms + [part[index * rows : (index + 1) * rows]]
                    for terms, part in zip(pair, moved)
                ]
                for index, pair in enumerate(sums)
            ]
            folded = self.fold(sums, level)

    def hop(self, value, shift=1):
        return lax.ppermute(
            value, "tensor", [(i, (i + shift) % self.ring) for i in range(self.ring)]
        )

    def spread(self, value):
        ring = self.ring
        return [value] + [
            lax.ppermute(value, "tensor", [(i, (i - j) % ring) for i in range(ring)])
            for j in range(1, ring)
        ]

    def collect(self, parts):
        ring = self.ring
        total = parts[0]
        for j in range(1, ring):
            moved = lax.ppermute(
                parts[j].astype(jnp.bfloat16), "tensor", [(i, (i + j) % ring) for i in range(ring)]
            )
            total = total + moved.astype(jnp.float32)
        return total

    def exchange(self, parts):
        ring = self.ring
        return [parts[0]] + [
            lax.ppermute(parts[j], "tensor", [(i, (i + j) % ring) for i in range(ring)])
            for j in range(1, ring)
        ]


def totals_of(sums, moved):
    rows = moved[0].shape[0] // len(sums)
    result = []
    for index, pair in enumerate(sums):
        halves = []
        for terms, last in zip(pair, moved):
            total = last[index * rows : (index + 1) * rows].astype(jnp.float32)
            for term in terms:
                total = total + term[:rows].astype(jnp.float32)
            halves.append(total)
        result.append(jnp.concatenate(halves, axis=1))
    return result


def back_norm(grad_normed, scaled, inverse, scale_row):
    grad_scaled = grad_normed * scale_row
    projection = jnp.mean(grad_scaled * scaled, axis=-1, keepdims=True)
    return inverse * (grad_scaled - scaled * projection)


def per_device(
    tokens,
    seq_lengths,
    attention_gain,
    query_matrix,
    key_matrix,
    value_matrix,
    output_weight,
    feedforward_gain,
    gate_weight,
    up_weight,
    down_weight,
    cotangent,
):
    mover = Mover()
    dp_count = mover.dp_count
    ring = mover.ring
    dp_place = lax.axis_index("dp").astype(jnp.int32).reshape(1)
    ring_place = lax.axis_index("tensor")
    place = ring_place.astype(jnp.int32).reshape(1)
    _, local_rows, model_width = tokens.shape
    complete_rows = local_rows * ring
    hidden = gate_weight.shape[1]
    groups = key_matrix.shape[1] // HEAD_SIZE
    joint_width = groups * GROUP_WIDTH
    f32 = jnp.float32
    b16 = jnp.bfloat16

    doc_ids, positions = layout(seq_lengths, complete_rows)
    row_index = jnp.arange(complete_rows, dtype=jnp.int32)
    doc_ids = jnp.where(doc_ids[0] < PIECES, doc_ids[0], PIECES + row_index)

    def to_relative(values):
        view = values.reshape((ring, local_rows) + values.shape[1:])
        return jnp.roll(view, -(ring_place + 1), axis=0)[::-1].reshape(values.shape)

    doc_ids = to_relative(doc_ids)
    cosine, sine = rope_tables(to_relative(positions[0]), HEAD_SIZE)
    cosine_table = jnp.tile(cosine, (1, 128 // cosine.shape[1]))
    sine_table = jnp.tile(jnp.concatenate([-sine, sine], axis=1), (1, 128 // HEAD_SIZE))

    own_gains = jnp.pad(jnp.stack([attention_gain, feedforward_gain]), ((0, 126), (0, 0)))
    joint_matrix, packed = pack(query_matrix, key_matrix, value_matrix, own_gains, groups)
    joint_full = mover.gather(packed)
    output_parts = mover.spread(output_weight.T)
    up_shard = jnp.pad(
        jnp.concatenate([gate_weight, up_weight], axis=1), ((0, 0), (model_width, 0))
    )
    output_parts, cosine_table, sine_table, doc_ids, up_shard, down_shard = together(
        output_parts, cosine_table, sine_table, doc_ids, up_shard, down_weight.T
    )
    local_tokens = tokens[0]
    token_chunks = [local_tokens, mover.hop(local_tokens)]
    up_shard = join(output_parts, up_shard)
    up_full = mover.gather(up_shard)
    down_full = mover.gather(tie(down_shard, up_shard))
    gains = joint_full[:, joint_width : joint_width + 2].T.astype(f32)

    def projection(kept, index):
        return project(
            token_chunks[index],
            gains,
            joint_full,
            cosine_table,
            sine_table,
            kept,
            index,
            ring,
            groups,
        )

    kept = projection(None, 0)
    for j in range(1, ring):
        token_chunks[j], kept, gains = together(token_chunks[j], kept, gains)
        if j + 1 < ring:
            token_chunks.append(mover.hop(token_chunks[j]))
        else:
            local_cotangent = tie(cotangent[0], token_chunks[j])
            moved = mover.hop(local_cotangent)
        kept = projection(kept, j)
    normed_one, joint = kept
    attended, totals = attention_forward(joint, doc_ids, place, ring, groups)
    moved, attended = together(moved, attended)
    cotangent_chunks = [local_cotangent, moved]
    attended_parts = [attended]
    while len(attended_parts) < ring:
        part = mover.hop(attended_parts[-1], -1)
        if len(attended_parts) == ring - 1:
            partial, attended_local = heads_product(
                tie(attended_parts, attended_parts[-1]), up_full, token_chunks
            )
            part, partial, attended_local = together(part, partial, attended_local)
        attended_parts.append(part)
    moved, last = together(moved, attended_parts[-1])

    pairs = ring // 2
    moved = mover.hop(moved)
    hidden_res, normed_two, attended_last = after_attention(partial, last, up_full, gains, ring)
    upward = up_chunk(normed_two, up_full, None, 0, pairs)
    downward = None
    grads = []

    def chunks_of(pair):
        return [cotangent_chunks[(2 * pair + i) % ring] for i in (1, 2)]

    def lower(pair, kept):
        return down_chunk(
            chunks_of(pair), upward[0], upward[1], down_full, up_full, kept, pair, pairs
        )

    for j in range(2, ring):
        if j > 2:
            moved = mover.hop(moved)
            if j % 2:
                downward, parts = lower((j - 3) // 2, downward)
                grads.extend(parts)
            else:
                upward = up_chunk(normed_two, up_full, upward, j // 2 - 1, pairs)
        moved, upward, downward, grads = together(moved, upward, downward, grads)
        cotangent_chunks.append(moved)

    def weights(xs, ys, received=None):
        return weight_product([(xs, ys)], dp_place, dp_count, received)

    ordered = cotangent_chunks[1:] + cotangent_chunks[:1]
    total = grads[0]
    moved = mover.hop(total)
    upward = up_chunk(tie(normed_two, total), up_full, upward, pairs - 1, pairs)
    product = upward[2]
    down_part = weights(ordered, [product])
    moved, upward, down_part = together(moved, upward, down_part)
    down_part = mover.swap(down_part, 1)
    for j in range(2, ring):
        total = add(moved, grads[j - 1])
        moved = mover.hop(total)
        if j == 2:
            downward, parts = lower(pairs - 1, tie(downward, total))
            grads.extend(parts)
            moved, downward, grads = together(moved, downward, grads)
            grad_gate, grad_up = downward
        if j == 3:
            gate_part = weights([tie(normed_two, total)], [grad_gate])
            branch = transposed_product(
                [tie(product, gate_part)], down_full, 0, ring // 2, 0, 2
            )
            down_part = weights(tie(ordered, branch), [product], down_part)
            moved, gate_part, branch, down_part = together(moved, gate_part, branch, down_part)
    gate_part = mover.swap(gate_part, 1)
    down_part = mover.begin(down_part)
    grad_hidden, grad_branch, grad_parts = residual_gradient(
        local_cotangent, hidden_res, moved, grads[-1], gains, up_full, ring
    )
    grad_hidden, grad_branch, grad_parts, gate_part = together(
        grad_hidden, grad_branch, grad_parts, gate_part
    )

    grad_parts = mover.exchange(grad_parts)
    output_part = weights([grad_branch], [attended_local, attended_last])
    gate_part = weights([tie(normed_two, output_part)], [grad_gate], gate_part)
    grad_parts, output_part, gate_part, down_part = together(
        grad_parts, output_part, gate_part, down_part
    )
    grad_joint = []
    sent = 0
    folded = []
    moved = branch[0]
    for group in range(groups):
        moved = mover.hop(moved)
        sent += 1
        if group == 0:
            output_part = mover.swap(output_part, 1)
            gate_part = mover.begin(gate_part)
        else:
            output_part = mover.begin(output_part)
        grad_joint.append(
            attention_backward(
                joint,
                attended,
                tie(grad_parts, grad_joint),
                totals,
                doc_ids,
                cosine_table,
                sine_table,
                place,
                group,
            )
        )
        if group == 0:
            output_part = weights(
                [tie(grad_branch, grad_joint)], [attended_local, attended_last], output_part
            )
        if group + 1 == groups:
            grads = transposed_product(grad_joint, joint_full, 0, ring)
            folded = mover.fold(tie([gate_part, down_part], grads))
        moved, grad_joint, grads, gate_part, output_part, folded = together(
            moved, grad_joint, grads, gate_part, output_part, folded
        )
        if group + 1 < groups:
            moved = add(moved, branch[sent])
    if groups == 1:
        output_part = mover.begin(output_part)
    branch_moved = moved
    moved = grads[0]

    def last_weights(total, received):
        return weight_product(
            [([tie(normed_two, total)], [grad_up]), ([normed_one], grad_joint)],
            dp_place,
            dp_count,
            received,
        )

    for j in range(1, ring):
        total = grads[1] if j == 1 else add(moved, grads[j])
        moved = mover.hop(total)
        if j == 1:
            first_parts = mover.advance([gate_part, down_part], folded)
            folded = mover.fold(tie([output_part], total))
            last_part = last_weights(folded, None)
            branch = branch + transposed_product(
                [tie(product, last_part)], down_full, 0, ring // 2, 1, 2
            )
            next_branch = add(branch_moved, branch[sent])
            moved, last_part, branch, folded, first_parts, next_branch = together(
                moved, last_part, branch, folded, first_parts, next_branch
            )
        if j == 2:
            output_part = mover.advance([output_part], folded)
            last_part = last_weights(total, mover.swap(last_part, 1))
            gate_out, down_out = totals_of(*first_parts)
            down_out = down_out.T
            moved, last_part, output_part, gate_out, down_out = together(
                moved, last_part, output_part, gate_out, down_out
            )
        if j == 3:
            last_part = mover.begin(last_part)
            branch_moved = mover.hop(tie(next_branch, total))
            sent += 1
            output_out = jnp.split(totals_of(*output_part)[0], ring, axis=1)
            moved, last_part, output_out = together(moved, last_part, output_out)
    folded, output_out = together(mover.fold([last_part]), output_out)
    last_part = mover.advance([last_part], folded)
    output_out = mover.collect(output_out[:-1] + [tie(output_out[-1], last_part)]).T
    scaled_one, inverse_one = norm_rows(local_tokens.astype(f32))
    local_one = moved.astype(f32) + grads[0].astype(f32)
    input_gradient = grad_hidden + back_norm(local_one, scaled_one, inverse_one, gains[:1])
    branch_moved = tie(branch_moved, last_part)
    for j in range(sent, ring - 1):
        branch_moved = mover.hop(add(branch_moved, branch[j]))
    block_output = (
        hidden_res + (branch_moved.astype(f32) + branch[-1].astype(f32))
    ).astype(b16)
    last_out = totals_of(*last_part)[0]
    up_out, joint_out = last_out[:, :hidden], last_out[:, hidden:]

    sums = jnp.stack(
        [
            jnp.sum(joint_out * joint_matrix.astype(f32), axis=1) / attention_gain.astype(f32),
            jnp.sum(gate_out * gate_weight.astype(f32) + up_out * up_weight.astype(f32), axis=1)
            / feedforward_gain.astype(f32),
        ]
    )
    gain_out = sums
    for shift in range(1, ring):
        gain_out = gain_out + lax.ppermute(
            sums, "tensor", [(i, (i + shift) % ring) for i in range(ring)]
        )

    def ungrouped(first, width):
        return jnp.concatenate(
            [
                joint_out[:, g * GROUP_WIDTH + first : g * GROUP_WIDTH + first + width]
                for g in range(groups)
            ],
            axis=1,
        )

    return (
        block_output[None],
        input_gradient[None],
        gain_out[0],
        ungrouped(0, GROUP_QUERY),
        ungrouped(GROUP_QUERY, HEAD_SIZE),
        ungrouped(GROUP_QUERY + HEAD_SIZE, HEAD_SIZE),
        output_out,
        gain_out[1],
        gate_out,
        up_out,
        down_out,
    )


def solution(mesh):
    return jax.shard_map(
        per_device,
        mesh=mesh,
        in_specs=(
            P("dp", "tensor", None),
            P("dp", None),
            P("dp"),
            P("dp", "tensor"),
            P("dp", "tensor"),
            P("dp", "tensor"),
            P("tensor", "dp"),
            P("dp"),
            P("dp", "tensor"),
            P("dp", "tensor"),
            P("tensor", "dp"),
            P("dp", "tensor", None),
        ),
        out_specs=(
            P("dp", "tensor", None),
            P("dp", "tensor", None),
            P("dp"),
            P("dp", "tensor"),
            P("dp", "tensor"),
            P("dp", "tensor"),
            P("tensor", "dp"),
            P("dp"),
            P("dp", "tensor"),
            P("dp", "tensor"),
            P("tensor", "dp"),
        ),
        check_vma=False,
    )
```

```python
import functools
import math

import jax
import jax.numpy as jnp
from jax import lax
from jax.experimental import pallas as pl
from jax.experimental.pallas import tpu as pltpu
from jax.sharding import PartitionSpec as P

QUERY_HEADS = 32
KEY_VALUE_HEADS = 8
HEAD_SIZE = 64
PIECES = 4


EPSILON = 1e-05
ROPE_BASE = 500000.0
NEGATIVE = -1e30
GROUP_QUERY = QUERY_HEADS // KEY_VALUE_HEADS * HEAD_SIZE
GROUP_WIDTH = GROUP_QUERY + 2 * HEAD_SIZE
KERNEL_VMEM = 60 * 1024 * 1024
SMALL_COST = pl.CostEstimate(flops=1, bytes_accessed=1, transcendentals=0)


def layout(lengths, complete_rows):
    doc_ends = jnp.cumsum(lengths, axis=-1)
    row_index = jnp.arange(complete_rows, dtype=jnp.int32)
    piece_count = lengths.shape[-1]
    doc_ids = jnp.sum((row_index[None, :, None] >= doc_ends[:, None, :]).astype(jnp.int32), axis=2)
    starts = doc_ends - lengths
    chosen = doc_ids[:, :, None] == jnp.arange(piece_count, dtype=jnp.int32)[None, None, :]
    doc_begin = jnp.sum(jnp.where(chosen, starts[:, None, :], 0), axis=2) + jnp.where(
        doc_ids == piece_count, doc_ends[:, -1:], 0
    )
    return (doc_ids, row_index[None, :] - doc_begin)


def rope_tables(positions, head_dim):
    half_dim = head_dim // 2
    frequency = ROPE_BASE ** (-(jnp.arange(half_dim, dtype=jnp.float32) * (2.0 / head_dim)))
    angles = positions.astype(jnp.float32)[..., None] * frequency
    return (jnp.cos(angles), jnp.sin(angles))


def norm_rows(values):
    inverse = lax.rsqrt(jnp.mean(values * values, axis=-1, keepdims=True) + EPSILON)
    return (values * inverse, inverse)


def dot_nt(left, right):
    return lax.dot_general(
        left, right, (((1,), (1,)), ((), ())), preferred_element_type=jnp.float32
    )


def dot_nn(left, right):
    return jnp.dot(left, right, preferred_element_type=jnp.float32)


def dot_tn(left, right):
    return lax.dot_general(
        left, right, (((0,), (0,)), ((), ())), preferred_element_type=jnp.float32
    )


def tile_of(size, limit=512):
    tile = limit
    while size % tile:
        tile //= 2
    return tile


def parameters():
    return pltpu.CompilerParams(vmem_limit_bytes=KERNEL_VMEM)


def swap_halves(values):
    lane = lax.broadcasted_iota(jnp.int32, values.shape, 1)
    half = HEAD_SIZE // 2
    return jnp.where(
        lane % HEAD_SIZE < half, pltpu.roll(values, 128 - half, 1), pltpu.roll(values, half, 1)
    )


def turned(values, cosine, sine, start):
    result = values * cosine + swap_halves(values) * sine
    rotated = GROUP_WIDTH - HEAD_SIZE
    if start + 128 <= rotated:
        return result
    lane = lax.broadcasted_iota(jnp.int32, values.shape, 1)
    return jnp.where(lane < rotated - start, result, values)


def project_kernel(x_ref, gain_ref, weight_ref, cos_ref, sin_ref, *refs):
    normed_ref, joint_ref = refs[-2:]

    @pl.when(pl.program_id(0) == 0)
    def _():
        values = x_ref[...].astype(jnp.float32)
        inverse = lax.rsqrt(jnp.mean(values * values, axis=-1, keepdims=True) + EPSILON)
        normed_ref[...] = (values * inverse * gain_ref[:1, :]).astype(jnp.bfloat16)

    product = dot_nn(normed_ref[...], weight_ref[...])
    for start in range(0, GROUP_WIDTH, 128):
        part = turned(product[:, start : start + 128], cos_ref[...], sin_ref[...], start)
        if start < GROUP_QUERY:
            part = part * HEAD_SIZE ** (-0.5)
        joint_ref[:, start : start + 128] = part.astype(jnp.bfloat16)


def project(x, gain, weight, cosine, sine, kept, index, count, groups):
    rows, depth = x.shape
    specs = [
        pl.BlockSpec((rows, depth), lambda g: (0, 0)),
        pl.BlockSpec((2, depth), lambda g: (0, 0)),
        pl.BlockSpec((depth, GROUP_WIDTH), lambda g: (0, g)),
        pl.BlockSpec((rows, 128), lambda g: (index, 0)),
        pl.BlockSpec((rows, 128), lambda g: (index, 0)),
    ]
    operands = [x, gain, weight, cosine, sine]
    aliases = {}
    if kept is not None:
        specs.extend([pl.BlockSpec(memory_space=pl.ANY)] * 2)
        aliases = {len(operands) + i: i for i in range(2)}
        operands.extend(kept)
    return pl.pallas_call(
        project_kernel,
        grid=(groups,),
        in_specs=specs,
        out_specs=[
            pl.BlockSpec((rows, depth), lambda g: (index, 0)),
            pl.BlockSpec((rows, GROUP_WIDTH), lambda g: (index, g)),
        ],
        out_shape=[
            jax.ShapeDtypeStruct((rows * count, depth), jnp.bfloat16),
            jax.ShapeDtypeStruct((rows * count, GROUP_WIDTH * groups), jnp.bfloat16),
        ],
        input_output_aliases=aliases,
        compiler_params=parameters(),
        cost_estimate=SMALL_COST,
        name="project",
    )(*operands)


def ring_offset(place, chunk, count, rows):
    return pl.multiple_of(lax.rem(place - chunk + count, count) * rows, rows)


def stack_heads(target, source):
    rows, width = source.shape
    for head in range(width // HEAD_SIZE):
        target[head * rows : (head + 1) * rows, :] = source[
            :, head * HEAD_SIZE : (head + 1) * HEAD_SIZE
        ]


def fill_bias(bias, key_docs, query_docs, earlier):
    rows = key_docs.shape[0]
    row_index = lax.broadcasted_iota(jnp.int32, (rows, rows), 0)
    column_index = lax.broadcasted_iota(jnp.int32, (rows, rows), 1)
    same = (key_docs == query_docs) & ((row_index <= column_index) | earlier)
    values = jnp.where(same, 0.0, NEGATIVE)
    for first in range(0, bias.shape[1], rows):
        bias[:, first : first + rows] = values


def forward_kernel(
    count,
    place_ref,
    own_ref,
    all_ref,
    docq_ref,
    dock_ref,
    o_ref,
    lse_ref,
    bias,
    queries,
    values_all,
    mixed,
):
    chunk = pl.program_id(1)
    place = place_ref[0]
    rows = own_ref.shape[0]
    heads = GROUP_QUERY // HEAD_SIZE
    stack_heads(queries, own_ref.at[:, :GROUP_QUERY])

    @pl.when(chunk == 0)
    def _():
        values = all_ref[:, GROUP_QUERY:].astype(jnp.float32)
        values_all[...] = values.T[HEAD_SIZE:].astype(jnp.bfloat16)

    mixed[...] = jnp.zeros_like(mixed)

    def block(j, carry):
        peaks, total = carry
        offset = ring_offset(place, j, count, rows)
        piece = pl.ds(offset, rows)
        fill_bias(bias, dock_ref[piece, :], docq_ref[...], j < chunk)
        keys = all_ref[piece, GROUP_QUERY : GROUP_QUERY + HEAD_SIZE]
        scores = dot_nt(keys, queries[...]) + bias[...]
        higher = jnp.maximum(peaks, jnp.max(scores, axis=0, keepdims=True))
        probs = jnp.exp(scores - higher)
        scale = jnp.exp(peaks - higher)
        mixed[...] = mixed[...] * scale + dot_nn(
            values_all[:, piece], probs.astype(jnp.bfloat16)
        )
        return higher, total * scale + jnp.sum(probs, axis=0, keepdims=True)

    peaks, total = lax.fori_loop(
        0,
        chunk + 1,
        block,
        (
            jnp.full((1, heads * rows), NEGATIVE, jnp.float32),
            jnp.zeros((1, heads * rows), jnp.float32),
        ),
    )
    lse_ref[:1, :] = peaks + jnp.log(total)
    result = mixed[...] / total
    for head in range(0, heads, 2):
        pair = jnp.concatenate(
            [result[:, (head + i) * rows : (head + i + 1) * rows] for i in range(2)], axis=0
        )
        o_ref[:, head * HEAD_SIZE : (head + 2) * HEAD_SIZE] = pair.T.astype(jnp.bfloat16)


def attention_forward(joint, docs, place, count, groups):
    total_rows = joint.shape[0]
    rows = total_rows // count
    stacked = rows * GROUP_QUERY // HEAD_SIZE

    def block(c, place_ref):
        return lax.rem(place_ref[0] - c + count, count)

    spec = pltpu.PrefetchScalarGridSpec(
        num_scalar_prefetch=1,
        grid=(groups, count),
        in_specs=[
            pl.BlockSpec((rows, GROUP_WIDTH), lambda g, c, p: (block(c, p), g)),
            pl.BlockSpec((total_rows, GROUP_WIDTH), lambda g, c, p: (0, g)),
            pl.BlockSpec((1, rows), lambda g, c, p: (0, block(c, p))),
            pl.BlockSpec((total_rows, 1), lambda g, c, p: (0, 0)),
        ],
        out_specs=[
            pl.BlockSpec((rows, GROUP_QUERY), lambda g, c, p: (block(c, p), g)),
            pl.BlockSpec((8, stacked), lambda g, c, p: (g, block(c, p))),
        ],
        scratch_shapes=[
            pltpu.VMEM((rows, stacked), jnp.float32),
            pltpu.VMEM((stacked, HEAD_SIZE), jnp.bfloat16),
            pltpu.VMEM((HEAD_SIZE, total_rows), jnp.bfloat16),
            pltpu.VMEM((HEAD_SIZE, stacked), jnp.float32),
        ],
    )
    return pl.pallas_call(
        functools.partial(forward_kernel, count),
        grid_spec=spec,
        out_shape=[
            jax.ShapeDtypeStruct((total_rows, GROUP_QUERY * groups), jnp.bfloat16),
            jax.ShapeDtypeStruct((8 * groups, stacked * count), jnp.float32),
        ],
        compiler_params=parameters(),
        cost_estimate=SMALL_COST,
        name="attend",
    )(place, joint, joint, docs[None, :], docs[:, None])


def backward_kernel(count, place_ref, *refs):
    own_ref, all_ref, o_ref = refs[:3]
    lse_ref, docq_ref, dock_ref, cos_ref, sin_ref = refs[3 + count : 8 + count]
    out_ref, bias, queries, grads, keys_all, values_all, sum_q, sum_k, sum_v = refs[8 + count :]
    chunk = pl.program_id(0)
    place = place_ref[0]
    rows = own_ref.shape[0]
    heads = GROUP_QUERY // HEAD_SIZE
    stack_heads(queries, own_ref.at[:, :GROUP_QUERY])
    for index in range(count):

        @pl.when(lax.rem(place - chunk + count, count) == index)
        def _():
            stack_heads(grads, refs[3 + index])

    @pl.when(chunk == 0)
    def _():
        keys_all[...] = all_ref[:, GROUP_QUERY : GROUP_QUERY + HEAD_SIZE]
        values_all[...] = all_ref[:, GROUP_QUERY + HEAD_SIZE :]
        sum_k[...] = jnp.zeros_like(sum_k)
        sum_v[...] = jnp.zeros_like(sum_v)

    sum_q[...] = jnp.zeros_like(sum_q)
    ones = jnp.ones((8, HEAD_SIZE), jnp.bfloat16)
    inner = []
    for head in range(heads):
        attended = o_ref[:, head * HEAD_SIZE : (head + 1) * HEAD_SIZE].astype(jnp.float32)
        both = attended * grads[head * rows : (head + 1) * rows, :].astype(jnp.float32)
        high = both.astype(jnp.bfloat16)
        low = (both - high.astype(jnp.float32)).astype(jnp.bfloat16)
        inner.append((dot_nt(ones, high) + dot_nt(ones, low))[:1])
    inner = jnp.concatenate(inner, axis=1)

    def block(j, carry):
        offset = ring_offset(place, j, count, rows)
        piece = pl.ds(offset, rows)
        fill_bias(bias, dock_ref[piece, :], docq_ref[...], j < chunk)
        probs = jnp.exp(dot_nt(keys_all[piece, :], queries[...]) + bias[...] - lse_ref[:1, :])
        grad_probs = dot_nt(values_all[piece, :], grads[...])
        grad_scores = (probs * (grad_probs - inner)).astype(jnp.bfloat16)
        sum_v[piece, :] += dot_nn(probs.astype(jnp.bfloat16), grads[...])
        sum_k[piece, :] += dot_nn(grad_scores, queries[...])
        sum_q[...] += dot_tn(grad_scores, keys_all[piece, :])
        return carry

    lax.fori_loop(0, chunk + 1, block, 0)
    own = pl.ds(ring_offset(place, chunk, count, rows), rows)
    for first in range(0, heads, 2):
        start = first * HEAD_SIZE
        part = jnp.concatenate(
            [sum_q[(first + i) * rows : (first + i + 1) * rows, :] for i in range(2)], axis=1
        )
        part = turned(part, cos_ref[own, :], -sin_ref[own, :], start)
        out_ref[own, start : start + 128] = (part * HEAD_SIZE ** (-0.5)).astype(jnp.bfloat16)

    @pl.when(chunk == count - 1)
    def _():
        part = jnp.concatenate([sum_k[...], sum_v[...]], axis=1)
        part = turned(part, cos_ref[...], -sin_ref[...], GROUP_QUERY)
        out_ref[:, GROUP_QUERY:] = part.astype(jnp.bfloat16)


def attention_backward(joint, attended, grads, lse, docs, cosine, sine, place, group):
    count = len(grads)
    total_rows = joint.shape[0]
    rows = total_rows // count
    stacked = rows * GROUP_QUERY // HEAD_SIZE

    def block(c, place_ref):
        return lax.rem(place_ref[0] - c + count, count)

    table = pl.BlockSpec((total_rows, 128), lambda c, p: (0, 0))
    spec = pltpu.PrefetchScalarGridSpec(
        num_scalar_prefetch=1,
        grid=(count,),
        in_specs=[
            pl.BlockSpec((rows, GROUP_WIDTH), lambda c, p: (block(c, p), group)),
            pl.BlockSpec((total_rows, GROUP_WIDTH), lambda c, p: (0, group)),
            pl.BlockSpec((rows, GROUP_QUERY), lambda c, p: (block(c, p), group)),
            *[pl.BlockSpec((rows, GROUP_QUERY), lambda c, p: (0, group))] * count,
            pl.BlockSpec((8, stacked), lambda c, p: (group, block(c, p))),
            pl.BlockSpec((1, rows), lambda c, p: (0, block(c, p))),
            pl.BlockSpec((total_rows, 1), lambda c, p: (0, 0)),
            table,
            table,
        ],
        out_specs=pl.BlockSpec((total_rows, GROUP_WIDTH), lambda c, p: (0, 0)),
        scratch_shapes=[
            pltpu.VMEM((rows, stacked), jnp.float32),
            *[pltpu.VMEM((stacked, HEAD_SIZE), jnp.bfloat16)] * 2,
            *[pltpu.VMEM((total_rows, HEAD_SIZE), jnp.bfloat16)] * 2,
            pltpu.VMEM((stacked, HEAD_SIZE), jnp.float32),
            *[pltpu.VMEM((total_rows, HEAD_SIZE), jnp.float32)] * 2,
        ],
    )
    return pl.pallas_call(
        functools.partial(backward_kernel, count),
        grid_spec=spec,
        out_shape=jax.ShapeDtypeStruct((total_rows, GROUP_WIDTH), jnp.bfloat16),
        compiler_params=parameters(),
        cost_estimate=SMALL_COST,
        name="attend_back",
    )(
        place,
        joint,
        joint,
        attended,
        *grads,
        lse,
        docs[None, :],
        docs[:, None],
        cosine,
        sine,
    )


def pack_kernel(groups, query_ref, key_ref, value_ref, gain_ref, joint_ref, out_ref):
    for g in range(groups):
        start = g * GROUP_WIDTH
        columns = slice(g * HEAD_SIZE, (g + 1) * HEAD_SIZE)
        joint_ref[:, start : start + GROUP_QUERY] = query_ref[
            :, g * GROUP_QUERY : (g + 1) * GROUP_QUERY
        ]
        joint_ref[:, start + GROUP_QUERY : start + GROUP_WIDTH] = jnp.concatenate(
            [key_ref[:, columns], value_ref[:, columns]], axis=1
        )
    width = groups * GROUP_WIDTH
    out_ref[:, :width] = joint_ref[...]
    out_ref[:, width:] = gain_ref[...].astype(jnp.float32).T.astype(jnp.bfloat16)


def pack(query, key, value, gains, groups):
    rows = query.shape[0]
    width = groups * GROUP_WIDTH
    return pl.pallas_call(
        functools.partial(pack_kernel, groups),
        out_shape=[
            jax.ShapeDtypeStruct((rows, width), jnp.bfloat16),
            jax.ShapeDtypeStruct((rows, width + 128), jnp.bfloat16),
        ],
        compiler_params=parameters(),
        cost_estimate=SMALL_COST,
        name="pack",
    )(query, key, value, gains)


def join_kernel(*refs):
    place = 0
    for ref in refs[:-2]:
        size = ref.shape[1]
        refs[-1][:, place : place + size] = ref[...]
        place += size


def join(parts, rest):
    rows = rest.shape[0]
    width = sum(part.shape[1] for part in parts)
    return pl.pallas_call(
        join_kernel,
        grid=(1,),
        in_specs=[pl.BlockSpec(part.shape, lambda i: (0, 0)) for part in parts]
        + [pl.BlockSpec(memory_space=pl.ANY)],
        out_specs=pl.BlockSpec((rows, width), lambda i: (0, 0)),
        out_shape=jax.ShapeDtypeStruct(rest.shape, rest.dtype),
        input_output_aliases={len(parts): 0},
        compiler_params=parameters(),
        cost_estimate=SMALL_COST,
        name="join",
    )(*parts, rest)


def transposed_kernel(count, parts, *refs):
    total = dot_nt(refs[0][...], refs[count][...])
    for index in range(1, count):
        total += dot_nt(refs[index][...], refs[count + index][...])
    rows = total.shape[0] // parts
    for index in range(parts):
        refs[2 * count + index][...] = total[index * rows : (index + 1) * rows].astype(
            jnp.bfloat16
        )


def transposed_product(xs, weight, column, parts, block=0, blocks=1):
    rows, depth = xs[0].shape
    rows //= blocks
    width = weight.shape[0]
    tile = tile_of(width)
    specs = [pl.BlockSpec((rows, depth), lambda t: (block, 0))] * len(xs)
    for index in range(len(xs)):
        specs.append(pl.BlockSpec((tile, depth), lambda t, index=index: (t, column + index)))
    part = (rows // parts, width)
    return pl.pallas_call(
        functools.partial(transposed_kernel, len(xs), parts),
        grid=(width // tile,),
        in_specs=specs,
        out_specs=[pl.BlockSpec((part[0], tile), lambda t: (0, t))] * parts,
        out_shape=[jax.ShapeDtypeStruct(part, jnp.bfloat16)] * parts,
        compiler_params=parameters(),
        cost_estimate=SMALL_COST,
        name="transposed",
    )(*xs, *[weight] * len(xs))


def heads_kernel(count, *refs):
    parts = refs[:count]
    weight_ref = refs[count]
    tokens = refs[count + 1 : -2]
    out_ref, local_ref = refs[-2:]
    step = pl.program_id(0)
    width = parts[0].shape[1]

    @pl.when(step == 0)
    def _():
        for j in range(count):
            local_ref[:, j * width : (j + 1) * width] = parts[j][...]

    for j in range(count):
        term = dot_nt(parts[j][...], weight_ref[:, j * width : (j + 1) * width])
        if j == 0:
            out_ref[...] = term
        else:
            out_ref[...] += term
    for index in range(len(tokens)):

        @pl.when(step == index)
        def _():
            out_ref[...] += tokens[index][...].astype(jnp.float32)


def heads_product(parts, weight, tokens):
    blocks = len(tokens)
    rows, width = tokens[0].shape
    depth = parts[0].shape[1]
    specs = [
        pl.BlockSpec((rows, depth), lambda i, j=j: (lax.rem(i + j, blocks), 0))
        for j in range(len(parts))
    ]
    whole = pl.BlockSpec((rows, width), lambda i: (0, 0), pipeline_mode=pl.Buffered(1))
    return pl.pallas_call(
        functools.partial(heads_kernel, len(parts)),
        grid=(blocks,),
        in_specs=[
            *specs,
            pl.BlockSpec(
                (width, depth * len(parts)), lambda i: (0, 0), pipeline_mode=pl.Buffered(1)
            ),
            *[whole] * blocks,
        ],
        out_specs=[
            pl.BlockSpec((rows, width), lambda i: (i, 0)),
            pl.BlockSpec((rows, depth * len(parts)), lambda i: (0, 0)),
        ],
        out_shape=[
            jax.ShapeDtypeStruct((rows * blocks, width), jnp.float32),
            jax.ShapeDtypeStruct((rows, depth * len(parts)), jnp.bfloat16),
        ],
        compiler_params=parameters(),
        cost_estimate=SMALL_COST,
        name="heads_product",
    )(*parts, weight, *tokens)


def attended_kernel(
    partial_ref, last_ref, weight_ref, gain_ref, hidden_ref, normed_ref, local_ref
):
    values = partial_ref[...] + dot_nt(last_ref[...], weight_ref[...])

    @pl.when(pl.program_id(0) == 0)
    def _():
        hidden_ref[...] = values
        local_ref[...] = last_ref[...]

    inverse = lax.rsqrt(jnp.mean(values * values, axis=-1, keepdims=True) + EPSILON)
    normed_ref[...] = (values * inverse * gain_ref[1:, :]).astype(jnp.bfloat16)


def after_attention(partial, last, weight, gain, count):
    total_rows, width = partial.shape
    rows = total_rows // count
    depth = last.shape[1]
    return pl.pallas_call(
        attended_kernel,
        grid=(count,),
        in_specs=[
            pl.BlockSpec((rows, width), lambda i: (i, 0)),
            pl.BlockSpec((rows, depth), lambda i: (lax.rem(i + count - 1, count), 0)),
            pl.BlockSpec((width, depth), lambda i: (0, count - 1)),
            pl.BlockSpec((2, width), lambda i: (0, 0)),
        ],
        out_specs=[
            pl.BlockSpec((rows, width), lambda i: (0, 0)),
            pl.BlockSpec((rows, width), lambda i: (lax.rem(i + count - 1, count), 0)),
            pl.BlockSpec((rows, depth), lambda i: (0, 0)),
        ],
        out_shape=[
            jax.ShapeDtypeStruct((rows, width), jnp.float32),
            jax.ShapeDtypeStruct((total_rows, width), jnp.bfloat16),
            jax.ShapeDtypeStruct((rows, depth), jnp.bfloat16),
        ],
        compiler_params=parameters(),
        cost_estimate=SMALL_COST,
        name="after_attention",
    )(partial, last, weight, gain)


def up_kernel(x_ref, gate_ref, up_ref, *refs):
    a_ref, u_ref, g_ref = refs[-3:]
    gate = dot_nn(x_ref[...], gate_ref[...])
    up = dot_nn(x_ref[...], up_ref[...])
    a_ref[...] = gate.astype(jnp.bfloat16)
    u_ref[...] = up.astype(jnp.bfloat16)
    g_ref[...] = (gate * jax.nn.sigmoid(gate) * up).astype(jnp.bfloat16)


def up_chunk(x, weight, kept, index, count):
    total_rows, depth = x.shape
    rows = total_rows // count
    hidden = (weight.shape[1] - depth) // 2
    tile = tile_of(hidden)
    tiles = hidden // tile
    start = depth // tile
    specs = [
        pl.BlockSpec((rows, depth), lambda t: (index, 0)),
        pl.BlockSpec((depth, tile), lambda t: (0, start + t)),
        pl.BlockSpec((depth, tile), lambda t: (0, start + tiles + t)),
    ]
    operands = [x, weight, weight]
    aliases = {}
    if kept is not None:
        specs.extend([pl.BlockSpec(memory_space=pl.ANY)] * 3)
        aliases = {len(operands) + i: i for i in range(3)}
        operands.extend(kept)
    return pl.pallas_call(
        up_kernel,
        grid=(tiles,),
        in_specs=specs,
        out_specs=[pl.BlockSpec((rows, tile), lambda t: (index, t))] * 3,
        out_shape=[jax.ShapeDtypeStruct((total_rows, hidden), jnp.bfloat16)] * 3,
        input_output_aliases=aliases,
        compiler_params=parameters(),
        cost_estimate=SMALL_COST,
        name="up_chunk",
    )(*operands)


def down_kernel(parts, tiles, *refs):
    down_ref, a_ref, u_ref, gate_ref, up_ref = refs[parts : parts + 5]
    da_ref, du_ref = refs[-5 - parts : -3 - parts]
    dx_refs = refs[-3 - parts : -3]
    da_kept, du_kept, e_out = refs[-3:]
    step = pl.program_id(0)

    @pl.when(step == 0)
    def _():
        rows = refs[0].shape[0]
        for index in range(parts):
            e_out[index * rows : (index + 1) * rows, :] = refs[index][...]

    @pl.when(step < tiles)
    def _():
        grad = dot_nn(e_out[...], down_ref[...])
        gate = a_ref[...].astype(jnp.float32)
        up = u_ref[...].astype(jnp.float32)
        sigmoid = jax.nn.sigmoid(gate)
        da = (grad * up * sigmoid * (1.0 + gate * (1.0 - sigmoid))).astype(jnp.bfloat16)
        du = (grad * gate * sigmoid).astype(jnp.bfloat16)
        da_ref[...] = da
        du_ref[...] = du
        tile = da.shape[1]
        for index in range(tiles):

            @pl.when(step == index)
            def _():
                da_kept[:, index * tile : (index + 1) * tile] = da
                du_kept[:, index * tile : (index + 1) * tile] = du

    @pl.when(step >= tiles)
    def _():
        total = dot_nt(da_kept[...], gate_ref[...]) + dot_nt(du_kept[...], up_ref[...])
        rows = total.shape[0] // parts
        for index in range(parts):
            dx_refs[index][...] = total[index * rows : (index + 1) * rows].astype(jnp.bfloat16)


def down_chunk(es, a, u, down_weight, weight, kept, index, count):
    depth, hidden = down_weight.shape
    rows = len(es) * es[0].shape[0]
    start = depth // hidden
    tile = tile_of(hidden)
    tiles = hidden // tile
    row_tile = tile_of(depth)

    def column(t):
        return jnp.minimum(t, tiles - 1)

    def row(t):
        return jnp.maximum(t - tiles, 0)

    specs = [pl.BlockSpec(es[0].shape, lambda t: (0, 0))] * len(es) + [
        pl.BlockSpec((depth, tile), lambda t: (0, column(t))),
        pl.BlockSpec((rows, tile), lambda t: (index, column(t))),
        pl.BlockSpec((rows, tile), lambda t: (index, column(t))),
        pl.BlockSpec((row_tile, hidden), lambda t: (row(t), start)),
        pl.BlockSpec((row_tile, hidden), lambda t: (row(t), start + 1)),
    ]
    operands = [*es, down_weight, a, u, weight, weight]
    part = es[0].shape
    shapes = [
        jax.ShapeDtypeStruct((rows * count, hidden), jnp.bfloat16),
        jax.ShapeDtypeStruct((rows * count, hidden), jnp.bfloat16),
        *[jax.ShapeDtypeStruct(part, jnp.bfloat16)] * len(es),
    ]
    aliases = {}
    if kept is not None:
        specs.extend([pl.BlockSpec(memory_space=pl.ANY)] * 2)
        aliases = {len(operands) + i: i for i in range(2)}
        operands.extend(kept)
    result = pl.pallas_call(
        functools.partial(down_kernel, len(es), tiles),
        grid=(tiles + depth // row_tile,),
        in_specs=specs,
        out_specs=[
            pl.BlockSpec((rows, tile), lambda t: (index, column(t))),
            pl.BlockSpec((rows, tile), lambda t: (index, column(t))),
            *[pl.BlockSpec((part[0], row_tile), lambda t: (0, row(t)))] * len(es),
        ],
        out_shape=shapes,
        input_output_aliases=aliases,
        scratch_shapes=[
            pltpu.VMEM((rows, hidden), jnp.bfloat16),
            pltpu.VMEM((rows, hidden), jnp.bfloat16),
            pltpu.VMEM((rows, depth), jnp.bfloat16),
        ],
        compiler_params=parameters(),
        cost_estimate=SMALL_COST,
        name="down_chunk",
    )(*operands)
    return result[:2], list(result[2:])


def weight_kernel(counts, blocks, split, place_ref, *refs):
    step = pl.program_id(0)
    total_refs = sum(parts + widths for parts, widths in counts)
    received = refs[total_refs] if len(refs) > total_refs + 1 else None
    place = 0
    column = 0
    for parts, widths in counts:
        x = refs[place][...]
        if parts > 1:
            x = jnp.concatenate([ref[...] for ref in refs[place : place + parts]], axis=0)
        for y_ref in refs[place + parts : place + parts + widths]:
            width = y_ref.shape[1]
            cuts = set(range(0, width, 1024)) | {width}
            if column < split < column + width and split:
                cuts.add(split - column)
            cuts = sorted(cuts)
            for first, last in zip(cuts[:-1], cuts[1:]):
                total = dot_tn(x, y_ref[:, first:last])
                start, end = column + first, column + last
                if received is None:
                    refs[-1][:, start:end] = total.astype(jnp.bfloat16)
                    continue
                total += received[:, start:end].astype(jnp.float32)
                total = total.astype(jnp.bfloat16)
                if split == 0:
                    refs[-1][:, start:end] = total
                    continue
                low = start < split
                keep = step < blocks // 2 if low else lax.rem(step, 2) == 0
                keep_ref, send_ref = refs[-4:-2] if low else refs[-2:]
                columns = slice(start, end) if low else slice(start - split, end - split)

                @pl.when(keep)
                def _():
                    keep_ref[:, columns] = total

                @pl.when(jnp.logical_not(keep))
                def _():
                    send_ref[:, columns] = total

            column += width
        place += parts + widths


def weight_product(pairs, place, count, received, ordered=False):
    depth = pairs[0][0][0].shape[1]
    blocks = count // 2
    tile = depth // count
    total = sum(y.shape[1] for _, ys in pairs for y in ys)
    split = 0 if ordered else -(-total // 256) * 128
    side = 1 if received is None else 0

    def source(t, p):
        if ordered:
            return 2 * t + lax.rem(p[0] + side, 2)
        return lax.bitwise_xor(p[0], 2 * t + side)

    whole = pl.BlockSpec((tile, total), lambda t, p: (t, 0))
    if received is None or ordered:
        out_specs = whole
        out_shape = jax.ShapeDtypeStruct((depth // 2, total), jnp.bfloat16)
    else:
        half = blocks // 2
        out_specs = [
            pl.BlockSpec((tile, split), lambda t, p: (jnp.minimum(t, half - 1), 0)),
            pl.BlockSpec((tile, split), lambda t, p: (jnp.maximum(t - half, 0), 0)),
            pl.BlockSpec((tile, total - split), lambda t, p: (t // 2, 0)),
            pl.BlockSpec((tile, total - split), lambda t, p: (t // 2, 0)),
        ]
        out_shape = [
            jax.ShapeDtypeStruct((depth // 4, width), jnp.bfloat16)
            for width in (split, split, total - split, total - split)
        ]
    specs = []
    operands = []
    for xs, ys in pairs:
        for x in xs:
            specs.append(pl.BlockSpec((x.shape[0], tile), lambda t, p: (0, source(t, p))))
        specs += [
            pl.BlockSpec(y.shape, lambda t, p: (0, 0), pipeline_mode=pl.Buffered(1)) for y in ys
        ]
        operands.extend([*xs, *ys])
    if received is not None:
        specs.append(whole)
        operands.append(received)
    return pl.pallas_call(
        functools.partial(
            weight_kernel, [(len(xs), len(ys)) for xs, ys in pairs], blocks, split
        ),
        grid_spec=pltpu.PrefetchScalarGridSpec(
            num_scalar_prefetch=1, grid=(blocks,), in_specs=specs, out_specs=out_specs
        ),
        out_shape=out_shape,
        compiler_params=parameters(),
        cost_estimate=SMALL_COST,
        name="weight_product",
    )(place, *operands)


def fold_kernel(counts, *refs):
    outs = refs[sum(counts) :]
    place = 0
    row = 0
    for index, count in enumerate(counts):
        total = refs[place][...].astype(jnp.float32)
        for ref in refs[place + 1 : place + count]:
            total += ref[...].astype(jnp.float32)
        out = outs[index % 2]
        rows = total.shape[0]
        out[row : row + rows, :] = total.astype(jnp.bfloat16)
        row += rows * (index % 2)
        place += count


def fold(sums, rows):
    counts = [len(terms) for pair in sums for terms in pair]
    values = [value for pair in sums for terms in pair for value in terms]
    widths = [terms[0].shape[1] for terms in sums[0]]
    steps = 2 if all(width % 256 == 0 for width in widths) else 1
    return pl.pallas_call(
        functools.partial(fold_kernel, counts),
        grid=(steps,),
        in_specs=[
            pl.BlockSpec((rows, value.shape[1] // steps), lambda t: (1, t)) for value in values
        ],
        out_specs=[
            pl.BlockSpec((rows * len(sums), width // steps), lambda t: (0, t))
            for width in widths
        ],
        out_shape=[
            jax.ShapeDtypeStruct((rows * len(sums), width), jnp.bfloat16) for width in widths
        ],
        compiler_params=parameters(),
        cost_estimate=SMALL_COST,
        name="fold",
    )(*values)


def residual_kernel(parts, e_ref, hidden_ref, first_ref, second_ref, gain_ref, weight_ref, *refs):
    dh_ref, dz_ref = refs[:2]
    dh, dz = refs[-2:]
    step = pl.program_id(0)
    tile = weight_ref.shape[1]

    @pl.when(step == 0)
    def _():
        values = hidden_ref[...]
        inverse = lax.rsqrt(jnp.mean(values * values, axis=-1, keepdims=True) + EPSILON)
        scaled = values * inverse
        grad = first_ref[...].astype(jnp.float32) + second_ref[...].astype(jnp.float32)
        grad = grad * gain_ref[1:, :]
        projection = jnp.mean(grad * scaled, axis=-1, keepdims=True)
        total = e_ref[...].astype(jnp.float32) + inverse * (grad - scaled * projection)
        dh[...] = total
        dz[...] = total.astype(jnp.bfloat16)

    result = dot_nn(dz[...], weight_ref[...]).astype(jnp.bfloat16)
    for index in range(parts):

        @pl.when(step == index)
        def _():
            columns = slice(index * tile, (index + 1) * tile)
            dh_ref[...] = dh[:, columns]
            dz_ref[...] = dz[:, columns]
            refs[2 + index][...] = result


def residual_gradient(e, hidden_res, first, second, gain, weight, parts):
    rows, depth = e.shape
    tile = depth // parts
    whole = pl.BlockSpec((rows, depth), lambda t: (0, 0))
    column = pl.BlockSpec((rows, tile), lambda t: (0, t))
    result = pl.pallas_call(
        functools.partial(residual_kernel, parts),
        grid=(parts,),
        in_specs=[
            whole,
            whole,
            whole,
            whole,
            pl.BlockSpec((2, depth), lambda t: (0, 0)),
            pl.BlockSpec((depth, tile), lambda t: (0, t)),
        ],
        out_specs=[column, column] + [pl.BlockSpec((rows, tile), lambda t: (0, 0))] * parts,
        out_shape=[
            jax.ShapeDtypeStruct((rows, depth), jnp.float32),
            jax.ShapeDtypeStruct((rows, depth), jnp.bfloat16),
            *[jax.ShapeDtypeStruct((rows, tile), jnp.bfloat16)] * parts,
        ],
        scratch_shapes=[
            pltpu.VMEM((rows, depth), jnp.float32),
            pltpu.VMEM((rows, depth), jnp.bfloat16),
        ],
        compiler_params=parameters(),
        cost_estimate=SMALL_COST,
        name="residual_gradient",
    )(e, hidden_res, first, second, gain, weight)
    return result[0], result[1], list(result[2:])


def tie(value, *others):
    return lax.optimization_barrier((value, others))[0]


def together(*values):
    return lax.optimization_barrier(values)


def add(first, second):
    return (first.astype(jnp.float32) + second.astype(jnp.float32)).astype(jnp.bfloat16)


class Mover:
    def __init__(self):
        self.dp_count = lax.axis_size("dp")
        self.ring = lax.axis_size("tensor")
        self.steps = []
        step = 2
        while step < self.dp_count:
            self.steps.append(step)
            step *= 2

    def swap(self, value, step):
        return lax.ppermute(value, "dp", [(i, i ^ step) for i in range(self.dp_count)])

    def gather(self, shard):
        return lax.all_gather(shard, "dp", axis=0, tiled=True)


    def send(self, pieces, level):
        orders = (self.steps[::-1], self.steps[:1] + self.steps[:0:-1])
        return [self.swap(piece, order[level]) for piece, order in zip(pieces, orders)]

    def begin(self, pieces):
        moved = self.send([pieces[1], pieces[3]], 0)
        return [[pieces[0], moved[0]], [pieces[2], moved[1]]]

    def fold(self, sums, level=1):
        return fold(sums, sums[0][0][0].shape[0] >> level)

    def advance(self, sums, folded):
        level = 1
        while True:
            moved = self.send(folded, level)
            level += 1
            if level == len(self.steps):
                return sums, moved
            rows = moved[0].shape[0] // len(sums)
            sums = [
                [
                    terms + [part[index * rows : (index + 1) * rows]]
                    for terms, part in zip(pair, moved)
                ]
                for index, pair in enumerate(sums)
            ]
            folded = self.fold(sums, level)

    def advance_all(self, sums):
        widths = {pair[0][0].shape[1] for pair in sums}
        parts = [sums] if len(widths) == 1 else [[pair] for pair in sums]
        return [self.advance(part, self.fold(part)) for part in parts]

    def scatter(self, total):
        groups = [list(range(core, self.dp_count, 2)) for core in range(2)]
        return lax.psum_scatter(
            total, "dp", scatter_dimension=0, tiled=True, axis_index_groups=groups
        )

    def hop(self, value, shift=1):
        return lax.ppermute(
            value, "tensor", [(i, (i + shift) % self.ring) for i in range(self.ring)]
        )

    def spread(self, value):
        ring = self.ring
        return [value] + [
            lax.ppermute(value, "tensor", [(i, (i - j) % ring) for i in range(ring)])
            for j in range(1, ring)
        ]

    def collect(self, parts):
        ring = self.ring
        total = parts[0]
        for j in range(1, ring):
            moved = lax.ppermute(
                parts[j].astype(jnp.bfloat16), "tensor", [(i, (i + j) % ring) for i in range(ring)]
            )
            total = total + moved.astype(jnp.float32)
        return total

    def exchange(self, parts):
        ring = self.ring
        return [parts[0]] + [
            lax.ppermute(parts[j], "tensor", [(i, (i + j) % ring) for i in range(ring)])
            for j in range(1, ring)
        ]


def totals_of(sums, moved):
    rows = moved[0].shape[0] // len(sums)
    result = []
    for index, pair in enumerate(sums):
        halves = []
        for terms, last in zip(pair, moved):
            total = last[index * rows : (index + 1) * rows].astype(jnp.float32)
            for term in terms:
                total = total + term[:rows].astype(jnp.float32)
            halves.append(total)
        result.append(jnp.concatenate(halves, axis=1))
    return result


def back_norm(grad_normed, scaled, inverse, scale_row):
    grad_scaled = grad_normed * scale_row
    projection = jnp.mean(grad_scaled * scaled, axis=-1, keepdims=True)
    return inverse * (grad_scaled - scaled * projection)


def per_device(
    tokens,
    seq_lengths,
    attention_gain,
    query_matrix,
    key_matrix,
    value_matrix,
    output_weight,
    feedforward_gain,
    gate_weight,
    up_weight,
    down_weight,
    cotangent,
):
    mover = Mover()
    dp_count = mover.dp_count
    ring = mover.ring
    dp_place = lax.axis_index("dp").astype(jnp.int32).reshape(1)
    ring_place = lax.axis_index("tensor")
    place = ring_place.astype(jnp.int32).reshape(1)
    _, local_rows, model_width = tokens.shape
    complete_rows = local_rows * ring
    hidden = gate_weight.shape[1]
    groups = key_matrix.shape[1] // HEAD_SIZE
    joint_width = groups * GROUP_WIDTH
    f32 = jnp.float32
    b16 = jnp.bfloat16

    doc_ids, positions = layout(seq_lengths, complete_rows)
    row_index = jnp.arange(complete_rows, dtype=jnp.int32)
    doc_ids = jnp.where(doc_ids[0] < PIECES, doc_ids[0], PIECES + row_index)

    def to_relative(values):
        view = values.reshape((ring, local_rows) + values.shape[1:])
        return jnp.roll(view, -(ring_place + 1), axis=0)[::-1].reshape(values.shape)

    doc_ids = to_relative(doc_ids)
    cosine, sine = rope_tables(to_relative(positions[0]), HEAD_SIZE)
    cosine_table = jnp.tile(cosine, (1, 128 // cosine.shape[1]))
    sine_table = jnp.tile(jnp.concatenate([-sine, sine], axis=1), (1, 128 // HEAD_SIZE))

    own_gains = jnp.pad(jnp.stack([attention_gain, feedforward_gain]), ((0, 126), (0, 0)))
    joint_matrix, packed = pack(query_matrix, key_matrix, value_matrix, own_gains, groups)
    joint_full = mover.gather(packed)
    output_parts = mover.spread(output_weight.T)
    up_shard = jnp.pad(
        jnp.concatenate([gate_weight, up_weight], axis=1), ((0, 0), (model_width, 0))
    )
    output_parts, cosine_table, sine_table, doc_ids, up_shard, down_shard = together(
        output_parts, cosine_table, sine_table, doc_ids, up_shard, down_weight.T
    )
    local_tokens = tokens[0]
    token_chunks = [local_tokens, mover.hop(local_tokens)]
    up_shard = join(output_parts, up_shard)
    up_full = mover.gather(up_shard)
    down_full = mover.gather(tie(down_shard, up_shard))
    gains = joint_full[:, joint_width : joint_width + 2].T.astype(f32)

    def projection(kept, index):
        return project(
            token_chunks[index],
            gains,
            joint_full,
            cosine_table,
            sine_table,
            kept,
            index,
            ring,
            groups,
        )

    kept = projection(None, 0)
    for j in range(1, ring):
        token_chunks[j], kept, gains = together(token_chunks[j], kept, gains)
        if j + 1 < ring:
            token_chunks.append(mover.hop(token_chunks[j]))
        else:
            local_cotangent = tie(cotangent[0], token_chunks[j])
            moved = mover.hop(local_cotangent)
        kept = projection(kept, j)
    normed_one, joint = kept
    attended, totals = attention_forward(joint, doc_ids, place, ring, groups)
    moved, attended = together(moved, attended)
    cotangent_chunks = [local_cotangent, moved]
    attended_parts = [attended]
    while len(attended_parts) < ring:
        part = mover.hop(attended_parts[-1], -1)
        if len(attended_parts) == ring - 1:
            partial, attended_local = heads_product(
                tie(attended_parts, attended_parts[-1]), up_full, token_chunks
            )
            part, partial, attended_local = together(part, partial, attended_local)
        attended_parts.append(part)
    moved, last = together(moved, attended_parts[-1])

    pairs = ring // 2
    moved = mover.hop(moved)
    hidden_res, normed_two, attended_last = after_attention(partial, last, up_full, gains, ring)
    upward = up_chunk(normed_two, up_full, None, 0, pairs)
    downward = None
    grads = []

    def chunks_of(pair):
        return [cotangent_chunks[(2 * pair + i) % ring] for i in (1, 2)]

    def lower(pair, kept):
        return down_chunk(
            chunks_of(pair), upward[0], upward[1], down_full, up_full, kept, pair, pairs
        )

    for j in range(2, ring):
        if j > 2:
            moved = mover.hop(moved)
            if j % 2:
                downward, parts = lower((j - 3) // 2, downward)
                grads.extend(parts)
            else:
                upward = up_chunk(normed_two, up_full, upward, j // 2 - 1, pairs)
        moved, upward, downward, grads = together(moved, upward, downward, grads)
        cotangent_chunks.append(moved)

    def weights(xs, ys, received=None):
        return weight_product([(xs, ys)], dp_place, dp_count, received)

    ordered = cotangent_chunks[1:] + cotangent_chunks[:1]
    total = grads[0]
    moved = mover.hop(total)
    upward = up_chunk(tie(normed_two, total), up_full, upward, pairs - 1, pairs)
    product = upward[2]
    down_part = weight_product([(ordered, [product])], dp_place, dp_count, None, True)
    moved, upward, down_part = together(moved, upward, down_part)
    down_part = mover.swap(down_part, 1)
    for j in range(2, ring):
        total = add(moved, grads[j - 1])
        moved = mover.hop(total)
        if j == 2:
            downward, parts = lower(pairs - 1, tie(downward, total))
            grads.extend(parts)
            moved, downward, grads = together(moved, downward, grads)
            grad_gate, grad_up = downward
        if j == 3:
            gate_part = weights([tie(normed_two, total)], [grad_gate])
            branch = transposed_product(
                [tie(product, gate_part)], down_full, 0, ring // 2, 0, 2
            )
            down_part = weight_product(
                [(tie(ordered, branch), [product])], dp_place, dp_count, down_part, True
            )
            moved, gate_part, branch, down_part = together(moved, gate_part, branch, down_part)
    gate_part = mover.swap(gate_part, 1)
    down_out = mover.scatter(down_part)
    grad_hidden, grad_branch, grad_parts = residual_gradient(
        local_cotangent, hidden_res, moved, grads[-1], gains, up_full, ring
    )
    grad_hidden, grad_branch, grad_parts, gate_part = together(
        grad_hidden, grad_branch, grad_parts, gate_part
    )

    grad_parts = mover.exchange(grad_parts)
    output_part = weights([grad_branch], [attended_local, attended_last])
    gate_part = weights([tie(normed_two, output_part)], [grad_gate], gate_part)
    grad_parts, output_part, gate_part = together(grad_parts, output_part, gate_part)
    grad_joint = []
    sent = 0
    moved = branch[0]
    for group in range(groups):
        moved = mover.hop(moved)
        sent += 1
        if group == 0:
            output_part = mover.swap(output_part, 1)
        else:
            output_part = mover.begin(output_part)
        grad_joint.append(
            attention_backward(
                joint,
                attended,
                tie(grad_parts, grad_joint),
                totals,
                doc_ids,
                cosine_table,
                sine_table,
                place,
                group,
            )
        )
        if group == 0:
            output_part = weights(
                [tie(grad_branch, grad_joint)], [attended_local, attended_last], output_part
            )
        if group + 1 == groups:
            grads = transposed_product(grad_joint, joint_full, 0, ring)
        moved, grad_joint, grads, output_part, down_out = together(
            moved, grad_joint, grads, output_part, down_out
        )
        if group + 1 < groups:
            moved = add(moved, branch[sent])
    if groups == 1:
        output_part = mover.begin(output_part)
    branch_moved = moved
    moved = grads[0]

    def last_weights(total, received):
        return weight_product(
            [([tie(normed_two, total)], [grad_up]), ([normed_one], grad_joint)],
            dp_place,
            dp_count,
            received,
        )

    for j in range(1, ring):
        total = grads[1] if j == 1 else add(moved, grads[j])
        moved = mover.hop(total)
        if j == 1:
            gate_part = mover.begin(gate_part)
            last_part = last_weights(total, None)
            branch = branch + transposed_product(
                [tie(product, last_part)], down_full, 0, ring // 2, 1, 2
            )
            moved, last_part, branch, output_part, gate_part = together(
                moved, last_part, branch, output_part, gate_part
            )
        if j == 2:
            both_parts = tie([output_part, gate_part], total)
            both_parts = mover.advance_all(both_parts)
            next_branch = add(branch_moved, branch[sent])
            last_part = last_weights(next_branch, mover.swap(last_part, 1))
            moved, last_part, both_parts, next_branch = together(
                moved, last_part, both_parts, next_branch
            )
        if j == 3:
            last_part = mover.begin(last_part)
            branch_moved = mover.hop(tie(next_branch, total))
            sent += 1
            output_out, gate_out = [total for part in both_parts for total in totals_of(*part)]
            output_out = jnp.split(output_out, ring, axis=1)
            moved, last_part, output_out = together(moved, last_part, output_out)
    folded, output_out = together(mover.fold([last_part]), output_out)
    last_part = mover.advance([last_part], folded)
    output_out = mover.collect(output_out[:-1] + [tie(output_out[-1], last_part)]).T
    scaled_one, inverse_one = norm_rows(local_tokens.astype(f32))
    local_one = moved.astype(f32) + grads[0].astype(f32)
    input_gradient = grad_hidden + back_norm(local_one, scaled_one, inverse_one, gains[:1])
    branch_moved = tie(branch_moved, last_part)
    for j in range(sent, ring - 1):
        branch_moved = mover.hop(add(branch_moved, branch[j]))
    block_output = (
        hidden_res + (branch_moved.astype(f32) + branch[-1].astype(f32))
    ).astype(b16)
    last_out = totals_of(*last_part)[0]
    up_out, joint_out = last_out[:, :hidden], last_out[:, hidden:]

    sums = jnp.stack(
        [
            jnp.sum(joint_out * joint_matrix.astype(f32), axis=1) / attention_gain.astype(f32),
            jnp.sum(gate_out * gate_weight.astype(f32) + up_out * up_weight.astype(f32), axis=1)
            / feedforward_gain.astype(f32),
        ]
    )
    gain_out = sums
    for shift in range(1, ring):
        gain_out = gain_out + lax.ppermute(
            sums, "tensor", [(i, (i + shift) % ring) for i in range(ring)]
        )

    def ungrouped(first, width):
        return jnp.concatenate(
            [
                joint_out[:, g * GROUP_WIDTH + first : g * GROUP_WIDTH + first + width]
                for g in range(groups)
            ],
            axis=1,
        )

    return (
        block_output[None],
        input_gradient[None],
        gain_out[0],
        ungrouped(0, GROUP_QUERY),
        ungrouped(GROUP_QUERY, HEAD_SIZE),
        ungrouped(GROUP_QUERY + HEAD_SIZE, HEAD_SIZE),
        output_out,
        gain_out[1],
        gate_out,
        up_out,
        down_out.astype(f32).T,
    )


def solution(mesh):
    return jax.shard_map(
        per_device,
        mesh=mesh,
        in_specs=(
            P("dp", "tensor", None),
            P("dp", None),
            P("dp"),
            P("dp", "tensor"),
            P("dp", "tensor"),
            P("dp", "tensor"),
            P("tensor", "dp"),
            P("dp"),
            P("dp", "tensor"),
            P("dp", "tensor"),
            P("tensor", "dp"),
            P("dp", "tensor", None),
        ),
        out_specs=(
            P("dp", "tensor", None),
            P("dp", "tensor", None),
            P("dp"),
            P("dp", "tensor"),
            P("dp", "tensor"),
            P("dp", "tensor"),
            P("tensor", "dp"),
            P("dp"),
            P("dp", "tensor"),
            P("dp", "tensor"),
            P("tensor", "dp"),
        ),
        check_vma=False,
    )
```

```python
import functools
import math

import jax
import jax.numpy as jnp
from jax import lax
from jax.experimental import pallas as pl
from jax.experimental.pallas import tpu as pltpu
from jax.sharding import PartitionSpec as P

QUERY_HEADS = 32
KEY_VALUE_HEADS = 8
HEAD_SIZE = 64
PIECES = 4


EPSILON = 1e-05
ROPE_BASE = 500000.0
NEGATIVE = -1e30
GROUP_QUERY = QUERY_HEADS // KEY_VALUE_HEADS * HEAD_SIZE
GROUP_WIDTH = GROUP_QUERY + 2 * HEAD_SIZE
KERNEL_VMEM = 60 * 1024 * 1024
SMALL_COST = pl.CostEstimate(flops=1, bytes_accessed=1, transcendentals=0)


def layout(lengths, complete_rows):
    doc_ends = jnp.cumsum(lengths, axis=-1)
    row_index = jnp.arange(complete_rows, dtype=jnp.int32)
    piece_count = lengths.shape[-1]
    doc_ids = jnp.sum((row_index[None, :, None] >= doc_ends[:, None, :]).astype(jnp.int32), axis=2)
    starts = doc_ends - lengths
    chosen = doc_ids[:, :, None] == jnp.arange(piece_count, dtype=jnp.int32)[None, None, :]
    doc_begin = jnp.sum(jnp.where(chosen, starts[:, None, :], 0), axis=2) + jnp.where(
        doc_ids == piece_count, doc_ends[:, -1:], 0
    )
    return (doc_ids, row_index[None, :] - doc_begin)


def rope_tables(positions, head_dim):
    half_dim = head_dim // 2
    frequency = ROPE_BASE ** (-(jnp.arange(half_dim, dtype=jnp.float32) * (2.0 / head_dim)))
    angles = positions.astype(jnp.float32)[..., None] * frequency
    return (jnp.cos(angles), jnp.sin(angles))


def norm_rows(values):
    inverse = lax.rsqrt(jnp.mean(values * values, axis=-1, keepdims=True) + EPSILON)
    return (values * inverse, inverse)


def dot_nt(left, right):
    return lax.dot_general(
        left, right, (((1,), (1,)), ((), ())), preferred_element_type=jnp.float32
    )


def dot_nn(left, right):
    return jnp.dot(left, right, preferred_element_type=jnp.float32)


def dot_tn(left, right):
    return lax.dot_general(
        left, right, (((0,), (0,)), ((), ())), preferred_element_type=jnp.float32
    )


def tile_of(size, limit=512):
    tile = limit
    while size % tile:
        tile //= 2
    return tile


def parameters():
    return pltpu.CompilerParams(vmem_limit_bytes=KERNEL_VMEM)


def swap_halves(values):
    lane = lax.broadcasted_iota(jnp.int32, values.shape, 1)
    half = HEAD_SIZE // 2
    return jnp.where(
        lane % HEAD_SIZE < half, pltpu.roll(values, 128 - half, 1), pltpu.roll(values, half, 1)
    )


def turned(values, cosine, sine, start):
    result = values * cosine + swap_halves(values) * sine
    rotated = GROUP_WIDTH - HEAD_SIZE
    if start + 128 <= rotated:
        return result
    lane = lax.broadcasted_iota(jnp.int32, values.shape, 1)
    return jnp.where(lane < rotated - start, result, values)


def project_kernel(x_ref, gain_ref, weight_ref, cos_ref, sin_ref, *refs):
    normed_ref, joint_ref = refs[-2:]

    @pl.when(pl.program_id(0) == 0)
    def _():
        values = x_ref[...].astype(jnp.float32)
        inverse = lax.rsqrt(jnp.mean(values * values, axis=-1, keepdims=True) + EPSILON)
        normed_ref[...] = (values * inverse * gain_ref[:1, :]).astype(jnp.bfloat16)

    product = dot_nn(normed_ref[...], weight_ref[...])
    for start in range(0, GROUP_WIDTH, 128):
        part = turned(product[:, start : start + 128], cos_ref[...], sin_ref[...], start)
        if start < GROUP_QUERY:
            part = part * HEAD_SIZE ** (-0.5)
        joint_ref[:, start : start + 128] = part.astype(jnp.bfloat16)


def project(x, gain, weight, cosine, sine, kept, index, count, groups):
    rows, depth = x.shape
    specs = [
        pl.BlockSpec((rows, depth), lambda g: (0, 0)),
        pl.BlockSpec((2, depth), lambda g: (0, 0)),
        pl.BlockSpec((depth, GROUP_WIDTH), lambda g: (0, g)),
        pl.BlockSpec((rows, 128), lambda g: (index, 0)),
        pl.BlockSpec((rows, 128), lambda g: (index, 0)),
    ]
    operands = [x, gain, weight, cosine, sine]
    aliases = {}
    if kept is not None:
        specs.extend([pl.BlockSpec(memory_space=pl.ANY)] * 2)
        aliases = {len(operands) + i: i for i in range(2)}
        operands.extend(kept)
    return pl.pallas_call(
        project_kernel,
        grid=(groups,),
        in_specs=specs,
        out_specs=[
            pl.BlockSpec((rows, depth), lambda g: (index, 0)),
            pl.BlockSpec((rows, GROUP_WIDTH), lambda g: (index, g)),
        ],
        out_shape=[
            jax.ShapeDtypeStruct((rows * count, depth), jnp.bfloat16),
            jax.ShapeDtypeStruct((rows * count, GROUP_WIDTH * groups), jnp.bfloat16),
        ],
        input_output_aliases=aliases,
        compiler_params=parameters(),
        cost_estimate=SMALL_COST,
        name="project",
    )(*operands)


def ring_offset(place, chunk, count, rows):
    return pl.multiple_of(lax.rem(place - chunk + count, count) * rows, rows)


def stack_heads(target, source):
    rows, width = source.shape
    for head in range(width // HEAD_SIZE):
        target[head * rows : (head + 1) * rows, :] = source[
            :, head * HEAD_SIZE : (head + 1) * HEAD_SIZE
        ]


def fill_bias(bias, key_docs, query_docs, earlier):
    rows = key_docs.shape[0]
    row_index = lax.broadcasted_iota(jnp.int32, (rows, rows), 0)
    column_index = lax.broadcasted_iota(jnp.int32, (rows, rows), 1)
    same = (key_docs == query_docs) & ((row_index <= column_index) | earlier)
    values = jnp.where(same, 0.0, NEGATIVE)
    for first in range(0, bias.shape[1], rows):
        bias[:, first : first + rows] = values


def forward_kernel(
    count,
    place_ref,
    own_ref,
    all_ref,
    docq_ref,
    dock_ref,
    o_ref,
    lse_ref,
    bias,
    queries,
    values_all,
    mixed,
):
    chunk = pl.program_id(1)
    place = place_ref[0]
    rows = own_ref.shape[0]
    heads = GROUP_QUERY // HEAD_SIZE
    stack_heads(queries, own_ref.at[:, :GROUP_QUERY])

    @pl.when(chunk == 0)
    def _():
        values = all_ref[:, GROUP_QUERY:].astype(jnp.float32)
        values_all[...] = values.T[HEAD_SIZE:].astype(jnp.bfloat16)

    mixed[...] = jnp.zeros_like(mixed)

    def block(j, carry):
        peaks, total = carry
        offset = ring_offset(place, j, count, rows)
        piece = pl.ds(offset, rows)
        fill_bias(bias, dock_ref[piece, :], docq_ref[...], j < chunk)
        keys = all_ref[piece, GROUP_QUERY : GROUP_QUERY + HEAD_SIZE]
        scores = dot_nt(keys, queries[...]) + bias[...]
        higher = jnp.maximum(peaks, jnp.max(scores, axis=0, keepdims=True))
        probs = jnp.exp(scores - higher)
        scale = jnp.exp(peaks - higher)
        mixed[...] = mixed[...] * scale + dot_nn(
            values_all[:, piece], probs.astype(jnp.bfloat16)
        )
        return higher, total * scale + jnp.sum(probs, axis=0, keepdims=True)

    peaks, total = lax.fori_loop(
        0,
        chunk + 1,
        block,
        (
            jnp.full((1, heads * rows), NEGATIVE, jnp.float32),
            jnp.zeros((1, heads * rows), jnp.float32),
        ),
    )
    lse_ref[:1, :] = peaks + jnp.log(total)
    result = mixed[...] / total
    for head in range(0, heads, 2):
        pair = jnp.concatenate(
            [result[:, (head + i) * rows : (head + i + 1) * rows] for i in range(2)], axis=0
        )
        o_ref[:, head * HEAD_SIZE : (head + 2) * HEAD_SIZE] = pair.T.astype(jnp.bfloat16)


def attention_forward(joint, docs, place, count, groups):
    total_rows = joint.shape[0]
    rows = total_rows // count
    stacked = rows * GROUP_QUERY // HEAD_SIZE

    def block(c, place_ref):
        return lax.rem(place_ref[0] - c + count, count)

    spec = pltpu.PrefetchScalarGridSpec(
        num_scalar_prefetch=1,
        grid=(groups, count),
        in_specs=[
            pl.BlockSpec((rows, GROUP_WIDTH), lambda g, c, p: (block(c, p), g)),
            pl.BlockSpec((total_rows, GROUP_WIDTH), lambda g, c, p: (0, g)),
            pl.BlockSpec((1, rows), lambda g, c, p: (0, block(c, p))),
            pl.BlockSpec((total_rows, 1), lambda g, c, p: (0, 0)),
        ],
        out_specs=[
            pl.BlockSpec((rows, GROUP_QUERY), lambda g, c, p: (block(c, p), g)),
            pl.BlockSpec((8, stacked), lambda g, c, p: (g, block(c, p))),
        ],
        scratch_shapes=[
            pltpu.VMEM((rows, stacked), jnp.float32),
            pltpu.VMEM((stacked, HEAD_SIZE), jnp.bfloat16),
            pltpu.VMEM((HEAD_SIZE, total_rows), jnp.bfloat16),
            pltpu.VMEM((HEAD_SIZE, stacked), jnp.float32),
        ],
    )
    return pl.pallas_call(
        functools.partial(forward_kernel, count),
        grid_spec=spec,
        out_shape=[
            jax.ShapeDtypeStruct((total_rows, GROUP_QUERY * groups), jnp.bfloat16),
            jax.ShapeDtypeStruct((8 * groups, stacked * count), jnp.float32),
        ],
        compiler_params=parameters(),
        cost_estimate=SMALL_COST,
        name="attend",
    )(place, joint, joint, docs[None, :], docs[:, None])


def backward_kernel(count, place_ref, *refs):
    own_ref, all_ref, o_ref = refs[:3]
    lse_ref, docq_ref, dock_ref, cos_ref, sin_ref = refs[3 + count : 8 + count]
    out_ref, bias, queries, grads, keys_all, values_all, sum_q, sum_k, sum_v = refs[8 + count :]
    chunk = pl.program_id(0)
    place = place_ref[0]
    rows = own_ref.shape[0]
    heads = GROUP_QUERY // HEAD_SIZE
    stack_heads(queries, own_ref.at[:, :GROUP_QUERY])
    for index in range(count):

        @pl.when(lax.rem(place - chunk + count, count) == index)
        def _():
            stack_heads(grads, refs[3 + index])

    @pl.when(chunk == 0)
    def _():
        keys_all[...] = all_ref[:, GROUP_QUERY : GROUP_QUERY + HEAD_SIZE]
        values_all[...] = all_ref[:, GROUP_QUERY + HEAD_SIZE :]
        sum_k[...] = jnp.zeros_like(sum_k)
        sum_v[...] = jnp.zeros_like(sum_v)

    sum_q[...] = jnp.zeros_like(sum_q)
    ones = jnp.ones((8, HEAD_SIZE), jnp.bfloat16)
    inner = []
    for head in range(heads):
        attended = o_ref[:, head * HEAD_SIZE : (head + 1) * HEAD_SIZE].astype(jnp.float32)
        both = attended * grads[head * rows : (head + 1) * rows, :].astype(jnp.float32)
        high = both.astype(jnp.bfloat16)
        low = (both - high.astype(jnp.float32)).astype(jnp.bfloat16)
        inner.append((dot_nt(ones, high) + dot_nt(ones, low))[:1])
    inner = jnp.concatenate(inner, axis=1)

    def block(j, carry):
        offset = ring_offset(place, j, count, rows)
        piece = pl.ds(offset, rows)
        fill_bias(bias, dock_ref[piece, :], docq_ref[...], j < chunk)
        probs = jnp.exp(dot_nt(keys_all[piece, :], queries[...]) + bias[...] - lse_ref[:1, :])
        grad_probs = dot_nt(values_all[piece, :], grads[...])
        grad_scores = (probs * (grad_probs - inner)).astype(jnp.bfloat16)
        sum_v[piece, :] += dot_nn(probs.astype(jnp.bfloat16), grads[...])
        sum_k[piece, :] += dot_nn(grad_scores, queries[...])
        sum_q[...] += dot_tn(grad_scores, keys_all[piece, :])
        return carry

    lax.fori_loop(0, chunk + 1, block, 0)
    own = pl.ds(ring_offset(place, chunk, count, rows), rows)
    for first in range(0, heads, 2):
        start = first * HEAD_SIZE
        part = jnp.concatenate(
            [sum_q[(first + i) * rows : (first + i + 1) * rows, :] for i in range(2)], axis=1
        )
        part = turned(part, cos_ref[own, :], -sin_ref[own, :], start)
        out_ref[own, start : start + 128] = (part * HEAD_SIZE ** (-0.5)).astype(jnp.bfloat16)

    @pl.when(chunk == count - 1)
    def _():
        part = jnp.concatenate([sum_k[...], sum_v[...]], axis=1)
        part = turned(part, cos_ref[...], -sin_ref[...], GROUP_QUERY)
        out_ref[:, GROUP_QUERY:] = part.astype(jnp.bfloat16)


def attention_backward(joint, attended, grads, lse, docs, cosine, sine, place, group):
    count = len(grads)
    total_rows = joint.shape[0]
    rows = total_rows // count
    stacked = rows * GROUP_QUERY // HEAD_SIZE

    def block(c, place_ref):
        return lax.rem(place_ref[0] - c + count, count)

    table = pl.BlockSpec((total_rows, 128), lambda c, p: (0, 0))
    spec = pltpu.PrefetchScalarGridSpec(
        num_scalar_prefetch=1,
        grid=(count,),
        in_specs=[
            pl.BlockSpec((rows, GROUP_WIDTH), lambda c, p: (block(c, p), group)),
            pl.BlockSpec((total_rows, GROUP_WIDTH), lambda c, p: (0, group)),
            pl.BlockSpec((rows, GROUP_QUERY), lambda c, p: (block(c, p), group)),
            *[pl.BlockSpec((rows, GROUP_QUERY), lambda c, p: (0, group))] * count,
            pl.BlockSpec((8, stacked), lambda c, p: (group, block(c, p))),
            pl.BlockSpec((1, rows), lambda c, p: (0, block(c, p))),
            pl.BlockSpec((total_rows, 1), lambda c, p: (0, 0)),
            table,
            table,
        ],
        out_specs=pl.BlockSpec((total_rows, GROUP_WIDTH), lambda c, p: (0, 0)),
        scratch_shapes=[
            pltpu.VMEM((rows, stacked), jnp.float32),
            *[pltpu.VMEM((stacked, HEAD_SIZE), jnp.bfloat16)] * 2,
            *[pltpu.VMEM((total_rows, HEAD_SIZE), jnp.bfloat16)] * 2,
            pltpu.VMEM((stacked, HEAD_SIZE), jnp.float32),
            *[pltpu.VMEM((total_rows, HEAD_SIZE), jnp.float32)] * 2,
        ],
    )
    return pl.pallas_call(
        functools.partial(backward_kernel, count),
        grid_spec=spec,
        out_shape=jax.ShapeDtypeStruct((total_rows, GROUP_WIDTH), jnp.bfloat16),
        compiler_params=parameters(),
        cost_estimate=SMALL_COST,
        name="attend_back",
    )(
        place,
        joint,
        joint,
        attended,
        *grads,
        lse,
        docs[None, :],
        docs[:, None],
        cosine,
        sine,
    )


def pack_kernel(groups, query_ref, key_ref, value_ref, gain_ref, joint_ref, out_ref):
    for g in range(groups):
        start = g * GROUP_WIDTH
        columns = slice(g * HEAD_SIZE, (g + 1) * HEAD_SIZE)
        joint_ref[:, start : start + GROUP_QUERY] = query_ref[
            :, g * GROUP_QUERY : (g + 1) * GROUP_QUERY
        ]
        joint_ref[:, start + GROUP_QUERY : start + GROUP_WIDTH] = jnp.concatenate(
            [key_ref[:, columns], value_ref[:, columns]], axis=1
        )
    width = groups * GROUP_WIDTH
    out_ref[:, :width] = joint_ref[...]
    out_ref[:, width:] = gain_ref[...].astype(jnp.float32).T.astype(jnp.bfloat16)


def pack(query, key, value, gains, groups):
    rows = query.shape[0]
    width = groups * GROUP_WIDTH
    return pl.pallas_call(
        functools.partial(pack_kernel, groups),
        out_shape=[
            jax.ShapeDtypeStruct((rows, width), jnp.bfloat16),
            jax.ShapeDtypeStruct((rows, width + 128), jnp.bfloat16),
        ],
        compiler_params=parameters(),
        cost_estimate=SMALL_COST,
        name="pack",
    )(query, key, value, gains)


def join_kernel(*refs):
    place = 0
    for ref in refs[:-2]:
        size = ref.shape[1]
        refs[-1][:, place : place + size] = ref[...]
        place += size


def join(parts, rest):
    rows = rest.shape[0]
    width = sum(part.shape[1] for part in parts)
    return pl.pallas_call(
        join_kernel,
        grid=(1,),
        in_specs=[pl.BlockSpec(part.shape, lambda i: (0, 0)) for part in parts]
        + [pl.BlockSpec(memory_space=pl.ANY)],
        out_specs=pl.BlockSpec((rows, width), lambda i: (0, 0)),
        out_shape=jax.ShapeDtypeStruct(rest.shape, rest.dtype),
        input_output_aliases={len(parts): 0},
        compiler_params=parameters(),
        cost_estimate=SMALL_COST,
        name="join",
    )(*parts, rest)


def transposed_kernel(count, parts, *refs):
    total = dot_nt(refs[0][...], refs[count][...])
    for index in range(1, count):
        total += dot_nt(refs[index][...], refs[count + index][...])
    rows = total.shape[0] // parts
    for index in range(parts):
        refs[2 * count + index][...] = total[index * rows : (index + 1) * rows].astype(
            jnp.bfloat16
        )


def transposed_product(xs, weight, column, parts, block=0, blocks=1):
    rows, depth = xs[0].shape
    rows //= blocks
    width = weight.shape[0]
    tile = tile_of(width)
    specs = [pl.BlockSpec((rows, depth), lambda t: (block, 0))] * len(xs)
    for index in range(len(xs)):
        specs.append(pl.BlockSpec((tile, depth), lambda t, index=index: (t, column + index)))
    part = (rows // parts, width)
    return pl.pallas_call(
        functools.partial(transposed_kernel, len(xs), parts),
        grid=(width // tile,),
        in_specs=specs,
        out_specs=[pl.BlockSpec((part[0], tile), lambda t: (0, t))] * parts,
        out_shape=[jax.ShapeDtypeStruct(part, jnp.bfloat16)] * parts,
        compiler_params=parameters(),
        cost_estimate=SMALL_COST,
        name="transposed",
    )(*xs, *[weight] * len(xs))


def heads_kernel(count, *refs):
    parts = refs[:count]
    weight_ref = refs[count]
    tokens = refs[count + 1 : -2]
    out_ref, local_ref = refs[-2:]
    step = pl.program_id(0)
    width = parts[0].shape[1]

    @pl.when(step == 0)
    def _():
        for j in range(count):
            local_ref[:, j * width : (j + 1) * width] = parts[j][...]

    for j in range(count):
        term = dot_nt(parts[j][...], weight_ref[:, j * width : (j + 1) * width])
        if j == 0:
            out_ref[...] = term
        else:
            out_ref[...] += term
    for index in range(len(tokens)):

        @pl.when(step == index)
        def _():
            out_ref[...] += tokens[index][...].astype(jnp.float32)


def heads_product(parts, weight, tokens):
    blocks = len(tokens)
    rows, width = tokens[0].shape
    depth = parts[0].shape[1]
    specs = [
        pl.BlockSpec((rows, depth), lambda i, j=j: (lax.rem(i + j, blocks), 0))
        for j in range(len(parts))
    ]
    whole = pl.BlockSpec((rows, width), lambda i: (0, 0), pipeline_mode=pl.Buffered(1))
    return pl.pallas_call(
        functools.partial(heads_kernel, len(parts)),
        grid=(blocks,),
        in_specs=[
            *specs,
            pl.BlockSpec(
                (width, depth * len(parts)), lambda i: (0, 0), pipeline_mode=pl.Buffered(1)
            ),
            *[whole] * blocks,
        ],
        out_specs=[
            pl.BlockSpec((rows, width), lambda i: (i, 0)),
            pl.BlockSpec((rows, depth * len(parts)), lambda i: (0, 0)),
        ],
        out_shape=[
            jax.ShapeDtypeStruct((rows * blocks, width), jnp.float32),
            jax.ShapeDtypeStruct((rows, depth * len(parts)), jnp.bfloat16),
        ],
        compiler_params=parameters(),
        cost_estimate=SMALL_COST,
        name="heads_product",
    )(*parts, weight, *tokens)


def attended_kernel(
    partial_ref, last_ref, weight_ref, gain_ref, hidden_ref, normed_ref, local_ref
):
    values = partial_ref[...] + dot_nt(last_ref[...], weight_ref[...])

    @pl.when(pl.program_id(0) == 0)
    def _():
        hidden_ref[...] = values
        local_ref[...] = last_ref[...]

    inverse = lax.rsqrt(jnp.mean(values * values, axis=-1, keepdims=True) + EPSILON)
    normed_ref[...] = (values * inverse * gain_ref[1:, :]).astype(jnp.bfloat16)


def after_attention(partial, last, weight, gain, count):
    total_rows, width = partial.shape
    rows = total_rows // count
    depth = last.shape[1]
    return pl.pallas_call(
        attended_kernel,
        grid=(count,),
        in_specs=[
            pl.BlockSpec((rows, width), lambda i: (i, 0)),
            pl.BlockSpec((rows, depth), lambda i: (lax.rem(i + count - 1, count), 0)),
            pl.BlockSpec((width, depth), lambda i: (0, count - 1)),
            pl.BlockSpec((2, width), lambda i: (0, 0)),
        ],
        out_specs=[
            pl.BlockSpec((rows, width), lambda i: (0, 0)),
            pl.BlockSpec((rows, width), lambda i: (lax.rem(i + count - 1, count), 0)),
            pl.BlockSpec((rows, depth), lambda i: (0, 0)),
        ],
        out_shape=[
            jax.ShapeDtypeStruct((rows, width), jnp.float32),
            jax.ShapeDtypeStruct((total_rows, width), jnp.bfloat16),
            jax.ShapeDtypeStruct((rows, depth), jnp.bfloat16),
        ],
        compiler_params=parameters(),
        cost_estimate=SMALL_COST,
        name="after_attention",
    )(partial, last, weight, gain)


def up_kernel(x_ref, gate_ref, up_ref, *refs):
    a_ref, u_ref, g_ref = refs[-3:]
    gate = dot_nn(x_ref[...], gate_ref[...])
    up = dot_nn(x_ref[...], up_ref[...])
    a_ref[...] = gate.astype(jnp.bfloat16)
    u_ref[...] = up.astype(jnp.bfloat16)
    g_ref[...] = (gate * jax.nn.sigmoid(gate) * up).astype(jnp.bfloat16)


def up_chunk(x, weight, kept, index, count):
    total_rows, depth = x.shape
    rows = total_rows // count
    hidden = (weight.shape[1] - depth) // 2
    tile = tile_of(hidden)
    tiles = hidden // tile
    start = depth // tile
    specs = [
        pl.BlockSpec((rows, depth), lambda t: (index, 0)),
        pl.BlockSpec((depth, tile), lambda t: (0, start + t)),
        pl.BlockSpec((depth, tile), lambda t: (0, start + tiles + t)),
    ]
    operands = [x, weight, weight]
    aliases = {}
    if kept is not None:
        specs.extend([pl.BlockSpec(memory_space=pl.ANY)] * 3)
        aliases = {len(operands) + i: i for i in range(3)}
        operands.extend(kept)
    return pl.pallas_call(
        up_kernel,
        grid=(tiles,),
        in_specs=specs,
        out_specs=[pl.BlockSpec((rows, tile), lambda t: (index, t))] * 3,
        out_shape=[jax.ShapeDtypeStruct((total_rows, hidden), jnp.bfloat16)] * 3,
        input_output_aliases=aliases,
        compiler_params=parameters(),
        cost_estimate=SMALL_COST,
        name="up_chunk",
    )(*operands)


def down_kernel(parts, tiles, *refs):
    down_ref, a_ref, u_ref, gate_ref, up_ref = refs[parts : parts + 5]
    da_ref, du_ref = refs[-5 - parts : -3 - parts]
    dx_refs = refs[-3 - parts : -3]
    da_kept, du_kept, e_out = refs[-3:]
    step = pl.program_id(0)

    @pl.when(step == 0)
    def _():
        rows = refs[0].shape[0]
        for index in range(parts):
            e_out[index * rows : (index + 1) * rows, :] = refs[index][...]

    @pl.when(step < tiles)
    def _():
        grad = dot_nn(e_out[...], down_ref[...])
        gate = a_ref[...].astype(jnp.float32)
        up = u_ref[...].astype(jnp.float32)
        sigmoid = jax.nn.sigmoid(gate)
        da = (grad * up * sigmoid * (1.0 + gate * (1.0 - sigmoid))).astype(jnp.bfloat16)
        du = (grad * gate * sigmoid).astype(jnp.bfloat16)
        da_ref[...] = da
        du_ref[...] = du
        tile = da.shape[1]
        for index in range(tiles):

            @pl.when(step == index)
            def _():
                da_kept[:, index * tile : (index + 1) * tile] = da
                du_kept[:, index * tile : (index + 1) * tile] = du

    @pl.when(step >= tiles)
    def _():
        total = dot_nt(da_kept[...], gate_ref[...]) + dot_nt(du_kept[...], up_ref[...])
        rows = total.shape[0] // parts
        for index in range(parts):
            dx_refs[index][...] = total[index * rows : (index + 1) * rows].astype(jnp.bfloat16)


def down_chunk(es, a, u, down_weight, weight, kept, index, count):
    depth, hidden = down_weight.shape
    rows = len(es) * es[0].shape[0]
    start = depth // hidden
    tile = tile_of(hidden)
    tiles = hidden // tile
    row_tile = tile_of(depth)

    def column(t):
        return jnp.minimum(t, tiles - 1)

    def row(t):
        return jnp.maximum(t - tiles, 0)

    specs = [pl.BlockSpec(es[0].shape, lambda t: (0, 0))] * len(es) + [
        pl.BlockSpec((depth, tile), lambda t: (0, column(t))),
        pl.BlockSpec((rows, tile), lambda t: (index, column(t))),
        pl.BlockSpec((rows, tile), lambda t: (index, column(t))),
        pl.BlockSpec((row_tile, hidden), lambda t: (row(t), start)),
        pl.BlockSpec((row_tile, hidden), lambda t: (row(t), start + 1)),
    ]
    operands = [*es, down_weight, a, u, weight, weight]
    part = es[0].shape
    shapes = [
        jax.ShapeDtypeStruct((rows * count, hidden), jnp.bfloat16),
        jax.ShapeDtypeStruct((rows * count, hidden), jnp.bfloat16),
        *[jax.ShapeDtypeStruct(part, jnp.bfloat16)] * len(es),
    ]
    aliases = {}
    if kept is not None:
        specs.extend([pl.BlockSpec(memory_space=pl.ANY)] * 2)
        aliases = {len(operands) + i: i for i in range(2)}
        operands.extend(kept)
    result = pl.pallas_call(
        functools.partial(down_kernel, len(es), tiles),
        grid=(tiles + depth // row_tile,),
        in_specs=specs,
        out_specs=[
            pl.BlockSpec((rows, tile), lambda t: (index, column(t))),
            pl.BlockSpec((rows, tile), lambda t: (index, column(t))),
            *[pl.BlockSpec((part[0], row_tile), lambda t: (0, row(t)))] * len(es),
        ],
        out_shape=shapes,
        input_output_aliases=aliases,
        scratch_shapes=[
            pltpu.VMEM((rows, hidden), jnp.bfloat16),
            pltpu.VMEM((rows, hidden), jnp.bfloat16),
            pltpu.VMEM((rows, depth), jnp.bfloat16),
        ],
        compiler_params=parameters(),
        cost_estimate=SMALL_COST,
        name="down_chunk",
    )(*operands)
    return result[:2], list(result[2:])


def weight_kernel(counts, blocks, split, place_ref, *refs):
    step = pl.program_id(0)
    total_refs = sum(parts + widths for parts, widths in counts)
    received = refs[total_refs] if len(refs) > total_refs + 1 else None
    place = 0
    column = 0
    for parts, widths in counts:
        x = refs[place][...]
        if parts > 1:
            x = jnp.concatenate([ref[...] for ref in refs[place : place + parts]], axis=0)
        for y_ref in refs[place + parts : place + parts + widths]:
            width = y_ref.shape[1]
            cuts = set(range(0, width, 1024)) | {width}
            if column < split < column + width and split:
                cuts.add(split - column)
            cuts = sorted(cuts)
            for first, last in zip(cuts[:-1], cuts[1:]):
                total = dot_tn(x, y_ref[:, first:last])
                start, end = column + first, column + last
                if received is None:
                    refs[-1][:, start:end] = total.astype(jnp.bfloat16)
                    continue
                total += received[:, start:end].astype(jnp.float32)
                total = total.astype(jnp.bfloat16)
                if split == 0:
                    refs[-1][:, start:end] = total
                    continue
                low = start < split
                keep = step < blocks // 2 if low else lax.rem(step, 2) == 0
                keep_ref, send_ref = refs[-4:-2] if low else refs[-2:]
                columns = slice(start, end) if low else slice(start - split, end - split)

                @pl.when(keep)
                def _():
                    keep_ref[:, columns] = total

                @pl.when(jnp.logical_not(keep))
                def _():
                    send_ref[:, columns] = total

            column += width
        place += parts + widths


def weight_product(pairs, place, count, received, ordered=False):
    depth = pairs[0][0][0].shape[1]
    blocks = count // 2
    tile = depth // count
    total = sum(y.shape[1] for _, ys in pairs for y in ys)
    split = 0 if ordered else -(-total // 256) * 128
    side = 1 if received is None else 0

    def source(t, p):
        if ordered:
            return 2 * t + lax.rem(p[0] + side, 2)
        return lax.bitwise_xor(p[0], 2 * t + side)

    whole = pl.BlockSpec((tile, total), lambda t, p: (t, 0))
    if received is None or ordered:
        out_specs = whole
        out_shape = jax.ShapeDtypeStruct((depth // 2, total), jnp.bfloat16)
    else:
        half = blocks // 2
        out_specs = [
            pl.BlockSpec((tile, split), lambda t, p: (jnp.minimum(t, half - 1), 0)),
            pl.BlockSpec((tile, split), lambda t, p: (jnp.maximum(t - half, 0), 0)),
            pl.BlockSpec((tile, total - split), lambda t, p: (t // 2, 0)),
            pl.BlockSpec((tile, total - split), lambda t, p: (t // 2, 0)),
        ]
        out_shape = [
            jax.ShapeDtypeStruct((depth // 4, width), jnp.bfloat16)
            for width in (split, split, total - split, total - split)
        ]
    specs = []
    operands = []
    for xs, ys in pairs:
        for x in xs:
            specs.append(pl.BlockSpec((x.shape[0], tile), lambda t, p: (0, source(t, p))))
        specs += [
            pl.BlockSpec(y.shape, lambda t, p: (0, 0), pipeline_mode=pl.Buffered(1)) for y in ys
        ]
        operands.extend([*xs, *ys])
    if received is not None:
        specs.append(whole)
        operands.append(received)
    return pl.pallas_call(
        functools.partial(
            weight_kernel, [(len(xs), len(ys)) for xs, ys in pairs], blocks, split
        ),
        grid_spec=pltpu.PrefetchScalarGridSpec(
            num_scalar_prefetch=1, grid=(blocks,), in_specs=specs, out_specs=out_specs
        ),
        out_shape=out_shape,
        compiler_params=parameters(),
        cost_estimate=SMALL_COST,
        name="weight_product",
    )(place, *operands)


def fold_kernel(counts, *refs):
    outs = refs[sum(counts) :]
    place = 0
    row = 0
    for index, count in enumerate(counts):
        total = refs[place][...].astype(jnp.float32)
        for ref in refs[place + 1 : place + count]:
            total += ref[...].astype(jnp.float32)
        out = outs[index % 2]
        rows = total.shape[0]
        out[row : row + rows, :] = total.astype(jnp.bfloat16)
        row += rows * (index % 2)
        place += count


def fold(sums, rows):
    counts = [len(terms) for pair in sums for terms in pair]
    values = [value for pair in sums for terms in pair for value in terms]
    widths = [terms[0].shape[1] for terms in sums[0]]
    steps = 2 if all(width % 256 == 0 for width in widths) else 1
    return pl.pallas_call(
        functools.partial(fold_kernel, counts),
        grid=(steps,),
        in_specs=[
            pl.BlockSpec((rows, value.shape[1] // steps), lambda t: (1, t)) for value in values
        ],
        out_specs=[
            pl.BlockSpec((rows * len(sums), width // steps), lambda t: (0, t))
            for width in widths
        ],
        out_shape=[
            jax.ShapeDtypeStruct((rows * len(sums), width), jnp.bfloat16) for width in widths
        ],
        compiler_params=parameters(),
        cost_estimate=SMALL_COST,
        name="fold",
    )(*values)


def residual_kernel(parts, e_ref, hidden_ref, first_ref, second_ref, gain_ref, weight_ref, *refs):
    dh_ref, dz_ref = refs[:2]
    dh, dz = refs[-2:]
    step = pl.program_id(0)
    tile = weight_ref.shape[1]

    @pl.when(step == 0)
    def _():
        values = hidden_ref[...]
        inverse = lax.rsqrt(jnp.mean(values * values, axis=-1, keepdims=True) + EPSILON)
        scaled = values * inverse
        grad = first_ref[...].astype(jnp.float32) + second_ref[...].astype(jnp.float32)
        grad = grad * gain_ref[1:, :]
        projection = jnp.mean(grad * scaled, axis=-1, keepdims=True)
        total = e_ref[...].astype(jnp.float32) + inverse * (grad - scaled * projection)
        dh[...] = total
        dz[...] = total.astype(jnp.bfloat16)

    result = dot_nn(dz[...], weight_ref[...]).astype(jnp.bfloat16)
    for index in range(parts):

        @pl.when(step == index)
        def _():
            columns = slice(index * tile, (index + 1) * tile)
            dh_ref[...] = dh[:, columns]
            dz_ref[...] = dz[:, columns]
            refs[2 + index][...] = result


def residual_gradient(e, hidden_res, first, second, gain, weight, parts):
    rows, depth = e.shape
    tile = depth // parts
    whole = pl.BlockSpec((rows, depth), lambda t: (0, 0))
    column = pl.BlockSpec((rows, tile), lambda t: (0, t))
    result = pl.pallas_call(
        functools.partial(residual_kernel, parts),
        grid=(parts,),
        in_specs=[
            whole,
            whole,
            whole,
            whole,
            pl.BlockSpec((2, depth), lambda t: (0, 0)),
            pl.BlockSpec((depth, tile), lambda t: (0, t)),
        ],
        out_specs=[column, column] + [pl.BlockSpec((rows, tile), lambda t: (0, 0))] * parts,
        out_shape=[
            jax.ShapeDtypeStruct((rows, depth), jnp.float32),
            jax.ShapeDtypeStruct((rows, depth), jnp.bfloat16),
            *[jax.ShapeDtypeStruct((rows, tile), jnp.bfloat16)] * parts,
        ],
        scratch_shapes=[
            pltpu.VMEM((rows, depth), jnp.float32),
            pltpu.VMEM((rows, depth), jnp.bfloat16),
        ],
        compiler_params=parameters(),
        cost_estimate=SMALL_COST,
        name="residual_gradient",
    )(e, hidden_res, first, second, gain, weight)
    return result[0], result[1], list(result[2:])


def tie(value, *others):
    return lax.optimization_barrier((value, others))[0]


def together(*values):
    return lax.optimization_barrier(values)


def add(first, second):
    return (first.astype(jnp.float32) + second.astype(jnp.float32)).astype(jnp.bfloat16)


class Mover:
    def __init__(self):
        self.dp_count = lax.axis_size("dp")
        self.ring = lax.axis_size("tensor")
        self.steps = []
        step = 2
        while step < self.dp_count:
            self.steps.append(step)
            step *= 2

    def swap(self, value, step):
        return lax.ppermute(value, "dp", [(i, i ^ step) for i in range(self.dp_count)])

    def gather(self, shard):
        return lax.all_gather(shard, "dp", axis=0, tiled=True)


    def send(self, pieces, level):
        orders = (self.steps[::-1], self.steps[:1] + self.steps[:0:-1])
        return [self.swap(piece, order[level]) for piece, order in zip(pieces, orders)]

    def begin(self, pieces):
        moved = self.send([pieces[1], pieces[3]], 0)
        return [[pieces[0], moved[0]], [pieces[2], moved[1]]]

    def fold(self, sums, level=1):
        return fold(sums, sums[0][0][0].shape[0] >> level)

    def advance(self, sums, folded):
        level = 1
        while True:
            moved = self.send(folded, level)
            level += 1
            if level == len(self.steps):
                return sums, moved
            rows = moved[0].shape[0] // len(sums)
            sums = [
                [
                    terms + [part[index * rows : (index + 1) * rows]]
                    for terms, part in zip(pair, moved)
                ]
                for index, pair in enumerate(sums)
            ]
            folded = self.fold(sums, level)

    def advance_all(self, sums):
        widths = {pair[0][0].shape[1] for pair in sums}
        parts = [sums] if len(widths) == 1 else [[pair] for pair in sums]
        return [self.advance(part, self.fold(part)) for part in parts]

    def scatter(self, total):
        groups = [list(range(core, self.dp_count, 2)) for core in range(2)]
        return lax.psum_scatter(
            total, "dp", scatter_dimension=0, tiled=True, axis_index_groups=groups
        )

    def hop(self, value, shift=1):
        return lax.ppermute(
            value, "tensor", [(i, (i + shift) % self.ring) for i in range(self.ring)]
        )

    def spread(self, value):
        ring = self.ring
        return [value] + [
            lax.ppermute(value, "tensor", [(i, (i - j) % ring) for i in range(ring)])
            for j in range(1, ring)
        ]

    def collect(self, parts):
        ring = self.ring
        total = parts[0]
        for j in range(1, ring):
            moved = lax.ppermute(
                parts[j].astype(jnp.bfloat16), "tensor", [(i, (i + j) % ring) for i in range(ring)]
            )
            total = total + moved.astype(jnp.float32)
        return total

    def exchange(self, parts):
        ring = self.ring
        return [parts[0]] + [
            lax.ppermute(parts[j], "tensor", [(i, (i + j) % ring) for i in range(ring)])
            for j in range(1, ring)
        ]


def totals_of(sums, moved):
    rows = moved[0].shape[0] // len(sums)
    result = []
    for index, pair in enumerate(sums):
        halves = []
        for terms, last in zip(pair, moved):
            total = last[index * rows : (index + 1) * rows].astype(jnp.float32)
            for term in terms:
                total = total + term[:rows].astype(jnp.float32)
            halves.append(total)
        result.append(jnp.concatenate(halves, axis=1))
    return result


def back_norm(grad_normed, scaled, inverse, scale_row):
    grad_scaled = grad_normed * scale_row
    projection = jnp.mean(grad_scaled * scaled, axis=-1, keepdims=True)
    return inverse * (grad_scaled - scaled * projection)


def per_device(
    tokens,
    seq_lengths,
    attention_gain,
    query_matrix,
    key_matrix,
    value_matrix,
    output_weight,
    feedforward_gain,
    gate_weight,
    up_weight,
    down_weight,
    cotangent,
):
    mover = Mover()
    dp_count = mover.dp_count
    ring = mover.ring
    dp_place = lax.axis_index("dp").astype(jnp.int32).reshape(1)
    ring_place = lax.axis_index("tensor")
    place = ring_place.astype(jnp.int32).reshape(1)
    _, local_rows, model_width = tokens.shape
    complete_rows = local_rows * ring
    hidden = gate_weight.shape[1]
    groups = key_matrix.shape[1] // HEAD_SIZE
    joint_width = groups * GROUP_WIDTH
    f32 = jnp.float32
    b16 = jnp.bfloat16

    doc_ids, positions = layout(seq_lengths, complete_rows)
    row_index = jnp.arange(complete_rows, dtype=jnp.int32)
    doc_ids = jnp.where(doc_ids[0] < PIECES, doc_ids[0], PIECES + row_index)

    def to_relative(values):
        view = values.reshape((ring, local_rows) + values.shape[1:])
        return jnp.roll(view, -(ring_place + 1), axis=0)[::-1].reshape(values.shape)

    doc_ids = to_relative(doc_ids)
    cosine, sine = rope_tables(to_relative(positions[0]), HEAD_SIZE)
    cosine_table = jnp.tile(cosine, (1, 128 // cosine.shape[1]))
    sine_table = jnp.tile(jnp.concatenate([-sine, sine], axis=1), (1, 128 // HEAD_SIZE))

    own_gains = jnp.pad(jnp.stack([attention_gain, feedforward_gain]), ((0, 126), (0, 0)))
    joint_matrix, packed = pack(query_matrix, key_matrix, value_matrix, own_gains, groups)
    joint_full = mover.gather(packed)
    output_parts = mover.spread(output_weight.T)
    up_shard = jnp.pad(
        jnp.concatenate([gate_weight, up_weight], axis=1), ((0, 0), (model_width, 0))
    )
    output_parts, cosine_table, sine_table, doc_ids, up_shard, down_shard = together(
        output_parts, cosine_table, sine_table, doc_ids, up_shard, down_weight.T
    )
    local_tokens = tokens[0]
    token_chunks = [local_tokens, mover.hop(local_tokens)]
    up_shard = join(output_parts, up_shard)
    up_full = mover.gather(up_shard)
    down_full = mover.gather(tie(down_shard, up_shard))
    gains = joint_full[:, joint_width : joint_width + 2].T.astype(f32)

    def projection(kept, index):
        return project(
            token_chunks[index],
            gains,
            joint_full,
            cosine_table,
            sine_table,
            kept,
            index,
            ring,
            groups,
        )

    kept = projection(None, 0)
    for j in range(1, ring):
        token_chunks[j], kept, gains = together(token_chunks[j], kept, gains)
        if j + 1 < ring:
            token_chunks.append(mover.hop(token_chunks[j]))
        else:
            local_cotangent = tie(cotangent[0], token_chunks[j])
            moved = mover.hop(local_cotangent)
        kept = projection(kept, j)
    normed_one, joint = kept
    attended, totals = attention_forward(joint, doc_ids, place, ring, groups)
    moved, attended = together(moved, attended)
    cotangent_chunks = [local_cotangent, moved]
    attended_parts = [attended]
    while len(attended_parts) < ring:
        part = mover.hop(attended_parts[-1], -1)
        if len(attended_parts) == ring - 1:
            partial, attended_local = heads_product(
                tie(attended_parts, attended_parts[-1]), up_full, token_chunks
            )
            part, partial, attended_local = together(part, partial, attended_local)
        attended_parts.append(part)
    moved, last = together(moved, attended_parts[-1])

    pairs = ring // 2
    moved = mover.hop(moved)
    hidden_res, normed_two, attended_last = after_attention(partial, last, up_full, gains, ring)
    upward = up_chunk(normed_two, up_full, None, 0, pairs)
    downward = None
    grads = []

    def chunks_of(pair):
        return [cotangent_chunks[(2 * pair + i) % ring] for i in (1, 2)]

    def lower(pair, kept):
        return down_chunk(
            chunks_of(pair), upward[0], upward[1], down_full, up_full, kept, pair, pairs
        )

    for j in range(2, ring):
        if j > 2:
            moved = mover.hop(moved)
            if j % 2:
                downward, parts = lower((j - 3) // 2, downward)
                grads.extend(parts)
            else:
                upward = up_chunk(normed_two, up_full, upward, j // 2 - 1, pairs)
        moved, upward, downward, grads = together(moved, upward, downward, grads)
        cotangent_chunks.append(moved)

    def weights(xs, ys, received=None):
        return weight_product([(xs, ys)], dp_place, dp_count, received)

    ordered = cotangent_chunks[1:] + cotangent_chunks[:1]
    total = grads[0]
    moved = mover.hop(total)
    upward = up_chunk(tie(normed_two, total), up_full, upward, pairs - 1, pairs)
    product = upward[2]
    down_part = weight_product([(ordered, [product])], dp_place, dp_count, None, True)
    moved, upward, down_part = together(moved, upward, down_part)
    down_part = mover.swap(down_part, 1)
    for j in range(2, ring):
        total = add(moved, grads[j - 1])
        moved = mover.hop(total)
        if j == 2:
            downward, parts = lower(pairs - 1, tie(downward, total))
            grads.extend(parts)
            moved, downward, grads = together(moved, downward, grads)
            grad_gate, grad_up = downward
        if j == 3:
            gate_part = weights([tie(normed_two, total)], [grad_gate])
            branch = transposed_product(
                [tie(product, gate_part)], down_full, 0, ring // 2, 0, 2
            )
            down_part = weight_product(
                [(tie(ordered, branch), [product])], dp_place, dp_count, down_part, True
            )
            moved, gate_part, branch, down_part = together(moved, gate_part, branch, down_part)
    gate_part = mover.swap(gate_part, 1)
    down_out = mover.scatter(down_part)
    grad_hidden, grad_branch, grad_parts = residual_gradient(
        local_cotangent, hidden_res, moved, grads[-1], gains, up_full, ring
    )
    grad_hidden, grad_branch, grad_parts, gate_part = together(
        grad_hidden, grad_branch, grad_parts, gate_part
    )

    grad_parts = mover.exchange(grad_parts)
    output_part = weights([grad_branch], [attended_local, attended_last])
    gate_part = weights([tie(normed_two, output_part)], [grad_gate], gate_part)
    grad_parts, output_part, gate_part = together(grad_parts, output_part, gate_part)
    grad_joint = []
    sent = 0
    moved = branch[0]
    for group in range(groups):
        moved = mover.hop(moved)
        sent += 1
        if group == 0:
            output_part = mover.swap(output_part, 1)
        else:
            output_part = mover.begin(output_part)
        grad_joint.append(
            attention_backward(
                joint,
                attended,
                tie(grad_parts, grad_joint),
                totals,
                doc_ids,
                cosine_table,
                sine_table,
                place,
                group,
            )
        )
        if group == 0:
            output_part = weights(
                [tie(grad_branch, grad_joint)], [attended_local, attended_last], output_part
            )
        if group + 1 == groups:
            grads = transposed_product(grad_joint, joint_full, 0, ring)
        moved, grad_joint, grads, output_part, down_out = together(
            moved, grad_joint, grads, output_part, down_out
        )
        if group + 1 < groups:
            moved = add(moved, branch[sent])
    if groups == 1:
        output_part = mover.begin(output_part)
    branch_moved = moved
    moved = grads[0]

    def last_weights(total, received):
        return weight_product(
            [([tie(normed_two, total)], [grad_up]), ([normed_one], grad_joint)],
            dp_place,
            dp_count,
            received,
        )

    for j in range(1, ring):
        total = grads[1] if j == 1 else add(moved, grads[j])
        moved = mover.hop(total)
        if j == 1:
            gate_part = mover.begin(gate_part)
            last_part = last_weights(total, None)
            branch = branch + transposed_product(
                [tie(product, last_part)], down_full, 0, ring // 2, 1, 2
            )
            next_branch = add(branch_moved, branch[sent])
            moved, last_part, branch, output_part, gate_part, next_branch = together(
                moved, last_part, branch, output_part, gate_part, next_branch
            )
        if j == 2:
            both_parts = tie([output_part, gate_part], total)
            both_parts = mover.advance_all(both_parts)
            last_part = last_weights(total, mover.swap(last_part, 1))
            moved, last_part, both_parts = together(moved, last_part, both_parts)
            down_out = tie(down_out, both_parts)
        if j == 3:
            last_part = mover.begin(last_part)
            branch_moved = mover.hop(tie(next_branch, total))
            sent += 1
            output_out, gate_out = [total for part in both_parts for total in totals_of(*part)]
            output_out = jnp.split(output_out, ring, axis=1)
            moved, last_part, output_out = together(moved, last_part, output_out)
    folded, output_out = together(mover.fold([last_part]), output_out)
    last_part = mover.advance([last_part], folded)
    output_out = mover.collect(output_out[:-1] + [tie(output_out[-1], last_part[1][1])]).T
    scaled_one, inverse_one = norm_rows(local_tokens.astype(f32))
    local_one = moved.astype(f32) + grads[0].astype(f32)
    input_gradient = grad_hidden + back_norm(local_one, scaled_one, inverse_one, gains[:1])
    branch_moved, last_part = together(branch_moved, last_part)
    for j in range(sent, ring - 1):
        branch_moved = mover.hop(add(branch_moved, branch[j]))
    block_output = (
        hidden_res + (branch_moved.astype(f32) + branch[-1].astype(f32))
    ).astype(b16)
    last_out = totals_of(*last_part)[0]
    up_out, joint_out = last_out[:, :hidden], last_out[:, hidden:]

    sums = jnp.stack(
        [
            jnp.sum(joint_out * joint_matrix.astype(f32), axis=1) / attention_gain.astype(f32),
            jnp.sum(gate_out * gate_weight.astype(f32) + up_out * up_weight.astype(f32), axis=1)
            / feedforward_gain.astype(f32),
        ]
    )
    gain_out = sums
    for shift in range(1, ring):
        gain_out = gain_out + tie(
            lax.ppermute(sums, "tensor", [(i, (i + shift) % ring) for i in range(ring)]),
            output_out,
        )

    def ungrouped(first, width):
        return jnp.concatenate(
            [
                joint_out[:, g * GROUP_WIDTH + first : g * GROUP_WIDTH + first + width]
                for g in range(groups)
            ],
            axis=1,
        )

    return (
        block_output[None],
        input_gradient[None],
        gain_out[0],
        ungrouped(0, GROUP_QUERY),
        ungrouped(GROUP_QUERY, HEAD_SIZE),
        ungrouped(GROUP_QUERY + HEAD_SIZE, HEAD_SIZE),
        output_out,
        gain_out[1],
        gate_out,
        up_out,
        down_out.astype(f32).T,
    )


def solution(mesh):
    return jax.shard_map(
        per_device,
        mesh=mesh,
        in_specs=(
            P("dp", "tensor", None),
            P("dp", None),
            P("dp"),
            P("dp", "tensor"),
            P("dp", "tensor"),
            P("dp", "tensor"),
            P("tensor", "dp"),
            P("dp"),
            P("dp", "tensor"),
            P("dp", "tensor"),
            P("tensor", "dp"),
            P("dp", "tensor", None),
        ),
        out_specs=(
            P("dp", "tensor", None),
            P("dp", "tensor", None),
            P("dp"),
            P("dp", "tensor"),
            P("dp", "tensor"),
            P("dp", "tensor"),
            P("tensor", "dp"),
            P("dp"),
            P("dp", "tensor"),
            P("dp", "tensor"),
            P("tensor", "dp"),
        ),
        check_vma=False,
    )
```

```python
import functools
import math

import jax
import jax.numpy as jnp
from jax import lax
from jax.experimental import pallas as pl
from jax.experimental.pallas import tpu as pltpu
from jax.sharding import PartitionSpec as P

QUERY_HEADS = 32
KEY_VALUE_HEADS = 8
HEAD_SIZE = 64
PIECES = 4


EPSILON = 1e-05
ROPE_BASE = 500000.0
NEGATIVE = -1e30
GROUP_QUERY = QUERY_HEADS // KEY_VALUE_HEADS * HEAD_SIZE
GROUP_WIDTH = GROUP_QUERY + 2 * HEAD_SIZE
KERNEL_VMEM = 60 * 1024 * 1024
SMALL_COST = pl.CostEstimate(flops=1, bytes_accessed=1, transcendentals=0)


def layout(lengths, complete_rows):
    doc_ends = jnp.cumsum(lengths, axis=-1)
    row_index = jnp.arange(complete_rows, dtype=jnp.int32)
    piece_count = lengths.shape[-1]
    doc_ids = jnp.sum((row_index[None, :, None] >= doc_ends[:, None, :]).astype(jnp.int32), axis=2)
    starts = doc_ends - lengths
    chosen = doc_ids[:, :, None] == jnp.arange(piece_count, dtype=jnp.int32)[None, None, :]
    doc_begin = jnp.sum(jnp.where(chosen, starts[:, None, :], 0), axis=2) + jnp.where(
        doc_ids == piece_count, doc_ends[:, -1:], 0
    )
    return (doc_ids, row_index[None, :] - doc_begin)


def rope_tables(positions, head_dim):
    half_dim = head_dim // 2
    frequency = ROPE_BASE ** (-(jnp.arange(half_dim, dtype=jnp.float32) * (2.0 / head_dim)))
    angles = positions.astype(jnp.float32)[..., None] * frequency
    return (jnp.cos(angles), jnp.sin(angles))


def norm_rows(values):
    inverse = lax.rsqrt(jnp.mean(values * values, axis=-1, keepdims=True) + EPSILON)
    return (values * inverse, inverse)


def dot_nt(left, right):
    return lax.dot_general(
        left, right, (((1,), (1,)), ((), ())), preferred_element_type=jnp.float32
    )


def dot_nn(left, right):
    return jnp.dot(left, right, preferred_element_type=jnp.float32)


def dot_tn(left, right):
    return lax.dot_general(
        left, right, (((0,), (0,)), ((), ())), preferred_element_type=jnp.float32
    )


def tile_of(size, limit=512):
    tile = limit
    while size % tile:
        tile //= 2
    return tile


def parameters():
    return pltpu.CompilerParams(vmem_limit_bytes=KERNEL_VMEM)


def swap_halves(values):
    lane = lax.broadcasted_iota(jnp.int32, values.shape, 1)
    half = HEAD_SIZE // 2
    return jnp.where(
        lane % HEAD_SIZE < half, pltpu.roll(values, 128 - half, 1), pltpu.roll(values, half, 1)
    )


def turned(values, cosine, sine, start):
    result = values * cosine + swap_halves(values) * sine
    rotated = GROUP_WIDTH - HEAD_SIZE
    if start + 128 <= rotated:
        return result
    lane = lax.broadcasted_iota(jnp.int32, values.shape, 1)
    return jnp.where(lane < rotated - start, result, values)


def project_kernel(x_ref, gain_ref, weight_ref, cos_ref, sin_ref, *refs):
    normed_ref, joint_ref = refs[-2:]

    @pl.when(pl.program_id(0) == 0)
    def _():
        values = x_ref[...].astype(jnp.float32)
        inverse = lax.rsqrt(jnp.mean(values * values, axis=-1, keepdims=True) + EPSILON)
        normed_ref[...] = (values * inverse * gain_ref[:1, :]).astype(jnp.bfloat16)

    product = dot_nn(normed_ref[...], weight_ref[...])
    for start in range(0, GROUP_WIDTH, 128):
        part = turned(product[:, start : start + 128], cos_ref[...], sin_ref[...], start)
        if start < GROUP_QUERY:
            part = part * HEAD_SIZE ** (-0.5)
        joint_ref[:, start : start + 128] = part.astype(jnp.bfloat16)


def project(x, gain, weight, cosine, sine, kept, index, count, groups):
    rows, depth = x.shape
    specs = [
        pl.BlockSpec((rows, depth), lambda g: (0, 0)),
        pl.BlockSpec((2, depth), lambda g: (0, 0)),
        pl.BlockSpec((depth, GROUP_WIDTH), lambda g: (0, g)),
        pl.BlockSpec((rows, 128), lambda g: (index, 0)),
        pl.BlockSpec((rows, 128), lambda g: (index, 0)),
    ]
    operands = [x, gain, weight, cosine, sine]
    aliases = {}
    if kept is not None:
        specs.extend([pl.BlockSpec(memory_space=pl.ANY)] * 2)
        aliases = {len(operands) + i: i for i in range(2)}
        operands.extend(kept)
    return pl.pallas_call(
        project_kernel,
        grid=(groups,),
        in_specs=specs,
        out_specs=[
            pl.BlockSpec((rows, depth), lambda g: (index, 0)),
            pl.BlockSpec((rows, GROUP_WIDTH), lambda g: (index, g)),
        ],
        out_shape=[
            jax.ShapeDtypeStruct((rows * count, depth), jnp.bfloat16),
            jax.ShapeDtypeStruct((rows * count, GROUP_WIDTH * groups), jnp.bfloat16),
        ],
        input_output_aliases=aliases,
        compiler_params=parameters(),
        cost_estimate=SMALL_COST,
        name="project",
    )(*operands)


def ring_offset(place, chunk, count, rows):
    return pl.multiple_of(lax.rem(place - chunk + count, count) * rows, rows)


def stack_heads(target, source):
    rows, width = source.shape
    for head in range(width // HEAD_SIZE):
        target[head * rows : (head + 1) * rows, :] = source[
            :, head * HEAD_SIZE : (head + 1) * HEAD_SIZE
        ]


def fill_bias(bias, key_docs, query_docs, earlier):
    rows = key_docs.shape[0]
    row_index = lax.broadcasted_iota(jnp.int32, (rows, rows), 0)
    column_index = lax.broadcasted_iota(jnp.int32, (rows, rows), 1)
    same = (key_docs == query_docs) & ((row_index <= column_index) | earlier)
    values = jnp.where(same, 0.0, NEGATIVE)
    for first in range(0, bias.shape[1], rows):
        bias[:, first : first + rows] = values


def forward_kernel(
    count,
    place_ref,
    own_ref,
    all_ref,
    docq_ref,
    dock_ref,
    o_ref,
    lse_ref,
    bias,
    queries,
    values_all,
    mixed,
):
    chunk = pl.program_id(1)
    place = place_ref[0]
    rows = own_ref.shape[0]
    heads = GROUP_QUERY // HEAD_SIZE
    stack_heads(queries, own_ref.at[:, :GROUP_QUERY])

    @pl.when(chunk == 0)
    def _():
        values = all_ref[:, GROUP_QUERY:].astype(jnp.float32)
        values_all[...] = values.T[HEAD_SIZE:].astype(jnp.bfloat16)

    mixed[...] = jnp.zeros_like(mixed)

    def block(j, carry):
        peaks, total = carry
        offset = ring_offset(place, j, count, rows)
        piece = pl.ds(offset, rows)
        fill_bias(bias, dock_ref[piece, :], docq_ref[...], j < chunk)
        keys = all_ref[piece, GROUP_QUERY : GROUP_QUERY + HEAD_SIZE]
        scores = dot_nt(keys, queries[...]) + bias[...]
        higher = jnp.maximum(peaks, jnp.max(scores, axis=0, keepdims=True))
        probs = jnp.exp(scores - higher)
        scale = jnp.exp(peaks - higher)
        mixed[...] = mixed[...] * scale + dot_nn(
            values_all[:, piece], probs.astype(jnp.bfloat16)
        )
        return higher, total * scale + jnp.sum(probs, axis=0, keepdims=True)

    peaks, total = lax.fori_loop(
        0,
        chunk + 1,
        block,
        (
            jnp.full((1, heads * rows), NEGATIVE, jnp.float32),
            jnp.zeros((1, heads * rows), jnp.float32),
        ),
    )
    lse_ref[:1, :] = peaks + jnp.log(total)
    result = mixed[...] / total
    for head in range(0, heads, 2):
        pair = jnp.concatenate(
            [result[:, (head + i) * rows : (head + i + 1) * rows] for i in range(2)], axis=0
        )
        o_ref[:, head * HEAD_SIZE : (head + 2) * HEAD_SIZE] = pair.T.astype(jnp.bfloat16)


def attention_forward(joint, docs, place, count, groups):
    total_rows = joint.shape[0]
    rows = total_rows // count
    stacked = rows * GROUP_QUERY // HEAD_SIZE

    def block(c, place_ref):
        return lax.rem(place_ref[0] - c + count, count)

    spec = pltpu.PrefetchScalarGridSpec(
        num_scalar_prefetch=1,
        grid=(groups, count),
        in_specs=[
            pl.BlockSpec((rows, GROUP_WIDTH), lambda g, c, p: (block(c, p), g)),
            pl.BlockSpec((total_rows, GROUP_WIDTH), lambda g, c, p: (0, g)),
            pl.BlockSpec((1, rows), lambda g, c, p: (0, block(c, p))),
            pl.BlockSpec((total_rows, 1), lambda g, c, p: (0, 0)),
        ],
        out_specs=[
            pl.BlockSpec((rows, GROUP_QUERY), lambda g, c, p: (block(c, p), g)),
            pl.BlockSpec((8, stacked), lambda g, c, p: (g, block(c, p))),
        ],
        scratch_shapes=[
            pltpu.VMEM((rows, stacked), jnp.float32),
            pltpu.VMEM((stacked, HEAD_SIZE), jnp.bfloat16),
            pltpu.VMEM((HEAD_SIZE, total_rows), jnp.bfloat16),
            pltpu.VMEM((HEAD_SIZE, stacked), jnp.float32),
        ],
    )
    return pl.pallas_call(
        functools.partial(forward_kernel, count),
        grid_spec=spec,
        out_shape=[
            jax.ShapeDtypeStruct((total_rows, GROUP_QUERY * groups), jnp.bfloat16),
            jax.ShapeDtypeStruct((8 * groups, stacked * count), jnp.float32),
        ],
        compiler_params=parameters(),
        cost_estimate=SMALL_COST,
        name="attend",
    )(place, joint, joint, docs[None, :], docs[:, None])


def backward_kernel(count, place_ref, *refs):
    own_ref, all_ref, o_ref = refs[:3]
    lse_ref, docq_ref, dock_ref, cos_ref, sin_ref = refs[3 + count : 8 + count]
    out_ref, bias, queries, grads, keys_all, values_all, sum_q, sum_k, sum_v = refs[8 + count :]
    chunk = pl.program_id(0)
    place = place_ref[0]
    rows = own_ref.shape[0]
    heads = GROUP_QUERY // HEAD_SIZE
    stack_heads(queries, own_ref.at[:, :GROUP_QUERY])
    for index in range(count):

        @pl.when(lax.rem(place - chunk + count, count) == index)
        def _():
            stack_heads(grads, refs[3 + index])

    @pl.when(chunk == 0)
    def _():
        keys_all[...] = all_ref[:, GROUP_QUERY : GROUP_QUERY + HEAD_SIZE]
        values_all[...] = all_ref[:, GROUP_QUERY + HEAD_SIZE :]
        sum_k[...] = jnp.zeros_like(sum_k)
        sum_v[...] = jnp.zeros_like(sum_v)

    sum_q[...] = jnp.zeros_like(sum_q)
    ones = jnp.ones((8, HEAD_SIZE), jnp.bfloat16)
    inner = []
    for head in range(heads):
        attended = o_ref[:, head * HEAD_SIZE : (head + 1) * HEAD_SIZE].astype(jnp.float32)
        both = attended * grads[head * rows : (head + 1) * rows, :].astype(jnp.float32)
        high = both.astype(jnp.bfloat16)
        low = (both - high.astype(jnp.float32)).astype(jnp.bfloat16)
        inner.append((dot_nt(ones, high) + dot_nt(ones, low))[:1])
    inner = jnp.concatenate(inner, axis=1)

    def block(j, carry):
        offset = ring_offset(place, j, count, rows)
        piece = pl.ds(offset, rows)
        fill_bias(bias, dock_ref[piece, :], docq_ref[...], j < chunk)
        probs = jnp.exp(dot_nt(keys_all[piece, :], queries[...]) + bias[...] - lse_ref[:1, :])
        grad_probs = dot_nt(values_all[piece, :], grads[...])
        grad_scores = (probs * (grad_probs - inner)).astype(jnp.bfloat16)
        sum_v[piece, :] += dot_nn(probs.astype(jnp.bfloat16), grads[...])
        sum_k[piece, :] += dot_nn(grad_scores, queries[...])
        sum_q[...] += dot_tn(grad_scores, keys_all[piece, :])
        return carry

    lax.fori_loop(0, chunk + 1, block, 0)
    own = pl.ds(ring_offset(place, chunk, count, rows), rows)
    for first in range(0, heads, 2):
        start = first * HEAD_SIZE
        part = jnp.concatenate(
            [sum_q[(first + i) * rows : (first + i + 1) * rows, :] for i in range(2)], axis=1
        )
        part = turned(part, cos_ref[own, :], -sin_ref[own, :], start)
        out_ref[own, start : start + 128] = (part * HEAD_SIZE ** (-0.5)).astype(jnp.bfloat16)

    @pl.when(chunk == count - 1)
    def _():
        part = jnp.concatenate([sum_k[...], sum_v[...]], axis=1)
        part = turned(part, cos_ref[...], -sin_ref[...], GROUP_QUERY)
        out_ref[:, GROUP_QUERY:] = part.astype(jnp.bfloat16)


def attention_backward(joint, attended, grads, lse, docs, cosine, sine, place, group):
    count = len(grads)
    total_rows = joint.shape[0]
    rows = total_rows // count
    stacked = rows * GROUP_QUERY // HEAD_SIZE

    def block(c, place_ref):
        return lax.rem(place_ref[0] - c + count, count)

    table = pl.BlockSpec((total_rows, 128), lambda c, p: (0, 0))
    spec = pltpu.PrefetchScalarGridSpec(
        num_scalar_prefetch=1,
        grid=(count,),
        in_specs=[
            pl.BlockSpec((rows, GROUP_WIDTH), lambda c, p: (block(c, p), group)),
            pl.BlockSpec((total_rows, GROUP_WIDTH), lambda c, p: (0, group)),
            pl.BlockSpec((rows, GROUP_QUERY), lambda c, p: (block(c, p), group)),
            *[pl.BlockSpec((rows, GROUP_QUERY), lambda c, p: (0, group))] * count,
            pl.BlockSpec((8, stacked), lambda c, p: (group, block(c, p))),
            pl.BlockSpec((1, rows), lambda c, p: (0, block(c, p))),
            pl.BlockSpec((total_rows, 1), lambda c, p: (0, 0)),
            table,
            table,
        ],
        out_specs=pl.BlockSpec((total_rows, GROUP_WIDTH), lambda c, p: (0, 0)),
        scratch_shapes=[
            pltpu.VMEM((rows, stacked), jnp.float32),
            *[pltpu.VMEM((stacked, HEAD_SIZE), jnp.bfloat16)] * 2,
            *[pltpu.VMEM((total_rows, HEAD_SIZE), jnp.bfloat16)] * 2,
            pltpu.VMEM((stacked, HEAD_SIZE), jnp.float32),
            *[pltpu.VMEM((total_rows, HEAD_SIZE), jnp.float32)] * 2,
        ],
    )
    return pl.pallas_call(
        functools.partial(backward_kernel, count),
        grid_spec=spec,
        out_shape=jax.ShapeDtypeStruct((total_rows, GROUP_WIDTH), jnp.bfloat16),
        compiler_params=parameters(),
        cost_estimate=SMALL_COST,
        name="attend_back",
    )(
        place,
        joint,
        joint,
        attended,
        *grads,
        lse,
        docs[None, :],
        docs[:, None],
        cosine,
        sine,
    )


def pack_kernel(groups, query_ref, key_ref, value_ref, gain_ref, joint_ref, out_ref):
    for g in range(groups):
        start = g * GROUP_WIDTH
        columns = slice(g * HEAD_SIZE, (g + 1) * HEAD_SIZE)
        joint_ref[:, start : start + GROUP_QUERY] = query_ref[
            :, g * GROUP_QUERY : (g + 1) * GROUP_QUERY
        ]
        joint_ref[:, start + GROUP_QUERY : start + GROUP_WIDTH] = jnp.concatenate(
            [key_ref[:, columns], value_ref[:, columns]], axis=1
        )
    width = groups * GROUP_WIDTH
    out_ref[:, :width] = joint_ref[...]
    out_ref[:, width:] = gain_ref[...].astype(jnp.float32).T.astype(jnp.bfloat16)


def pack(query, key, value, gains, groups):
    rows = query.shape[0]
    width = groups * GROUP_WIDTH
    return pl.pallas_call(
        functools.partial(pack_kernel, groups),
        out_shape=[
            jax.ShapeDtypeStruct((rows, width), jnp.bfloat16),
            jax.ShapeDtypeStruct((rows, width + 128), jnp.bfloat16),
        ],
        compiler_params=parameters(),
        cost_estimate=SMALL_COST,
        name="pack",
    )(query, key, value, gains)


def join_kernel(*refs):
    place = 0
    for ref in refs[:-2]:
        size = ref.shape[1]
        refs[-1][:, place : place + size] = ref[...]
        place += size


def join(parts, rest):
    rows = rest.shape[0]
    width = sum(part.shape[1] for part in parts)
    return pl.pallas_call(
        join_kernel,
        grid=(1,),
        in_specs=[pl.BlockSpec(part.shape, lambda i: (0, 0)) for part in parts]
        + [pl.BlockSpec(memory_space=pl.ANY)],
        out_specs=pl.BlockSpec((rows, width), lambda i: (0, 0)),
        out_shape=jax.ShapeDtypeStruct(rest.shape, rest.dtype),
        input_output_aliases={len(parts): 0},
        compiler_params=parameters(),
        cost_estimate=SMALL_COST,
        name="join",
    )(*parts, rest)


def transposed_kernel(count, parts, *refs):
    total = dot_nt(refs[0][...], refs[count][...])
    for index in range(1, count):
        total += dot_nt(refs[index][...], refs[count + index][...])
    rows = total.shape[0] // parts
    for index in range(parts):
        refs[2 * count + index][...] = total[index * rows : (index + 1) * rows].astype(
            jnp.bfloat16
        )


def transposed_product(xs, weight, column, parts, block=0, blocks=1):
    rows, depth = xs[0].shape
    rows //= blocks
    width = weight.shape[0]
    tile = tile_of(width)
    specs = [pl.BlockSpec((rows, depth), lambda t: (block, 0))] * len(xs)
    for index in range(len(xs)):
        specs.append(pl.BlockSpec((tile, depth), lambda t, index=index: (t, column + index)))
    part = (rows // parts, width)
    return pl.pallas_call(
        functools.partial(transposed_kernel, len(xs), parts),
        grid=(width // tile,),
        in_specs=specs,
        out_specs=[pl.BlockSpec((part[0], tile), lambda t: (0, t))] * parts,
        out_shape=[jax.ShapeDtypeStruct(part, jnp.bfloat16)] * parts,
        compiler_params=parameters(),
        cost_estimate=SMALL_COST,
        name="transposed",
    )(*xs, *[weight] * len(xs))


def heads_kernel(count, *refs):
    parts = refs[:count]
    weight_ref = refs[count]
    tokens = refs[count + 1 : -2]
    out_ref, local_ref = refs[-2:]
    step = pl.program_id(0)
    width = parts[0].shape[1]

    @pl.when(step == 0)
    def _():
        for j in range(count):
            local_ref[:, j * width : (j + 1) * width] = parts[j][...]

    for j in range(count):
        term = dot_nt(parts[j][...], weight_ref[:, j * width : (j + 1) * width])
        if j == 0:
            out_ref[...] = term
        else:
            out_ref[...] += term
    for index in range(len(tokens)):

        @pl.when(step == index)
        def _():
            out_ref[...] += tokens[index][...].astype(jnp.float32)


def heads_product(parts, weight, tokens):
    blocks = len(tokens)
    rows, width = tokens[0].shape
    depth = parts[0].shape[1]
    specs = [
        pl.BlockSpec((rows, depth), lambda i, j=j: (lax.rem(i + j, blocks), 0))
        for j in range(len(parts))
    ]
    whole = pl.BlockSpec((rows, width), lambda i: (0, 0), pipeline_mode=pl.Buffered(1))
    return pl.pallas_call(
        functools.partial(heads_kernel, len(parts)),
        grid=(blocks,),
        in_specs=[
            *specs,
            pl.BlockSpec(
                (width, depth * len(parts)), lambda i: (0, 0), pipeline_mode=pl.Buffered(1)
            ),
            *[whole] * blocks,
        ],
        out_specs=[
            pl.BlockSpec((rows, width), lambda i: (i, 0)),
            pl.BlockSpec((rows, depth * len(parts)), lambda i: (0, 0)),
        ],
        out_shape=[
            jax.ShapeDtypeStruct((rows * blocks, width), jnp.float32),
            jax.ShapeDtypeStruct((rows, depth * len(parts)), jnp.bfloat16),
        ],
        compiler_params=parameters(),
        cost_estimate=SMALL_COST,
        name="heads_product",
    )(*parts, weight, *tokens)


def attended_kernel(
    partial_ref, last_ref, weight_ref, gain_ref, hidden_ref, normed_ref, local_ref
):
    values = partial_ref[...] + dot_nt(last_ref[...], weight_ref[...])

    @pl.when(pl.program_id(0) == 0)
    def _():
        hidden_ref[...] = values
        local_ref[...] = last_ref[...]

    inverse = lax.rsqrt(jnp.mean(values * values, axis=-1, keepdims=True) + EPSILON)
    normed_ref[...] = (values * inverse * gain_ref[1:, :]).astype(jnp.bfloat16)


def after_attention(partial, last, weight, gain, count):
    total_rows, width = partial.shape
    rows = total_rows // count
    depth = last.shape[1]
    return pl.pallas_call(
        attended_kernel,
        grid=(count,),
        in_specs=[
            pl.BlockSpec((rows, width), lambda i: (i, 0)),
            pl.BlockSpec((rows, depth), lambda i: (lax.rem(i + count - 1, count), 0)),
            pl.BlockSpec((width, depth), lambda i: (0, count - 1)),
            pl.BlockSpec((2, width), lambda i: (0, 0)),
        ],
        out_specs=[
            pl.BlockSpec((rows, width), lambda i: (0, 0)),
            pl.BlockSpec((rows, width), lambda i: (lax.rem(i + count - 1, count), 0)),
            pl.BlockSpec((rows, depth), lambda i: (0, 0)),
        ],
        out_shape=[
            jax.ShapeDtypeStruct((rows, width), jnp.float32),
            jax.ShapeDtypeStruct((total_rows, width), jnp.bfloat16),
            jax.ShapeDtypeStruct((rows, depth), jnp.bfloat16),
        ],
        compiler_params=parameters(),
        cost_estimate=SMALL_COST,
        name="after_attention",
    )(partial, last, weight, gain)


def up_kernel(x_ref, gate_ref, up_ref, *refs):
    a_ref, u_ref, g_ref = refs[-3:]
    gate = dot_nn(x_ref[...], gate_ref[...])
    up = dot_nn(x_ref[...], up_ref[...])
    a_ref[...] = gate.astype(jnp.bfloat16)
    u_ref[...] = up.astype(jnp.bfloat16)
    g_ref[...] = (gate * jax.nn.sigmoid(gate) * up).astype(jnp.bfloat16)


def up_chunk(x, weight, kept, index, count):
    total_rows, depth = x.shape
    rows = total_rows // count
    hidden = (weight.shape[1] - depth) // 2
    tile = tile_of(hidden)
    tiles = hidden // tile
    start = depth // tile
    specs = [
        pl.BlockSpec((rows, depth), lambda t: (index, 0)),
        pl.BlockSpec((depth, tile), lambda t: (0, start + t)),
        pl.BlockSpec((depth, tile), lambda t: (0, start + tiles + t)),
    ]
    operands = [x, weight, weight]
    aliases = {}
    if kept is not None:
        specs.extend([pl.BlockSpec(memory_space=pl.ANY)] * 3)
        aliases = {len(operands) + i: i for i in range(3)}
        operands.extend(kept)
    return pl.pallas_call(
        up_kernel,
        grid=(tiles,),
        in_specs=specs,
        out_specs=[pl.BlockSpec((rows, tile), lambda t: (index, t))] * 3,
        out_shape=[jax.ShapeDtypeStruct((total_rows, hidden), jnp.bfloat16)] * 3,
        input_output_aliases=aliases,
        compiler_params=parameters(),
        cost_estimate=SMALL_COST,
        name="up_chunk",
    )(*operands)


def down_kernel(parts, tiles, *refs):
    down_ref, a_ref, u_ref, gate_ref, up_ref = refs[parts : parts + 5]
    da_ref, du_ref = refs[-5 - parts : -3 - parts]
    dx_refs = refs[-3 - parts : -3]
    da_kept, du_kept, e_out = refs[-3:]
    step = pl.program_id(0)

    @pl.when(step == 0)
    def _():
        rows = refs[0].shape[0]
        for index in range(parts):
            e_out[index * rows : (index + 1) * rows, :] = refs[index][...]

    @pl.when(step < tiles)
    def _():
        grad = dot_nn(e_out[...], down_ref[...])
        gate = a_ref[...].astype(jnp.float32)
        up = u_ref[...].astype(jnp.float32)
        sigmoid = jax.nn.sigmoid(gate)
        da = (grad * up * sigmoid * (1.0 + gate * (1.0 - sigmoid))).astype(jnp.bfloat16)
        du = (grad * gate * sigmoid).astype(jnp.bfloat16)
        da_ref[...] = da
        du_ref[...] = du
        tile = da.shape[1]
        for index in range(tiles):

            @pl.when(step == index)
            def _():
                da_kept[:, index * tile : (index + 1) * tile] = da
                du_kept[:, index * tile : (index + 1) * tile] = du

    @pl.when(step >= tiles)
    def _():
        total = dot_nt(da_kept[...], gate_ref[...]) + dot_nt(du_kept[...], up_ref[...])
        rows = total.shape[0] // parts
        for index in range(parts):
            dx_refs[index][...] = total[index * rows : (index + 1) * rows].astype(jnp.bfloat16)


def down_chunk(es, a, u, down_weight, weight, kept, index, count):
    depth, hidden = down_weight.shape
    rows = len(es) * es[0].shape[0]
    start = depth // hidden
    tile = tile_of(hidden)
    tiles = hidden // tile
    row_tile = tile_of(depth)

    def column(t):
        return jnp.minimum(t, tiles - 1)

    def row(t):
        return jnp.maximum(t - tiles, 0)

    specs = [pl.BlockSpec(es[0].shape, lambda t: (0, 0))] * len(es) + [
        pl.BlockSpec((depth, tile), lambda t: (0, column(t))),
        pl.BlockSpec((rows, tile), lambda t: (index, column(t))),
        pl.BlockSpec((rows, tile), lambda t: (index, column(t))),
        pl.BlockSpec((row_tile, hidden), lambda t: (row(t), start)),
        pl.BlockSpec((row_tile, hidden), lambda t: (row(t), start + 1)),
    ]
    operands = [*es, down_weight, a, u, weight, weight]
    part = es[0].shape
    shapes = [
        jax.ShapeDtypeStruct((rows * count, hidden), jnp.bfloat16),
        jax.ShapeDtypeStruct((rows * count, hidden), jnp.bfloat16),
        *[jax.ShapeDtypeStruct(part, jnp.bfloat16)] * len(es),
    ]
    aliases = {}
    if kept is not None:
        specs.extend([pl.BlockSpec(memory_space=pl.ANY)] * 2)
        aliases = {len(operands) + i: i for i in range(2)}
        operands.extend(kept)
    result = pl.pallas_call(
        functools.partial(down_kernel, len(es), tiles),
        grid=(tiles + depth // row_tile,),
        in_specs=specs,
        out_specs=[
            pl.BlockSpec((rows, tile), lambda t: (index, column(t))),
            pl.BlockSpec((rows, tile), lambda t: (index, column(t))),
            *[pl.BlockSpec((part[0], row_tile), lambda t: (0, row(t)))] * len(es),
        ],
        out_shape=shapes,
        input_output_aliases=aliases,
        scratch_shapes=[
            pltpu.VMEM((rows, hidden), jnp.bfloat16),
            pltpu.VMEM((rows, hidden), jnp.bfloat16),
            pltpu.VMEM((rows, depth), jnp.bfloat16),
        ],
        compiler_params=parameters(),
        cost_estimate=SMALL_COST,
        name="down_chunk",
    )(*operands)
    return result[:2], list(result[2:])


def weight_kernel(counts, blocks, split, place_ref, *refs):
    step = pl.program_id(0)
    total_refs = sum(parts + widths for parts, widths in counts)
    received = refs[total_refs] if len(refs) > total_refs + 1 else None
    place = 0
    column = 0
    for parts, widths in counts:
        x = refs[place][...]
        if parts > 1:
            x = jnp.concatenate([ref[...] for ref in refs[place : place + parts]], axis=0)
        for y_ref in refs[place + parts : place + parts + widths]:
            width = y_ref.shape[1]
            cuts = set(range(0, width, 1024)) | {width}
            if column < split < column + width and split:
                cuts.add(split - column)
            cuts = sorted(cuts)
            for first, last in zip(cuts[:-1], cuts[1:]):
                total = dot_tn(x, y_ref[:, first:last])
                start, end = column + first, column + last
                if received is None:
                    refs[-1][:, start:end] = total.astype(jnp.bfloat16)
                    continue
                total += received[:, start:end].astype(jnp.float32)
                total = total.astype(jnp.bfloat16)
                if split == 0:
                    refs[-1][:, start:end] = total
                    continue
                low = start < split
                keep = step < blocks // 2 if low else lax.rem(step, 2) == 0
                keep_ref, send_ref = refs[-4:-2] if low else refs[-2:]
                columns = slice(start, end) if low else slice(start - split, end - split)

                @pl.when(keep)
                def _():
                    keep_ref[:, columns] = total

                @pl.when(jnp.logical_not(keep))
                def _():
                    send_ref[:, columns] = total

            column += width
        place += parts + widths


def weight_product(pairs, place, count, received, ordered=False):
    depth = pairs[0][0][0].shape[1]
    blocks = count // 2
    tile = depth // count
    total = sum(y.shape[1] for _, ys in pairs for y in ys)
    split = 0 if ordered else -(-total // 256) * 128
    side = 1 if received is None else 0

    def source(t, p):
        if ordered:
            return 2 * t + lax.rem(p[0] + side, 2)
        return lax.bitwise_xor(p[0], 2 * t + side)

    whole = pl.BlockSpec((tile, total), lambda t, p: (t, 0))
    if received is None or ordered:
        out_specs = whole
        out_shape = jax.ShapeDtypeStruct((depth // 2, total), jnp.bfloat16)
    else:
        half = blocks // 2
        out_specs = [
            pl.BlockSpec((tile, split), lambda t, p: (jnp.minimum(t, half - 1), 0)),
            pl.BlockSpec((tile, split), lambda t, p: (jnp.maximum(t - half, 0), 0)),
            pl.BlockSpec((tile, total - split), lambda t, p: (t // 2, 0)),
            pl.BlockSpec((tile, total - split), lambda t, p: (t // 2, 0)),
        ]
        out_shape = [
            jax.ShapeDtypeStruct((depth // 4, width), jnp.bfloat16)
            for width in (split, split, total - split, total - split)
        ]
    specs = []
    operands = []
    for xs, ys in pairs:
        for x in xs:
            specs.append(pl.BlockSpec((x.shape[0], tile), lambda t, p: (0, source(t, p))))
        specs += [
            pl.BlockSpec(y.shape, lambda t, p: (0, 0), pipeline_mode=pl.Buffered(1)) for y in ys
        ]
        operands.extend([*xs, *ys])
    if received is not None:
        specs.append(whole)
        operands.append(received)
    return pl.pallas_call(
        functools.partial(
            weight_kernel, [(len(xs), len(ys)) for xs, ys in pairs], blocks, split
        ),
        grid_spec=pltpu.PrefetchScalarGridSpec(
            num_scalar_prefetch=1, grid=(blocks,), in_specs=specs, out_specs=out_specs
        ),
        out_shape=out_shape,
        compiler_params=parameters(),
        cost_estimate=SMALL_COST,
        name="weight_product",
    )(place, *operands)


def fold_kernel(counts, *refs):
    outs = refs[sum(counts) :]
    place = 0
    row = 0
    for index, count in enumerate(counts):
        total = refs[place][...].astype(jnp.float32)
        for ref in refs[place + 1 : place + count]:
            total += ref[...].astype(jnp.float32)
        out = outs[index % 2]
        rows = total.shape[0]
        out[row : row + rows, :] = total.astype(jnp.bfloat16)
        row += rows * (index % 2)
        place += count


def fold(sums, rows):
    counts = [len(terms) for pair in sums for terms in pair]
    values = [value for pair in sums for terms in pair for value in terms]
    widths = [terms[0].shape[1] for terms in sums[0]]
    steps = 2 if all(width % 256 == 0 for width in widths) else 1
    return pl.pallas_call(
        functools.partial(fold_kernel, counts),
        grid=(steps,),
        in_specs=[
            pl.BlockSpec((rows, value.shape[1] // steps), lambda t: (1, t)) for value in values
        ],
        out_specs=[
            pl.BlockSpec((rows * len(sums), width // steps), lambda t: (0, t))
            for width in widths
        ],
        out_shape=[
            jax.ShapeDtypeStruct((rows * len(sums), width), jnp.bfloat16) for width in widths
        ],
        compiler_params=parameters(),
        cost_estimate=SMALL_COST,
        name="fold",
    )(*values)


def residual_kernel(parts, e_ref, hidden_ref, first_ref, second_ref, gain_ref, weight_ref, *refs):
    dh_ref, dz_ref = refs[:2]
    dh, dz = refs[-2:]
    step = pl.program_id(0)
    tile = weight_ref.shape[1]

    @pl.when(step == 0)
    def _():
        values = hidden_ref[...]
        inverse = lax.rsqrt(jnp.mean(values * values, axis=-1, keepdims=True) + EPSILON)
        scaled = values * inverse
        grad = first_ref[...].astype(jnp.float32) + second_ref[...].astype(jnp.float32)
        grad = grad * gain_ref[1:, :]
        projection = jnp.mean(grad * scaled, axis=-1, keepdims=True)
        total = e_ref[...].astype(jnp.float32) + inverse * (grad - scaled * projection)
        dh[...] = total
        dz[...] = total.astype(jnp.bfloat16)

    result = dot_nn(dz[...], weight_ref[...]).astype(jnp.bfloat16)
    for index in range(parts):

        @pl.when(step == index)
        def _():
            columns = slice(index * tile, (index + 1) * tile)
            dh_ref[...] = dh[:, columns]
            dz_ref[...] = dz[:, columns]
            refs[2 + index][...] = result


def residual_gradient(e, hidden_res, first, second, gain, weight, parts):
    rows, depth = e.shape
    tile = depth // parts
    whole = pl.BlockSpec((rows, depth), lambda t: (0, 0))
    column = pl.BlockSpec((rows, tile), lambda t: (0, t))
    result = pl.pallas_call(
        functools.partial(residual_kernel, parts),
        grid=(parts,),
        in_specs=[
            whole,
            whole,
            whole,
            whole,
            pl.BlockSpec((2, depth), lambda t: (0, 0)),
            pl.BlockSpec((depth, tile), lambda t: (0, t)),
        ],
        out_specs=[column, column] + [pl.BlockSpec((rows, tile), lambda t: (0, 0))] * parts,
        out_shape=[
            jax.ShapeDtypeStruct((rows, depth), jnp.float32),
            jax.ShapeDtypeStruct((rows, depth), jnp.bfloat16),
            *[jax.ShapeDtypeStruct((rows, tile), jnp.bfloat16)] * parts,
        ],
        scratch_shapes=[
            pltpu.VMEM((rows, depth), jnp.float32),
            pltpu.VMEM((rows, depth), jnp.bfloat16),
        ],
        compiler_params=parameters(),
        cost_estimate=SMALL_COST,
        name="residual_gradient",
    )(e, hidden_res, first, second, gain, weight)
    return result[0], result[1], list(result[2:])


def tie(value, *others):
    return lax.optimization_barrier((value, others))[0]


def together(*values):
    return lax.optimization_barrier(values)


def add(first, second):
    return (first.astype(jnp.float32) + second.astype(jnp.float32)).astype(jnp.bfloat16)


class Mover:
    def __init__(self):
        self.dp_count = lax.axis_size("dp")
        self.ring = lax.axis_size("tensor")
        self.steps = []
        step = 2
        while step < self.dp_count:
            self.steps.append(step)
            step *= 2

    def swap(self, value, step):
        return lax.ppermute(value, "dp", [(i, i ^ step) for i in range(self.dp_count)])

    def gather(self, shard):
        return lax.all_gather(shard, "dp", axis=0, tiled=True)


    def send(self, pieces, level):
        orders = (self.steps[::-1], self.steps[:1] + self.steps[:0:-1])
        return [self.swap(piece, order[level]) for piece, order in zip(pieces, orders)]

    def begin(self, pieces):
        moved = self.send([pieces[1], pieces[3]], 0)
        return [[pieces[0], moved[0]], [pieces[2], moved[1]]]

    def fold(self, sums, level=1):
        return fold(sums, sums[0][0][0].shape[0] >> level)

    def advance(self, sums, folded):
        level = 1
        while True:
            moved = self.send(folded, level)
            level += 1
            if level == len(self.steps):
                return sums, moved
            rows = moved[0].shape[0] // len(sums)
            sums = [
                [
                    terms + [part[index * rows : (index + 1) * rows]]
                    for terms, part in zip(pair, moved)
                ]
                for index, pair in enumerate(sums)
            ]
            folded = self.fold(sums, level)

    def advance_all(self, sums):
        widths = {pair[0][0].shape[1] for pair in sums}
        parts = [sums] if len(widths) == 1 else [[pair] for pair in sums]
        return [self.advance(part, self.fold(part)) for part in parts]

    def scatter(self, total):
        groups = [list(range(core, self.dp_count, 2)) for core in range(2)]
        return lax.psum_scatter(
            total, "dp", scatter_dimension=0, tiled=True, axis_index_groups=groups
        )

    def hop(self, value, shift=1):
        return lax.ppermute(
            value, "tensor", [(i, (i + shift) % self.ring) for i in range(self.ring)]
        )

    def spread(self, value):
        ring = self.ring
        return [value] + [
            lax.ppermute(value, "tensor", [(i, (i - j) % ring) for i in range(ring)])
            for j in range(1, ring)
        ]

    def collect(self, parts):
        ring = self.ring
        total = parts[0]
        for j in range(1, ring):
            moved = lax.ppermute(
                parts[j].astype(jnp.bfloat16), "tensor", [(i, (i + j) % ring) for i in range(ring)]
            )
            total = total + moved.astype(jnp.float32)
        return total

    def exchange(self, parts):
        ring = self.ring
        return [parts[0]] + [
            lax.ppermute(parts[j], "tensor", [(i, (i + j) % ring) for i in range(ring)])
            for j in range(1, ring)
        ]


def totals_of(sums, moved):
    rows = moved[0].shape[0] // len(sums)
    result = []
    for index, pair in enumerate(sums):
        halves = []
        for terms, last in zip(pair, moved):
            total = last[index * rows : (index + 1) * rows].astype(jnp.float32)
            for term in terms:
                total = total + term[:rows].astype(jnp.float32)
            halves.append(total)
        result.append(jnp.concatenate(halves, axis=1))
    return result


def back_norm(grad_normed, scaled, inverse, scale_row):
    grad_scaled = grad_normed * scale_row
    projection = jnp.mean(grad_scaled * scaled, axis=-1, keepdims=True)
    return inverse * (grad_scaled - scaled * projection)


def per_device(
    tokens,
    seq_lengths,
    attention_gain,
    query_matrix,
    key_matrix,
    value_matrix,
    output_weight,
    feedforward_gain,
    gate_weight,
    up_weight,
    down_weight,
    cotangent,
):
    mover = Mover()
    dp_count = mover.dp_count
    ring = mover.ring
    dp_place = lax.axis_index("dp").astype(jnp.int32).reshape(1)
    ring_place = lax.axis_index("tensor")
    place = ring_place.astype(jnp.int32).reshape(1)
    _, local_rows, model_width = tokens.shape
    complete_rows = local_rows * ring
    hidden = gate_weight.shape[1]
    groups = key_matrix.shape[1] // HEAD_SIZE
    joint_width = groups * GROUP_WIDTH
    f32 = jnp.float32
    b16 = jnp.bfloat16

    doc_ids, positions = layout(seq_lengths, complete_rows)
    row_index = jnp.arange(complete_rows, dtype=jnp.int32)
    doc_ids = jnp.where(doc_ids[0] < PIECES, doc_ids[0], PIECES + row_index)

    def to_relative(values):
        view = values.reshape((ring, local_rows) + values.shape[1:])
        return jnp.roll(view, -(ring_place + 1), axis=0)[::-1].reshape(values.shape)

    doc_ids = to_relative(doc_ids)
    cosine, sine = rope_tables(to_relative(positions[0]), HEAD_SIZE)
    cosine_table = jnp.tile(cosine, (1, 128 // cosine.shape[1]))
    sine_table = jnp.tile(jnp.concatenate([-sine, sine], axis=1), (1, 128 // HEAD_SIZE))

    own_gains = jnp.pad(jnp.stack([attention_gain, feedforward_gain]), ((0, 126), (0, 0)))
    joint_matrix, packed = pack(query_matrix, key_matrix, value_matrix, own_gains, groups)
    joint_full = mover.gather(packed)
    output_parts = mover.spread(output_weight.T)
    up_shard = jnp.pad(
        jnp.concatenate([gate_weight, up_weight], axis=1), ((0, 0), (model_width, 0))
    )
    output_parts, cosine_table, sine_table, doc_ids, up_shard, down_shard = together(
        output_parts, cosine_table, sine_table, doc_ids, up_shard, down_weight.T
    )
    local_tokens = tokens[0]
    token_chunks = [local_tokens, mover.hop(local_tokens)]
    up_shard = join(output_parts, up_shard)
    up_full = mover.gather(up_shard)
    down_full = mover.gather(tie(down_shard, up_shard))
    gains = joint_full[:, joint_width : joint_width + 2].T.astype(f32)

    def projection(kept, index):
        return project(
            token_chunks[index],
            gains,
            joint_full,
            cosine_table,
            sine_table,
            kept,
            index,
            ring,
            groups,
        )

    kept = projection(None, 0)
    for j in range(1, ring):
        token_chunks[j], kept, gains = together(token_chunks[j], kept, gains)
        if j + 1 < ring:
            token_chunks.append(mover.hop(token_chunks[j]))
        else:
            local_cotangent = tie(cotangent[0], token_chunks[j])
            moved = mover.hop(local_cotangent)
        kept = projection(kept, j)
    normed_one, joint = kept
    attended, totals = attention_forward(joint, doc_ids, place, ring, groups)
    moved, attended = together(moved, attended)
    cotangent_chunks = [local_cotangent, moved]
    attended_parts = [attended]
    while len(attended_parts) < ring:
        part = mover.hop(attended_parts[-1], -1)
        if len(attended_parts) == ring - 1:
            partial, attended_local = heads_product(
                tie(attended_parts, attended_parts[-1]), up_full, token_chunks
            )
            part, partial, attended_local = together(part, partial, attended_local)
        attended_parts.append(part)
    moved, last = together(moved, attended_parts[-1])

    pairs = ring // 2
    moved = mover.hop(moved)
    hidden_res, normed_two, attended_last = after_attention(partial, last, up_full, gains, ring)
    upward = up_chunk(normed_two, up_full, None, 0, pairs)
    downward = None
    grads = []

    def chunks_of(pair):
        return [cotangent_chunks[(2 * pair + i) % ring] for i in (1, 2)]

    def lower(pair, kept):
        return down_chunk(
            chunks_of(pair), upward[0], upward[1], down_full, up_full, kept, pair, pairs
        )

    for j in range(2, ring):
        if j > 2:
            moved = mover.hop(moved)
            if j % 2:
                downward, parts = lower((j - 3) // 2, downward)
                grads.extend(parts)
            else:
                upward = up_chunk(normed_two, up_full, upward, j // 2 - 1, pairs)
        moved, upward, downward, grads = together(moved, upward, downward, grads)
        cotangent_chunks.append(moved)

    def weights(xs, ys, received=None):
        return weight_product([(xs, ys)], dp_place, dp_count, received)

    ordered = cotangent_chunks[1:] + cotangent_chunks[:1]
    total = grads[0]
    moved = mover.hop(total)
    upward = up_chunk(tie(normed_two, total), up_full, upward, pairs - 1, pairs)
    product = upward[2]
    down_part = weight_product([(ordered, [product])], dp_place, dp_count, None, True)
    moved, upward, down_part = together(moved, upward, down_part)
    down_part = mover.swap(down_part, 1)
    for j in range(2, ring):
        total = add(moved, grads[j - 1])
        moved = mover.hop(total)
        if j == 2:
            downward, parts = lower(pairs - 1, tie(downward, total))
            grads.extend(parts)
            moved, downward, grads = together(moved, downward, grads)
            grad_gate, grad_up = downward
        if j == 3:
            gate_part = weights([tie(normed_two, total)], [grad_gate])
            branch = transposed_product(
                [tie(product, gate_part)], down_full, 0, ring // 2, 0, 2
            )
            down_part = weight_product(
                [(tie(ordered, branch), [product])], dp_place, dp_count, down_part, True
            )
            moved, gate_part, branch, down_part = together(moved, gate_part, branch, down_part)
    gate_part = mover.swap(gate_part, 1)
    down_out = mover.scatter(down_part)
    grad_hidden, grad_branch, grad_parts = residual_gradient(
        local_cotangent, hidden_res, moved, grads[-1], gains, up_full, ring
    )
    grad_hidden, grad_branch, grad_parts, gate_part = together(
        grad_hidden, grad_branch, grad_parts, gate_part
    )

    grad_parts = mover.exchange(grad_parts)
    output_part = weights([grad_branch], [attended_local, attended_last])
    gate_part = weights([tie(normed_two, output_part)], [grad_gate], gate_part)
    grad_parts, output_part, gate_part = together(grad_parts, output_part, gate_part)
    grad_joint = []
    sent = 0
    moved = branch[0]
    for group in range(groups):
        moved = mover.hop(moved)
        sent += 1
        if group == 0:
            output_part = mover.swap(output_part, 1)
        else:
            output_part = mover.begin(output_part)
        grad_joint.append(
            attention_backward(
                joint,
                attended,
                tie(grad_parts, grad_joint),
                totals,
                doc_ids,
                cosine_table,
                sine_table,
                place,
                group,
            )
        )
        if group == 0:
            output_part = weights(
                [tie(grad_branch, grad_joint)], [attended_local, attended_last], output_part
            )
        if group + 1 == groups:
            grads = transposed_product(grad_joint, joint_full, 0, ring)
        moved, grad_joint, grads, output_part, down_out = together(
            moved, grad_joint, grads, output_part, down_out
        )
        if group + 1 < groups:
            moved = add(moved, branch[sent])
    if groups == 1:
        output_part = mover.begin(output_part)
    branch_moved = moved
    moved = grads[0]

    def last_weights(total, received):
        return weight_product(
            [([tie(normed_two, total)], [grad_up]), ([normed_one], grad_joint)],
            dp_place,
            dp_count,
            received,
        )

    for j in range(1, ring):
        total = grads[1] if j == 1 else add(moved, grads[j])
        moved = mover.hop(total)
        if j == 1:
            gate_part = mover.begin(gate_part)
            last_part = last_weights(total, None)
            branch = branch + transposed_product(
                [tie(product, last_part)], down_full, 0, ring // 2, 1, 2
            )
            next_branch = add(branch_moved, branch[sent])
            moved, last_part, branch, output_part, gate_part, next_branch = together(
                moved, last_part, branch, output_part, gate_part, next_branch
            )
        if j == 2:
            both_parts = tie([output_part, gate_part], total)
            both_parts = mover.advance_all(both_parts)
            last_part = last_weights(total, mover.swap(last_part, 1))
            moved, _, both_parts = together(moved, last_part, both_parts)
            down_out = tie(down_out, both_parts)
        if j == 3:
            last_part = mover.begin(last_part)
            branch_moved = mover.hop(tie(next_branch, total))
            sent += 1
            output_out, gate_out = [total for part in both_parts for total in totals_of(*part)]
            output_out = jnp.split(output_out, ring, axis=1)
            moved, last_part, output_out = together(moved, last_part, output_out)
    folded, output_out = together(mover.fold([last_part]), output_out)
    last_part = mover.advance([last_part], folded)
    output_out = mover.collect(output_out[:-1] + [tie(output_out[-1], last_part[1][1])]).T
    scaled_one, inverse_one = norm_rows(local_tokens.astype(f32))
    local_one = moved.astype(f32) + grads[0].astype(f32)
    input_gradient = grad_hidden + back_norm(local_one, scaled_one, inverse_one, gains[:1])
    branch_moved, last_part = together(branch_moved, last_part)
    for j in range(sent, ring - 1):
        branch_moved = mover.hop(add(branch_moved, branch[j]))
    block_output = (
        hidden_res + (branch_moved.astype(f32) + branch[-1].astype(f32))
    ).astype(b16)
    last_out = totals_of(*last_part)[0]
    up_out, joint_out = last_out[:, :hidden], last_out[:, hidden:]

    sums = jnp.stack(
        [
            jnp.sum(joint_out * joint_matrix.astype(f32), axis=1) / attention_gain.astype(f32),
            jnp.sum(gate_out * gate_weight.astype(f32) + up_out * up_weight.astype(f32), axis=1)
            / feedforward_gain.astype(f32),
        ]
    )
    gain_out = sums
    for shift in range(1, ring):
        gain_out = gain_out + tie(
            lax.ppermute(sums, "tensor", [(i, (i + shift) % ring) for i in range(ring)]),
            output_out,
        )

    def ungrouped(first, width):
        return jnp.concatenate(
            [
                joint_out[:, g * GROUP_WIDTH + first : g * GROUP_WIDTH + first + width]
                for g in range(groups)
            ],
            axis=1,
        )

    return (
        block_output[None],
        input_gradient[None],
        gain_out[0],
        ungrouped(0, GROUP_QUERY),
        ungrouped(GROUP_QUERY, HEAD_SIZE),
        ungrouped(GROUP_QUERY + HEAD_SIZE, HEAD_SIZE),
        output_out,
        gain_out[1],
        gate_out,
        up_out,
        down_out.astype(f32).T,
    )


def solution(mesh):
    return jax.shard_map(
        per_device,
        mesh=mesh,
        in_specs=(
            P("dp", "tensor", None),
            P("dp", None),
            P("dp"),
            P("dp", "tensor"),
            P("dp", "tensor"),
            P("dp", "tensor"),
            P("tensor", "dp"),
            P("dp"),
            P("dp", "tensor"),
            P("dp", "tensor"),
            P("tensor", "dp"),
            P("dp", "tensor", None),
        ),
        out_specs=(
            P("dp", "tensor", None),
            P("dp", "tensor", None),
            P("dp"),
            P("dp", "tensor"),
            P("dp", "tensor"),
            P("dp", "tensor"),
            P("tensor", "dp"),
            P("dp"),
            P("dp", "tensor"),
            P("dp", "tensor"),
            P("tensor", "dp"),
        ),
        check_vma=False,
    )
```

```python
import functools
import math

import jax
import jax.numpy as jnp
from jax import lax
from jax.experimental import pallas as pl
from jax.experimental.pallas import tpu as pltpu
from jax.sharding import PartitionSpec as P

QUERY_HEADS = 32
KEY_VALUE_HEADS = 8
HEAD_SIZE = 64
PIECES = 4


EPSILON = 1e-05
ROPE_BASE = 500000.0
NEGATIVE = -1e30
GROUP_QUERY = QUERY_HEADS // KEY_VALUE_HEADS * HEAD_SIZE
GROUP_WIDTH = GROUP_QUERY + 2 * HEAD_SIZE
KERNEL_VMEM = 60 * 1024 * 1024
SMALL_COST = pl.CostEstimate(flops=1, bytes_accessed=1, transcendentals=0)


def layout(lengths, complete_rows):
    doc_ends = jnp.cumsum(lengths, axis=-1)
    row_index = jnp.arange(complete_rows, dtype=jnp.int32)
    piece_count = lengths.shape[-1]
    doc_ids = jnp.sum((row_index[None, :, None] >= doc_ends[:, None, :]).astype(jnp.int32), axis=2)
    starts = doc_ends - lengths
    chosen = doc_ids[:, :, None] == jnp.arange(piece_count, dtype=jnp.int32)[None, None, :]
    doc_begin = jnp.sum(jnp.where(chosen, starts[:, None, :], 0), axis=2) + jnp.where(
        doc_ids == piece_count, doc_ends[:, -1:], 0
    )
    return (doc_ids, row_index[None, :] - doc_begin)


def rope_tables(positions, head_dim):
    half_dim = head_dim // 2
    frequency = ROPE_BASE ** (-(jnp.arange(half_dim, dtype=jnp.float32) * (2.0 / head_dim)))
    angles = positions.astype(jnp.float32)[..., None] * frequency
    return (jnp.cos(angles), jnp.sin(angles))


def norm_rows(values):
    inverse = lax.rsqrt(jnp.mean(values * values, axis=-1, keepdims=True) + EPSILON)
    return (values * inverse, inverse)


def dot_nt(left, right):
    return lax.dot_general(
        left, right, (((1,), (1,)), ((), ())), preferred_element_type=jnp.float32
    )


def dot_nn(left, right):
    return jnp.dot(left, right, preferred_element_type=jnp.float32)


def dot_tn(left, right):
    return lax.dot_general(
        left, right, (((0,), (0,)), ((), ())), preferred_element_type=jnp.float32
    )


def tile_of(size, limit=512):
    tile = limit
    while size % tile:
        tile //= 2
    return tile


def parameters():
    return pltpu.CompilerParams(vmem_limit_bytes=KERNEL_VMEM)


def swap_halves(values):
    lane = lax.broadcasted_iota(jnp.int32, values.shape, 1)
    half = HEAD_SIZE // 2
    return jnp.where(
        lane % HEAD_SIZE < half, pltpu.roll(values, 128 - half, 1), pltpu.roll(values, half, 1)
    )


def turned(values, cosine, sine, start):
    result = values * cosine + swap_halves(values) * sine
    rotated = GROUP_WIDTH - HEAD_SIZE
    if start + 128 <= rotated:
        return result
    lane = lax.broadcasted_iota(jnp.int32, values.shape, 1)
    return jnp.where(lane < rotated - start, result, values)


def project_kernel(x_ref, gain_ref, weight_ref, cos_ref, sin_ref, *refs):
    normed_ref, joint_ref = refs[-2:]

    @pl.when(pl.program_id(0) == 0)
    def _():
        values = x_ref[...].astype(jnp.float32)
        inverse = lax.rsqrt(jnp.mean(values * values, axis=-1, keepdims=True) + EPSILON)
        normed_ref[...] = (values * inverse * gain_ref[:1, :]).astype(jnp.bfloat16)

    product = dot_nn(normed_ref[...], weight_ref[...])
    for start in range(0, GROUP_WIDTH, 128):
        part = turned(product[:, start : start + 128], cos_ref[...], sin_ref[...], start)
        if start < GROUP_QUERY:
            part = part * HEAD_SIZE ** (-0.5)
        joint_ref[:, start : start + 128] = part.astype(jnp.bfloat16)


def project(x, gain, weight, cosine, sine, kept, index, count, groups):
    rows, depth = x.shape
    specs = [
        pl.BlockSpec((rows, depth), lambda g: (0, 0)),
        pl.BlockSpec((2, depth), lambda g: (0, 0)),
        pl.BlockSpec((depth, GROUP_WIDTH), lambda g: (0, g)),
        pl.BlockSpec((rows, 128), lambda g: (index, 0)),
        pl.BlockSpec((rows, 128), lambda g: (index, 0)),
    ]
    operands = [x, gain, weight, cosine, sine]
    aliases = {}
    if kept is not None:
        specs.extend([pl.BlockSpec(memory_space=pl.ANY)] * 2)
        aliases = {len(operands) + i: i for i in range(2)}
        operands.extend(kept)
    return pl.pallas_call(
        project_kernel,
        grid=(groups,),
        in_specs=specs,
        out_specs=[
            pl.BlockSpec((rows, depth), lambda g: (index, 0)),
            pl.BlockSpec((rows, GROUP_WIDTH), lambda g: (index, g)),
        ],
        out_shape=[
            jax.ShapeDtypeStruct((rows * count, depth), jnp.bfloat16),
            jax.ShapeDtypeStruct((rows * count, GROUP_WIDTH * groups), jnp.bfloat16),
        ],
        input_output_aliases=aliases,
        compiler_params=parameters(),
        cost_estimate=SMALL_COST,
        name="project",
    )(*operands)


def ring_offset(place, chunk, count, rows):
    return pl.multiple_of(lax.rem(place - chunk + count, count) * rows, rows)


def stack_heads(target, source):
    rows, width = source.shape
    for head in range(width // HEAD_SIZE):
        target[head * rows : (head + 1) * rows, :] = source[
            :, head * HEAD_SIZE : (head + 1) * HEAD_SIZE
        ]


def fill_bias(bias, key_docs, query_docs, earlier):
    rows = key_docs.shape[0]
    row_index = lax.broadcasted_iota(jnp.int32, (rows, rows), 0)
    column_index = lax.broadcasted_iota(jnp.int32, (rows, rows), 1)
    same = (key_docs == query_docs) & ((row_index <= column_index) | earlier)
    values = jnp.where(same, 0.0, NEGATIVE)
    for first in range(0, bias.shape[1], rows):
        bias[:, first : first + rows] = values


def forward_kernel(
    count,
    place_ref,
    own_ref,
    all_ref,
    docq_ref,
    dock_ref,
    o_ref,
    lse_ref,
    bias,
    queries,
    values_all,
    mixed,
):
    chunk = pl.program_id(1)
    place = place_ref[0]
    rows = own_ref.shape[0]
    heads = GROUP_QUERY // HEAD_SIZE
    stack_heads(queries, own_ref.at[:, :GROUP_QUERY])

    @pl.when(chunk == 0)
    def _():
        values = all_ref[:, GROUP_QUERY:].astype(jnp.float32)
        values_all[...] = values.T[HEAD_SIZE:].astype(jnp.bfloat16)

    mixed[...] = jnp.zeros_like(mixed)

    def block(j, carry):
        peaks, total = carry
        offset = ring_offset(place, j, count, rows)
        piece = pl.ds(offset, rows)
        fill_bias(bias, dock_ref[piece, :], docq_ref[...], j < chunk)
        keys = all_ref[piece, GROUP_QUERY : GROUP_QUERY + HEAD_SIZE]
        scores = dot_nt(keys, queries[...]) + bias[...]
        higher = jnp.maximum(peaks, jnp.max(scores, axis=0, keepdims=True))
        probs = jnp.exp(scores - higher)
        scale = jnp.exp(peaks - higher)
        mixed[...] = mixed[...] * scale + dot_nn(
            values_all[:, piece], probs.astype(jnp.bfloat16)
        )
        return higher, total * scale + jnp.sum(probs, axis=0, keepdims=True)

    peaks, total = lax.fori_loop(
        0,
        chunk + 1,
        block,
        (
            jnp.full((1, heads * rows), NEGATIVE, jnp.float32),
            jnp.zeros((1, heads * rows), jnp.float32),
        ),
    )
    lse_ref[:1, :] = peaks + jnp.log(total)
    result = mixed[...] / total
    for head in range(0, heads, 2):
        pair = jnp.concatenate(
            [result[:, (head + i) * rows : (head + i + 1) * rows] for i in range(2)], axis=0
        )
        o_ref[:, head * HEAD_SIZE : (head + 2) * HEAD_SIZE] = pair.T.astype(jnp.bfloat16)


def attention_forward(joint, docs, place, count, groups):
    total_rows = joint.shape[0]
    rows = total_rows // count
    stacked = rows * GROUP_QUERY // HEAD_SIZE

    def block(c, place_ref):
        return lax.rem(place_ref[0] - c + count, count)

    spec = pltpu.PrefetchScalarGridSpec(
        num_scalar_prefetch=1,
        grid=(groups, count),
        in_specs=[
            pl.BlockSpec((rows, GROUP_WIDTH), lambda g, c, p: (block(c, p), g)),
            pl.BlockSpec((total_rows, GROUP_WIDTH), lambda g, c, p: (0, g)),
            pl.BlockSpec((1, rows), lambda g, c, p: (0, block(c, p))),
            pl.BlockSpec((total_rows, 1), lambda g, c, p: (0, 0)),
        ],
        out_specs=[
            pl.BlockSpec((rows, GROUP_QUERY), lambda g, c, p: (block(c, p), g)),
            pl.BlockSpec((8, stacked), lambda g, c, p: (g, block(c, p))),
        ],
        scratch_shapes=[
            pltpu.VMEM((rows, stacked), jnp.float32),
            pltpu.VMEM((stacked, HEAD_SIZE), jnp.bfloat16),
            pltpu.VMEM((HEAD_SIZE, total_rows), jnp.bfloat16),
            pltpu.VMEM((HEAD_SIZE, stacked), jnp.float32),
        ],
    )
    return pl.pallas_call(
        functools.partial(forward_kernel, count),
        grid_spec=spec,
        out_shape=[
            jax.ShapeDtypeStruct((total_rows, GROUP_QUERY * groups), jnp.bfloat16),
            jax.ShapeDtypeStruct((8 * groups, stacked * count), jnp.float32),
        ],
        compiler_params=parameters(),
        cost_estimate=SMALL_COST,
        name="attend",
    )(place, joint, joint, docs[None, :], docs[:, None])


def backward_kernel(count, place_ref, *refs):
    own_ref, all_ref, o_ref = refs[:3]
    lse_ref, docq_ref, dock_ref, cos_ref, sin_ref = refs[3 + count : 8 + count]
    out_ref, bias, queries, grads, keys_all, values_all, sum_q, sum_k, sum_v = refs[8 + count :]
    chunk = pl.program_id(0)
    place = place_ref[0]
    rows = own_ref.shape[0]
    heads = GROUP_QUERY // HEAD_SIZE
    stack_heads(queries, own_ref.at[:, :GROUP_QUERY])
    for index in range(count):

        @pl.when(lax.rem(place - chunk + count, count) == index)
        def _():
            stack_heads(grads, refs[3 + index])

    @pl.when(chunk == 0)
    def _():
        keys_all[...] = all_ref[:, GROUP_QUERY : GROUP_QUERY + HEAD_SIZE]
        values_all[...] = all_ref[:, GROUP_QUERY + HEAD_SIZE :]
        sum_k[...] = jnp.zeros_like(sum_k)
        sum_v[...] = jnp.zeros_like(sum_v)

    sum_q[...] = jnp.zeros_like(sum_q)
    ones = jnp.ones((8, HEAD_SIZE), jnp.bfloat16)
    inner = []
    for head in range(heads):
        attended = o_ref[:, head * HEAD_SIZE : (head + 1) * HEAD_SIZE].astype(jnp.float32)
        both = attended * grads[head * rows : (head + 1) * rows, :].astype(jnp.float32)
        high = both.astype(jnp.bfloat16)
        low = (both - high.astype(jnp.float32)).astype(jnp.bfloat16)
        inner.append((dot_nt(ones, high) + dot_nt(ones, low))[:1])
    inner = jnp.concatenate(inner, axis=1)

    def block(j, carry):
        offset = ring_offset(place, j, count, rows)
        piece = pl.ds(offset, rows)
        fill_bias(bias, dock_ref[piece, :], docq_ref[...], j < chunk)
        probs = jnp.exp(dot_nt(keys_all[piece, :], queries[...]) + bias[...] - lse_ref[:1, :])
        grad_probs = dot_nt(values_all[piece, :], grads[...])
        grad_scores = (probs * (grad_probs - inner)).astype(jnp.bfloat16)
        sum_v[piece, :] += dot_nn(probs.astype(jnp.bfloat16), grads[...])
        sum_k[piece, :] += dot_nn(grad_scores, queries[...])
        sum_q[...] += dot_tn(grad_scores, keys_all[piece, :])
        return carry

    lax.fori_loop(0, chunk + 1, block, 0)
    own = pl.ds(ring_offset(place, chunk, count, rows), rows)
    for first in range(0, heads, 2):
        start = first * HEAD_SIZE
        part = jnp.concatenate(
            [sum_q[(first + i) * rows : (first + i + 1) * rows, :] for i in range(2)], axis=1
        )
        part = turned(part, cos_ref[own, :], -sin_ref[own, :], start)
        out_ref[own, start : start + 128] = (part * HEAD_SIZE ** (-0.5)).astype(jnp.bfloat16)

    @pl.when(chunk == count - 1)
    def _():
        part = jnp.concatenate([sum_k[...], sum_v[...]], axis=1)
        part = turned(part, cos_ref[...], -sin_ref[...], GROUP_QUERY)
        out_ref[:, GROUP_QUERY:] = part.astype(jnp.bfloat16)


def attention_backward(joint, attended, grads, lse, docs, cosine, sine, place, group):
    count = len(grads)
    total_rows = joint.shape[0]
    rows = total_rows // count
    stacked = rows * GROUP_QUERY // HEAD_SIZE

    def block(c, place_ref):
        return lax.rem(place_ref[0] - c + count, count)

    table = pl.BlockSpec((total_rows, 128), lambda c, p: (0, 0))
    spec = pltpu.PrefetchScalarGridSpec(
        num_scalar_prefetch=1,
        grid=(count,),
        in_specs=[
            pl.BlockSpec((rows, GROUP_WIDTH), lambda c, p: (block(c, p), group)),
            pl.BlockSpec((total_rows, GROUP_WIDTH), lambda c, p: (0, group)),
            pl.BlockSpec((rows, GROUP_QUERY), lambda c, p: (block(c, p), group)),
            *[pl.BlockSpec((rows, GROUP_QUERY), lambda c, p: (0, group))] * count,
            pl.BlockSpec((8, stacked), lambda c, p: (group, block(c, p))),
            pl.BlockSpec((1, rows), lambda c, p: (0, block(c, p))),
            pl.BlockSpec((total_rows, 1), lambda c, p: (0, 0)),
            table,
            table,
        ],
        out_specs=pl.BlockSpec((total_rows, GROUP_WIDTH), lambda c, p: (0, 0)),
        scratch_shapes=[
            pltpu.VMEM((rows, stacked), jnp.float32),
            *[pltpu.VMEM((stacked, HEAD_SIZE), jnp.bfloat16)] * 2,
            *[pltpu.VMEM((total_rows, HEAD_SIZE), jnp.bfloat16)] * 2,
            pltpu.VMEM((stacked, HEAD_SIZE), jnp.float32),
            *[pltpu.VMEM((total_rows, HEAD_SIZE), jnp.float32)] * 2,
        ],
    )
    return pl.pallas_call(
        functools.partial(backward_kernel, count),
        grid_spec=spec,
        out_shape=jax.ShapeDtypeStruct((total_rows, GROUP_WIDTH), jnp.bfloat16),
        compiler_params=parameters(),
        cost_estimate=SMALL_COST,
        name="attend_back",
    )(
        place,
        joint,
        joint,
        attended,
        *grads,
        lse,
        docs[None, :],
        docs[:, None],
        cosine,
        sine,
    )


def pack_kernel(
    groups, query_ref, key_ref, value_ref, first_ref, second_ref, joint_ref, out_ref
):
    for g in range(groups):
        start = g * GROUP_WIDTH
        columns = slice(g * HEAD_SIZE, (g + 1) * HEAD_SIZE)
        joint_ref[:, start : start + GROUP_QUERY] = query_ref[
            :, g * GROUP_QUERY : (g + 1) * GROUP_QUERY
        ]
        joint_ref[:, start + GROUP_QUERY : start + GROUP_WIDTH] = jnp.concatenate(
            [key_ref[:, columns], value_ref[:, columns]], axis=1
        )
    width = groups * GROUP_WIDTH
    out_ref[:, :width] = joint_ref[...]
    row = lax.broadcasted_iota(jnp.int32, (128, query_ref.shape[0]), 0)
    gains = jnp.where(row == 0, first_ref[...].astype(jnp.float32)[None, :], 0.0)
    gains = jnp.where(row == 1, second_ref[...].astype(jnp.float32)[None, :], gains)
    out_ref[:, width:] = gains.T.astype(jnp.bfloat16)


def pack(query, key, value, first, second, groups):
    rows = query.shape[0]
    width = groups * GROUP_WIDTH
    return pl.pallas_call(
        functools.partial(pack_kernel, groups),
        out_shape=[
            jax.ShapeDtypeStruct((rows, width), jnp.bfloat16),
            jax.ShapeDtypeStruct((rows, width + 128), jnp.bfloat16),
        ],
        compiler_params=parameters(),
        cost_estimate=SMALL_COST,
        name="pack",
    )(query, key, value, first, second)


def join_kernel(*refs):
    place = 0
    for ref in refs[:-2]:
        size = ref.shape[1]
        refs[-1][:, place : place + size] = ref[...]
        place += size


def join(parts, rest):
    rows = rest.shape[0]
    width = sum(part.shape[1] for part in parts)
    return pl.pallas_call(
        join_kernel,
        grid=(1,),
        in_specs=[pl.BlockSpec(part.shape, lambda i: (0, 0)) for part in parts]
        + [pl.BlockSpec(memory_space=pl.ANY)],
        out_specs=pl.BlockSpec((rows, width), lambda i: (0, 0)),
        out_shape=jax.ShapeDtypeStruct(rest.shape, rest.dtype),
        input_output_aliases={len(parts): 0},
        compiler_params=parameters(),
        cost_estimate=SMALL_COST,
        name="join",
    )(*parts, rest)


def transposed_kernel(count, parts, *refs):
    total = dot_nt(refs[0][...], refs[count][...])
    for index in range(1, count):
        total += dot_nt(refs[index][...], refs[count + index][...])
    rows = total.shape[0] // parts
    for index in range(parts):
        refs[2 * count + index][...] = total[index * rows : (index + 1) * rows].astype(
            jnp.bfloat16
        )


def transposed_product(xs, weight, column, parts, block=0, blocks=1):
    rows, depth = xs[0].shape
    rows //= blocks
    width = weight.shape[0]
    tile = tile_of(width)
    specs = [pl.BlockSpec((rows, depth), lambda t: (block, 0))] * len(xs)
    for index in range(len(xs)):
        specs.append(pl.BlockSpec((tile, depth), lambda t, index=index: (t, column + index)))
    part = (rows // parts, width)
    return pl.pallas_call(
        functools.partial(transposed_kernel, len(xs), parts),
        grid=(width // tile,),
        in_specs=specs,
        out_specs=[pl.BlockSpec((part[0], tile), lambda t: (0, t))] * parts,
        out_shape=[jax.ShapeDtypeStruct(part, jnp.bfloat16)] * parts,
        compiler_params=parameters(),
        cost_estimate=SMALL_COST,
        name="transposed",
    )(*xs, *[weight] * len(xs))


def heads_kernel(count, *refs):
    parts = refs[:count]
    weight_ref = refs[count]
    tokens = refs[count + 1 : -2]
    out_ref, local_ref = refs[-2:]
    step = pl.program_id(0)
    width = parts[0].shape[1]

    @pl.when(step == 0)
    def _():
        for j in range(count):
            local_ref[:, j * width : (j + 1) * width] = parts[j][...]

    for j in range(count):
        term = dot_nt(parts[j][...], weight_ref[:, j * width : (j + 1) * width])
        if j == 0:
            out_ref[...] = term
        else:
            out_ref[...] += term
    for index in range(len(tokens)):

        @pl.when(step == index)
        def _():
            out_ref[...] += tokens[index][...].astype(jnp.float32)


def heads_product(parts, weight, tokens):
    blocks = len(tokens)
    rows, width = tokens[0].shape
    depth = parts[0].shape[1]
    specs = [
        pl.BlockSpec((rows, depth), lambda i, j=j: (lax.rem(i + j, blocks), 0))
        for j in range(len(parts))
    ]
    whole = pl.BlockSpec((rows, width), lambda i: (0, 0), pipeline_mode=pl.Buffered(1))
    return pl.pallas_call(
        functools.partial(heads_kernel, len(parts)),
        grid=(blocks,),
        in_specs=[
            *specs,
            pl.BlockSpec(
                (width, depth * len(parts)), lambda i: (0, 0), pipeline_mode=pl.Buffered(1)
            ),
            *[whole] * blocks,
        ],
        out_specs=[
            pl.BlockSpec((rows, width), lambda i: (i, 0)),
            pl.BlockSpec((rows, depth * len(parts)), lambda i: (0, 0)),
        ],
        out_shape=[
            jax.ShapeDtypeStruct((rows * blocks, width), jnp.float32),
            jax.ShapeDtypeStruct((rows, depth * len(parts)), jnp.bfloat16),
        ],
        compiler_params=parameters(),
        cost_estimate=SMALL_COST,
        name="heads_product",
    )(*parts, weight, *tokens)


def attended_kernel(
    partial_ref, last_ref, weight_ref, gain_ref, hidden_ref, normed_ref, local_ref
):
    values = partial_ref[...] + dot_nt(last_ref[...], weight_ref[...])

    @pl.when(pl.program_id(0) == 0)
    def _():
        hidden_ref[...] = values
        local_ref[...] = last_ref[...]

    inverse = lax.rsqrt(jnp.mean(values * values, axis=-1, keepdims=True) + EPSILON)
    normed_ref[...] = (values * inverse * gain_ref[1:, :]).astype(jnp.bfloat16)


def after_attention(partial, last, weight, gain, count):
    total_rows, width = partial.shape
    rows = total_rows // count
    depth = last.shape[1]
    return pl.pallas_call(
        attended_kernel,
        grid=(count,),
        in_specs=[
            pl.BlockSpec((rows, width), lambda i: (i, 0)),
            pl.BlockSpec((rows, depth), lambda i: (lax.rem(i + count - 1, count), 0)),
            pl.BlockSpec((width, depth), lambda i: (0, count - 1)),
            pl.BlockSpec((2, width), lambda i: (0, 0)),
        ],
        out_specs=[
            pl.BlockSpec((rows, width), lambda i: (0, 0)),
            pl.BlockSpec((rows, width), lambda i: (lax.rem(i + count - 1, count), 0)),
            pl.BlockSpec((rows, depth), lambda i: (0, 0)),
        ],
        out_shape=[
            jax.ShapeDtypeStruct((rows, width), jnp.float32),
            jax.ShapeDtypeStruct((total_rows, width), jnp.bfloat16),
            jax.ShapeDtypeStruct((rows, depth), jnp.bfloat16),
        ],
        compiler_params=parameters(),
        cost_estimate=SMALL_COST,
        name="after_attention",
    )(partial, last, weight, gain)


def up_kernel(x_ref, gate_ref, up_ref, *refs):
    a_ref, u_ref, g_ref = refs[-3:]
    gate = dot_nn(x_ref[...], gate_ref[...])
    up = dot_nn(x_ref[...], up_ref[...])
    a_ref[...] = gate.astype(jnp.bfloat16)
    u_ref[...] = up.astype(jnp.bfloat16)
    g_ref[...] = (gate * jax.nn.sigmoid(gate) * up).astype(jnp.bfloat16)


def up_chunk(x, weight, kept, index, count):
    total_rows, depth = x.shape
    rows = total_rows // count
    hidden = (weight.shape[1] - depth) // 2
    tile = tile_of(hidden)
    tiles = hidden // tile
    start = depth // tile
    specs = [
        pl.BlockSpec((rows, depth), lambda t: (index, 0)),
        pl.BlockSpec((depth, tile), lambda t: (0, start + t)),
        pl.BlockSpec((depth, tile), lambda t: (0, start + tiles + t)),
    ]
    operands = [x, weight, weight]
    aliases = {}
    if kept is not None:
        specs.extend([pl.BlockSpec(memory_space=pl.ANY)] * 3)
        aliases = {len(operands) + i: i for i in range(3)}
        operands.extend(kept)
    return pl.pallas_call(
        up_kernel,
        grid=(tiles,),
        in_specs=specs,
        out_specs=[pl.BlockSpec((rows, tile), lambda t: (index, t))] * 3,
        out_shape=[jax.ShapeDtypeStruct((total_rows, hidden), jnp.bfloat16)] * 3,
        input_output_aliases=aliases,
        compiler_params=parameters(),
        cost_estimate=SMALL_COST,
        name="up_chunk",
    )(*operands)


def down_kernel(parts, tiles, *refs):
    down_ref, a_ref, u_ref, gate_ref, up_ref = refs[parts : parts + 5]
    da_ref, du_ref = refs[-5 - parts : -3 - parts]
    dx_refs = refs[-3 - parts : -3]
    da_kept, du_kept, e_out = refs[-3:]
    step = pl.program_id(0)

    @pl.when(step == 0)
    def _():
        rows = refs[0].shape[0]
        for index in range(parts):
            e_out[index * rows : (index + 1) * rows, :] = refs[index][...]

    @pl.when(step < tiles)
    def _():
        grad = dot_nn(e_out[...], down_ref[...])
        gate = a_ref[...].astype(jnp.float32)
        up = u_ref[...].astype(jnp.float32)
        sigmoid = jax.nn.sigmoid(gate)
        da = (grad * up * sigmoid * (1.0 + gate * (1.0 - sigmoid))).astype(jnp.bfloat16)
        du = (grad * gate * sigmoid).astype(jnp.bfloat16)
        da_ref[...] = da
        du_ref[...] = du
        tile = da.shape[1]
        for index in range(tiles):

            @pl.when(step == index)
            def _():
                da_kept[:, index * tile : (index + 1) * tile] = da
                du_kept[:, index * tile : (index + 1) * tile] = du

    @pl.when(step >= tiles)
    def _():
        total = dot_nt(da_kept[...], gate_ref[...]) + dot_nt(du_kept[...], up_ref[...])
        rows = total.shape[0] // parts
        for index in range(parts):
            dx_refs[index][...] = total[index * rows : (index + 1) * rows].astype(jnp.bfloat16)


def down_chunk(es, a, u, down_weight, weight, kept, index, count):
    depth, hidden = down_weight.shape
    rows = len(es) * es[0].shape[0]
    start = depth // hidden
    tile = tile_of(hidden)
    tiles = hidden // tile
    row_tile = tile_of(depth)

    def column(t):
        return jnp.minimum(t, tiles - 1)

    def row(t):
        return jnp.maximum(t - tiles, 0)

    specs = [pl.BlockSpec(es[0].shape, lambda t: (0, 0))] * len(es) + [
        pl.BlockSpec((depth, tile), lambda t: (0, column(t))),
        pl.BlockSpec((rows, tile), lambda t: (index, column(t))),
        pl.BlockSpec((rows, tile), lambda t: (index, column(t))),
        pl.BlockSpec((row_tile, hidden), lambda t: (row(t), start)),
        pl.BlockSpec((row_tile, hidden), lambda t: (row(t), start + 1)),
    ]
    operands = [*es, down_weight, a, u, weight, weight]
    part = es[0].shape
    shapes = [
        jax.ShapeDtypeStruct((rows * count, hidden), jnp.bfloat16),
        jax.ShapeDtypeStruct((rows * count, hidden), jnp.bfloat16),
        *[jax.ShapeDtypeStruct(part, jnp.bfloat16)] * len(es),
    ]
    aliases = {}
    if kept is not None:
        specs.extend([pl.BlockSpec(memory_space=pl.ANY)] * 2)
        aliases = {len(operands) + i: i for i in range(2)}
        operands.extend(kept)
    result = pl.pallas_call(
        functools.partial(down_kernel, len(es), tiles),
        grid=(tiles + depth // row_tile,),
        in_specs=specs,
        out_specs=[
            pl.BlockSpec((rows, tile), lambda t: (index, column(t))),
            pl.BlockSpec((rows, tile), lambda t: (index, column(t))),
            *[pl.BlockSpec((part[0], row_tile), lambda t: (0, row(t)))] * len(es),
        ],
        out_shape=shapes,
        input_output_aliases=aliases,
        scratch_shapes=[
            pltpu.VMEM((rows, hidden), jnp.bfloat16),
            pltpu.VMEM((rows, hidden), jnp.bfloat16),
            pltpu.VMEM((rows, depth), jnp.bfloat16),
        ],
        compiler_params=parameters(),
        cost_estimate=SMALL_COST,
        name="down_chunk",
    )(*operands)
    return result[:2], list(result[2:])


def weight_kernel(counts, blocks, split, place_ref, *refs):
    step = pl.program_id(0)
    total_refs = sum(parts + widths for parts, widths in counts)
    received = refs[total_refs] if len(refs) > total_refs + 1 else None
    place = 0
    column = 0
    for parts, widths in counts:
        x = refs[place][...]
        if parts > 1:
            x = jnp.concatenate([ref[...] for ref in refs[place : place + parts]], axis=0)
        for y_ref in refs[place + parts : place + parts + widths]:
            width = y_ref.shape[1]
            cuts = set(range(0, width, 1024)) | {width}
            if column < split < column + width and split:
                cuts.add(split - column)
            cuts = sorted(cuts)
            for first, last in zip(cuts[:-1], cuts[1:]):
                total = dot_tn(x, y_ref[:, first:last])
                start, end = column + first, column + last
                if received is None:
                    refs[-1][:, start:end] = total.astype(jnp.bfloat16)
                    continue
                total += received[:, start:end].astype(jnp.float32)
                total = total.astype(jnp.bfloat16)
                if split == 0:
                    refs[-1][:, start:end] = total
                    continue
                low = start < split
                keep = step < blocks // 2 if low else lax.rem(step, 2) == 0
                keep_ref, send_ref = refs[-4:-2] if low else refs[-2:]
                columns = slice(start, end) if low else slice(start - split, end - split)

                @pl.when(keep)
                def _():
                    keep_ref[:, columns] = total

                @pl.when(jnp.logical_not(keep))
                def _():
                    send_ref[:, columns] = total

            column += width
        place += parts + widths


def weight_product(pairs, place, count, received, ordered=False):
    depth = pairs[0][0][0].shape[1]
    blocks = count // 2
    tile = depth // count
    total = sum(y.shape[1] for _, ys in pairs for y in ys)
    split = 0 if ordered else -(-total // 256) * 128
    side = 1 if received is None else 0

    def source(t, p):
        if ordered:
            return 2 * t + lax.rem(p[0] + side, 2)
        return lax.bitwise_xor(p[0], 2 * t + side)

    whole = pl.BlockSpec((tile, total), lambda t, p: (t, 0))
    if received is None or ordered:
        out_specs = whole
        out_shape = jax.ShapeDtypeStruct((depth // 2, total), jnp.bfloat16)
    else:
        half = blocks // 2
        out_specs = [
            pl.BlockSpec((tile, split), lambda t, p: (jnp.minimum(t, half - 1), 0)),
            pl.BlockSpec((tile, split), lambda t, p: (jnp.maximum(t - half, 0), 0)),
            pl.BlockSpec((tile, total - split), lambda t, p: (t // 2, 0)),
            pl.BlockSpec((tile, total - split), lambda t, p: (t // 2, 0)),
        ]
        out_shape = [
            jax.ShapeDtypeStruct((depth // 4, width), jnp.bfloat16)
            for width in (split, split, total - split, total - split)
        ]
    specs = []
    operands = []
    for xs, ys in pairs:
        for x in xs:
            specs.append(pl.BlockSpec((x.shape[0], tile), lambda t, p: (0, source(t, p))))
        specs += [
            pl.BlockSpec(y.shape, lambda t, p: (0, 0), pipeline_mode=pl.Buffered(1)) for y in ys
        ]
        operands.extend([*xs, *ys])
    if received is not None:
        specs.append(whole)
        operands.append(received)
    return pl.pallas_call(
        functools.partial(
            weight_kernel, [(len(xs), len(ys)) for xs, ys in pairs], blocks, split
        ),
        grid_spec=pltpu.PrefetchScalarGridSpec(
            num_scalar_prefetch=1, grid=(blocks,), in_specs=specs, out_specs=out_specs
        ),
        out_shape=out_shape,
        compiler_params=parameters(),
        cost_estimate=SMALL_COST,
        name="weight_product",
    )(place, *operands)


def fold_kernel(counts, *refs):
    outs = refs[sum(counts) :]
    place = 0
    row = 0
    for index, count in enumerate(counts):
        total = refs[place][...].astype(jnp.float32)
        for ref in refs[place + 1 : place + count]:
            total += ref[...].astype(jnp.float32)
        out = outs[index % 2]
        rows = total.shape[0]
        out[row : row + rows, :] = total.astype(jnp.bfloat16)
        row += rows * (index % 2)
        place += count


def fold(sums, rows):
    counts = [len(terms) for pair in sums for terms in pair]
    values = [value for pair in sums for terms in pair for value in terms]
    widths = [terms[0].shape[1] for terms in sums[0]]
    steps = 2 if all(width % 256 == 0 for width in widths) else 1
    return pl.pallas_call(
        functools.partial(fold_kernel, counts),
        grid=(steps,),
        in_specs=[
            pl.BlockSpec((rows, value.shape[1] // steps), lambda t: (1, t)) for value in values
        ],
        out_specs=[
            pl.BlockSpec((rows * len(sums), width // steps), lambda t: (0, t))
            for width in widths
        ],
        out_shape=[
            jax.ShapeDtypeStruct((rows * len(sums), width), jnp.bfloat16) for width in widths
        ],
        compiler_params=parameters(),
        cost_estimate=SMALL_COST,
        name="fold",
    )(*values)


def residual_kernel(parts, e_ref, hidden_ref, first_ref, second_ref, gain_ref, weight_ref, *refs):
    dh_ref, dz_ref = refs[:2]
    dh, dz = refs[-2:]
    step = pl.program_id(0)
    tile = weight_ref.shape[1]

    @pl.when(step == 0)
    def _():
        values = hidden_ref[...]
        inverse = lax.rsqrt(jnp.mean(values * values, axis=-1, keepdims=True) + EPSILON)
        scaled = values * inverse
        grad = first_ref[...].astype(jnp.float32) + second_ref[...].astype(jnp.float32)
        grad = grad * gain_ref[1:, :]
        projection = jnp.mean(grad * scaled, axis=-1, keepdims=True)
        total = e_ref[...].astype(jnp.float32) + inverse * (grad - scaled * projection)
        dh[...] = total
        dz[...] = total.astype(jnp.bfloat16)

    result = dot_nn(dz[...], weight_ref[...]).astype(jnp.bfloat16)
    for index in range(parts):

        @pl.when(step == index)
        def _():
            columns = slice(index * tile, (index + 1) * tile)
            dh_ref[...] = dh[:, columns]
            dz_ref[...] = dz[:, columns]
            refs[2 + index][...] = result


def residual_gradient(e, hidden_res, first, second, gain, weight, parts):
    rows, depth = e.shape
    tile = depth // parts
    whole = pl.BlockSpec((rows, depth), lambda t: (0, 0))
    column = pl.BlockSpec((rows, tile), lambda t: (0, t))
    result = pl.pallas_call(
        functools.partial(residual_kernel, parts),
        grid=(parts,),
        in_specs=[
            whole,
            whole,
            whole,
            whole,
            pl.BlockSpec((2, depth), lambda t: (0, 0)),
            pl.BlockSpec((depth, tile), lambda t: (0, t)),
        ],
        out_specs=[column, column] + [pl.BlockSpec((rows, tile), lambda t: (0, 0))] * parts,
        out_shape=[
            jax.ShapeDtypeStruct((rows, depth), jnp.float32),
            jax.ShapeDtypeStruct((rows, depth), jnp.bfloat16),
            *[jax.ShapeDtypeStruct((rows, tile), jnp.bfloat16)] * parts,
        ],
        scratch_shapes=[
            pltpu.VMEM((rows, depth), jnp.float32),
            pltpu.VMEM((rows, depth), jnp.bfloat16),
        ],
        compiler_params=parameters(),
        cost_estimate=SMALL_COST,
        name="residual_gradient",
    )(e, hidden_res, first, second, gain, weight)
    return result[0], result[1], list(result[2:])


def tie(value, *others):
    return lax.optimization_barrier((value, others))[0]


def together(*values):
    return lax.optimization_barrier(values)


def add(first, second):
    return (first.astype(jnp.float32) + second.astype(jnp.float32)).astype(jnp.bfloat16)


class Mover:
    def __init__(self):
        self.dp_count = lax.axis_size("dp")
        self.ring = lax.axis_size("tensor")
        self.steps = []
        step = 2
        while step < self.dp_count:
            self.steps.append(step)
            step *= 2

    def swap(self, value, step):
        return lax.ppermute(value, "dp", [(i, i ^ step) for i in range(self.dp_count)])

    def gather(self, shard):
        return lax.all_gather(shard, "dp", axis=0, tiled=True)


    def send(self, pieces, level):
        orders = (self.steps[::-1], self.steps[:1] + self.steps[:0:-1])
        return [self.swap(piece, order[level]) for piece, order in zip(pieces, orders)]

    def begin(self, pieces):
        moved = self.send([pieces[1], pieces[3]], 0)
        return [[pieces[0], moved[0]], [pieces[2], moved[1]]]

    def fold(self, sums, level=1):
        return fold(sums, sums[0][0][0].shape[0] >> level)

    def advance(self, sums, folded):
        level = 1
        while True:
            moved = self.send(folded, level)
            level += 1
            if level == len(self.steps):
                return sums, moved
            rows = moved[0].shape[0] // len(sums)
            sums = [
                [
                    terms + [part[index * rows : (index + 1) * rows]]
                    for terms, part in zip(pair, moved)
                ]
                for index, pair in enumerate(sums)
            ]
            folded = self.fold(sums, level)

    def advance_all(self, sums):
        widths = {pair[0][0].shape[1] for pair in sums}
        parts = [sums] if len(widths) == 1 else [[pair] for pair in sums]
        return [self.advance(part, self.fold(part)) for part in parts]

    def scatter(self, total):
        groups = [list(range(core, self.dp_count, 2)) for core in range(2)]
        return lax.psum_scatter(
            total, "dp", scatter_dimension=0, tiled=True, axis_index_groups=groups
        )

    def hop(self, value, shift=1):
        return lax.ppermute(
            value, "tensor", [(i, (i + shift) % self.ring) for i in range(self.ring)]
        )

    def spread(self, value):
        ring = self.ring
        return [value] + [
            lax.ppermute(value, "tensor", [(i, (i - j) % ring) for i in range(ring)])
            for j in range(1, ring)
        ]

    def collect(self, parts):
        ring = self.ring
        total = parts[0]
        for j in range(1, ring):
            moved = lax.ppermute(
                parts[j].astype(jnp.bfloat16), "tensor", [(i, (i + j) % ring) for i in range(ring)]
            )
            total = total + moved.astype(jnp.float32)
        return total

    def exchange(self, parts):
        ring = self.ring
        return [parts[0]] + [
            lax.ppermute(parts[j], "tensor", [(i, (i + j) % ring) for i in range(ring)])
            for j in range(1, ring)
        ]


def totals_of(sums, moved):
    rows = moved[0].shape[0] // len(sums)
    result = []
    for index, pair in enumerate(sums):
        halves = []
        for terms, last in zip(pair, moved):
            total = last[index * rows : (index + 1) * rows].astype(jnp.float32)
            for term in terms:
                total = total + term[:rows].astype(jnp.float32)
            halves.append(total)
        result.append(jnp.concatenate(halves, axis=1))
    return result


def back_norm(grad_normed, scaled, inverse, scale_row):
    grad_scaled = grad_normed * scale_row
    projection = jnp.mean(grad_scaled * scaled, axis=-1, keepdims=True)
    return inverse * (grad_scaled - scaled * projection)


def per_device(
    tokens,
    seq_lengths,
    attention_gain,
    query_matrix,
    key_matrix,
    value_matrix,
    output_weight,
    feedforward_gain,
    gate_weight,
    up_weight,
    down_weight,
    cotangent,
):
    mover = Mover()
    dp_count = mover.dp_count
    ring = mover.ring
    dp_place = lax.axis_index("dp").astype(jnp.int32).reshape(1)
    ring_place = lax.axis_index("tensor")
    place = ring_place.astype(jnp.int32).reshape(1)
    _, local_rows, model_width = tokens.shape
    complete_rows = local_rows * ring
    hidden = gate_weight.shape[1]
    groups = key_matrix.shape[1] // HEAD_SIZE
    joint_width = groups * GROUP_WIDTH
    f32 = jnp.float32
    b16 = jnp.bfloat16

    doc_ids, positions = layout(seq_lengths, complete_rows)
    row_index = jnp.arange(complete_rows, dtype=jnp.int32)
    doc_ids = jnp.where(doc_ids[0] < PIECES, doc_ids[0], PIECES + row_index)

    def to_relative(values):
        view = values.reshape((ring, local_rows) + values.shape[1:])
        return jnp.roll(view, -(ring_place + 1), axis=0)[::-1].reshape(values.shape)

    doc_ids = to_relative(doc_ids)
    cosine, sine = rope_tables(to_relative(positions[0]), HEAD_SIZE)
    cosine_table = jnp.tile(cosine, (1, 128 // cosine.shape[1]))
    sine_table = jnp.tile(jnp.concatenate([-sine, sine], axis=1), (1, 128 // HEAD_SIZE))

    joint_matrix, packed = pack(
        query_matrix, key_matrix, value_matrix, attention_gain, feedforward_gain, groups
    )
    joint_full = mover.gather(packed)
    output_parts = mover.spread(output_weight.T)
    up_shard = jnp.pad(
        jnp.concatenate([gate_weight, up_weight], axis=1), ((0, 0), (model_width, 0))
    )
    output_parts, cosine_table, sine_table, doc_ids, up_shard, down_shard = together(
        output_parts, cosine_table, sine_table, doc_ids, up_shard, down_weight.T
    )
    local_tokens = tokens[0]
    token_chunks = [local_tokens, mover.hop(local_tokens)]
    up_shard = join(output_parts, up_shard)
    up_full = mover.gather(up_shard)
    down_full = mover.gather(tie(down_shard, up_shard))
    gains = joint_full[:, joint_width : joint_width + 2].T.astype(f32)

    def projection(kept, index):
        return project(
            token_chunks[index],
            gains,
            joint_full,
            cosine_table,
            sine_table,
            kept,
            index,
            ring,
            groups,
        )

    kept = projection(None, 0)
    for j in range(1, ring):
        token_chunks[j], kept, gains = together(token_chunks[j], kept, gains)
        if j + 1 < ring:
            token_chunks.append(mover.hop(token_chunks[j]))
        else:
            local_cotangent = tie(cotangent[0], token_chunks[j])
            moved = mover.hop(local_cotangent)
        kept = projection(kept, j)
    normed_one, joint = kept
    attended, totals = attention_forward(joint, doc_ids, place, ring, groups)
    moved, attended = together(moved, attended)
    cotangent_chunks = [local_cotangent, moved]
    attended_parts = [attended]
    while len(attended_parts) < ring:
        part = mover.hop(attended_parts[-1], -1)
        if len(attended_parts) == ring - 1:
            partial, attended_local = heads_product(
                tie(attended_parts, attended_parts[-1]), up_full, token_chunks
            )
            part, partial, attended_local = together(part, partial, attended_local)
        attended_parts.append(part)
    moved, last = together(moved, attended_parts[-1])

    pairs = ring // 2
    moved = mover.hop(moved)
    hidden_res, normed_two, attended_last = after_attention(partial, last, up_full, gains, ring)
    upward = up_chunk(normed_two, up_full, None, 0, pairs)
    downward = None
    grads = []

    def chunks_of(pair):
        return [cotangent_chunks[(2 * pair + i) % ring] for i in (1, 2)]

    def lower(pair, kept):
        return down_chunk(
            chunks_of(pair), upward[0], upward[1], down_full, up_full, kept, pair, pairs
        )

    for j in range(2, ring):
        if j > 2:
            moved = mover.hop(moved)
            if j % 2:
                downward, parts = lower((j - 3) // 2, downward)
                grads.extend(parts)
            else:
                upward = up_chunk(normed_two, up_full, upward, j // 2 - 1, pairs)
        moved, upward, downward, grads = together(moved, upward, downward, grads)
        cotangent_chunks.append(moved)

    def weights(xs, ys, received=None):
        return weight_product([(xs, ys)], dp_place, dp_count, received)

    ordered = cotangent_chunks[1:] + cotangent_chunks[:1]
    total = grads[0]
    moved = mover.hop(total)
    upward = up_chunk(tie(normed_two, total), up_full, upward, pairs - 1, pairs)
    product = upward[2]
    down_part = weight_product([(ordered, [product])], dp_place, dp_count, None, True)
    moved, upward, down_part = together(moved, upward, down_part)
    down_part = mover.swap(down_part, 1)
    for j in range(2, ring):
        total = add(moved, grads[j - 1])
        moved = mover.hop(total)
        if j == 2:
            downward, parts = lower(pairs - 1, tie(downward, total))
            grads.extend(parts)
            moved, downward, grads = together(moved, downward, grads)
            grad_gate, grad_up = downward
        if j == 3:
            gate_part = weights([tie(normed_two, total)], [grad_gate])
            branch = transposed_product(
                [tie(product, gate_part)], down_full, 0, ring // 2, 0, 2
            )
            down_part = weight_product(
                [(tie(ordered, branch), [product])], dp_place, dp_count, down_part, True
            )
            moved, gate_part, branch, down_part = together(moved, gate_part, branch, down_part)
    gate_part = mover.swap(gate_part, 1)
    down_out = mover.scatter(down_part)
    grad_hidden, grad_branch, grad_parts = residual_gradient(
        local_cotangent, hidden_res, moved, grads[-1], gains, up_full, ring
    )
    grad_hidden, grad_branch, grad_parts, gate_part = together(
        grad_hidden, grad_branch, grad_parts, gate_part
    )

    grad_parts = mover.exchange(grad_parts)
    output_part = weights([grad_branch], [attended_local, attended_last])
    gate_part = weights([tie(normed_two, output_part)], [grad_gate], gate_part)
    grad_parts, output_part, gate_part = together(grad_parts, output_part, gate_part)
    grad_joint = []
    sent = 0
    moved = branch[0]
    for group in range(groups):
        moved = mover.hop(moved)
        sent += 1
        if group == 0:
            output_part = mover.swap(output_part, 1)
        else:
            output_part = mover.begin(output_part)
        grad_joint.append(
            attention_backward(
                joint,
                attended,
                tie(grad_parts, grad_joint),
                totals,
                doc_ids,
                cosine_table,
                sine_table,
                place,
                group,
            )
        )
        if group == 0:
            output_part = weights(
                [tie(grad_branch, grad_joint)], [attended_local, attended_last], output_part
            )
        if group + 1 == groups:
            grads = transposed_product(grad_joint, joint_full, 0, ring)
        moved, grad_joint, grads, output_part, down_out = together(
            moved, grad_joint, grads, output_part, down_out
        )
        if group + 1 < groups:
            moved = add(moved, branch[sent])
    if groups == 1:
        output_part = mover.begin(output_part)
    branch_moved = moved
    moved = grads[0]

    def last_weights(total, received):
        return weight_product(
            [([tie(normed_two, total)], [grad_up]), ([normed_one], grad_joint)],
            dp_place,
            dp_count,
            received,
        )

    for j in range(1, ring):
        total = grads[1] if j == 1 else add(moved, grads[j])
        moved = mover.hop(total)
        if j == 1:
            gate_part = mover.begin(gate_part)
            last_part = last_weights(total, None)
            branch = branch + transposed_product(
                [tie(product, last_part)], down_full, 0, ring // 2, 1, 2
            )
            next_branch = add(branch_moved, branch[sent])
            moved, last_part, branch, output_part, gate_part, next_branch = together(
                moved, last_part, branch, output_part, gate_part, next_branch
            )
        if j == 2:
            both_parts = tie([output_part, gate_part], total)
            both_parts = mover.advance_all(both_parts)
            last_part = last_weights(total, mover.swap(last_part, 1))
            moved, _, both_parts = together(moved, last_part, both_parts)
            down_out = tie(down_out, both_parts)
        if j == 3:
            last_part = mover.begin(last_part)
            branch_moved = mover.hop(tie(next_branch, total))
            sent += 1
            output_out, gate_out = [total for part in both_parts for total in totals_of(*part)]
            output_out = jnp.split(output_out, ring, axis=1)
            moved, last_part, output_out = together(moved, last_part, output_out)
    folded, output_out = together(mover.fold([last_part]), output_out)
    last_part = mover.advance([last_part], folded)
    output_out = mover.collect(output_out[:-1] + [tie(output_out[-1], last_part[1][1])]).T
    scaled_one, inverse_one = norm_rows(local_tokens.astype(f32))
    local_one = moved.astype(f32) + grads[0].astype(f32)
    input_gradient = grad_hidden + back_norm(local_one, scaled_one, inverse_one, gains[:1])
    branch_moved, last_part = together(branch_moved, last_part)
    for j in range(sent, ring - 1):
        branch_moved = mover.hop(add(branch_moved, branch[j]))
    block_output = (
        hidden_res + (branch_moved.astype(f32) + branch[-1].astype(f32))
    ).astype(b16)
    last_out = totals_of(*last_part)[0]
    up_out, joint_out = last_out[:, :hidden], last_out[:, hidden:]

    sums = jnp.stack(
        [
            jnp.sum(joint_out * joint_matrix.astype(f32), axis=1) / attention_gain.astype(f32),
            jnp.sum(gate_out * gate_weight.astype(f32) + up_out * up_weight.astype(f32), axis=1)
            / feedforward_gain.astype(f32),
        ]
    )
    gain_out = sums
    for shift in range(1, ring):
        gain_out = gain_out + tie(
            lax.ppermute(sums, "tensor", [(i, (i + shift) % ring) for i in range(ring)]),
            output_out,
        )

    def ungrouped(first, width):
        return jnp.concatenate(
            [
                joint_out[:, g * GROUP_WIDTH + first : g * GROUP_WIDTH + first + width]
                for g in range(groups)
            ],
            axis=1,
        )

    return (
        block_output[None],
        input_gradient[None],
        gain_out[0],
        ungrouped(0, GROUP_QUERY),
        ungrouped(GROUP_QUERY, HEAD_SIZE),
        ungrouped(GROUP_QUERY + HEAD_SIZE, HEAD_SIZE),
        output_out,
        gain_out[1],
        gate_out,
        up_out,
        down_out.astype(f32).T,
    )


def solution(mesh):
    return jax.shard_map(
        per_device,
        mesh=mesh,
        in_specs=(
            P("dp", "tensor", None),
            P("dp", None),
            P("dp"),
            P("dp", "tensor"),
            P("dp", "tensor"),
            P("dp", "tensor"),
            P("tensor", "dp"),
            P("dp"),
            P("dp", "tensor"),
            P("dp", "tensor"),
            P("tensor", "dp"),
            P("dp", "tensor", None),
        ),
        out_specs=(
            P("dp", "tensor", None),
            P("dp", "tensor", None),
            P("dp"),
            P("dp", "tensor"),
            P("dp", "tensor"),
            P("dp", "tensor"),
            P("tensor", "dp"),
            P("dp"),
            P("dp", "tensor"),
            P("dp", "tensor"),
            P("tensor", "dp"),
        ),
        check_vma=False,
    )
```

```python
import functools
import math

import jax
import jax.numpy as jnp
from jax import lax
from jax.experimental import pallas as pl
from jax.experimental.pallas import tpu as pltpu
from jax.sharding import PartitionSpec as P

QUERY_HEADS = 32
KEY_VALUE_HEADS = 8
HEAD_SIZE = 64
PIECES = 4


EPSILON = 1e-05
ROPE_BASE = 500000.0
NEGATIVE = -1e30
GROUP_QUERY = QUERY_HEADS // KEY_VALUE_HEADS * HEAD_SIZE
GROUP_WIDTH = GROUP_QUERY + 2 * HEAD_SIZE
KERNEL_VMEM = 60 * 1024 * 1024
SMALL_COST = pl.CostEstimate(flops=1, bytes_accessed=1, transcendentals=0)


def layout(lengths, complete_rows):
    doc_ends = jnp.cumsum(lengths, axis=-1)
    row_index = jnp.arange(complete_rows, dtype=jnp.int32)
    piece_count = lengths.shape[-1]
    doc_ids = jnp.sum((row_index[None, :, None] >= doc_ends[:, None, :]).astype(jnp.int32), axis=2)
    starts = doc_ends - lengths
    chosen = doc_ids[:, :, None] == jnp.arange(piece_count, dtype=jnp.int32)[None, None, :]
    doc_begin = jnp.sum(jnp.where(chosen, starts[:, None, :], 0), axis=2) + jnp.where(
        doc_ids == piece_count, doc_ends[:, -1:], 0
    )
    return (doc_ids, row_index[None, :] - doc_begin)


def rope_tables(positions, head_dim):
    half_dim = head_dim // 2
    frequency = ROPE_BASE ** (-(jnp.arange(half_dim, dtype=jnp.float32) * (2.0 / head_dim)))
    angles = positions.astype(jnp.float32)[..., None] * frequency
    return (jnp.cos(angles), jnp.sin(angles))


def norm_rows(values):
    inverse = lax.rsqrt(jnp.mean(values * values, axis=-1, keepdims=True) + EPSILON)
    return (values * inverse, inverse)


def dot_nt(left, right):
    return lax.dot_general(
        left, right, (((1,), (1,)), ((), ())), preferred_element_type=jnp.float32
    )


def dot_nn(left, right):
    return jnp.dot(left, right, preferred_element_type=jnp.float32)


def dot_tn(left, right):
    return lax.dot_general(
        left, right, (((0,), (0,)), ((), ())), preferred_element_type=jnp.float32
    )


def tile_of(size, limit=512):
    tile = limit
    while size % tile:
        tile //= 2
    return tile


def parameters():
    return pltpu.CompilerParams(vmem_limit_bytes=KERNEL_VMEM)


def swap_halves(values):
    lane = lax.broadcasted_iota(jnp.int32, values.shape, 1)
    half = HEAD_SIZE // 2
    return jnp.where(
        lane % HEAD_SIZE < half, pltpu.roll(values, 128 - half, 1), pltpu.roll(values, half, 1)
    )


def turned(values, cosine, sine, start):
    result = values * cosine + swap_halves(values) * sine
    rotated = GROUP_WIDTH - HEAD_SIZE
    if start + 128 <= rotated:
        return result
    lane = lax.broadcasted_iota(jnp.int32, values.shape, 1)
    return jnp.where(lane < rotated - start, result, values)


def project_kernel(x_ref, gain_ref, weight_ref, cos_ref, sin_ref, *refs):
    normed_ref, joint_ref = refs[-2:]

    @pl.when(pl.program_id(0) == 0)
    def _():
        values = x_ref[...].astype(jnp.float32)
        inverse = lax.rsqrt(jnp.mean(values * values, axis=-1, keepdims=True) + EPSILON)
        normed_ref[...] = (values * inverse * gain_ref[:1, :]).astype(jnp.bfloat16)

    product = dot_nn(normed_ref[...], weight_ref[...])
    for start in range(0, GROUP_WIDTH, 128):
        part = turned(product[:, start : start + 128], cos_ref[...], sin_ref[...], start)
        if start < GROUP_QUERY:
            part = part * HEAD_SIZE ** (-0.5)
        joint_ref[:, start : start + 128] = part.astype(jnp.bfloat16)


def project(x, gain, weight, cosine, sine, kept, index, count, groups):
    rows, depth = x.shape
    specs = [
        pl.BlockSpec((rows, depth), lambda g: (0, 0)),
        pl.BlockSpec((2, depth), lambda g: (0, 0)),
        pl.BlockSpec((depth, GROUP_WIDTH), lambda g: (0, g)),
        pl.BlockSpec((rows, 128), lambda g: (index, 0)),
        pl.BlockSpec((rows, 128), lambda g: (index, 0)),
    ]
    operands = [x, gain, weight, cosine, sine]
    aliases = {}
    if kept is not None:
        specs.extend([pl.BlockSpec(memory_space=pl.ANY)] * 2)
        aliases = {len(operands) + i: i for i in range(2)}
        operands.extend(kept)
    return pl.pallas_call(
        project_kernel,
        grid=(groups,),
        in_specs=specs,
        out_specs=[
            pl.BlockSpec((rows, depth), lambda g: (index, 0)),
            pl.BlockSpec((rows, GROUP_WIDTH), lambda g: (index, g)),
        ],
        out_shape=[
            jax.ShapeDtypeStruct((rows * count, depth), jnp.bfloat16),
            jax.ShapeDtypeStruct((rows * count, GROUP_WIDTH * groups), jnp.bfloat16),
        ],
        input_output_aliases=aliases,
        compiler_params=parameters(),
        cost_estimate=SMALL_COST,
        name="project",
    )(*operands)


def ring_offset(place, chunk, count, rows):
    return pl.multiple_of(lax.rem(place - chunk + count, count) * rows, rows)


def stack_heads(target, source):
    rows, width = source.shape
    for head in range(width // HEAD_SIZE):
        target[head * rows : (head + 1) * rows, :] = source[
            :, head * HEAD_SIZE : (head + 1) * HEAD_SIZE
        ]


def fill_bias(bias, key_docs, query_docs, earlier):
    rows = key_docs.shape[0]
    row_index = lax.broadcasted_iota(jnp.int32, (rows, rows), 0)
    column_index = lax.broadcasted_iota(jnp.int32, (rows, rows), 1)
    same = (key_docs == query_docs) & ((row_index <= column_index) | earlier)
    values = jnp.where(same, 0.0, NEGATIVE)
    for first in range(0, bias.shape[1], rows):
        bias[:, first : first + rows] = values


def forward_kernel(
    count,
    place_ref,
    own_ref,
    all_ref,
    docq_ref,
    dock_ref,
    o_ref,
    lse_ref,
    bias,
    queries,
    values_all,
    mixed,
):
    chunk = pl.program_id(1)
    place = place_ref[0]
    rows = own_ref.shape[0]
    heads = GROUP_QUERY // HEAD_SIZE
    stack_heads(queries, own_ref.at[:, :GROUP_QUERY])

    @pl.when(chunk == 0)
    def _():
        values = all_ref[:, GROUP_QUERY:].astype(jnp.float32)
        values_all[...] = values.T[HEAD_SIZE:].astype(jnp.bfloat16)

    mixed[...] = jnp.zeros_like(mixed)

    def block(j, carry):
        peaks, total = carry
        offset = ring_offset(place, j, count, rows)
        piece = pl.ds(offset, rows)
        fill_bias(bias, dock_ref[piece, :], docq_ref[...], j < chunk)
        keys = all_ref[piece, GROUP_QUERY : GROUP_QUERY + HEAD_SIZE]
        scores = dot_nt(keys, queries[...]) + bias[...]
        higher = jnp.maximum(peaks, jnp.max(scores, axis=0, keepdims=True))
        probs = jnp.exp(scores - higher)
        scale = jnp.exp(peaks - higher)
        mixed[...] = mixed[...] * scale + dot_nn(
            values_all[:, piece], probs.astype(jnp.bfloat16)
        )
        return higher, total * scale + jnp.sum(probs, axis=0, keepdims=True)

    peaks, total = lax.fori_loop(
        0,
        chunk + 1,
        block,
        (
            jnp.full((1, heads * rows), NEGATIVE, jnp.float32),
            jnp.zeros((1, heads * rows), jnp.float32),
        ),
    )
    lse_ref[:1, :] = peaks + jnp.log(total)
    result = mixed[...] / total
    for head in range(0, heads, 2):
        pair = jnp.concatenate(
            [result[:, (head + i) * rows : (head + i + 1) * rows] for i in range(2)], axis=0
        )
        o_ref[:, head * HEAD_SIZE : (head + 2) * HEAD_SIZE] = pair.T.astype(jnp.bfloat16)


def attention_forward(joint, docs, place, count, groups):
    total_rows = joint.shape[0]
    rows = total_rows // count
    stacked = rows * GROUP_QUERY // HEAD_SIZE

    def block(c, place_ref):
        return lax.rem(place_ref[0] - c + count, count)

    spec = pltpu.PrefetchScalarGridSpec(
        num_scalar_prefetch=1,
        grid=(groups, count),
        in_specs=[
            pl.BlockSpec((rows, GROUP_WIDTH), lambda g, c, p: (block(c, p), g)),
            pl.BlockSpec((total_rows, GROUP_WIDTH), lambda g, c, p: (0, g)),
            pl.BlockSpec((1, rows), lambda g, c, p: (0, block(c, p))),
            pl.BlockSpec((total_rows, 1), lambda g, c, p: (0, 0)),
        ],
        out_specs=[
            pl.BlockSpec((rows, GROUP_QUERY), lambda g, c, p: (block(c, p), g)),
            pl.BlockSpec((8, stacked), lambda g, c, p: (g, block(c, p))),
        ],
        scratch_shapes=[
            pltpu.VMEM((rows, stacked), jnp.float32),
            pltpu.VMEM((stacked, HEAD_SIZE), jnp.bfloat16),
            pltpu.VMEM((HEAD_SIZE, total_rows), jnp.bfloat16),
            pltpu.VMEM((HEAD_SIZE, stacked), jnp.float32),
        ],
    )
    return pl.pallas_call(
        functools.partial(forward_kernel, count),
        grid_spec=spec,
        out_shape=[
            jax.ShapeDtypeStruct((total_rows, GROUP_QUERY * groups), jnp.bfloat16),
            jax.ShapeDtypeStruct((8 * groups, stacked * count), jnp.float32),
        ],
        compiler_params=parameters(),
        cost_estimate=SMALL_COST,
        name="attend",
    )(place, joint, joint, docs[None, :], docs[:, None])


def backward_kernel(count, place_ref, *refs):
    own_ref, all_ref, o_ref = refs[:3]
    lse_ref, docq_ref, dock_ref, cos_ref, sin_ref = refs[3 + count : 8 + count]
    out_ref, bias, queries, grads, keys_all, values_all, sum_q, sum_k, sum_v = refs[8 + count :]
    chunk = pl.program_id(0)
    place = place_ref[0]
    rows = own_ref.shape[0]
    heads = GROUP_QUERY // HEAD_SIZE
    stack_heads(queries, own_ref.at[:, :GROUP_QUERY])
    for index in range(count):

        @pl.when(lax.rem(place - chunk + count, count) == index)
        def _():
            stack_heads(grads, refs[3 + index])

    @pl.when(chunk == 0)
    def _():
        keys_all[...] = all_ref[:, GROUP_QUERY : GROUP_QUERY + HEAD_SIZE]
        values_all[...] = all_ref[:, GROUP_QUERY + HEAD_SIZE :]
        sum_k[...] = jnp.zeros_like(sum_k)
        sum_v[...] = jnp.zeros_like(sum_v)

    sum_q[...] = jnp.zeros_like(sum_q)
    ones = jnp.ones((8, HEAD_SIZE), jnp.bfloat16)
    inner = []
    for head in range(heads):
        attended = o_ref[:, head * HEAD_SIZE : (head + 1) * HEAD_SIZE].astype(jnp.float32)
        both = attended * grads[head * rows : (head + 1) * rows, :].astype(jnp.float32)
        high = both.astype(jnp.bfloat16)
        low = (both - high.astype(jnp.float32)).astype(jnp.bfloat16)
        inner.append((dot_nt(ones, high) + dot_nt(ones, low))[:1])
    inner = jnp.concatenate(inner, axis=1)

    def block(j, carry):
        offset = ring_offset(place, j, count, rows)
        piece = pl.ds(offset, rows)
        fill_bias(bias, dock_ref[piece, :], docq_ref[...], j < chunk)
        probs = jnp.exp(dot_nt(keys_all[piece, :], queries[...]) + bias[...] - lse_ref[:1, :])
        grad_probs = dot_nt(values_all[piece, :], grads[...])
        grad_scores = (probs * (grad_probs - inner)).astype(jnp.bfloat16)
        sum_v[piece, :] += dot_nn(probs.astype(jnp.bfloat16), grads[...])
        sum_k[piece, :] += dot_nn(grad_scores, queries[...])
        sum_q[...] += dot_tn(grad_scores, keys_all[piece, :])
        return carry

    lax.fori_loop(0, chunk + 1, block, 0)
    own = pl.ds(ring_offset(place, chunk, count, rows), rows)
    for first in range(0, heads, 2):
        start = first * HEAD_SIZE
        part = jnp.concatenate(
            [sum_q[(first + i) * rows : (first + i + 1) * rows, :] for i in range(2)], axis=1
        )
        part = turned(part, cos_ref[own, :], -sin_ref[own, :], start)
        out_ref[own, start : start + 128] = (part * HEAD_SIZE ** (-0.5)).astype(jnp.bfloat16)

    @pl.when(chunk == count - 1)
    def _():
        part = jnp.concatenate([sum_k[...], sum_v[...]], axis=1)
        part = turned(part, cos_ref[...], -sin_ref[...], GROUP_QUERY)
        out_ref[:, GROUP_QUERY:] = part.astype(jnp.bfloat16)


def attention_backward(joint, attended, grads, lse, docs, cosine, sine, place, group):
    count = len(grads)
    total_rows = joint.shape[0]
    rows = total_rows // count
    stacked = rows * GROUP_QUERY // HEAD_SIZE

    def block(c, place_ref):
        return lax.rem(place_ref[0] - c + count, count)

    table = pl.BlockSpec((total_rows, 128), lambda c, p: (0, 0))
    spec = pltpu.PrefetchScalarGridSpec(
        num_scalar_prefetch=1,
        grid=(count,),
        in_specs=[
            pl.BlockSpec((rows, GROUP_WIDTH), lambda c, p: (block(c, p), group)),
            pl.BlockSpec((total_rows, GROUP_WIDTH), lambda c, p: (0, group)),
            pl.BlockSpec((rows, GROUP_QUERY), lambda c, p: (block(c, p), group)),
            *[pl.BlockSpec((rows, GROUP_QUERY), lambda c, p: (0, group))] * count,
            pl.BlockSpec((8, stacked), lambda c, p: (group, block(c, p))),
            pl.BlockSpec((1, rows), lambda c, p: (0, block(c, p))),
            pl.BlockSpec((total_rows, 1), lambda c, p: (0, 0)),
            table,
            table,
        ],
        out_specs=pl.BlockSpec((total_rows, GROUP_WIDTH), lambda c, p: (0, 0)),
        scratch_shapes=[
            pltpu.VMEM((rows, stacked), jnp.float32),
            *[pltpu.VMEM((stacked, HEAD_SIZE), jnp.bfloat16)] * 2,
            *[pltpu.VMEM((total_rows, HEAD_SIZE), jnp.bfloat16)] * 2,
            pltpu.VMEM((stacked, HEAD_SIZE), jnp.float32),
            *[pltpu.VMEM((total_rows, HEAD_SIZE), jnp.float32)] * 2,
        ],
    )
    return pl.pallas_call(
        functools.partial(backward_kernel, count),
        grid_spec=spec,
        out_shape=jax.ShapeDtypeStruct((total_rows, GROUP_WIDTH), jnp.bfloat16),
        compiler_params=parameters(),
        cost_estimate=SMALL_COST,
        name="attend_back",
    )(
        place,
        joint,
        joint,
        attended,
        *grads,
        lse,
        docs[None, :],
        docs[:, None],
        cosine,
        sine,
    )


def pack_kernel(
    groups, query_ref, key_ref, value_ref, first_ref, second_ref, joint_ref, out_ref
):
    for g in range(groups):
        start = g * GROUP_WIDTH
        columns = slice(g * HEAD_SIZE, (g + 1) * HEAD_SIZE)
        joint_ref[:, start : start + GROUP_QUERY] = query_ref[
            :, g * GROUP_QUERY : (g + 1) * GROUP_QUERY
        ]
        joint_ref[:, start + GROUP_QUERY : start + GROUP_WIDTH] = jnp.concatenate(
            [key_ref[:, columns], value_ref[:, columns]], axis=1
        )
    width = groups * GROUP_WIDTH
    out_ref[:, :width] = joint_ref[...]
    row = lax.broadcasted_iota(jnp.int32, (128, query_ref.shape[0]), 0)
    gains = jnp.where(row == 0, first_ref[...].astype(jnp.float32)[None, :], 0.0)
    gains = jnp.where(row == 1, second_ref[...].astype(jnp.float32)[None, :], gains)
    out_ref[:, width:] = gains.T.astype(jnp.bfloat16)


def pack(query, key, value, first, second, groups):
    rows = query.shape[0]
    width = groups * GROUP_WIDTH
    return pl.pallas_call(
        functools.partial(pack_kernel, groups),
        out_shape=[
            jax.ShapeDtypeStruct((rows, width), jnp.bfloat16),
            jax.ShapeDtypeStruct((rows, width + 128), jnp.bfloat16),
        ],
        compiler_params=parameters(),
        cost_estimate=SMALL_COST,
        name="pack",
    )(query, key, value, first, second)


def join_kernel(*refs):
    place = 0
    for ref in refs[:-2]:
        size = ref.shape[1]
        refs[-1][:, place : place + size] = ref[...]
        place += size


def join(parts, rest):
    rows = rest.shape[0]
    width = sum(part.shape[1] for part in parts)
    return pl.pallas_call(
        join_kernel,
        grid=(1,),
        in_specs=[pl.BlockSpec(part.shape, lambda i: (0, 0)) for part in parts]
        + [pl.BlockSpec(memory_space=pl.ANY)],
        out_specs=pl.BlockSpec((rows, width), lambda i: (0, 0)),
        out_shape=jax.ShapeDtypeStruct(rest.shape, rest.dtype),
        input_output_aliases={len(parts): 0},
        compiler_params=parameters(),
        cost_estimate=SMALL_COST,
        name="join",
    )(*parts, rest)


def transposed_kernel(count, parts, *refs):
    total = dot_nt(refs[0][...], refs[count][...])
    for index in range(1, count):
        total += dot_nt(refs[index][...], refs[count + index][...])
    rows = total.shape[0] // parts
    for index in range(parts):
        refs[2 * count + index][...] = total[index * rows : (index + 1) * rows].astype(
            jnp.bfloat16
        )


def transposed_product(xs, weight, column, parts, block=0, blocks=1):
    rows, depth = xs[0].shape
    rows //= blocks
    width = weight.shape[0]
    tile = tile_of(width)
    specs = [pl.BlockSpec((rows, depth), lambda t: (block, 0))] * len(xs)
    for index in range(len(xs)):
        specs.append(pl.BlockSpec((tile, depth), lambda t, index=index: (t, column + index)))
    part = (rows // parts, width)
    return pl.pallas_call(
        functools.partial(transposed_kernel, len(xs), parts),
        grid=(width // tile,),
        in_specs=specs,
        out_specs=[pl.BlockSpec((part[0], tile), lambda t: (0, t))] * parts,
        out_shape=[jax.ShapeDtypeStruct(part, jnp.bfloat16)] * parts,
        compiler_params=parameters(),
        cost_estimate=SMALL_COST,
        name="transposed",
    )(*xs, *[weight] * len(xs))


def heads_kernel(count, *refs):
    parts = refs[:count]
    weight_ref = refs[count]
    tokens = refs[count + 1 : -2]
    out_ref, local_ref = refs[-2:]
    step = pl.program_id(0)
    width = parts[0].shape[1]

    @pl.when(step == 0)
    def _():
        for j in range(count):
            local_ref[:, j * width : (j + 1) * width] = parts[j][...]

    for j in range(count):
        term = dot_nt(parts[j][...], weight_ref[:, j * width : (j + 1) * width])
        if j == 0:
            out_ref[...] = term
        else:
            out_ref[...] += term
    for index in range(len(tokens)):

        @pl.when(step == index)
        def _():
            out_ref[...] += tokens[index][...].astype(jnp.float32)


def heads_product(parts, weight, tokens):
    blocks = len(tokens)
    rows, width = tokens[0].shape
    depth = parts[0].shape[1]
    specs = [
        pl.BlockSpec((rows, depth), lambda i, j=j: (lax.rem(i + j, blocks), 0))
        for j in range(len(parts))
    ]
    whole = pl.BlockSpec((rows, width), lambda i: (0, 0), pipeline_mode=pl.Buffered(1))
    return pl.pallas_call(
        functools.partial(heads_kernel, len(parts)),
        grid=(blocks,),
        in_specs=[
            *specs,
            pl.BlockSpec(
                (width, depth * len(parts)), lambda i: (0, 0), pipeline_mode=pl.Buffered(1)
            ),
            *[whole] * blocks,
        ],
        out_specs=[
            pl.BlockSpec((rows, width), lambda i: (i, 0)),
            pl.BlockSpec((rows, depth * len(parts)), lambda i: (0, 0)),
        ],
        out_shape=[
            jax.ShapeDtypeStruct((rows * blocks, width), jnp.float32),
            jax.ShapeDtypeStruct((rows, depth * len(parts)), jnp.bfloat16),
        ],
        compiler_params=parameters(),
        cost_estimate=SMALL_COST,
        name="heads_product",
    )(*parts, weight, *tokens)


def attended_kernel(
    partial_ref, last_ref, weight_ref, gain_ref, hidden_ref, normed_ref, local_ref
):
    values = partial_ref[...] + dot_nt(last_ref[...], weight_ref[...])

    @pl.when(pl.program_id(0) == 0)
    def _():
        hidden_ref[...] = values
        local_ref[...] = last_ref[...]

    inverse = lax.rsqrt(jnp.mean(values * values, axis=-1, keepdims=True) + EPSILON)
    normed_ref[...] = (values * inverse * gain_ref[1:, :]).astype(jnp.bfloat16)


def after_attention(partial, last, weight, gain, count):
    total_rows, width = partial.shape
    rows = total_rows // count
    depth = last.shape[1]
    return pl.pallas_call(
        attended_kernel,
        grid=(count,),
        in_specs=[
            pl.BlockSpec((rows, width), lambda i: (i, 0)),
            pl.BlockSpec((rows, depth), lambda i: (lax.rem(i + count - 1, count), 0)),
            pl.BlockSpec((width, depth), lambda i: (0, count - 1)),
            pl.BlockSpec((2, width), lambda i: (0, 0)),
        ],
        out_specs=[
            pl.BlockSpec((rows, width), lambda i: (0, 0)),
            pl.BlockSpec((rows, width), lambda i: (lax.rem(i + count - 1, count), 0)),
            pl.BlockSpec((rows, depth), lambda i: (0, 0)),
        ],
        out_shape=[
            jax.ShapeDtypeStruct((rows, width), jnp.float32),
            jax.ShapeDtypeStruct((total_rows, width), jnp.bfloat16),
            jax.ShapeDtypeStruct((rows, depth), jnp.bfloat16),
        ],
        compiler_params=parameters(),
        cost_estimate=SMALL_COST,
        name="after_attention",
    )(partial, last, weight, gain)


def up_kernel(x_ref, gate_ref, up_ref, *refs):
    a_ref, u_ref, g_ref = refs[-3:]
    gate = dot_nn(x_ref[...], gate_ref[...])
    up = dot_nn(x_ref[...], up_ref[...])
    a_ref[...] = gate.astype(jnp.bfloat16)
    u_ref[...] = up.astype(jnp.bfloat16)
    g_ref[...] = (gate * jax.nn.sigmoid(gate) * up).astype(jnp.bfloat16)


def up_chunk(x, weight, kept, index, count):
    total_rows, depth = x.shape
    rows = total_rows // count
    hidden = (weight.shape[1] - depth) // 2
    tile = tile_of(hidden)
    tiles = hidden // tile
    start = depth // tile
    specs = [
        pl.BlockSpec((rows, depth), lambda t: (index, 0)),
        pl.BlockSpec((depth, tile), lambda t: (0, start + t)),
        pl.BlockSpec((depth, tile), lambda t: (0, start + tiles + t)),
    ]
    operands = [x, weight, weight]
    aliases = {}
    if kept is not None:
        specs.extend([pl.BlockSpec(memory_space=pl.ANY)] * 3)
        aliases = {len(operands) + i: i for i in range(3)}
        operands.extend(kept)
    return pl.pallas_call(
        up_kernel,
        grid=(tiles,),
        in_specs=specs,
        out_specs=[pl.BlockSpec((rows, tile), lambda t: (index, t))] * 3,
        out_shape=[jax.ShapeDtypeStruct((total_rows, hidden), jnp.bfloat16)] * 3,
        input_output_aliases=aliases,
        compiler_params=parameters(),
        cost_estimate=SMALL_COST,
        name="up_chunk",
    )(*operands)


def down_kernel(parts, tiles, *refs):
    down_ref, a_ref, u_ref, gate_ref, up_ref = refs[parts : parts + 5]
    da_ref, du_ref = refs[-5 - parts : -3 - parts]
    dx_refs = refs[-3 - parts : -3]
    da_kept, du_kept, e_out = refs[-3:]
    step = pl.program_id(0)

    @pl.when(step == 0)
    def _():
        rows = refs[0].shape[0]
        for index in range(parts):
            e_out[index * rows : (index + 1) * rows, :] = refs[index][...]

    @pl.when(step < tiles)
    def _():
        grad = dot_nn(e_out[...], down_ref[...])
        gate = a_ref[...].astype(jnp.float32)
        up = u_ref[...].astype(jnp.float32)
        sigmoid = jax.nn.sigmoid(gate)
        da = (grad * up * sigmoid * (1.0 + gate * (1.0 - sigmoid))).astype(jnp.bfloat16)
        du = (grad * gate * sigmoid).astype(jnp.bfloat16)
        da_ref[...] = da
        du_ref[...] = du
        tile = da.shape[1]
        for index in range(tiles):

            @pl.when(step == index)
            def _():
                da_kept[:, index * tile : (index + 1) * tile] = da
                du_kept[:, index * tile : (index + 1) * tile] = du

    @pl.when(step >= tiles)
    def _():
        total = dot_nt(da_kept[...], gate_ref[...]) + dot_nt(du_kept[...], up_ref[...])
        rows = total.shape[0] // parts
        for index in range(parts):
            dx_refs[index][...] = total[index * rows : (index + 1) * rows].astype(jnp.bfloat16)


def down_chunk(es, a, u, down_weight, weight, kept, index, count):
    depth, hidden = down_weight.shape
    rows = len(es) * es[0].shape[0]
    start = depth // hidden
    tile = tile_of(hidden)
    tiles = hidden // tile
    row_tile = tile_of(depth)

    def column(t):
        return jnp.minimum(t, tiles - 1)

    def row(t):
        return jnp.maximum(t - tiles, 0)

    specs = [pl.BlockSpec(es[0].shape, lambda t: (0, 0))] * len(es) + [
        pl.BlockSpec((depth, tile), lambda t: (0, column(t))),
        pl.BlockSpec((rows, tile), lambda t: (index, column(t))),
        pl.BlockSpec((rows, tile), lambda t: (index, column(t))),
        pl.BlockSpec((row_tile, hidden), lambda t: (row(t), start)),
        pl.BlockSpec((row_tile, hidden), lambda t: (row(t), start + 1)),
    ]
    operands = [*es, down_weight, a, u, weight, weight]
    part = es[0].shape
    shapes = [
        jax.ShapeDtypeStruct((rows * count, hidden), jnp.bfloat16),
        jax.ShapeDtypeStruct((rows * count, hidden), jnp.bfloat16),
        *[jax.ShapeDtypeStruct(part, jnp.bfloat16)] * len(es),
    ]
    aliases = {}
    if kept is not None:
        specs.extend([pl.BlockSpec(memory_space=pl.ANY)] * 2)
        aliases = {len(operands) + i: i for i in range(2)}
        operands.extend(kept)
    result = pl.pallas_call(
        functools.partial(down_kernel, len(es), tiles),
        grid=(tiles + depth // row_tile,),
        in_specs=specs,
        out_specs=[
            pl.BlockSpec((rows, tile), lambda t: (index, column(t))),
            pl.BlockSpec((rows, tile), lambda t: (index, column(t))),
            *[pl.BlockSpec((part[0], row_tile), lambda t: (0, row(t)))] * len(es),
        ],
        out_shape=shapes,
        input_output_aliases=aliases,
        scratch_shapes=[
            pltpu.VMEM((rows, hidden), jnp.bfloat16),
            pltpu.VMEM((rows, hidden), jnp.bfloat16),
            pltpu.VMEM((rows, depth), jnp.bfloat16),
        ],
        compiler_params=parameters(),
        cost_estimate=SMALL_COST,
        name="down_chunk",
    )(*operands)
    return result[:2], list(result[2:])


def weight_kernel(counts, blocks, split, place_ref, *refs):
    step = pl.program_id(0)
    total_refs = sum(parts + widths for parts, widths in counts)
    received = refs[total_refs] if len(refs) > total_refs + 1 else None
    place = 0
    column = 0
    for parts, widths in counts:
        x = refs[place][...]
        if parts > 1:
            x = jnp.concatenate([ref[...] for ref in refs[place : place + parts]], axis=0)
        x = x.T
        for y_ref in refs[place + parts : place + parts + widths]:
            width = y_ref.shape[1]
            cuts = set(range(0, width, 1024)) | {width}
            if column < split < column + width and split:
                cuts.add(split - column)
            cuts = sorted(cuts)
            for first, last in zip(cuts[:-1], cuts[1:]):
                total = dot_nn(x, y_ref[:, first:last])
                start, end = column + first, column + last
                if received is None:
                    refs[-1][:, start:end] = total.astype(jnp.bfloat16)
                    continue
                total += received[:, start:end].astype(jnp.float32)
                total = total.astype(jnp.bfloat16)
                if split == 0:
                    refs[-1][:, start:end] = total
                    continue
                low = start < split
                keep = step < blocks // 2 if low else lax.rem(step, 2) == 0
                keep_ref, send_ref = refs[-4:-2] if low else refs[-2:]
                columns = slice(start, end) if low else slice(start - split, end - split)

                @pl.when(keep)
                def _():
                    keep_ref[:, columns] = total

                @pl.when(jnp.logical_not(keep))
                def _():
                    send_ref[:, columns] = total

            column += width
        place += parts + widths


def weight_product(pairs, place, count, received, ordered=False):
    depth = pairs[0][0][0].shape[1]
    blocks = count // 2
    tile = depth // count
    total = sum(y.shape[1] for _, ys in pairs for y in ys)
    split = 0 if ordered else -(-total // 256) * 128
    side = 1 if received is None else 0

    def source(t, p):
        if ordered:
            return 2 * t + lax.rem(p[0] + side, 2)
        return lax.bitwise_xor(p[0], 2 * t + side)

    whole = pl.BlockSpec((tile, total), lambda t, p: (t, 0))
    if received is None or ordered:
        out_specs = whole
        out_shape = jax.ShapeDtypeStruct((depth // 2, total), jnp.bfloat16)
    else:
        half = blocks // 2
        out_specs = [
            pl.BlockSpec((tile, split), lambda t, p: (jnp.minimum(t, half - 1), 0)),
            pl.BlockSpec((tile, split), lambda t, p: (jnp.maximum(t - half, 0), 0)),
            pl.BlockSpec((tile, total - split), lambda t, p: (t // 2, 0)),
            pl.BlockSpec((tile, total - split), lambda t, p: (t // 2, 0)),
        ]
        out_shape = [
            jax.ShapeDtypeStruct((depth // 4, width), jnp.bfloat16)
            for width in (split, split, total - split, total - split)
        ]
    specs = []
    operands = []
    for xs, ys in pairs:
        for x in xs:
            specs.append(pl.BlockSpec((x.shape[0], tile), lambda t, p: (0, source(t, p))))
        specs += [
            pl.BlockSpec(y.shape, lambda t, p: (0, 0), pipeline_mode=pl.Buffered(1)) for y in ys
        ]
        operands.extend([*xs, *ys])
    if received is not None:
        specs.append(whole)
        operands.append(received)
    return pl.pallas_call(
        functools.partial(
            weight_kernel, [(len(xs), len(ys)) for xs, ys in pairs], blocks, split
        ),
        grid_spec=pltpu.PrefetchScalarGridSpec(
            num_scalar_prefetch=1, grid=(blocks,), in_specs=specs, out_specs=out_specs
        ),
        out_shape=out_shape,
        compiler_params=parameters(),
        cost_estimate=SMALL_COST,
        name="weight_product",
    )(place, *operands)


def fold_kernel(counts, *refs):
    outs = refs[sum(counts) :]
    place = 0
    row = 0
    for index, count in enumerate(counts):
        total = refs[place][...].astype(jnp.float32)
        for ref in refs[place + 1 : place + count]:
            total += ref[...].astype(jnp.float32)
        out = outs[index % 2]
        rows = total.shape[0]
        out[row : row + rows, :] = total.astype(jnp.bfloat16)
        row += rows * (index % 2)
        place += count


def fold(sums, rows):
    counts = [len(terms) for pair in sums for terms in pair]
    values = [value for pair in sums for terms in pair for value in terms]
    widths = [terms[0].shape[1] for terms in sums[0]]
    steps = 2 if all(width % 256 == 0 for width in widths) else 1
    return pl.pallas_call(
        functools.partial(fold_kernel, counts),
        grid=(steps,),
        in_specs=[
            pl.BlockSpec((rows, value.shape[1] // steps), lambda t: (1, t)) for value in values
        ],
        out_specs=[
            pl.BlockSpec((rows * len(sums), width // steps), lambda t: (0, t))
            for width in widths
        ],
        out_shape=[
            jax.ShapeDtypeStruct((rows * len(sums), width), jnp.bfloat16) for width in widths
        ],
        compiler_params=parameters(),
        cost_estimate=SMALL_COST,
        name="fold",
    )(*values)


def residual_kernel(parts, e_ref, hidden_ref, first_ref, second_ref, gain_ref, weight_ref, *refs):
    dh_ref, dz_ref = refs[:2]
    dh, dz = refs[-2:]
    step = pl.program_id(0)
    tile = weight_ref.shape[1]

    @pl.when(step == 0)
    def _():
        values = hidden_ref[...]
        inverse = lax.rsqrt(jnp.mean(values * values, axis=-1, keepdims=True) + EPSILON)
        scaled = values * inverse
        grad = first_ref[...].astype(jnp.float32) + second_ref[...].astype(jnp.float32)
        grad = grad * gain_ref[1:, :]
        projection = jnp.mean(grad * scaled, axis=-1, keepdims=True)
        total = e_ref[...].astype(jnp.float32) + inverse * (grad - scaled * projection)
        dh[...] = total
        dz[...] = total.astype(jnp.bfloat16)

    result = dot_nn(dz[...], weight_ref[...]).astype(jnp.bfloat16)
    for index in range(parts):

        @pl.when(step == index)
        def _():
            columns = slice(index * tile, (index + 1) * tile)
            dh_ref[...] = dh[:, columns]
            dz_ref[...] = dz[:, columns]
            refs[2 + index][...] = result


def residual_gradient(e, hidden_res, first, second, gain, weight, parts):
    rows, depth = e.shape
    tile = depth // parts
    whole = pl.BlockSpec((rows, depth), lambda t: (0, 0))
    column = pl.BlockSpec((rows, tile), lambda t: (0, t))
    result = pl.pallas_call(
        functools.partial(residual_kernel, parts),
        grid=(parts,),
        in_specs=[
            whole,
            whole,
            whole,
            whole,
            pl.BlockSpec((2, depth), lambda t: (0, 0)),
            pl.BlockSpec((depth, tile), lambda t: (0, t)),
        ],
        out_specs=[column, column] + [pl.BlockSpec((rows, tile), lambda t: (0, 0))] * parts,
        out_shape=[
            jax.ShapeDtypeStruct((rows, depth), jnp.float32),
            jax.ShapeDtypeStruct((rows, depth), jnp.bfloat16),
            *[jax.ShapeDtypeStruct((rows, tile), jnp.bfloat16)] * parts,
        ],
        scratch_shapes=[
            pltpu.VMEM((rows, depth), jnp.float32),
            pltpu.VMEM((rows, depth), jnp.bfloat16),
        ],
        compiler_params=parameters(),
        cost_estimate=SMALL_COST,
        name="residual_gradient",
    )(e, hidden_res, first, second, gain, weight)
    return result[0], result[1], list(result[2:])


def tie(value, *others):
    return lax.optimization_barrier((value, others))[0]


def together(*values):
    return lax.optimization_barrier(values)


def add(first, second):
    return (first.astype(jnp.float32) + second.astype(jnp.float32)).astype(jnp.bfloat16)


class Mover:
    def __init__(self):
        self.dp_count = lax.axis_size("dp")
        self.ring = lax.axis_size("tensor")
        self.steps = []
        step = 2
        while step < self.dp_count:
            self.steps.append(step)
            step *= 2

    def swap(self, value, step):
        return lax.ppermute(value, "dp", [(i, i ^ step) for i in range(self.dp_count)])

    def gather(self, shard):
        return lax.all_gather(shard, "dp", axis=0, tiled=True)


    def send(self, pieces, level):
        orders = (self.steps[::-1], self.steps[:1] + self.steps[:0:-1])
        return [self.swap(piece, order[level]) for piece, order in zip(pieces, orders)]

    def begin(self, pieces):
        moved = self.send([pieces[1], pieces[3]], 0)
        return [[pieces[0], moved[0]], [pieces[2], moved[1]]]

    def fold(self, sums, level=1):
        return fold(sums, sums[0][0][0].shape[0] >> level)

    def advance(self, sums, folded):
        level = 1
        while True:
            moved = self.send(folded, level)
            level += 1
            if level == len(self.steps):
                return sums, moved
            rows = moved[0].shape[0] // len(sums)
            sums = [
                [
                    terms + [part[index * rows : (index + 1) * rows]]
                    for terms, part in zip(pair, moved)
                ]
                for index, pair in enumerate(sums)
            ]
            folded = self.fold(sums, level)

    def advance_all(self, sums):
        widths = {pair[0][0].shape[1] for pair in sums}
        parts = [sums] if len(widths) == 1 else [[pair] for pair in sums]
        return [self.advance(part, self.fold(part)) for part in parts]

    def scatter(self, total):
        groups = [list(range(core, self.dp_count, 2)) for core in range(2)]
        return lax.psum_scatter(
            total, "dp", scatter_dimension=0, tiled=True, axis_index_groups=groups
        )

    def hop(self, value, shift=1):
        return lax.ppermute(
            value, "tensor", [(i, (i + shift) % self.ring) for i in range(self.ring)]
        )

    def spread(self, value):
        ring = self.ring
        return [value] + [
            lax.ppermute(value, "tensor", [(i, (i - j) % ring) for i in range(ring)])
            for j in range(1, ring)
        ]

    def collect(self, parts):
        ring = self.ring
        total = parts[0]
        for j in range(1, ring):
            moved = lax.ppermute(
                parts[j].astype(jnp.bfloat16), "tensor", [(i, (i + j) % ring) for i in range(ring)]
            )
            total = total + moved.astype(jnp.float32)
        return total

    def exchange(self, parts):
        ring = self.ring
        return [parts[0]] + [
            lax.ppermute(parts[j], "tensor", [(i, (i + j) % ring) for i in range(ring)])
            for j in range(1, ring)
        ]


def totals_of(sums, moved):
    rows = moved[0].shape[0] // len(sums)
    result = []
    for index, pair in enumerate(sums):
        halves = []
        for terms, last in zip(pair, moved):
            total = last[index * rows : (index + 1) * rows].astype(jnp.float32)
            for term in terms:
                total = total + term[:rows].astype(jnp.float32)
            halves.append(total)
        result.append(jnp.concatenate(halves, axis=1))
    return result


def back_norm(grad_normed, scaled, inverse, scale_row):
    grad_scaled = grad_normed * scale_row
    projection = jnp.mean(grad_scaled * scaled, axis=-1, keepdims=True)
    return inverse * (grad_scaled - scaled * projection)


def per_device(
    tokens,
    seq_lengths,
    attention_gain,
    query_matrix,
    key_matrix,
    value_matrix,
    output_weight,
    feedforward_gain,
    gate_weight,
    up_weight,
    down_weight,
    cotangent,
):
    mover = Mover()
    dp_count = mover.dp_count
    ring = mover.ring
    dp_place = lax.axis_index("dp").astype(jnp.int32).reshape(1)
    ring_place = lax.axis_index("tensor")
    place = ring_place.astype(jnp.int32).reshape(1)
    _, local_rows, model_width = tokens.shape
    complete_rows = local_rows * ring
    hidden = gate_weight.shape[1]
    groups = key_matrix.shape[1] // HEAD_SIZE
    joint_width = groups * GROUP_WIDTH
    f32 = jnp.float32
    b16 = jnp.bfloat16

    doc_ids, positions = layout(seq_lengths, complete_rows)
    row_index = jnp.arange(complete_rows, dtype=jnp.int32)
    doc_ids = jnp.where(doc_ids[0] < PIECES, doc_ids[0], PIECES + row_index)

    def to_relative(values):
        view = values.reshape((ring, local_rows) + values.shape[1:])
        return jnp.roll(view, -(ring_place + 1), axis=0)[::-1].reshape(values.shape)

    doc_ids = to_relative(doc_ids)
    cosine, sine = rope_tables(to_relative(positions[0]), HEAD_SIZE)
    cosine_table = jnp.tile(cosine, (1, 128 // cosine.shape[1]))
    sine_table = jnp.tile(jnp.concatenate([-sine, sine], axis=1), (1, 128 // HEAD_SIZE))

    joint_matrix, packed = pack(
        query_matrix, key_matrix, value_matrix, attention_gain, feedforward_gain, groups
    )
    joint_full = mover.gather(packed)
    output_parts = mover.spread(output_weight.T)
    up_shard = jnp.pad(
        jnp.concatenate([gate_weight, up_weight], axis=1), ((0, 0), (model_width, 0))
    )
    output_parts, cosine_table, sine_table, doc_ids, up_shard, down_shard = together(
        output_parts, cosine_table, sine_table, doc_ids, up_shard, down_weight.T
    )
    local_tokens = tokens[0]
    token_chunks = [local_tokens, mover.hop(local_tokens)]
    up_shard = join(output_parts, up_shard)
    up_full = mover.gather(up_shard)
    down_full = mover.gather(tie(down_shard, up_shard))
    gains = joint_full[:, joint_width : joint_width + 2].T.astype(f32)

    def projection(kept, index):
        return project(
            token_chunks[index],
            gains,
            joint_full,
            cosine_table,
            sine_table,
            kept,
            index,
            ring,
            groups,
        )

    kept = projection(None, 0)
    for j in range(1, ring):
        token_chunks[j], kept, gains = together(token_chunks[j], kept, gains)
        if j + 1 < ring:
            token_chunks.append(mover.hop(token_chunks[j]))
        else:
            local_cotangent = tie(cotangent[0], token_chunks[j])
            moved = mover.hop(local_cotangent)
        kept = projection(kept, j)
    normed_one, joint = kept
    attended, totals = attention_forward(joint, doc_ids, place, ring, groups)
    moved, attended = together(moved, attended)
    cotangent_chunks = [local_cotangent, moved]
    attended_parts = [attended]
    while len(attended_parts) < ring:
        part = mover.hop(attended_parts[-1], -1)
        if len(attended_parts) == ring - 1:
            partial, attended_local = heads_product(
                tie(attended_parts, attended_parts[-1]), up_full, token_chunks
            )
            part, partial, attended_local = together(part, partial, attended_local)
        attended_parts.append(part)
    moved, last = together(moved, attended_parts[-1])

    pairs = ring // 2
    moved = mover.hop(moved)
    hidden_res, normed_two, attended_last = after_attention(partial, last, up_full, gains, ring)
    upward = up_chunk(normed_two, up_full, None, 0, pairs)
    downward = None
    grads = []

    def chunks_of(pair):
        return [cotangent_chunks[(2 * pair + i) % ring] for i in (1, 2)]

    def lower(pair, kept):
        return down_chunk(
            chunks_of(pair), upward[0], upward[1], down_full, up_full, kept, pair, pairs
        )

    for j in range(2, ring):
        if j > 2:
            moved = mover.hop(moved)
            if j % 2:
                downward, parts = lower((j - 3) // 2, downward)
                grads.extend(parts)
            else:
                upward = up_chunk(normed_two, up_full, upward, j // 2 - 1, pairs)
        moved, upward, downward, grads = together(moved, upward, downward, grads)
        cotangent_chunks.append(moved)

    def weights(xs, ys, received=None):
        return weight_product([(xs, ys)], dp_place, dp_count, received)

    ordered = cotangent_chunks[1:] + cotangent_chunks[:1]
    total = grads[0]
    moved = mover.hop(total)
    upward = up_chunk(tie(normed_two, total), up_full, upward, pairs - 1, pairs)
    product = upward[2]
    down_part = weight_product([(ordered, [product])], dp_place, dp_count, None, True)
    moved, upward, down_part = together(moved, upward, down_part)
    down_part = mover.swap(down_part, 1)
    for j in range(2, ring):
        total = add(moved, grads[j - 1])
        moved = mover.hop(total)
        if j == 2:
            downward, parts = lower(pairs - 1, tie(downward, total))
            grads.extend(parts)
            moved, downward, grads = together(moved, downward, grads)
            grad_gate, grad_up = downward
        if j == 3:
            gate_part = weights([tie(normed_two, total)], [grad_gate])
            branch = transposed_product(
                [tie(product, gate_part)], down_full, 0, ring // 2, 0, 2
            )
            down_part = weight_product(
                [(tie(ordered, branch), [product])], dp_place, dp_count, down_part, True
            )
            moved, gate_part, branch, down_part = together(moved, gate_part, branch, down_part)
    gate_part = mover.swap(gate_part, 1)
    down_out = mover.scatter(down_part)
    grad_hidden, grad_branch, grad_parts = residual_gradient(
        local_cotangent, hidden_res, moved, grads[-1], gains, up_full, ring
    )
    grad_hidden, grad_branch, grad_parts, gate_part = together(
        grad_hidden, grad_branch, grad_parts, gate_part
    )

    grad_parts = mover.exchange(grad_parts)
    output_part = weights([grad_branch], [attended_local, attended_last])
    gate_part = weights([tie(normed_two, output_part)], [grad_gate], gate_part)
    grad_parts, output_part, gate_part = together(grad_parts, output_part, gate_part)
    grad_joint = []
    sent = 0
    moved = branch[0]
    for group in range(groups):
        moved = mover.hop(moved)
        sent += 1
        if group == 0:
            output_part = mover.swap(output_part, 1)
        else:
            output_part = mover.begin(output_part)
        grad_joint.append(
            attention_backward(
                joint,
                attended,
                tie(grad_parts, grad_joint),
                totals,
                doc_ids,
                cosine_table,
                sine_table,
                place,
                group,
            )
        )
        if group == 0:
            output_part = weights(
                [tie(grad_branch, grad_joint)], [attended_local, attended_last], output_part
            )
        if group + 1 == groups:
            grads = transposed_product(grad_joint, joint_full, 0, ring)
        moved, grad_joint, grads, output_part, down_out = together(
            moved, grad_joint, grads, output_part, down_out
        )
        if group + 1 < groups:
            moved = add(moved, branch[sent])
    if groups == 1:
        output_part = mover.begin(output_part)
    branch_moved = moved
    moved = grads[0]

    def last_weights(total, received):
        return weight_product(
            [([tie(normed_two, total)], [grad_up]), ([normed_one], grad_joint)],
            dp_place,
            dp_count,
            received,
        )

    for j in range(1, ring):
        total = grads[1] if j == 1 else add(moved, grads[j])
        moved = mover.hop(total)
        if j == 1:
            gate_part = mover.begin(gate_part)
            last_part = last_weights(total, None)
            branch = branch + transposed_product(
                [tie(product, last_part)], down_full, 0, ring // 2, 1, 2
            )
            next_branch = add(branch_moved, branch[sent])
            moved, last_part, branch, output_part, gate_part, next_branch = together(
                moved, last_part, branch, output_part, gate_part, next_branch
            )
        if j == 2:
            both_parts = tie([output_part, gate_part], total)
            both_parts = mover.advance_all(both_parts)
            last_part = last_weights(total, mover.swap(last_part, 1))
            moved, _, both_parts = together(moved, last_part, both_parts)
            down_out = tie(down_out, both_parts)
        if j == 3:
            last_part = mover.begin(last_part)
            branch_moved = mover.hop(tie(next_branch, total))
            sent += 1
            output_out, gate_out = [total for part in both_parts for total in totals_of(*part)]
            output_out = jnp.split(output_out, ring, axis=1)
            moved, last_part, output_out = together(moved, last_part, output_out)
    folded, output_out = together(mover.fold([last_part]), output_out)
    last_part = mover.advance([last_part], folded)
    output_out = mover.collect(output_out[:-1] + [tie(output_out[-1], last_part[1][1])]).T
    scaled_one, inverse_one = norm_rows(local_tokens.astype(f32))
    local_one = moved.astype(f32) + grads[0].astype(f32)
    input_gradient = grad_hidden + back_norm(local_one, scaled_one, inverse_one, gains[:1])
    branch_moved, last_part = together(branch_moved, last_part)
    for j in range(sent, ring - 1):
        branch_moved = mover.hop(add(branch_moved, branch[j]))
    block_output = (
        hidden_res + (branch_moved.astype(f32) + branch[-1].astype(f32))
    ).astype(b16)
    last_out = totals_of(*last_part)[0]
    up_out, joint_out = last_out[:, :hidden], last_out[:, hidden:]

    sums = jnp.stack(
        [
            jnp.sum(joint_out * joint_matrix.astype(f32), axis=1) / attention_gain.astype(f32),
            jnp.sum(gate_out * gate_weight.astype(f32) + up_out * up_weight.astype(f32), axis=1)
            / feedforward_gain.astype(f32),
        ]
    )
    gain_out = sums
    for shift in range(1, ring):
        gain_out = gain_out + tie(
            lax.ppermute(sums, "tensor", [(i, (i + shift) % ring) for i in range(ring)]),
            output_out,
        )

    def ungrouped(first, width):
        return jnp.concatenate(
            [
                joint_out[:, g * GROUP_WIDTH + first : g * GROUP_WIDTH + first + width]
                for g in range(groups)
            ],
            axis=1,
        )

    return (
        block_output[None],
        input_gradient[None],
        gain_out[0],
        ungrouped(0, GROUP_QUERY),
        ungrouped(GROUP_QUERY, HEAD_SIZE),
        ungrouped(GROUP_QUERY + HEAD_SIZE, HEAD_SIZE),
        output_out,
        gain_out[1],
        gate_out,
        up_out,
        down_out.astype(f32).T,
    )


def solution(mesh):
    return jax.shard_map(
        per_device,
        mesh=mesh,
        in_specs=(
            P("dp", "tensor", None),
            P("dp", None),
            P("dp"),
            P("dp", "tensor"),
            P("dp", "tensor"),
            P("dp", "tensor"),
            P("tensor", "dp"),
            P("dp"),
            P("dp", "tensor"),
            P("dp", "tensor"),
            P("tensor", "dp"),
            P("dp", "tensor", None),
        ),
        out_specs=(
            P("dp", "tensor", None),
            P("dp", "tensor", None),
            P("dp"),
            P("dp", "tensor"),
            P("dp", "tensor"),
            P("dp", "tensor"),
            P("tensor", "dp"),
            P("dp"),
            P("dp", "tensor"),
            P("dp", "tensor"),
            P("tensor", "dp"),
        ),
        check_vma=False,
    )
```
